32 devices in a mesh: shard: 4 (over y, x), replica: 8 (over z, core).
Axes of the slice: x: 2, y: 2, z: 4, core: 2. Of those that a mesh axis runs over, the one named last changes fastest.
Arguments:
- tokens: bfloat16 [2, 8, 1024, 2048], P(None, 'replica', 'shard'), may hold values from -6 to 6
- gain_attn: bfloat16 [2048], P('shard'), may hold values from 0.099609375 to 1.8984375
- w_query: bfloat16 [2048, 2048], P('shard'), may hold values from -0.5 to 0.5
- w_key: bfloat16 [512, 2048], P('shard'), may hold values from -0.5 to 0.5
- w_value: bfloat16 [512, 2048], P('shard'), may hold values from -0.125 to 0.125
- w_out: bfloat16 [2048, 2048], P('shard'), may hold values from -2 to 2
- gain_ff: bfloat16 [2048], P('shard'), may hold values from 0.099609375 to 1.8984375
- w_gate: bfloat16 [8192, 2048], P('shard'), may hold values from -0.125 to 0.125
- w_up: bfloat16 [8192, 2048], P('shard'), may hold values from -0.125 to 0.125
- w_down: bfloat16 [8192, 2048], P('shard'), may hold values from -0.25 to 0.25
- cotangent: bfloat16 [2, 8, 1024, 2048], P(None, 'replica', 'shard'), may hold values from -6 to 6
- segment_ids: int32 [2, 8, 1024], P(None, 'replica', 'shard'), may hold values from 0 to 12, as said below
- parents: int32 [2, 8, 13], P(None, 'replica'), may hold values from 0 to 4, as said below
Outputs:
- output: bfloat16 [2, 8, 1024, 2048], P(None, 'replica', 'shard')
- input_grad: float32 [2, 8, 1024, 2048], P(None, 'replica', 'shard')
- grad_gain_attn: float32 [2048], P('shard')
- grad_query: float32 [2048, 2048], P('shard')
- grad_key: float32 [512, 2048], P('shard')
- grad_value: float32 [512, 2048], P('shard')
- grad_out: float32 [2048, 2048], P('shard')
- grad_gain_ff: float32 [2048], P('shard')
- grad_gate: float32 [8192, 2048], P('shard')
- grad_up: float32 [8192, 2048], P('shard')
- grad_down: float32 [8192, 2048], P('shard')
The draws below stay inside these ranges and needn't reach their ends.
Inputs may be any that keep to these rules, and one draw needn't show every extreme that they name: `segment_ids`: segment numbers never fall along a tree, begin at 0 (the trunk), and each of the 13 segments holds one token or more. `parents`: segment 0 is its own parent; segments 1 to 4 are children of segment 0; each later segment is a child of one of segments 1 to 4, and every one of those has a child.
All inputs are finite; a program needn't handle non-finite values.
Results may differ from the reference program's by a relative error of at most 0.02.
Values may be sent and summed in bfloat16 or wider, within the bound.
A program may use at most 384 MiB of HBM per device.

```python
import math
import jax
import jax.numpy as jnp
from jax import lax

D = 2048
HEADS = 32
KV_HEADS = 8
HEAD_DIM = 64
FF = 8192
KV = 512
TREE = 1024
MB = 2
TREES = 8
NSEG = 13
NBRANCH = 4


def draw_segment_ids(key, part):
    key = jax.random.fold_in(key, 11)
    count = MB * TREES
    key_trunk, key_weights = jax.random.split(key)
    trunk = TREE // 4 + jax.random.randint(key_trunk, (count,), 0, TREE // 4 + 1, dtype=jnp.int32)
    weights = jax.random.randint(key_weights, (count, NSEG - 1), 1, 5, dtype=jnp.int32)
    rest = TREE - trunk
    spare = rest - (NSEG - 1)
    lengths = 1 + spare[:, None] * weights // jnp.sum(weights, axis=1, keepdims=True)
    lengths = lengths.at[:, -1].add(rest - jnp.sum(lengths, axis=1))
    lengths = jnp.concatenate([trunk[:, None], lengths], axis=1)
    ends = jnp.cumsum(lengths, axis=1)
    places = jnp.arange(TREE, dtype=jnp.int32)
    segments = jnp.sum((places[None, :, None] >= ends[:, None, :NSEG - 1]).astype(jnp.int32), axis=2)
    return segments.reshape(MB, TREES, TREE).astype(jnp.int32)


def draw_parents(key, part):
    key = jax.random.fold_in(key, 23)
    count = MB * TREES
    key_order, key_rest = jax.random.split(key)
    scores = jax.random.randint(key_order, (count, NBRANCH), 0, 1000, dtype=jnp.int32) * NBRANCH + jnp.arange(NBRANCH, dtype=jnp.int32)[None, :]
    first_leaves = 1 + jnp.argsort(scores, axis=1).astype(jnp.int32)
    other_leaves = jax.random.randint(key_rest, (count, NSEG - 1 - 2 * NBRANCH), 1, NBRANCH + 1, dtype=jnp.int32)
    roots = jnp.zeros((count, 1 + NBRANCH), jnp.int32)
    table = jnp.concatenate([roots, first_leaves, other_leaves], axis=1)
    return table.reshape(MB, TREES, NSEG).astype(jnp.int32)


def block_levels(own_key, shape, pieces, smallest, top_value):
    loudness, own = 1.0, jax.random.fold_in(own_key, 6)
    for dim, shards_of in pieces:
        draws = jnp.exp(jax.random.uniform(jax.random.fold_in(own, dim), (shards_of,), jnp.float32, smallest / len(pieces), top_value / len(pieces)))
        loudness = loudness * jnp.repeat(draws, shape[dim] // shards_of).reshape([-1 if axis == dim else 1 for axis in range(len(shape))])
    return loudness


def normal_values(key, dims, width, limit, pieces=(), kind=jnp.bfloat16):
    values = jax.random.normal(key, dims, jnp.float32) * width
    if len(pieces) > 0:
        values = block_levels(key, dims, pieces, -0.22, 0.18) * values
    return jnp.clip(values, min=-limit, max=limit).astype(kind)


def setup_inputs(seed: int = 0) -> dict:
    seeds = jax.random.split(jax.random.key(seed), 14)
    tokens = normal_values(seeds[0], (MB, TREES, TREE, D), 1.0, 6.0, ((1, 8), (2, 4)))
    gain_attn = jnp.clip(1.0 + 0.18 * jax.random.normal(seeds[1], (D,), jnp.float32), 0.099609375, 1.8984375).astype(jnp.bfloat16)
    w_query = normal_values(seeds[2], (D, D), 0.08, 0.5, ((0, 4),))
    w_key = normal_values(seeds[3], (KV, D), 0.08, 0.5, ((0, 4),))
    w_value = normal_values(seeds[4], (KV, D), D ** -0.5, 0.125, ((0, 4),))
    w_out = normal_values(seeds[5], (D, D), 8 ** -0.5, 2.0, ((0, 4),))
    gain_ff = jnp.clip(1.0 + 0.18 * jax.random.normal(seeds[6], (D,), jnp.float32), 0.099609375, 1.8984375).astype(jnp.bfloat16)
    w_gate = normal_values(seeds[7], (FF, D), D ** -0.5, 0.125, ((0, 4),))
    w_up = normal_values(seeds[8], (FF, D), D ** -0.5, 0.125, ((0, 4),))
    w_down = normal_values(seeds[9], (FF, D), (FF // 16) ** -0.5, 0.25, ((0, 4),))
    cotangent = normal_values(seeds[10], (MB, TREES, TREE, D), 1.0, 6.0, ((1, 8), (2, 4)))
    segment_ids = draw_segment_ids(jax.random.fold_in(seeds[13], 71), 0)
    parents = draw_parents(jax.random.fold_in(seeds[13], 71), 0)
    return dict(tokens=tokens, gain_attn=gain_attn, w_query=w_query, w_key=w_key, w_value=w_value, w_out=w_out, gain_ff=gain_ff, w_gate=w_gate, w_up=w_up, w_down=w_down, cotangent=cotangent, segment_ids=segment_ids, parents=parents)


EPSILON = 1e-05
RESIDUAL = 0.22
ATTN_SCALE = 0.015625
ROPE_BASE = 10000000.0
NEGATIVE = -1e+30

@jax.custom_vjp
def low(v):
    return lax.optimization_barrier(v.astype(jnp.bfloat16)).astype(jnp.float32)

@jax.custom_vjp
def low_back(v):
    return v

def low_keep(v):
    return (low(v), None)

def low_pass(kept, grad):
    return (grad,)

def back_keep(v):
    return (v, None)

def back_low(kept, grad):
    return (low(grad),)
low.defvjp(low_keep, low_pass)
low_back.defvjp(back_keep, back_low)

def tree_layout(segment_row, parent_row):
    seg_numbers = jnp.arange(NSEG, dtype=jnp.int32)
    member = (segment_row[:, None] == seg_numbers[None, :]).astype(jnp.int32)
    lengths = lax.optimization_barrier(jnp.sum(member, axis=0))
    starts = jnp.cumsum(lengths) - lengths
    parent_hit = parent_row[:, None] == seg_numbers[None, :]
    grandparent = lax.optimization_barrier(jnp.sum(jnp.where(parent_hit, parent_row[None, :], 0), axis=1))
    itself = seg_numbers[:, None] == seg_numbers[None, :]
    related = itself | parent_hit | (grandparent[:, None] == seg_numbers[None, :])
    before = lax.optimization_barrier(jnp.sum(jnp.where(related & jnp.logical_not(itself), lengths[None, :], 0), axis=1))
    shift_seg = (before - starts).astype(jnp.int32)
    position = jnp.arange(segment_row.shape[0], dtype=jnp.int32) + lax.optimization_barrier(jnp.sum(member * shift_seg[None, :], axis=1)).astype(jnp.int32)
    return (position, related.astype(jnp.int32))

def allowed_mask(segment_row, related):
    row_links = related[segment_row.astype(jnp.int32)]
    link = row_links[:, segment_row.astype(jnp.int32)]
    index = jnp.arange(segment_row.shape[0], dtype=jnp.int32)
    return (link > 0) & (index[None, :] <= index[:, None])

def rotate(values, position, sign):
    half = values.shape[-1] // 2
    fraction = jnp.arange(half, dtype=jnp.float32) * (2.0 / values.shape[-1])
    freq = jnp.exp(-math.log(ROPE_BASE) * fraction)
    angle = position.astype(jnp.float32)[:, None] * freq[None, :]
    cosine = jnp.concatenate([jnp.cos(angle), jnp.cos(angle)], axis=-1)[:, None, :]
    sine = jnp.concatenate([jnp.sin(angle), jnp.sin(angle)], axis=-1)[:, None, :]
    turned = jnp.concatenate([-values[..., half:], values[..., :half]], axis=-1)
    return values * cosine + sign * turned * sine

def product(left, right):
    return jnp.dot(left, right, precision=lax.Precision.HIGHEST, preferred_element_type=jnp.float32)

def product_t(left, right):
    return lax.dot_general(left, right, (((1,), (1,)), ((), ())), precision=lax.Precision.HIGHEST, preferred_element_type=jnp.float32)

def normalize(values):
    return values * lax.rsqrt(lax.optimization_barrier(jnp.mean(values * values, axis=-1, keepdims=True)) + EPSILON)

def layer(inputs, gain_attn, w_query, w_key, w_value, w_out, gain_ff, w_gate, w_up, w_down, position, allowed):
    length = inputs.shape[0]
    group = HEADS // KV_HEADS
    normed = low(normalize(inputs) * gain_attn)
    query = low(rotate(low_back(product_t(normed, w_query)).reshape(length, HEADS, HEAD_DIM), position, 1.0))
    key_rows = low(rotate(low_back(product_t(normed, w_key)).reshape(length, KV_HEADS, HEAD_DIM), position, 1.0))
    value_rows = low(low_back(product_t(normed, w_value))).reshape(length, KV_HEADS, HEAD_DIM)
    query = query.reshape(length, KV_HEADS, group, HEAD_DIM)
    scores = low_back(jnp.einsum('qhgd,khd->hgqk', query, key_rows, precision=lax.Precision.HIGHEST) * ATTN_SCALE)
    masked = jnp.where(allowed[None, None], scores, NEGATIVE)
    expo = jnp.exp(masked - lax.optimization_barrier(jnp.max(masked, axis=-1, keepdims=True)))
    probs = low(expo / lax.optimization_barrier(jnp.sum(expo, axis=-1, keepdims=True)))
    mixed = jnp.einsum('hgqk,khd->qhgd', probs, value_rows, precision=lax.Precision.HIGHEST).reshape(length, HEADS * HEAD_DIM)
    attended = low(low_back(mixed))
    middle = inputs + RESIDUAL * low_back(product(attended, w_out))
    normed_ff = low(normalize(middle) * gain_ff)
    gate = low_back(product_t(normed_ff, w_gate))
    upper = low_back(product_t(normed_ff, w_up))
    hidden = low(gate * jax.nn.sigmoid(gate) * upper)
    return middle + RESIDUAL * low_back(product(hidden, w_down))

def reference(tokens, gain_attn, w_query, w_key, w_value, w_out, gain_ff, w_gate, w_up, w_down, cotangent, segment_ids, parents):
    weights = (gain_attn.astype(jnp.float32), w_query.astype(jnp.float32), w_key.astype(jnp.float32), w_value.astype(jnp.float32), w_out.astype(jnp.float32), gain_ff.astype(jnp.float32), w_gate.astype(jnp.float32), w_up.astype(jnp.float32), w_down.astype(jnp.float32))
    count = MB * TREES
    flat_tokens = tokens.reshape(count, TREE, D)
    flat_cot = cotangent.reshape(count, TREE, D)
    flat_segments = segment_ids.reshape(count, TREE)
    flat_parents = parents.reshape(count, NSEG)

    def one_tree(carry, items):
        inputs, cot, segment_row, parent_row = items
        position, related = tree_layout(segment_row, parent_row)
        allowed = allowed_mask(segment_row, related)

        def forward(values, *params):
            return layer(values, *params, position, allowed)
        result, pullback = jax.vjp(forward, inputs.astype(jnp.float32), *weights)
        grads = pullback(cot.astype(jnp.float32))
        carry = tuple((total + grad for total, grad in zip(carry, grads[1:])))
        return (carry, (result.astype(jnp.bfloat16), grads[0]))
    init = tuple((jnp.zeros(w.shape, jnp.float32) for w in weights))
    final, (results, input_grads) = lax.scan(one_tree, init, (flat_tokens, flat_cot, flat_segments, flat_parents))
    return (results.reshape(MB, TREES, TREE, D), input_grads.reshape(MB, TREES, TREE, D), final[0], final[1], final[2], final[3], final[4], final[5], final[6], final[7], final[8])
```

```python
import functools
import math

import jax
import jax.numpy as jnp
from jax import lax
from jax.experimental import pallas as pl
from jax.experimental.pallas import tpu as pltpu
from jax.sharding import PartitionSpec as P

HEADS = 32
KV_HEADS = 8
HEAD_DIM = 64
PAIR = 2 * HEAD_DIM
GROUP = HEADS // KV_HEADS

EPSILON = 1e-05
RESIDUAL = 0.22
ATTN_SCALE = 0.015625
ROPE_BASE = 10000000.0
NEGATIVE = -1e30
BF16 = jnp.bfloat16
F32 = jnp.float32


def dot_nt(left, right):
    return lax.dot_general(left, right, (((1,), (1,)), ((), ())), preferred_element_type=F32)


def dot_nn(left, right):
    return lax.dot_general(left, right, (((1,), (0,)), ((), ())), preferred_element_type=F32)


def dot_tn(left, right):
    return lax.dot_general(left, right, (((0,), (0,)), ((), ())), preferred_element_type=F32)


def tree_layout(segment_row, parent_row):
    seg_numbers = jnp.arange(parent_row.shape[0], dtype=jnp.int32)
    member = (segment_row[:, None] == seg_numbers[None, :]).astype(jnp.int32)
    lengths = jnp.sum(member, axis=0)
    earlier = seg_numbers[None, :] < seg_numbers[:, None]
    starts = jnp.sum(jnp.where(earlier, lengths[None, :], 0), axis=1)
    parent_hit = parent_row[:, None] == seg_numbers[None, :]
    grandparent = jnp.sum(jnp.where(parent_hit, parent_row[None, :], 0), axis=1)
    itself = seg_numbers[:, None] == seg_numbers[None, :]
    related = itself | parent_hit | (grandparent[:, None] == seg_numbers[None, :])
    before = jnp.sum(jnp.where(related & jnp.logical_not(itself), lengths[None, :], 0), axis=1)
    shift = jnp.sum(member * (before - starts)[None, :], axis=1)
    position = jnp.arange(segment_row.shape[0], dtype=jnp.int32) + shift
    pad = ((0, 0), (0, PAIR - parent_row.shape[0]))
    sees = dot_nn(member.astype(BF16), related.astype(BF16)).astype(BF16)
    return position, jnp.pad(member.astype(BF16), pad), jnp.pad(sees, pad)


def rope_tables(position):
    lane = jnp.arange(PAIR, dtype=jnp.int32) % HEAD_DIM
    half = HEAD_DIM // 2
    fraction = (lane % half).astype(F32) * (2.0 / HEAD_DIM)
    freq = jnp.exp(-math.log(ROPE_BASE) * fraction)
    angle = position.astype(F32)[:, None] * freq[None, :]
    return jnp.cos(angle), jnp.sin(angle) * jnp.where(lane < half, -1.0, 1.0)[None, :]


def swap_halves(block):
    lane = lax.broadcasted_iota(jnp.int32, block.shape, 1)
    half = HEAD_DIM // 2
    up = pltpu.roll(block, PAIR - half, 1)
    down = pltpu.roll(block, half, 1)
    return jnp.where(lane % HEAD_DIM < half, up, down)


def turn(block, cosine, sine):
    return block * cosine + swap_halves(block) * sine


def place_heads(wide, kv_heads, fill):
    placed = []
    for g in range(kv_heads):
        base = wide[:, (g // 2) * PAIR : (g // 2) * PAIR + PAIR] if wide.shape[1] >= PAIR else wide
        lane = lax.broadcasted_iota(jnp.int32, base.shape, 1)
        moved = pltpu.roll(base, HEAD_DIM, 1)
        for p in range(2):
            source = base if g % 2 == p else moved
            inside = (lane // HEAD_DIM) == p
            placed.append(jnp.where(inside, source, jnp.full_like(source, fill)))
    return placed


def attention_forward_kernel(
    kv_heads,
    blocks,
    order_ref,
    q_ref,
    kv_ref,
    cos_ref,
    sin_ref,
    member_ref,
    sees_ref,
    out_ref,
    q_out_ref,
    kv_out_ref,
    lse_ref,
    keys,
    values,
    bias,
):
    step = pl.program_id(0)
    rows = q_ref.shape[0]
    tree = rows * blocks
    kv_width = kv_heads * HEAD_DIM

    @pl.when(step == 0)
    def _():
        for b in range(blocks):
            here = pl.ds(b * rows, rows)
            raw = kv_ref[pl.ds(pl.multiple_of(order_ref[b] * rows, rows), rows), :]
            cosine, sine = cos_ref[here, :], sin_ref[here, :]
            if kv_width >= PAIR:
                turned = jnp.concatenate(
                    [
                        turn(raw[:, c : c + PAIR], cosine, sine)
                        for c in range(0, kv_width, PAIR)
                    ],
                    axis=1,
                )
                plain = raw[:, kv_width:]
            else:
                lane = lax.broadcasted_iota(jnp.int32, raw.shape, 1)
                turned = turn(raw, cosine, sine)
                plain = pltpu.roll(raw, HEAD_DIM, 1)
                both = jnp.where(lane < HEAD_DIM, turned, raw)
            if kv_width >= PAIR:
                both = jnp.concatenate([turned, plain], axis=1)
            kv_out_ref[here, :] = both.astype(BF16)
            for index, placed in enumerate(place_heads(turned, kv_heads, 0.0)):
                keys[index, here, :] = placed.astype(BF16)
            for index, placed in enumerate(place_heads(plain, kv_heads, 1.0)):
                values[index, here, :] = placed.astype(BF16)

    here = pl.ds(pl.multiple_of(step * rows, rows), rows)
    cosine, sine = cos_ref[here, :], sin_ref[here, :]
    for j in range(q_ref.shape[1] // PAIR):
        lanes = slice(j * PAIR, j * PAIR + PAIR)
        q_out_ref[:, lanes] = (turn(q_ref[:, lanes], cosine, sine).astype(BF16)) * BF16(ATTN_SCALE)

    link = dot_nt(sees_ref[here, :], member_ref[...])
    row_index = lax.broadcasted_iota(jnp.int32, (rows, tree), 0) + step * rows
    col_index = lax.broadcasted_iota(jnp.int32, (rows, tree), 1)
    bias[...] = jnp.where((link > 0.5) & (col_index <= row_index), 0.0, NEGATIVE)

    lane = lax.broadcasted_iota(jnp.int32, (rows, PAIR), 1)
    for block in range(blocks):
        width = (block + 1) * rows

        @pl.when(step == block)
        def _(width=width):
            lse = jnp.zeros((rows, PAIR), F32)
            for j in range(q_ref.shape[1] // PAIR):
                lanes = slice(j * PAIR, j * PAIR + PAIR)
                group = 2 * j // GROUP
                mixed, tops = [], []
                for p in range(2):
                    scores = dot_nt(q_out_ref[:, lanes], keys[group * 2 + p, :width, :])
                    scores = scores + bias[:, :width]
                    top = jnp.max(scores, axis=1, keepdims=True)
                    expo = jnp.exp(scores - top).astype(BF16)
                    mixed.append(dot_nn(expo, values[group * 2 + p, :width, :]))
                    tops.append(top)
                upper = lane >= HEAD_DIM
                total = pltpu.roll(jnp.where(upper, mixed[0], mixed[1]), HEAD_DIM, 1)
                out_ref[:, lanes] = (jnp.where(upper, mixed[1], mixed[0]) / total).astype(BF16)
                logs = jnp.log(total)
                lse = jnp.where(lane == 2 * j, tops[0] + logs[:, :1], lse)
                lse = jnp.where(lane == 2 * j + 1, tops[1] + logs[:, HEAD_DIM : HEAD_DIM + 1], lse)
            lse_ref[...] = lse


def attention_forward(order, qkv, cosine, sine, member, sees, q_width, blocks):
    tree = qkv.shape[0]
    rows = tree // blocks
    kv_width = (qkv.shape[1] - q_width) // 2
    kv_heads = kv_width // HEAD_DIM
    whole = lambda width: pl.BlockSpec((tree, width), lambda i, order: (0, 0))
    natural = lambda width: pl.BlockSpec((rows, width), lambda i, order: (i, 0))
    return pl.pallas_call(
        functools.partial(attention_forward_kernel, kv_heads, blocks),
        grid_spec=pltpu.PrefetchScalarGridSpec(
            num_scalar_prefetch=1,
            grid=(blocks,),
            in_specs=[
                pl.BlockSpec((rows, q_width), lambda i, order: (order[i], 0)),
                pl.BlockSpec((tree, 2 * kv_width), lambda i, order: (0, q_width // (2 * kv_width))),
                whole(PAIR),
                whole(PAIR),
                whole(PAIR),
                whole(PAIR),
            ],
            out_specs=[
                pl.BlockSpec((rows, q_width), lambda i, order: (order[i], 0)),
                natural(q_width),
                whole(2 * kv_width),
                natural(PAIR),
            ],
            scratch_shapes=[
                pltpu.VMEM((2 * kv_heads, tree, PAIR), BF16),
                pltpu.VMEM((2 * kv_heads, tree, PAIR), BF16),
                pltpu.VMEM((rows, tree), F32),
            ],
        ),
        out_shape=[
            jax.ShapeDtypeStruct((tree, q_width), BF16),
            jax.ShapeDtypeStruct((tree, q_width), BF16),
            jax.ShapeDtypeStruct((tree, 2 * kv_width), BF16),
            jax.ShapeDtypeStruct((tree, PAIR), F32),
        ],
        compiler_params=pltpu.CompilerParams(vmem_limit_bytes=40 << 20),
        cost_estimate=pl.CostEstimate(
            flops=10_000_000_000, bytes_accessed=12_000_000, transcendentals=5_000_000
        ),
        name="attention_forward",
    )(order, qkv, qkv, cosine, sine, member, sees)


def attention_backward_kernel(
    kv_heads,
    blocks,
    order_ref,
    grad_ref,
    q_ref,
    kv_ref,
    lse_ref,
    cos_ref,
    sin_ref,
    member_ref,
    sees_ref,
    dq_ref,
    dkv_ref,
    keys,
    values,
    bias,
    key_sum,
    value_sum,
):
    step = pl.program_id(0)
    rows = q_ref.shape[0]
    tree = rows * blocks
    kv_width = kv_heads * HEAD_DIM

    @pl.when(step == 0)
    def _():
        for b in range(blocks):
            here = pl.ds(b * rows, rows)
            both = kv_ref[here, :].astype(F32)
            if kv_width >= PAIR:
                turned, plain = both[:, :kv_width], both[:, kv_width:]
            else:
                turned, plain = both, pltpu.roll(both, HEAD_DIM, 1)
            for index, placed in enumerate(place_heads(turned, kv_heads, 0.0)):
                keys[index, here, :] = placed.astype(BF16)
            for index, placed in enumerate(place_heads(plain, kv_heads, 0.0)):
                values[index, here, :] = placed.astype(BF16)
        key_sum[...] = jnp.zeros_like(key_sum)
        value_sum[...] = jnp.zeros_like(value_sum)

    here = pl.ds(pl.multiple_of(step * rows, rows), rows)
    link = dot_nt(member_ref[...], sees_ref[here, :])
    key_index = lax.broadcasted_iota(jnp.int32, (tree, rows), 0)
    query_index = lax.broadcasted_iota(jnp.int32, (tree, rows), 1) + step * rows
    bias[...] = jnp.where((link > 0.5) & (key_index <= query_index), 0.0, NEGATIVE)
    lse_rows = jnp.transpose(lse_ref[...])

    for block in range(blocks):
        width = (block + 1) * rows

        @pl.when(step == block)
        def _(width=width):
            cosine, sine = cos_ref[here, :], sin_ref[here, :]
            for j in range(q_ref.shape[1] // PAIR):
                lanes = slice(j * PAIR, j * PAIR + PAIR)
                group = 2 * j // GROUP
                query, grad = q_ref[:, lanes], grad_ref[:, lanes]
                dq = jnp.zeros((rows, PAIR), F32)
                for p in range(2):
                    index, head = group * 2 + p, 2 * j + p
                    scores = dot_nt(keys[index, :width, :], query) + bias[:width, :]
                    probs = jnp.exp(scores - lse_rows[head : head + 1, :])
                    probs_grad = dot_nt(values[index, :width, :], grad)
                    value_sum[index, :width, :] += dot_nn(probs.astype(BF16), grad)
                    weighted = probs * probs_grad
                    delta = jnp.sum(weighted, axis=0, keepdims=True)
                    score_grad = (weighted - probs * delta).astype(BF16)
                    key_sum[index, :width, :] += dot_nn(score_grad, query)
                    dq = dq + dot_tn(score_grad, keys[index, :width, :])
                dq_ref[:, lanes] = turn(dq * ATTN_SCALE, cosine, -sine).astype(BF16)

    @pl.when(step == blocks - 1)
    def _():
        for b in range(blocks):
            here = pl.ds(b * rows, rows)
            there = pl.ds(pl.multiple_of(order_ref[b] * rows, rows), rows)
            cosine, sine = cos_ref[here, :], sin_ref[here, :]
            lane = lax.broadcasted_iota(jnp.int32, (rows, PAIR), 1)
            lower = lane < HEAD_DIM
            for c in range(0, kv_heads, 2):
                halves = []
                for acc in (key_sum, value_sum):
                    own, other = [], []
                    for g in range(c, min(c + 2, kv_heads)):
                        low, high = acc[g * 2, here, :], acc[g * 2 + 1, here, :]
                        own.append(low)
                        other.append(high)
                    first = own[0] + pltpu.roll(other[0], HEAD_DIM, 1)
                    if len(own) == 2:
                        second = other[1] + pltpu.roll(own[1], HEAD_DIM, 1)
                    else:
                        second = first
                    halves.append(jnp.where(lower, first, second))
                turned = turn(halves[0], cosine, -sine)
                if kv_width >= PAIR:
                    lanes = slice(c * HEAD_DIM, c * HEAD_DIM + PAIR)
                    dkv_ref[there, lanes] = turned.astype(BF16)
                    lanes = slice(kv_width + c * HEAD_DIM, kv_width + c * HEAD_DIM + PAIR)
                    dkv_ref[there, lanes] = halves[1].astype(BF16)
                else:
                    moved = pltpu.roll(halves[1], HEAD_DIM, 1)
                    dkv_ref[there, :] = jnp.where(lower, turned, moved).astype(BF16)


def attention_backward(order, grad, query, kv, lse, cosine, sine, member, sees, blocks):
    tree, q_width = query.shape
    rows = tree // blocks
    kv_width = kv.shape[1] // 2
    kv_heads = kv_width // HEAD_DIM
    whole = lambda width: pl.BlockSpec((tree, width), lambda i, order: (0, 0))
    natural = lambda width: pl.BlockSpec((rows, width), lambda i, order: (i, 0))
    ordered = lambda width: pl.BlockSpec((rows, width), lambda i, order: (order[i], 0))
    return pl.pallas_call(
        functools.partial(attention_backward_kernel, kv_heads, blocks),
        grid_spec=pltpu.PrefetchScalarGridSpec(
            num_scalar_prefetch=1,
            grid=(blocks,),
            in_specs=[
                ordered(q_width),
                natural(q_width),
                whole(2 * kv_width),
                natural(PAIR),
                whole(PAIR),
                whole(PAIR),
                whole(PAIR),
                whole(PAIR),
            ],
            out_specs=[ordered(q_width), whole(2 * kv_width)],
            scratch_shapes=[
                pltpu.VMEM((2 * kv_heads, tree, PAIR), BF16),
                pltpu.VMEM((2 * kv_heads, tree, PAIR), BF16),
                pltpu.VMEM((tree, rows), F32),
                pltpu.VMEM((2 * kv_heads, tree, PAIR), F32),
                pltpu.VMEM((2 * kv_heads, tree, PAIR), F32),
            ],
        ),
        out_shape=[
            jax.ShapeDtypeStruct((tree, q_width), BF16),
            jax.ShapeDtypeStruct((tree, 2 * kv_width), BF16),
        ],
        compiler_params=pltpu.CompilerParams(vmem_limit_bytes=48 << 20),
        cost_estimate=pl.CostEstimate(
            flops=20_000_000_000, bytes_accessed=12_000_000, transcendentals=5_000_000
        ),
        name="attention_backward",
    )(order, grad, query, kv, lse, cosine, sine, member, sees)


def sync(*values):
    return lax.optimization_barrier(values)


class Square:
    def __init__(self, shard, replica):
        self.shard, self.replica = shard, replica
        self.x = [(i, i ^ 1) for i in range(shard)]
        self.y = [(i, i ^ 2) for i in range(shard)]
        self.d = [(i, i ^ 3) for i in range(shard)]
        self.core = [(i, i ^ 1) for i in range(replica)]
        both = lambda pairs: [(2 * a + c, 2 * b + c) for a, b in pairs for c in range(2)]
        self.outer = both([(0, 1), (1, 0), (2, 3), (3, 2)])
        self.middle = both([(1, 2), (2, 1)])

    def order(self):
        return jnp.arange(self.shard, dtype=jnp.int32) ^ lax.axis_index("shard")

    def reorder(self, blocks, axis):
        me = lax.axis_index("shard")
        return jnp.concatenate(
            [lax.dynamic_slice_in_dim(blocks, n ^ me, 1, axis) for n in range(self.shard)], axis=axis
        )

    def gather_small(self, own):
        parts = [
            own,
            lax.ppermute(own, "shard", self.x),
            lax.ppermute(own, "shard", self.y),
            lax.ppermute(own, "shard", self.d),
        ]
        return self.reorder(jnp.stack(parts), 0)

    def gather_first(self, own):
        return lax.ppermute(own, "shard", self.x), lax.ppermute(own, "shard", self.y)

    def gather_second(self, own, got):
        from_x, from_y = got
        half = own.shape[0] // 2
        first = lax.ppermute(from_y[:half], "shard", self.x)
        second = lax.ppermute(from_x[half:], "shard", self.y)
        return [own, from_x, from_y, first, second]

    def split(self, part):
        trees, width = part.shape[0] // self.rows // 4, part.shape[1]
        return part.reshape(trees, 4, 2, self.rows // 2, width)

    def sum_first(self, part):
        pieces = self.split(part)
        send_x = jnp.stack([pieces[:, 1, 0], pieces[:, 3, 0]])
        send_y = jnp.stack([pieces[:, 2, 1], pieces[:, 3, 1]])
        return lax.ppermute(send_x, "shard", self.x), lax.ppermute(send_y, "shard", self.y)

    def sum_second(self, part, got):
        pieces = self.split(part)
        got_x, got_y = got
        next_y = (pieces[:, 2, 0].astype(F32) + got_x[1].astype(F32)).astype(BF16)
        next_x = (pieces[:, 1, 1].astype(F32) + got_y[1].astype(F32)).astype(BF16)
        return lax.ppermute(next_y, "shard", self.y), lax.ppermute(next_x, "shard", self.x)

    def sum_last(self, part, got, last):
        pieces = self.split(part)
        wide = lambda v: v.astype(F32)
        first = wide(pieces[:, 0, 0]) + wide(got[0][0]) + wide(last[0])
        second = wide(pieces[:, 0, 1]) + wide(got[1][0]) + wide(last[1])
        both = jnp.concatenate([first, second], axis=1)
        return [both[t] for t in range(both.shape[0])]

    def sum_small(self, values):
        share = values.shape[1] // self.shard
        blocks = values.reshape(values.shape[0], self.shard, share)
        blocks = self.reorder(blocks, 1)
        total = blocks[:, 0]
        for k, perm in ((1, self.x), (2, self.y), (3, self.d)):
            total = total + lax.ppermute(blocks[:, k], "shard", perm)
        for step in (1, 2, 4):
            perm = [(i, i ^ step) for i in range(self.replica)]
            total = total + lax.ppermute(total, "replica", perm)
        return total

    def start_line(self):
        self.entering = []
        self.waiting = []
        self.outer_flight = None
        self.middle_flight = None
        self.wholes = None
        self.finals = {}

    def feed(self, name, grad, chunks):
        half = grad.shape[0] // 2
        core = lax.axis_index("replica") % 2
        send = lax.dynamic_slice_in_dim(grad, (1 - core) * half, half, 0)
        got = lax.ppermute(send, "replica", self.core)
        rows = half // chunks
        self.finals[name] = [None] * chunks
        for c in range(chunks):
            keep = lax.dynamic_slice_in_dim(grad, core * half + c * rows, rows, 0)
            mine = keep.astype(F32) + got[c * rows : (c + 1) * rows].astype(F32)
            self.waiting.append((name, c, mine.astype(BF16)))

    def busy(self):
        return any(v is not None for v in (self.outer_flight, self.middle_flight, self.wholes)) or bool(
            self.waiting
        )

    def tick(self, *values):
        place = lax.axis_index("replica") // 2
        inner = (place == 1) | (place == 2)
        outer, middle = self.outer_flight, self.middle_flight
        flights = (outer and outer[2], middle and middle[2])
        chunk = self.waiting.pop(0) if self.waiting else None
        flights, mine, values = sync(flights, chunk and chunk[2], values)
        add = lambda a, b: (a.astype(F32) + b.astype(F32)).astype(BF16)
        whole = None
        if middle is not None:
            whole = (middle[0], add(middle[1], flights[1]))
        self.middle_flight = None
        if outer is not None:
            entered, left, _ = outer
            if left is not None:
                (name, c), value = left
                final = jnp.where(inner, value, flights[0][: value.shape[0]])
                self.finals[name][c] = (final, lax.ppermute(final, "replica", self.core))
            if entered is not None:
                key, own = entered
                pair = add(own, flights[0][: own.shape[0]])
                self.middle_flight = (key, pair, lax.ppermute(pair, "replica", self.middle))
        self.outer_flight = None
        if chunk is not None or whole is not None:
            entering = None if chunk is None else ((chunk[0], chunk[1]), mine)
            if entering is None:
                send = whole[1]
            elif whole is None:
                send = mine
            else:
                rows = max(mine.shape[0], whole[1].shape[0])
                pad = lambda v: jnp.pad(v, ((0, rows - v.shape[0]), (0, 0)))
                send = jnp.where(inner, pad(whole[1]), pad(mine))
            self.outer_flight = (entering, whole, lax.ppermute(send, "replica", self.outer))
        return values

    def finish(self, name):
        mine = jnp.concatenate([f for f, _ in self.finals[name]], axis=0)
        other = jnp.concatenate([o for _, o in self.finals[name]], axis=0)
        first = lax.axis_index("replica") % 2 == 0
        return jnp.concatenate(
            [jnp.where(first, mine, other), jnp.where(first, other, mine)], axis=0
        ).astype(F32)

    def drain(self):
        while self.waiting or self.outer_flight is not None or self.middle_flight is not None:
            self.tick()


class General:
    def __init__(self, shard, replica):
        self.shard, self.replica = shard, replica

    def order(self):
        return jnp.arange(self.shard, dtype=jnp.int32)

    def gather_small(self, own):
        return lax.all_gather(own, "shard", axis=0, tiled=False)

    def gather_first(self, own):
        return lax.all_gather(own, "shard", axis=0, tiled=True)

    def gather_second(self, own, got):
        return [got]

    def sum_first(self, part):
        return lax.psum_scatter(
            part.reshape(-1, self.shard * self.rows, part.shape[1]),
            "shard",
            scatter_dimension=1,
            tiled=True,
        )

    def sum_second(self, part, got):
        return ()

    def sum_last(self, part, got, last):
        return [got[t].astype(F32) for t in range(got.shape[0])]

    def sum_small(self, values):
        share = lax.psum_scatter(values, "shard", scatter_dimension=1, tiled=True)
        return lax.psum(share, "replica")

    def start_line(self):
        self.finals = {}

    def feed(self, name, grad, chunks):
        self.finals[name] = lax.psum(grad, "replica").astype(F32)

    def tick(self, *values):
        return values

    def drain(self):
        pass

    def finish(self, name):
        return self.finals[name]


def rms_scale(values):
    return lax.rsqrt(jnp.mean(values * values, axis=-1, keepdims=True) + EPSILON)


def normalized(piece, gain):
    values = piece.astype(F32)
    return (values * rms_scale(values) * gain).astype(BF16)


def norm_back(values, scale, gain, grad_in):
    scaled = values * scale
    weighted = grad_in * gain
    back = scale * (weighted - scaled * jnp.mean(weighted * scaled, axis=-1, keepdims=True))
    return back, jnp.sum(grad_in * scaled, axis=0)


def body(
    links,
    tokens,
    gain_attn,
    w_query,
    w_key,
    w_value,
    w_out,
    gain_ff,
    w_gate,
    w_up,
    w_down,
    cotangent,
    segment_ids,
    parents,
):
    trees, _, own_rows, width = tokens.shape
    shard = links.shard
    q_width, kv_width = w_query.shape[0], w_key.shape[0]
    tree_rows = own_rows * shard
    links.rows = own_rows
    links.start_line()
    order = links.order()
    share = gain_attn.shape[0]
    w_qkv = jnp.concatenate([w_query, w_key, w_value], axis=0)
    token_rows = [tokens[t, 0] for t in range(trees)]
    cot_rows = [cotangent[t, 0] for t in range(trees)]

    small = jnp.concatenate(
        [gain_attn, gain_ff] + [segment_ids[t, 0].astype(BF16) for t in range(trees)]
    )
    smalls = links.gather_small(small)
    got = links.gather_first(token_rows[0])
    got, smalls, token_rows = sync(got, smalls, token_rows)
    gain_first = smalls[:, :share].reshape(width).astype(F32)
    gain_second = smalls[:, share : 2 * share].reshape(width).astype(F32)
    masks, tables = [], []
    for t in range(trees):
        begin = 2 * share + t * own_rows
        segments = smalls[:, begin : begin + own_rows].reshape(tree_rows).astype(jnp.int32)
        position, member, sees = tree_layout(segments, parents[t, 0])
        masks.append((member, sees))
        tables.append(rope_tables(position))

    normed_all, saved = [], []

    def attention(t, pieces):
        normed = jnp.concatenate([normalized(piece, gain_first) for piece in pieces], axis=0)
        normed_all.append(normed)
        attended, query, kv, lse = attention_forward(
            order, dot_nt(normed, w_qkv), *tables[t], *masks[t], q_width, shard
        )
        saved.append((attended, query, kv, lse))
        return dot_nn(attended, w_out).astype(BF16)

    def after_attention(t, branch):
        value = token_rows[t].astype(F32) + RESIDUAL * branch
        scale = rms_scale(value)
        return value, scale, (value * scale * gain_second).astype(BF16)

    pieces_0 = links.gather_second(token_rows[0], got)
    got = links.gather_first(token_rows[1])
    pieces_0, got, cot_rows = sync(pieces_0, got, cot_rows)

    pieces_1 = links.gather_second(token_rows[1], got)
    cot_got = links.gather_first(cot_rows[0])
    part_0 = attention(0, pieces_0)
    part_0, pieces_1, cot_got = sync(part_0, pieces_1, cot_got)

    got_0 = links.sum_first(part_0)
    cot_pieces_0 = links.gather_second(cot_rows[0], cot_got)
    part_1 = attention(1, pieces_1)
    got_0, cot_pieces_0, part_1 = sync(got_0, cot_pieces_0, part_1)

    last_0 = links.sum_second(part_0, got_0)
    got_1 = links.sum_first(part_1)
    last_0, got_1 = sync(last_0, got_1)

    middle_0, scale_0, own_0 = after_attention(0, links.sum_last(part_0, got_0, last_0)[0])
    last_1 = links.sum_second(part_1, got_1)
    ff_got_0 = links.gather_first(own_0)
    ff_got_0, last_1 = sync(ff_got_0, last_1)

    middle_1, scale_1, own_1 = after_attention(1, links.sum_last(part_1, got_1, last_1)[0])
    ff_pieces_0 = links.gather_second(own_0, ff_got_0)
    ff_got_1 = links.gather_first(own_1)
    ff_pieces_0, ff_got_1 = sync(ff_pieces_0, ff_got_1)
    ff_pieces_1 = links.gather_second(own_1, ff_got_1)
    ff_pieces_0, ff_pieces_1, cot_rows, cot_pieces_0 = sync(
        ff_pieces_0, ff_pieces_1, cot_rows, cot_pieces_0
    )

    rows_all = jnp.concatenate(ff_pieces_0 + ff_pieces_1, axis=0)
    cot_got = links.gather_first(cot_rows[1])
    gate = dot_nt(rows_all, w_gate).astype(BF16)
    gate, cot_got, rows_all = sync(gate, cot_got, rows_all)
    cot_pieces_1 = links.gather_second(cot_rows[1], cot_got)
    upper = dot_nt(rows_all, w_up)
    wide = gate.astype(F32)
    hidden = (wide * jax.nn.sigmoid(wide) * upper).astype(BF16)
    upper = upper.astype(BF16)
    hidden, upper, gate, cot_pieces_1 = sync(hidden, upper, gate, cot_pieces_1)
    cot_all = jnp.concatenate(
        [(RESIDUAL * piece.astype(F32)).astype(BF16) for piece in cot_pieces_0 + cot_pieces_1], axis=0
    )
    hidden_grad = dot_nt(cot_all, w_down)
    wide = gate.astype(F32)
    sigma = jax.nn.sigmoid(wide)
    gate_grad = (
        hidden_grad * upper.astype(F32) * sigma * (1.0 + wide * (1.0 - sigma))
    ).astype(BF16)
    up_grad = (hidden_grad * wide * sigma).astype(BF16)
    gate_grad, up_grad, hidden, cot_all = sync(gate_grad, up_grad, hidden, cot_all)

    grad_down = dot_tn(hidden, cot_all).astype(BF16)
    grad_down, gate_grad, up_grad = sync(grad_down, gate_grad, up_grad)
    links.feed("down", grad_down, 2)
    ff_part = (dot_nn(gate_grad, w_gate) + dot_nn(up_grad, w_up)).astype(BF16)
    ff_part, gate_grad, up_grad, hidden = links.tick(ff_part, gate_grad, up_grad, hidden)

    ff_sum = links.sum_first(ff_part)
    grad_gate = dot_tn(gate_grad, rows_all).astype(BF16)
    grad_gate, up_grad, ff_sum = links.tick(grad_gate, up_grad, ff_sum)
    links.feed("gate", grad_gate, 2)
    ff_last = links.sum_second(ff_part, ff_sum)
    grad_up = dot_tn(up_grad, rows_all).astype(BF16)
    grad_up, hidden, ff_last = links.tick(grad_up, hidden, ff_last)
    links.feed("up", grad_up, 2)

    ff_grad = links.sum_last(ff_part, ff_sum, ff_last)
    out_own, middle_grads = [], []
    gain_ff_sum = jnp.zeros((width,), F32)
    for t, (middle, scale) in enumerate(((middle_0, scale_0), (middle_1, scale_1))):
        middle_back, term = norm_back(middle, scale, gain_second, ff_grad[t])
        gain_ff_sum = gain_ff_sum + term
        middle_grads.append(cot_rows[t].astype(F32) + middle_back)
        out_own.append((RESIDUAL * middle_grads[t]).astype(BF16))
    out_got_0 = links.gather_first(out_own[0])
    down_part = dot_nn(hidden, w_down).astype(BF16)
    down_part, out_got_0, out_own = links.tick(down_part, out_got_0, out_own)

    out_pieces_0 = links.gather_second(out_own[0], out_got_0)
    out_got_1 = links.gather_first(out_own[1])
    out_pieces_0, out_got_1, down_part = links.tick(out_pieces_0, out_got_1, down_part)

    def attention_back(t, out_all):
        attended, query, kv, lse = saved[t]
        attended_grad = dot_nt(out_all, w_out).astype(BF16)
        dq, dkv = attention_backward(
            order, attended_grad, query, kv, lse, *tables[t], *masks[t], shard
        )
        qkv_grad = jnp.concatenate([dq, dkv], axis=1)
        return qkv_grad, dot_nn(qkv_grad, w_qkv).astype(BF16)

    out_pieces_1 = links.gather_second(out_own[1], out_got_1)
    down_sum = links.sum_first(down_part)
    out_all_0 = jnp.concatenate(out_pieces_0, axis=0)
    qkv_grad_0, normed_part_0 = attention_back(0, out_all_0)
    qkv_grad_0, normed_part_0, out_pieces_1, down_sum = links.tick(
        qkv_grad_0, normed_part_0, out_pieces_1, down_sum
    )

    normed_sum_0 = links.sum_first(normed_part_0)
    down_last = links.sum_second(down_part, down_sum)
    out_all_1 = jnp.concatenate(out_pieces_1, axis=0)
    qkv_grad_1, normed_part_1 = attention_back(1, out_all_1)
    qkv_grad_1, normed_part_1, normed_sum_0, down_last = links.tick(
        qkv_grad_1, normed_part_1, normed_sum_0, down_last
    )

    normed_last_0 = links.sum_second(normed_part_0, normed_sum_0)
    normed_sum_1 = links.sum_first(normed_part_1)
    attended_all = jnp.concatenate([saved[t][0] for t in range(trees)], axis=0)
    grad_out = dot_tn(attended_all, jnp.concatenate([out_all_0, out_all_1], axis=0)).astype(BF16)
    grad_qkv = dot_tn(
        jnp.concatenate([qkv_grad_0, qkv_grad_1], axis=0), jnp.concatenate(normed_all, axis=0)
    ).astype(BF16)
    grad_out, grad_qkv, normed_last_0, normed_sum_1 = links.tick(
        grad_out, grad_qkv, normed_last_0, normed_sum_1
    )
    links.feed("out", grad_out, 1)
    links.feed("qkv", grad_qkv, 1)

    normed_last_1 = links.sum_second(normed_part_1, normed_sum_1)
    down = links.sum_last(down_part, down_sum, down_last)
    results = [
        (middle + RESIDUAL * down[t]).astype(BF16) for t, middle in enumerate((middle_0, middle_1))
    ]
    results, normed_last_1 = links.tick(results, normed_last_1)
    normed_grads = links.sum_last(normed_part_0, normed_sum_0, normed_last_0)
    normed_grads += links.sum_last(normed_part_1, normed_sum_1, normed_last_1)
    input_grads = []
    gain_attn_sum = jnp.zeros((width,), F32)
    for t in range(trees):
        inputs = token_rows[t].astype(F32)
        input_back, term = norm_back(inputs, rms_scale(inputs), gain_first, normed_grads[t])
        gain_attn_sum = gain_attn_sum + term
        input_grads.append(middle_grads[t] + input_back)
    gains = links.sum_small(jnp.stack([gain_attn_sum, gain_ff_sum]))
    links.drain()
    grad_qkv = links.finish("qkv")
    return (
        jnp.stack(results)[:, None],
        jnp.stack(input_grads)[:, None],
        gains[0],
        grad_qkv[:q_width],
        grad_qkv[q_width : q_width + kv_width],
        grad_qkv[q_width + kv_width :],
        links.finish("out"),
        gains[1],
        links.finish("gate"),
        links.finish("up"),
        links.finish("down"),
    )


def solution(mesh):
    shard, replica = mesh.shape["shard"], mesh.shape["replica"]
    links = (Square if (shard, replica) == (4, 8) else General)(shard, replica)
    in_specs = (
        P(None, "replica", "shard", None),
        P("shard"),
        P("shard", None),
        P("shard", None),
        P("shard", None),
        P("shard", None),
        P("shard"),
        P("shard", None),
        P("shard", None),
        P("shard", None),
        P(None, "replica", "shard", None),
        P(None, "replica", "shard"),
        P(None, "replica", None),
    )
    out_specs = (
        P(None, "replica", "shard", None),
        P(None, "replica", "shard", None),
        P("shard"),
        P("shard", None),
        P("shard", None),
        P("shard", None),
        P("shard", None),
        P("shard"),
        P("shard", None),
        P("shard", None),
        P("shard", None),
    )
    return jax.shard_map(
        functools.partial(body, links),
        mesh=mesh,
        in_specs=in_specs,
        out_specs=out_specs,
        check_vma=False,
    )
```

```python
import functools
import math

import jax
import jax.numpy as jnp
from jax import lax
from jax.experimental import pallas as pl
from jax.experimental.pallas import tpu as pltpu
from jax.sharding import PartitionSpec as P

HEADS = 32
KV_HEADS = 8
HEAD_DIM = 64
PAIR = 2 * HEAD_DIM
GROUP = HEADS // KV_HEADS

EPSILON = 1e-05
RESIDUAL = 0.22
ATTN_SCALE = 0.015625
ROPE_BASE = 10000000.0
NEGATIVE = -1e30
BF16 = jnp.bfloat16
F32 = jnp.float32


def dot_nt(left, right):
    return lax.dot_general(left, right, (((1,), (1,)), ((), ())), preferred_element_type=F32)


def dot_nn(left, right):
    return lax.dot_general(left, right, (((1,), (0,)), ((), ())), preferred_element_type=F32)


def dot_tn(left, right):
    return lax.dot_general(left, right, (((0,), (0,)), ((), ())), preferred_element_type=F32)


def tree_layout(segment_row, parent_row):
    seg_numbers = jnp.arange(parent_row.shape[0], dtype=jnp.int32)
    member = (segment_row[:, None] == seg_numbers[None, :]).astype(jnp.int32)
    lengths = jnp.sum(member, axis=0)
    earlier = seg_numbers[None, :] < seg_numbers[:, None]
    starts = jnp.sum(jnp.where(earlier, lengths[None, :], 0), axis=1)
    parent_hit = parent_row[:, None] == seg_numbers[None, :]
    grandparent = jnp.sum(jnp.where(parent_hit, parent_row[None, :], 0), axis=1)
    itself = seg_numbers[:, None] == seg_numbers[None, :]
    related = itself | parent_hit | (grandparent[:, None] == seg_numbers[None, :])
    before = jnp.sum(jnp.where(related & jnp.logical_not(itself), lengths[None, :], 0), axis=1)
    shift = jnp.sum(member * (before - starts)[None, :], axis=1)
    position = jnp.arange(segment_row.shape[0], dtype=jnp.int32) + shift
    pad = ((0, 0), (0, PAIR - parent_row.shape[0]))
    sees = dot_nn(member.astype(BF16), related.astype(BF16)).astype(BF16)
    return position, jnp.pad(member.astype(BF16), pad), jnp.pad(sees, pad)


def rope_tables(position):
    lane = jnp.arange(PAIR, dtype=jnp.int32) % HEAD_DIM
    half = HEAD_DIM // 2
    fraction = (lane % half).astype(F32) * (2.0 / HEAD_DIM)
    freq = jnp.exp(-math.log(ROPE_BASE) * fraction)
    angle = position.astype(F32)[:, None] * freq[None, :]
    return jnp.cos(angle), jnp.sin(angle) * jnp.where(lane < half, -1.0, 1.0)[None, :]


def swap_halves(block):
    lane = lax.broadcasted_iota(jnp.int32, block.shape, 1)
    half = HEAD_DIM // 2
    up = pltpu.roll(block, PAIR - half, 1)
    down = pltpu.roll(block, half, 1)
    return jnp.where(lane % HEAD_DIM < half, up, down)


def turn(block, cosine, sine):
    return block * cosine + swap_halves(block) * sine


def place_heads(wide, kv_heads, fill):
    placed = []
    for g in range(kv_heads):
        base = wide[:, (g // 2) * PAIR : (g // 2) * PAIR + PAIR] if wide.shape[1] >= PAIR else wide
        lane = lax.broadcasted_iota(jnp.int32, base.shape, 1)
        moved = pltpu.roll(base, HEAD_DIM, 1)
        for p in range(2):
            source = base if g % 2 == p else moved
            inside = (lane // HEAD_DIM) == p
            placed.append(jnp.where(inside, source, jnp.full_like(source, fill)))
    return placed


def attention_forward_kernel(
    kv_heads,
    blocks,
    order_ref,
    q_ref,
    kv_ref,
    cos_ref,
    sin_ref,
    member_ref,
    sees_ref,
    out_ref,
    q_out_ref,
    kv_out_ref,
    lse_ref,
    keys,
    values,
    bias,
):
    step = pl.program_id(0)
    rows = q_ref.shape[0]
    tree = rows * blocks
    kv_width = kv_heads * HEAD_DIM

    @pl.when(step == 0)
    def _():
        for b in range(blocks):
            here = pl.ds(b * rows, rows)
            raw = kv_ref[pl.ds(pl.multiple_of(order_ref[b] * rows, rows), rows), :]
            cosine, sine = cos_ref[here, :], sin_ref[here, :]
            if kv_width >= PAIR:
                turned = jnp.concatenate(
                    [
                        turn(raw[:, c : c + PAIR], cosine, sine)
                        for c in range(0, kv_width, PAIR)
                    ],
                    axis=1,
                )
                plain = raw[:, kv_width:]
            else:
                lane = lax.broadcasted_iota(jnp.int32, raw.shape, 1)
                turned = turn(raw, cosine, sine)
                plain = pltpu.roll(raw, HEAD_DIM, 1)
                both = jnp.where(lane < HEAD_DIM, turned, raw)
            if kv_width >= PAIR:
                both = jnp.concatenate([turned, plain], axis=1)
            kv_out_ref[here, :] = both.astype(BF16)
            for index, placed in enumerate(place_heads(turned, kv_heads, 0.0)):
                keys[index, here, :] = placed.astype(BF16)
            for index, placed in enumerate(place_heads(plain, kv_heads, 1.0)):
                values[index, here, :] = placed.astype(BF16)

    here = pl.ds(pl.multiple_of(step * rows, rows), rows)
    cosine, sine = cos_ref[here, :], sin_ref[here, :]
    for j in range(q_ref.shape[1] // PAIR):
        lanes = slice(j * PAIR, j * PAIR + PAIR)
        q_out_ref[:, lanes] = (turn(q_ref[:, lanes], cosine, sine).astype(BF16)) * BF16(ATTN_SCALE)

    link = dot_nt(sees_ref[here, :], member_ref[...])
    row_index = lax.broadcasted_iota(jnp.int32, (rows, tree), 0) + step * rows
    col_index = lax.broadcasted_iota(jnp.int32, (rows, tree), 1)
    bias[...] = jnp.where((link > 0.5) & (col_index <= row_index), 0.0, NEGATIVE)

    lane = lax.broadcasted_iota(jnp.int32, (rows, PAIR), 1)
    for block in range(blocks):
        width = (block + 1) * rows

        @pl.when(step == block)
        def _(width=width):
            lse = jnp.zeros((rows, PAIR), F32)
            for j in range(q_ref.shape[1] // PAIR):
                lanes = slice(j * PAIR, j * PAIR + PAIR)
                group = 2 * j // GROUP
                mixed, tops = [], []
                for p in range(2):
                    scores = dot_nt(q_out_ref[:, lanes], keys[group * 2 + p, :width, :])
                    scores = scores + bias[:, :width]
                    top = jnp.max(scores, axis=1, keepdims=True)
                    expo = jnp.exp(scores - top).astype(BF16)
                    mixed.append(dot_nn(expo, values[group * 2 + p, :width, :]))
                    tops.append(top)
                upper = lane >= HEAD_DIM
                total = pltpu.roll(jnp.where(upper, mixed[0], mixed[1]), HEAD_DIM, 1)
                out_ref[:, lanes] = (jnp.where(upper, mixed[1], mixed[0]) / total).astype(BF16)
                logs = jnp.log(total)
                lse = jnp.where(lane == 2 * j, tops[0] + logs[:, :1], lse)
                lse = jnp.where(lane == 2 * j + 1, tops[1] + logs[:, HEAD_DIM : HEAD_DIM + 1], lse)
            lse_ref[...] = lse


def attention_forward(order, qkv, cosine, sine, member, sees, q_width, blocks):
    tree = qkv.shape[0]
    rows = tree // blocks
    kv_width = (qkv.shape[1] - q_width) // 2
    kv_heads = kv_width // HEAD_DIM
    whole = lambda width: pl.BlockSpec((tree, width), lambda i, order: (0, 0))
    natural = lambda width: pl.BlockSpec((rows, width), lambda i, order: (i, 0))
    return pl.pallas_call(
        functools.partial(attention_forward_kernel, kv_heads, blocks),
        grid_spec=pltpu.PrefetchScalarGridSpec(
            num_scalar_prefetch=1,
            grid=(blocks,),
            in_specs=[
                pl.BlockSpec((rows, q_width), lambda i, order: (order[i], 0)),
                pl.BlockSpec((tree, 2 * kv_width), lambda i, order: (0, q_width // (2 * kv_width))),
                whole(PAIR),
                whole(PAIR),
                whole(PAIR),
                whole(PAIR),
            ],
            out_specs=[
                pl.BlockSpec((rows, q_width), lambda i, order: (order[i], 0)),
                natural(q_width),
                whole(2 * kv_width),
                natural(PAIR),
            ],
            scratch_shapes=[
                pltpu.VMEM((2 * kv_heads, tree, PAIR), BF16),
                pltpu.VMEM((2 * kv_heads, tree, PAIR), BF16),
                pltpu.VMEM((rows, tree), F32),
            ],
        ),
        out_shape=[
            jax.ShapeDtypeStruct((tree, q_width), BF16),
            jax.ShapeDtypeStruct((tree, q_width), BF16),
            jax.ShapeDtypeStruct((tree, 2 * kv_width), BF16),
            jax.ShapeDtypeStruct((tree, PAIR), F32),
        ],
        compiler_params=pltpu.CompilerParams(vmem_limit_bytes=40 << 20),
        cost_estimate=pl.CostEstimate(
            flops=10_000_000_000, bytes_accessed=12_000_000, transcendentals=5_000_000
        ),
        name="attention_forward",
    )(order, qkv, qkv, cosine, sine, member, sees)


def attention_backward_kernel(
    kv_heads,
    blocks,
    order_ref,
    grad_ref,
    q_ref,
    kv_ref,
    lse_ref,
    cos_ref,
    sin_ref,
    member_ref,
    sees_ref,
    dq_ref,
    dkv_ref,
    keys,
    values,
    bias,
    key_sum,
    value_sum,
):
    step = pl.program_id(0)
    rows = q_ref.shape[0]
    tree = rows * blocks
    kv_width = kv_heads * HEAD_DIM

    @pl.when(step == 0)
    def _():
        for b in range(blocks):
            here = pl.ds(b * rows, rows)
            both = kv_ref[here, :].astype(F32)
            if kv_width >= PAIR:
                turned, plain = both[:, :kv_width], both[:, kv_width:]
            else:
                turned, plain = both, pltpu.roll(both, HEAD_DIM, 1)
            for index, placed in enumerate(place_heads(turned, kv_heads, 0.0)):
                keys[index, here, :] = placed.astype(BF16)
            for index, placed in enumerate(place_heads(plain, kv_heads, 0.0)):
                values[index, here, :] = placed.astype(BF16)
        key_sum[...] = jnp.zeros_like(key_sum)
        value_sum[...] = jnp.zeros_like(value_sum)

    here = pl.ds(pl.multiple_of(step * rows, rows), rows)
    link = dot_nt(member_ref[...], sees_ref[here, :])
    key_index = lax.broadcasted_iota(jnp.int32, (tree, rows), 0)
    query_index = lax.broadcasted_iota(jnp.int32, (tree, rows), 1) + step * rows
    bias[...] = jnp.where((link > 0.5) & (key_index <= query_index), 0.0, NEGATIVE)
    lse_rows = jnp.transpose(lse_ref[...])

    for block in range(blocks):
        width = (block + 1) * rows

        @pl.when(step == block)
        def _(width=width):
            cosine, sine = cos_ref[here, :], sin_ref[here, :]
            for j in range(q_ref.shape[1] // PAIR):
                lanes = slice(j * PAIR, j * PAIR + PAIR)
                group = 2 * j // GROUP
                query, grad = q_ref[:, lanes], grad_ref[:, lanes]
                dq = jnp.zeros((rows, PAIR), F32)
                for p in range(2):
                    index, head = group * 2 + p, 2 * j + p
                    scores = dot_nt(keys[index, :width, :], query) + bias[:width, :]
                    probs = jnp.exp(scores - lse_rows[head : head + 1, :])
                    probs_grad = dot_nt(values[index, :width, :], grad)
                    value_sum[index, :width, :] += dot_nn(probs.astype(BF16), grad)
                    weighted = probs * probs_grad
                    delta = jnp.sum(weighted, axis=0, keepdims=True)
                    score_grad = (weighted - probs * delta).astype(BF16)
                    key_sum[index, :width, :] += dot_nn(score_grad, query)
                    dq = dq + dot_tn(score_grad, keys[index, :width, :])
                dq_ref[:, lanes] = turn(dq * ATTN_SCALE, cosine, -sine).astype(BF16)

    @pl.when(step == blocks - 1)
    def _():
        for b in range(blocks):
            here = pl.ds(b * rows, rows)
            there = pl.ds(pl.multiple_of(order_ref[b] * rows, rows), rows)
            cosine, sine = cos_ref[here, :], sin_ref[here, :]
            lane = lax.broadcasted_iota(jnp.int32, (rows, PAIR), 1)
            lower = lane < HEAD_DIM
            for c in range(0, kv_heads, 2):
                halves = []
                for acc in (key_sum, value_sum):
                    own, other = [], []
                    for g in range(c, min(c + 2, kv_heads)):
                        low, high = acc[g * 2, here, :], acc[g * 2 + 1, here, :]
                        own.append(low)
                        other.append(high)
                    first = own[0] + pltpu.roll(other[0], HEAD_DIM, 1)
                    if len(own) == 2:
                        second = other[1] + pltpu.roll(own[1], HEAD_DIM, 1)
                    else:
                        second = first
                    halves.append(jnp.where(lower, first, second))
                turned = turn(halves[0], cosine, -sine)
                if kv_width >= PAIR:
                    lanes = slice(c * HEAD_DIM, c * HEAD_DIM + PAIR)
                    dkv_ref[there, lanes] = turned.astype(BF16)
                    lanes = slice(kv_width + c * HEAD_DIM, kv_width + c * HEAD_DIM + PAIR)
                    dkv_ref[there, lanes] = halves[1].astype(BF16)
                else:
                    moved = pltpu.roll(halves[1], HEAD_DIM, 1)
                    dkv_ref[there, :] = jnp.where(lower, turned, moved).astype(BF16)


def attention_backward(order, grad, query, kv, lse, cosine, sine, member, sees, blocks):
    tree, q_width = query.shape
    rows = tree // blocks
    kv_width = kv.shape[1] // 2
    kv_heads = kv_width // HEAD_DIM
    whole = lambda width: pl.BlockSpec((tree, width), lambda i, order: (0, 0))
    natural = lambda width: pl.BlockSpec((rows, width), lambda i, order: (i, 0))
    ordered = lambda width: pl.BlockSpec((rows, width), lambda i, order: (order[i], 0))
    return pl.pallas_call(
        functools.partial(attention_backward_kernel, kv_heads, blocks),
        grid_spec=pltpu.PrefetchScalarGridSpec(
            num_scalar_prefetch=1,
            grid=(blocks,),
            in_specs=[
                ordered(q_width),
                natural(q_width),
                whole(2 * kv_width),
                natural(PAIR),
                whole(PAIR),
                whole(PAIR),
                whole(PAIR),
                whole(PAIR),
            ],
            out_specs=[ordered(q_width), whole(2 * kv_width)],
            scratch_shapes=[
                pltpu.VMEM((2 * kv_heads, tree, PAIR), BF16),
                pltpu.VMEM((2 * kv_heads, tree, PAIR), BF16),
                pltpu.VMEM((tree, rows), F32),
                pltpu.VMEM((2 * kv_heads, tree, PAIR), F32),
                pltpu.VMEM((2 * kv_heads, tree, PAIR), F32),
            ],
        ),
        out_shape=[
            jax.ShapeDtypeStruct((tree, q_width), BF16),
            jax.ShapeDtypeStruct((tree, 2 * kv_width), BF16),
        ],
        compiler_params=pltpu.CompilerParams(vmem_limit_bytes=48 << 20),
        cost_estimate=pl.CostEstimate(
            flops=20_000_000_000, bytes_accessed=12_000_000, transcendentals=5_000_000
        ),
        name="attention_backward",
    )(order, grad, query, kv, lse, cosine, sine, member, sees)


def sync(*values):
    return lax.optimization_barrier(values)


def assemble(where, chunks):
    rows, width = chunks[0][0].shape
    block = math.gcd(rows, 128)
    each = rows // block
    half = each * len(chunks)

    def source(c, k):
        def index(i, where):
            local = jnp.clip(i - (k // 2) * half - c * each, 0, each - 1)
            chosen = where[1] == (1 if k % 2 == 0 else 0)
            return (jnp.where(chosen, local, 0), 0)

        return pl.BlockSpec((block, width), index)

    def target(i, where):
        own = i < half
        return (jnp.where(own, where[0] * half + i, (1 - where[0]) * half + i - half), 0)

    def kernel(where_ref, *refs):
        i = pl.program_id(0)
        out = refs[-1]
        for c in range(len(chunks)):
            for k in range(4):
                begin = (k // 2) * half + c * each

                @pl.when(
                    (i >= begin)
                    & (i < begin + each)
                    & (where_ref[1] == (1 if k % 2 == 0 else 0))
                )
                def _(ref=refs[4 * c + k]):
                    out[...] = ref[...].astype(F32)

    return pl.pallas_call(
        kernel,
        grid_spec=pltpu.PrefetchScalarGridSpec(
            num_scalar_prefetch=1,
            grid=(2 * half,),
            in_specs=[source(c, k) for c in range(len(chunks)) for k in range(4)],
            out_specs=pl.BlockSpec((block, width), target),
        ),
        out_shape=jax.ShapeDtypeStruct((2 * half * block, width), F32),
        compiler_params=pltpu.CompilerParams(vmem_limit_bytes=40 << 20),
        cost_estimate=pl.CostEstimate(
            flops=0, bytes_accessed=12 * half * block * width, transcendentals=0
        ),
        name="assemble",
    )(where, *[array for chunk in chunks for array in chunk])


class Square:
    def __init__(self, shard, replica):
        self.shard, self.replica = shard, replica
        self.x = [(i, i ^ 1) for i in range(shard)]
        self.y = [(i, i ^ 2) for i in range(shard)]
        self.d = [(i, i ^ 3) for i in range(shard)]
        self.core = [(i, i ^ 1) for i in range(replica)]
        both = lambda pairs: [(2 * a + c, 2 * b + c) for a, b in pairs for c in range(2)]
        self.inward = both([(0, 1), (3, 2)])
        self.outward = both([(1, 0), (2, 3)])
        self.middle = both([(1, 2), (2, 1)])

    def order(self):
        return jnp.arange(self.shard, dtype=jnp.int32) ^ lax.axis_index("shard")

    def reorder(self, blocks, axis):
        me = lax.axis_index("shard")
        return jnp.concatenate(
            [lax.dynamic_slice_in_dim(blocks, n ^ me, 1, axis) for n in range(self.shard)], axis=axis
        )

    def gather_small(self, own):
        parts = [
            own,
            lax.ppermute(own, "shard", self.x),
            lax.ppermute(own, "shard", self.y),
            lax.ppermute(own, "shard", self.d),
        ]
        return self.reorder(jnp.stack(parts), 0)

    def gather_first(self, own):
        return lax.ppermute(own, "shard", self.x), lax.ppermute(own, "shard", self.y)

    def gather_second(self, own, got):
        from_x, from_y = got
        half = own.shape[0] // 2
        first = lax.ppermute(from_y[:half], "shard", self.x)
        second = lax.ppermute(from_x[half:], "shard", self.y)
        return [own, from_x, from_y, first, second]

    def split(self, part):
        trees, width = part.shape[0] // self.rows // 4, part.shape[1]
        return part.reshape(trees, 4, 2, self.rows // 2, width)

    def sum_first(self, part):
        pieces = self.split(part)
        send_x = jnp.stack([pieces[:, 1, 0], pieces[:, 3, 0]])
        send_y = jnp.stack([pieces[:, 2, 1], pieces[:, 3, 1]])
        return lax.ppermute(send_x, "shard", self.x), lax.ppermute(send_y, "shard", self.y)

    def sum_second(self, part, got):
        pieces = self.split(part)
        got_x, got_y = got
        next_y = (pieces[:, 2, 0].astype(F32) + got_x[1].astype(F32)).astype(BF16)
        next_x = (pieces[:, 1, 1].astype(F32) + got_y[1].astype(F32)).astype(BF16)
        return lax.ppermute(next_y, "shard", self.y), lax.ppermute(next_x, "shard", self.x)

    def sum_last(self, part, got, last):
        pieces = self.split(part)
        wide = lambda v: v.astype(F32)
        first = wide(pieces[:, 0, 0]) + wide(got[0][0]) + wide(last[0])
        second = wide(pieces[:, 0, 1]) + wide(got[1][0]) + wide(last[1])
        both = jnp.concatenate([first, second], axis=1)
        return [both[t] for t in range(both.shape[0])]

    def sum_small(self, values):
        share = values.shape[1] // self.shard
        blocks = values.reshape(values.shape[0], self.shard, share)
        blocks = self.reorder(blocks, 1)
        total = blocks[:, 0]
        for k, perm in ((1, self.x), (2, self.y), (3, self.d)):
            total = total + lax.ppermute(blocks[:, k], "shard", perm)
        for step in (1, 2, 4):
            perm = [(i, i ^ step) for i in range(self.replica)]
            total = total + lax.ppermute(total, "replica", perm)
        return total

    def start_line(self):
        self.waiting = []
        self.inward_flight = None
        self.middle_flight = None
        self.outward_flight = None
        self.finals = {}

    def feed(self, name, grad, chunks):
        half = grad.shape[0] // 2
        core = lax.axis_index("replica") % 2
        send = lax.dynamic_slice_in_dim(grad, (1 - core) * half, half, 0)
        got = lax.ppermute(send, "replica", self.core)
        rows = half // chunks
        self.finals[name] = [None] * chunks
        for c in range(chunks):
            keep = lax.dynamic_slice_in_dim(grad, core * half + c * rows, rows, 0)
            mine = keep.astype(F32) + got[c * rows : (c + 1) * rows].astype(F32)
            self.waiting.append(((name, c), mine.astype(BF16)))

    def tick(self, *values):
        flying = (self.inward_flight, self.middle_flight, self.outward_flight)
        chunk = self.waiting.pop(0) if self.waiting else None
        landed, mine, values = sync(
            tuple(f and f[-1] for f in flying), None if chunk is None else chunk[1], values
        )
        add = lambda a, b: (a.astype(F32) + b.astype(F32)).astype(BF16)
        move = lambda v, perm: lax.ppermute(v, "replica", perm)
        self.inward_flight = self.middle_flight = self.outward_flight = None
        if flying[0] is not None:
            pair = add(flying[0][1], landed[0])
            self.middle_flight = (flying[0][0], pair, move(pair, self.middle))
        if flying[1] is not None:
            whole = add(flying[1][1], landed[1])
            self.outward_flight = (flying[1][0], whole, move(whole, self.outward))
        if flying[2] is not None:
            (name, c), whole, _ = flying[2]
            self.finals[name][c] = (
                whole,
                landed[2],
                move(whole, self.core),
                move(landed[2], self.core),
            )
        if chunk is not None:
            self.inward_flight = (chunk[0], mine, move(mine, self.inward))
        return values

    def finish(self, name):
        place = lax.axis_index("replica")
        z = place // 2
        inner = ((z == 1) | (z == 2)).astype(jnp.int32)
        return assemble(jnp.stack([place % 2, inner]), self.finals[name])

    def drain(self):
        while self.waiting or self.inward_flight or self.middle_flight or self.outward_flight:
            self.tick()


class General:
    def __init__(self, shard, replica):
        self.shard, self.replica = shard, replica

    def order(self):
        return jnp.arange(self.shard, dtype=jnp.int32)

    def gather_small(self, own):
        return lax.all_gather(own, "shard", axis=0, tiled=False)

    def gather_first(self, own):
        return lax.all_gather(own, "shard", axis=0, tiled=True)

    def gather_second(self, own, got):
        return [got]

    def sum_first(self, part):
        return lax.psum_scatter(
            part.reshape(-1, self.shard * self.rows, part.shape[1]),
            "shard",
            scatter_dimension=1,
            tiled=True,
        )

    def sum_second(self, part, got):
        return ()

    def sum_last(self, part, got, last):
        return [got[t].astype(F32) for t in range(got.shape[0])]

    def sum_small(self, values):
        share = lax.psum_scatter(values, "shard", scatter_dimension=1, tiled=True)
        return lax.psum(share, "replica")

    def start_line(self):
        self.finals = {}

    def feed(self, name, grad, chunks):
        self.finals[name] = lax.psum(grad, "replica").astype(F32)

    def tick(self, *values):
        return values

    def drain(self):
        pass

    def finish(self, name):
        return self.finals[name]


def rms_scale(values):
    return lax.rsqrt(jnp.mean(values * values, axis=-1, keepdims=True) + EPSILON)


def normalized(piece, gain):
    values = piece.astype(F32)
    return (values * rms_scale(values) * gain).astype(BF16)


def norm_back(values, scale, gain, grad_in):
    scaled = values * scale
    weighted = grad_in * gain
    back = scale * (weighted - scaled * jnp.mean(weighted * scaled, axis=-1, keepdims=True))
    return back, jnp.sum(grad_in * scaled, axis=0)


def body(
    links,
    tokens,
    gain_attn,
    w_query,
    w_key,
    w_value,
    w_out,
    gain_ff,
    w_gate,
    w_up,
    w_down,
    cotangent,
    segment_ids,
    parents,
):
    trees, _, own_rows, width = tokens.shape
    shard = links.shard
    q_width, kv_width = w_query.shape[0], w_key.shape[0]
    tree_rows = own_rows * shard
    links.rows = own_rows
    links.start_line()
    order = links.order()
    share = gain_attn.shape[0]
    w_qkv = jnp.concatenate([w_query, w_key, w_value], axis=0)
    token_rows = [tokens[t, 0] for t in range(trees)]
    cot_rows = [cotangent[t, 0] for t in range(trees)]

    small = jnp.concatenate(
        [gain_attn, gain_ff] + [segment_ids[t, 0].astype(BF16) for t in range(trees)]
    )
    smalls = links.gather_small(small)
    got = links.gather_first(token_rows[0])
    got, smalls, token_rows = sync(got, smalls, token_rows)
    gain_first = smalls[:, :share].reshape(width).astype(F32)
    gain_second = smalls[:, share : 2 * share].reshape(width).astype(F32)
    masks, tables = [], []
    for t in range(trees):
        begin = 2 * share + t * own_rows
        segments = smalls[:, begin : begin + own_rows].reshape(tree_rows).astype(jnp.int32)
        position, member, sees = tree_layout(segments, parents[t, 0])
        masks.append((member, sees))
        tables.append(rope_tables(position))

    normed_all, saved = [], []

    def project(pieces):
        normed = jnp.concatenate([normalized(piece, gain_first) for piece in pieces], axis=0)
        normed_all.append(normed)
        return dot_nt(normed, w_qkv)

    def attention(t, qkv):
        attended, query, kv, lse = attention_forward(
            order, qkv, *tables[t], *masks[t], q_width, shard
        )
        saved.append((attended, query, kv, lse))
        return dot_nn(attended, w_out).astype(BF16)

    def after_attention(t, branch):
        value = token_rows[t].astype(F32) + RESIDUAL * branch
        scale = rms_scale(value)
        return value, scale, (value * scale * gain_second).astype(BF16)

    pieces_0 = links.gather_second(token_rows[0], got)
    got = links.gather_first(token_rows[1])
    pieces_0, got, cot_rows = sync(pieces_0, got, cot_rows)

    pieces_1 = links.gather_second(token_rows[1], got)
    cot_got = links.gather_first(cot_rows[0])
    part_0 = attention(0, project(pieces_0))
    part_0, pieces_1, cot_got = sync(part_0, pieces_1, cot_got)

    got_0 = links.sum_first(part_0)
    qkv_1 = project(pieces_1)
    got_0, qkv_1, cot_got = sync(got_0, qkv_1, cot_got)

    last_0 = links.sum_second(part_0, got_0)
    cot_pieces_0 = links.gather_second(cot_rows[0], cot_got)
    part_1 = attention(1, qkv_1)
    last_0, part_1 = sync(last_0, part_1)

    got_1 = links.sum_first(part_1)
    middle_0, scale_0, own_0 = after_attention(0, links.sum_last(part_0, got_0, last_0)[0])
    ff_got_0 = links.gather_first(own_0)
    got_1, own_0 = sync(got_1, own_0)

    last_1 = links.sum_second(part_1, got_1)
    last_1, ff_got_0 = sync(last_1, ff_got_0)

    ff_pieces_0 = links.gather_second(own_0, ff_got_0)
    middle_1, scale_1, own_1 = after_attention(1, links.sum_last(part_1, got_1, last_1)[0])
    ff_got_1 = links.gather_first(own_1)
    ff_pieces_0, ff_got_1, own_1, cot_pieces_0 = sync(ff_pieces_0, ff_got_1, own_1, cot_pieces_0)
    ff_pieces_1 = links.gather_second(own_1, ff_got_1)
    ff_pieces_0, ff_pieces_1, cot_rows, cot_pieces_0 = sync(
        ff_pieces_0, ff_pieces_1, cot_rows, cot_pieces_0
    )

    rows_all = jnp.concatenate(ff_pieces_0 + ff_pieces_1, axis=0)
    cot_got = links.gather_first(cot_rows[1])
    gate = dot_nt(rows_all, w_gate).astype(BF16)
    gate, cot_got, rows_all = sync(gate, cot_got, rows_all)
    cot_pieces_1 = links.gather_second(cot_rows[1], cot_got)
    upper = dot_nt(rows_all, w_up)
    wide = gate.astype(F32)
    hidden = (wide * jax.nn.sigmoid(wide) * upper).astype(BF16)
    upper = upper.astype(BF16)
    hidden, upper, gate, cot_pieces_1 = sync(hidden, upper, gate, cot_pieces_1)
    cot_all = jnp.concatenate(
        [(RESIDUAL * piece.astype(F32)).astype(BF16) for piece in cot_pieces_0 + cot_pieces_1], axis=0
    )
    grad_down = dot_tn(hidden, cot_all).astype(BF16)
    grad_down, hidden, cot_all, gate, upper = sync(grad_down, hidden, cot_all, gate, upper)
    links.feed("down", grad_down, 4)
    hidden_grad = dot_nt(cot_all, w_down)
    wide = gate.astype(F32)
    sigma = jax.nn.sigmoid(wide)
    gate_grad = (
        hidden_grad * upper.astype(F32) * sigma * (1.0 + wide * (1.0 - sigma))
    ).astype(BF16)
    up_grad = (hidden_grad * wide * sigma).astype(BF16)
    gate_grad, up_grad, hidden = links.tick(gate_grad, up_grad, hidden)

    half_part = dot_nn(gate_grad, w_gate)
    half_part, gate_grad, up_grad = links.tick(half_part, gate_grad, up_grad)
    ff_part = (half_part + dot_nn(up_grad, w_up)).astype(BF16)
    ff_part, gate_grad, up_grad, hidden = links.tick(ff_part, gate_grad, up_grad, hidden)

    ff_sum = links.sum_first(ff_part)
    grad_gate = dot_tn(gate_grad, rows_all).astype(BF16)
    grad_gate, up_grad, ff_sum = links.tick(grad_gate, up_grad, ff_sum)
    links.feed("gate", grad_gate, 4)
    ff_last = links.sum_second(ff_part, ff_sum)
    grad_up = dot_tn(up_grad, rows_all).astype(BF16)
    grad_up, hidden, ff_last = links.tick(grad_up, hidden, ff_last)
    links.feed("up", grad_up, 4)

    ff_grad = links.sum_last(ff_part, ff_sum, ff_last)
    out_own, middle_grads = [], []
    gain_ff_sum = jnp.zeros((width,), F32)
    for t, (middle, scale) in enumerate(((middle_0, scale_0), (middle_1, scale_1))):
        middle_back, term = norm_back(middle, scale, gain_second, ff_grad[t])
        gain_ff_sum = gain_ff_sum + term
        middle_grads.append(cot_rows[t].astype(F32) + middle_back)
        out_own.append((RESIDUAL * middle_grads[t]).astype(BF16))
    out_own, hidden = links.tick(out_own, hidden)
    out_got_0 = links.gather_first(out_own[0])
    down_part = dot_nn(hidden, w_down).astype(BF16)
    down_part, out_got_0, out_own = links.tick(down_part, out_got_0, out_own)

    out_pieces_0 = links.gather_second(out_own[0], out_got_0)
    out_got_1 = links.gather_first(out_own[1])
    out_pieces_0, out_got_1, down_part = links.tick(out_pieces_0, out_got_1, down_part)

    def attention_back(t, out_all):
        attended, query, kv, lse = saved[t]
        attended_grad = dot_nt(out_all, w_out).astype(BF16)
        dq, dkv = attention_backward(
            order, attended_grad, query, kv, lse, *tables[t], *masks[t], shard
        )
        qkv_grad = jnp.concatenate([dq, dkv], axis=1)
        (qkv_grad,) = links.tick(qkv_grad)
        return qkv_grad, dot_nn(qkv_grad, w_qkv).astype(BF16)

    out_pieces_1 = links.gather_second(out_own[1], out_got_1)
    down_sum = links.sum_first(down_part)
    out_all_0 = jnp.concatenate(out_pieces_0, axis=0)
    qkv_grad_0, normed_part_0 = attention_back(0, out_all_0)
    qkv_grad_0, normed_part_0, out_pieces_1, down_sum = links.tick(
        qkv_grad_0, normed_part_0, out_pieces_1, down_sum
    )

    normed_sum_0 = links.sum_first(normed_part_0)
    down_last = links.sum_second(down_part, down_sum)
    out_all_1 = jnp.concatenate(out_pieces_1, axis=0)
    qkv_grad_1, normed_part_1 = attention_back(1, out_all_1)
    qkv_grad_1, normed_part_1, normed_sum_0, down_last = links.tick(
        qkv_grad_1, normed_part_1, normed_sum_0, down_last
    )

    normed_last_0 = links.sum_second(normed_part_0, normed_sum_0)
    normed_sum_1 = links.sum_first(normed_part_1)
    attended_all = jnp.concatenate([saved[t][0] for t in range(trees)], axis=0)
    grad_out = dot_tn(attended_all, jnp.concatenate([out_all_0, out_all_1], axis=0)).astype(BF16)
    grad_out, qkv_grad_0, qkv_grad_1 = links.tick(grad_out, qkv_grad_0, qkv_grad_1)
    links.feed("out", grad_out, 1)
    grad_qkv = dot_tn(
        jnp.concatenate([qkv_grad_0, qkv_grad_1], axis=0), jnp.concatenate(normed_all, axis=0)
    ).astype(BF16)
    grad_qkv, normed_last_0, normed_sum_1 = links.tick(grad_qkv, normed_last_0, normed_sum_1)
    links.feed("qkv", grad_qkv, 2)

    normed_last_1 = links.sum_second(normed_part_1, normed_sum_1)
    down = links.sum_last(down_part, down_sum, down_last)
    results = [
        (middle + RESIDUAL * down[t]).astype(BF16) for t, middle in enumerate((middle_0, middle_1))
    ]
    results, normed_last_1 = links.tick(results, normed_last_1)
    normed_grads = links.sum_last(normed_part_0, normed_sum_0, normed_last_0)
    normed_grads += links.sum_last(normed_part_1, normed_sum_1, normed_last_1)
    input_grads = []
    gain_attn_sum = jnp.zeros((width,), F32)
    for t in range(trees):
        inputs = token_rows[t].astype(F32)
        input_back, term = norm_back(inputs, rms_scale(inputs), gain_first, normed_grads[t])
        gain_attn_sum = gain_attn_sum + term
        input_grads.append(middle_grads[t] + input_back)
    gains = links.sum_small(jnp.stack([gain_attn_sum, gain_ff_sum]))
    links.drain()
    grad_qkv = links.finish("qkv")
    return (
        jnp.stack(results)[:, None],
        jnp.stack(input_grads)[:, None],
        gains[0],
        grad_qkv[:q_width],
        grad_qkv[q_width : q_width + kv_width],
        grad_qkv[q_width + kv_width :],
        links.finish("out"),
        gains[1],
        links.finish("gate"),
        links.finish("up"),
        links.finish("down"),
    )


def solution(mesh):
    shard, replica = mesh.shape["shard"], mesh.shape["replica"]
    links = (Square if (shard, replica) == (4, 8) else General)(shard, replica)
    in_specs = (
        P(None, "replica", "shard", None),
        P("shard"),
        P("shard", None),
        P("shard", None),
        P("shard", None),
        P("shard", None),
        P("shard"),
        P("shard", None),
        P("shard", None),
        P("shard", None),
        P(None, "replica", "shard", None),
        P(None, "replica", "shard"),
        P(None, "replica", None),
    )
    out_specs = (
        P(None, "replica", "shard", None),
        P(None, "replica", "shard", None),
        P("shard"),
        P("shard", None),
        P("shard", None),
        P("shard", None),
        P("shard", None),
        P("shard"),
        P("shard", None),
        P("shard", None),
        P("shard", None),
    )
    return jax.shard_map(
        functools.partial(body, links),
        mesh=mesh,
        in_specs=in_specs,
        out_specs=out_specs,
        check_vma=False,
    )
```

```python
import functools
import math

import jax
import jax.numpy as jnp
from jax import lax
from jax.experimental import pallas as pl
from jax.experimental.pallas import tpu as pltpu
from jax.sharding import PartitionSpec as P

HEADS = 32
KV_HEADS = 8
HEAD_DIM = 64
PAIR = 2 * HEAD_DIM
GROUP = HEADS // KV_HEADS

EPSILON = 1e-05
RESIDUAL = 0.22
ATTN_SCALE = 0.015625
ROPE_BASE = 10000000.0
NEGATIVE = -1e30
BF16 = jnp.bfloat16
F32 = jnp.float32


def dot_nt(left, right):
    return lax.dot_general(left, right, (((1,), (1,)), ((), ())), preferred_element_type=F32)


def dot_nn(left, right):
    return lax.dot_general(left, right, (((1,), (0,)), ((), ())), preferred_element_type=F32)


def dot_tn(left, right):
    return lax.dot_general(left, right, (((0,), (0,)), ((), ())), preferred_element_type=F32)


def tree_layout(segment_row, parent_row):
    seg_numbers = jnp.arange(parent_row.shape[0], dtype=jnp.int32)
    member = (segment_row[:, None] == seg_numbers[None, :]).astype(jnp.int32)
    lengths = jnp.sum(member, axis=0)
    earlier = seg_numbers[None, :] < seg_numbers[:, None]
    starts = jnp.sum(jnp.where(earlier, lengths[None, :], 0), axis=1)
    parent_hit = parent_row[:, None] == seg_numbers[None, :]
    grandparent = jnp.sum(jnp.where(parent_hit, parent_row[None, :], 0), axis=1)
    itself = seg_numbers[:, None] == seg_numbers[None, :]
    related = itself | parent_hit | (grandparent[:, None] == seg_numbers[None, :])
    before = jnp.sum(jnp.where(related & jnp.logical_not(itself), lengths[None, :], 0), axis=1)
    shift = jnp.sum(member * (before - starts)[None, :], axis=1)
    position = jnp.arange(segment_row.shape[0], dtype=jnp.int32) + shift
    pad = ((0, 0), (0, PAIR - parent_row.shape[0]))
    sees = dot_nn(member.astype(BF16), related.astype(BF16)).astype(BF16)
    return position, jnp.pad(member.astype(BF16), pad), jnp.pad(sees, pad)


def rope_tables(position):
    lane = jnp.arange(PAIR, dtype=jnp.int32) % HEAD_DIM
    half = HEAD_DIM // 2
    fraction = (lane % half).astype(F32) * (2.0 / HEAD_DIM)
    freq = jnp.exp(-math.log(ROPE_BASE) * fraction)
    angle = position.astype(F32)[:, None] * freq[None, :]
    return jnp.cos(angle), jnp.sin(angle) * jnp.where(lane < half, -1.0, 1.0)[None, :]


MESH = pl.DeviceIdType.MESH
CHUNK = 64


def remote(source, target, sems, index, device):
    return pltpu.make_async_remote_copy(
        source, target, sems.at[0, index], sems.at[1, index], device_id=device, device_id_type=MESH
    )


class GatherJob:
    def __init__(self, own):
        self.operand = own
        self.rows, self.width = own.shape
        self.chunks = self.rows // CHUNK
        self.out_shape = jax.ShapeDtypeStruct((4 * self.rows, self.width), own.dtype)
        self.out_spec = pl.BlockSpec(memory_space=pl.ANY)

    def scratch(self):
        return [pltpu.SemaphoreType.DMA((2, 3 * self.chunks)), pltpu.SemaphoreType.DMA(())]

    def bind(self, operand, out, scratch, x, y):
        sems, local = scratch
        n, rows = self.chunks, self.rows
        at = lambda block, j: out.at[pl.ds(block * rows + j * CHUNK, CHUNK), :]
        own = lambda j: operand.at[pl.ds(j * CHUNK, CHUNK), :]
        self.local = pltpu.make_async_copy(operand, out.at[pl.ds(0, rows), :], local)
        self.to_x = [remote(own(j), at(1, j), sems, j, x) for j in range(n)]
        self.to_y = [remote(own(j), at(2, j), sems, n + j, y) for j in range(n)]
        self.on_x = [remote(at(2, j), at(3, j), sems, 2 * n + j, x) for j in range(n // 2)]
        self.on_y = [remote(at(1, j), at(3, j), sems, 2 * n + j, y) for j in range(n // 2, n)]

    def begin(self):
        n = self.chunks
        half = n // 2
        for k in range(n):
            self.to_x[(k + half) % n].start()
            self.to_y[k].start()
        self.local.start()

    def stages(self):
        def stage(k):
            half = self.chunks // 2
            self.to_y[k].wait_recv()
            self.on_x[k].start()
            self.to_x[half + k].wait_recv()
            self.on_y[k].start()

        return [functools.partial(stage, k) for k in range(self.chunks // 2)]

    def finish(self):
        half = self.chunks // 2
        for copy in self.to_x[:half] + self.to_y[half:] + self.on_x + self.on_y:
            copy.wait_recv()
        for copy in self.to_x + self.to_y + self.on_x + self.on_y:
            copy.wait_send()
        self.local.wait()


class SumJob:
    def __init__(self, part):
        self.operand = part
        self.rows, self.width = part.shape[0] // 4, part.shape[1]
        self.half = self.rows // 2
        self.chunks = self.half // CHUNK
        self.out_shape = jax.ShapeDtypeStruct((self.rows, self.width), F32)
        self.out_spec = pl.BlockSpec((self.rows, self.width), lambda *_: (0, 0))

    def scratch(self):
        return [
            pltpu.VMEM((4, self.half, self.width), BF16),
            pltpu.VMEM((6, self.half, self.width), BF16),
            pltpu.SemaphoreType.DMA((2, 6 * self.chunks)),
            pltpu.SemaphoreType.DMA((4,)),
        ]

    def bind(self, part, out, scratch, x, y):
        self.out = out
        self.mine, self.got, sems, local = scratch
        n, half = self.chunks, self.half
        rows = lambda block, second: pl.ds(block * self.rows + second * half, half)
        piece = lambda block, second, j: part.at[
            pl.ds(block * self.rows + second * half + j * CHUNK, CHUNK), :
        ]
        here = lambda ref, k, j: ref.at[k, pl.ds(j * CHUNK, CHUNK), :]
        self.loads = [
            pltpu.make_async_copy(part.at[rows(block, second), :], self.mine.at[k], local.at[k])
            for k, (block, second) in enumerate(((0, 0), (0, 1), (2, 0), (1, 1)))
        ]
        send = lambda k, source, device: [
            remote(source(j), here(self.got, k, j), sems, k * n + j, device) for j in range(n)
        ]
        self.sends = [
            send(0, lambda j: piece(1, 0, j), x),
            send(1, lambda j: piece(3, 0, j), x),
            send(2, lambda j: here(self.mine, 2, j), y),
            send(3, lambda j: piece(2, 1, j), y),
            send(4, lambda j: piece(3, 1, j), y),
            send(5, lambda j: here(self.mine, 3, j), x),
        ]

    def begin(self):
        for j in range(self.chunks):
            self.sends[1][j].start()
            self.sends[4][j].start()
        for load in self.loads:
            load.start()
        for j in range(self.chunks):
            self.sends[0][j].start()
            self.sends[3][j].start()

    def stages(self):
        def stage(j):
            if j == 0:
                for load in self.loads:
                    load.wait()
            rows = pl.ds(j * CHUNK, CHUNK)
            for first, second, own in ((1, 2, 2), (4, 5, 3)):
                self.sends[first][j].wait_recv()
                total = self.mine[own, rows, :].astype(F32) + self.got[first, rows, :].astype(F32)
                self.mine[own, rows, :] = total.astype(BF16)
                self.sends[second][j].start()

        return [functools.partial(stage, j) for j in range(self.chunks)]

    def finish(self):
        for j in range(self.chunks):
            rows = pl.ds(j * CHUNK, CHUNK)
            for own, one, two in ((0, 0, 2), (1, 3, 5)):
                self.sends[one][j].wait_recv()
                self.sends[two][j].wait_recv()
                self.out[pl.ds(own * self.half + j * CHUNK, CHUNK), :] = (
                    self.mine[own, rows, :].astype(F32)
                    + self.got[one, rows, :].astype(F32)
                    + self.got[two, rows, :].astype(F32)
                )
        for copies in self.sends:
            for copy in copies:
                copy.wait_send()


class Comm:
    def __init__(self, jobs, number):
        self.jobs, self.number = jobs, number
        self.operands = [job.operand for job in jobs]
        self.in_specs = [pl.BlockSpec(memory_space=pl.ANY) for _ in jobs]
        self.out_specs = [job.out_spec for job in jobs]
        self.out_shapes = [job.out_shape for job in jobs]
        self.scratch = [entry for job in jobs for entry in job.scratch()]

    def enter(self, operands, outs, scratch, now):
        shard, replica = lax.axis_index("shard"), lax.axis_index("replica")
        x = (shard + 1 - 2 * (shard % 2), replica)
        y = ((shard + 2) % 4, replica)
        scratch = list(scratch)
        for job, operand, out in zip(self.jobs, operands, outs):
            count = len(job.scratch())
            job.bind(operand, out, scratch[:count], x, y)
            scratch = scratch[count:]

        @pl.when(now)
        def _():
            barrier = pltpu.get_barrier_semaphore()
            for device in (x, y):
                pl.semaphore_signal(barrier, inc=1, device_id=device, device_id_type=MESH)
            pl.semaphore_wait(barrier, 2)
            for job in self.jobs:
                job.begin()

    def stages(self):
        return [stage for job in self.jobs for stage in job.stages()]

    def advance(self, step, steps):
        stages = self.stages()
        for index, stage in enumerate(stages):
            due = min(steps - 1, steps // 2 + index * (steps - steps // 2) // len(stages))
            pl.when(step == due)(stage)

    def finish(self, now):
        @pl.when(now)
        def _():
            for job in self.jobs:
                job.finish()


class NoComm:
    operands = in_specs = out_specs = out_shapes = scratch = ()
    number = None

    def enter(self, *_):
        pass

    def advance(self, *_):
        pass

    def finish(self, *_):
        pass


def comm_params(comm, vmem):
    if comm.number is None:
        return pltpu.CompilerParams(vmem_limit_bytes=vmem << 20)
    return pltpu.CompilerParams(
        vmem_limit_bytes=vmem << 20, collective_id=comm.number, has_side_effects=True
    )


def split_refs(refs, *counts):
    parts, begin = [], 0
    for count in counts:
        parts.append(refs[begin : begin + count])
        begin += count
    return parts


def transfer(comm):
    count = len(comm.operands)

    def kernel(*refs):
        operands, outs, scratch = split_refs(refs, count, count, len(comm.scratch))
        now = pl.program_id(0) == 0
        comm.enter(operands, outs, scratch, now)
        for stage in comm.stages():
            stage()
        comm.finish(now)

    return pl.pallas_call(
        kernel,
        grid=(1,),
        in_specs=comm.in_specs,
        out_specs=comm.out_specs,
        out_shape=comm.out_shapes,
        scratch_shapes=comm.scratch,
        compiler_params=comm_params(comm, 40),
        name="transfer",
    )(*comm.operands)


def products(items, block, comm):
    specs, shapes, out_specs, steps, rights = [], [], [], [], []
    total = sum((l.shape[1] if t else l.shape[0]) // block for l, _, t in items)
    begin = 0
    for left, right, transposed in items:
        size = left.shape[1] if transposed else left.shape[0]
        count = size // block

        def place(i, begin=begin, count=count):
            return jnp.clip(i - begin, 0, count - 1)

        if transposed:
            specs.append(pl.BlockSpec((left.shape[0], block), lambda i, p=place: (0, p(i))))
        else:
            specs.append(pl.BlockSpec((block, left.shape[1]), lambda i, p=place: (p(i), 0)))
        out_specs.append(pl.BlockSpec((block, right.shape[1]), lambda i, p=place: (p(i), 0)))
        shapes.append(jax.ShapeDtypeStruct((size, right.shape[1]), BF16))
        if not any(right is r for r in rights):
            rights.append(right)
        steps.append((begin, count))
        begin += count
    right_specs = [
        pl.BlockSpec(r.shape, lambda i: (0, 0), pipeline_mode=pl.Buffered(1)) for r in rights
    ]
    which = [next(k for k, r in enumerate(rights) if r is right) for _, right, _ in items]
    n = len(items)

    def kernel(*refs):
        lefts, held, operands, outs, comm_outs, scratch = split_refs(
            refs, n, len(rights), len(comm.operands), n, len(comm.operands), len(comm.scratch)
        )
        step = pl.program_id(0)
        comm.enter(operands, comm_outs, scratch, step == 0)
        comm.advance(step, total)
        for k, (_, _, transposed) in enumerate(items):
            begin, count = steps[k]

            @pl.when((step >= begin) & (step < begin + count))
            def _(k=k, transposed=transposed):
                dot = dot_tn if transposed else dot_nn
                outs[k][...] = dot(lefts[k][...], held[which[k]][...]).astype(BF16)

        comm.finish(step == total - 1)

    flops = 2 * sum(math.prod(l.shape) * r.shape[1] for l, r, _ in items)
    out = pl.pallas_call(
        kernel,
        grid=(total,),
        in_specs=specs + right_specs + list(comm.in_specs),
        out_specs=out_specs + list(comm.out_specs),
        out_shape=shapes + list(comm.out_shapes),
        scratch_shapes=list(comm.scratch),
        compiler_params=comm_params(comm, 58),
        cost_estimate=pl.CostEstimate(flops=flops, bytes_accessed=30_000_000, transcendentals=0),
        name="products",
    )(*[l for l, _, _ in items], *rights, *comm.operands)
    return out[:n], out[n:]


def swap_halves(block):
    lane = lax.broadcasted_iota(jnp.int32, block.shape, 1)
    half = HEAD_DIM // 2
    up = pltpu.roll(block, PAIR - half, 1)
    down = pltpu.roll(block, half, 1)
    return jnp.where(lane % HEAD_DIM < half, up, down)


def turn(block, cosine, sine):
    return block * cosine + swap_halves(block) * sine


def place_heads(wide, kv_heads, fill):
    placed = []
    for g in range(kv_heads):
        base = wide[:, (g // 2) * PAIR : (g // 2) * PAIR + PAIR] if wide.shape[1] >= PAIR else wide
        lane = lax.broadcasted_iota(jnp.int32, base.shape, 1)
        moved = pltpu.roll(base, HEAD_DIM, 1)
        for p in range(2):
            source = base if g % 2 == p else moved
            inside = (lane // HEAD_DIM) == p
            placed.append(jnp.where(inside, source, jnp.full_like(source, fill)))
    return placed


def attention_forward_kernel(kv_heads, blocks, place, comm, *refs):
    jobs = len(comm.operands)
    inputs, operands, outs, comm_outs, own, scratch = split_refs(
        refs, 6, jobs, 4, jobs, 3, len(comm.scratch)
    )
    q_ref, kv_ref, cos_ref, sin_ref, member_ref, sees_ref = inputs
    out_ref, q_out_ref, kv_out_ref, lse_ref = outs
    keys, values, bias = own
    step = pl.program_id(0)
    comm.enter(operands, comm_outs, scratch, step == 0)
    comm.advance(step, blocks)
    tree = q_ref.shape[0]
    rows = tree // blocks
    kv_width = kv_heads * HEAD_DIM

    @pl.when(step == 0)
    def _():
        for b in range(blocks):
            here = pl.ds(b * rows, rows)
            raw = kv_ref[pl.ds(pl.multiple_of(place(b) * rows, rows), rows), :]
            cosine, sine = cos_ref[here, :], sin_ref[here, :]
            if kv_width >= PAIR:
                turned = jnp.concatenate(
                    [
                        turn(raw[:, c : c + PAIR], cosine, sine)
                        for c in range(0, kv_width, PAIR)
                    ],
                    axis=1,
                )
                plain = raw[:, kv_width:]
            else:
                lane = lax.broadcasted_iota(jnp.int32, raw.shape, 1)
                turned = turn(raw, cosine, sine)
                plain = pltpu.roll(raw, HEAD_DIM, 1)
                both = jnp.where(lane < HEAD_DIM, turned, raw)
            if kv_width >= PAIR:
                both = jnp.concatenate([turned, plain], axis=1)
            kv_out_ref[here, :] = both.astype(BF16)
            for index, placed in enumerate(place_heads(turned, kv_heads, 0.0)):
                keys[index, here, :] = placed.astype(BF16)
            for index, placed in enumerate(place_heads(plain, kv_heads, 1.0)):
                values[index, here, :] = placed.astype(BF16)

    here = pl.ds(pl.multiple_of(step * rows, rows), rows)
    there = pl.ds(pl.multiple_of(place(step) * rows, rows), rows)
    cosine, sine = cos_ref[here, :], sin_ref[here, :]
    for j in range(q_ref.shape[1] // PAIR):
        lanes = slice(j * PAIR, j * PAIR + PAIR)
        turned = turn(q_ref[there, lanes], cosine, sine).astype(BF16)
        q_out_ref[:, lanes] = turned * BF16(ATTN_SCALE)

    link = dot_nt(sees_ref[here, :], member_ref[...])
    row_index = lax.broadcasted_iota(jnp.int32, (rows, tree), 0) + step * rows
    col_index = lax.broadcasted_iota(jnp.int32, (rows, tree), 1)
    bias[...] = jnp.where((link > 0.5) & (col_index <= row_index), 0.0, NEGATIVE)

    lane = lax.broadcasted_iota(jnp.int32, (rows, PAIR), 1)
    for block in range(blocks):
        width = (block + 1) * rows

        @pl.when(step == block)
        def _(width=width):
            lse = jnp.zeros((rows, PAIR), F32)
            for j in range(q_ref.shape[1] // PAIR):
                lanes = slice(j * PAIR, j * PAIR + PAIR)
                group = 2 * j // GROUP
                mixed, tops = [], []
                for p in range(2):
                    scores = dot_nt(q_out_ref[:, lanes], keys[group * 2 + p, :width, :])
                    scores = scores + bias[:, :width]
                    top = jnp.max(scores, axis=1, keepdims=True)
                    expo = jnp.exp(scores - top).astype(BF16)
                    mixed.append(dot_nn(expo, values[group * 2 + p, :width, :]))
                    tops.append(top)
                upper = lane >= HEAD_DIM
                total = pltpu.roll(jnp.where(upper, mixed[0], mixed[1]), HEAD_DIM, 1)
                out_ref[there, lanes] = (jnp.where(upper, mixed[1], mixed[0]) / total).astype(BF16)
                logs = jnp.log(total)
                lse = jnp.where(lane == 2 * j, tops[0] + logs[:, :1], lse)
                lse = jnp.where(lane == 2 * j + 1, tops[1] + logs[:, HEAD_DIM : HEAD_DIM + 1], lse)
            lse_ref[...] = lse

    comm.finish(step == blocks - 1)


def attention_forward(place, qkv, cosine, sine, member, sees, q_width, blocks, comm):
    tree = qkv.shape[0]
    rows = tree // blocks
    kv_width = (qkv.shape[1] - q_width) // 2
    kv_heads = kv_width // HEAD_DIM
    whole = lambda width: pl.BlockSpec((tree, width), lambda i: (0, 0))
    natural = lambda width: pl.BlockSpec((rows, width), lambda i: (i, 0))
    out = pl.pallas_call(
        functools.partial(attention_forward_kernel, kv_heads, blocks, place, comm),
        grid_spec=pl.GridSpec(
            grid=(blocks,),
            in_specs=[
                whole(q_width),
                pl.BlockSpec((tree, 2 * kv_width), lambda i: (0, q_width // (2 * kv_width))),
                whole(PAIR),
                whole(PAIR),
                whole(PAIR),
                whole(PAIR),
                *comm.in_specs,
            ],
            out_specs=[
                whole(q_width),
                natural(q_width),
                whole(2 * kv_width),
                natural(PAIR),
                *comm.out_specs,
            ],
            scratch_shapes=[
                pltpu.VMEM((2 * kv_heads, tree, PAIR), BF16),
                pltpu.VMEM((2 * kv_heads, tree, PAIR), BF16),
                pltpu.VMEM((rows, tree), F32),
                *comm.scratch,
            ],
        ),
        out_shape=[
            jax.ShapeDtypeStruct((tree, q_width), BF16),
            jax.ShapeDtypeStruct((tree, q_width), BF16),
            jax.ShapeDtypeStruct((tree, 2 * kv_width), BF16),
            jax.ShapeDtypeStruct((tree, PAIR), F32),
            *comm.out_shapes,
        ],
        compiler_params=comm_params(comm, 40),
        cost_estimate=pl.CostEstimate(
            flops=10_000_000_000, bytes_accessed=12_000_000, transcendentals=5_000_000
        ),
        name="attention_forward",
    )(qkv, qkv, cosine, sine, member, sees, *comm.operands)
    return out[:4], out[4:]


def attention_backward_kernel(kv_heads, blocks, place, comm, *refs):
    jobs = len(comm.operands)
    inputs, operands, outs, comm_outs, own, scratch = split_refs(
        refs, 8, jobs, 2, jobs, 5, len(comm.scratch)
    )
    grad_ref, q_ref, kv_ref, lse_ref, cos_ref, sin_ref, member_ref, sees_ref = inputs
    dq_ref, dkv_ref = outs
    keys, values, bias, key_sum, value_sum = own
    step = pl.program_id(0)
    comm.enter(operands, comm_outs, scratch, step == 0)
    comm.advance(step, blocks)
    tree, rows = grad_ref.shape[0], q_ref.shape[0]
    kv_width = kv_heads * HEAD_DIM

    @pl.when(step == 0)
    def _():
        for b in range(blocks):
            here = pl.ds(b * rows, rows)
            both = kv_ref[here, :].astype(F32)
            if kv_width >= PAIR:
                turned, plain = both[:, :kv_width], both[:, kv_width:]
            else:
                turned, plain = both, pltpu.roll(both, HEAD_DIM, 1)
            for index, placed in enumerate(place_heads(turned, kv_heads, 0.0)):
                keys[index, here, :] = placed.astype(BF16)
            for index, placed in enumerate(place_heads(plain, kv_heads, 0.0)):
                values[index, here, :] = placed.astype(BF16)
        key_sum[...] = jnp.zeros_like(key_sum)
        value_sum[...] = jnp.zeros_like(value_sum)

    here = pl.ds(pl.multiple_of(step * rows, rows), rows)
    there = pl.ds(pl.multiple_of(place(step) * rows, rows), rows)
    link = dot_nt(member_ref[...], sees_ref[here, :])
    key_index = lax.broadcasted_iota(jnp.int32, (tree, rows), 0)
    query_index = lax.broadcasted_iota(jnp.int32, (tree, rows), 1) + step * rows
    bias[...] = jnp.where((link > 0.5) & (key_index <= query_index), 0.0, NEGATIVE)
    lse_rows = jnp.transpose(lse_ref[...])

    for block in range(blocks):
        width = (block + 1) * rows

        @pl.when(step == block)
        def _(width=width):
            cosine, sine = cos_ref[here, :], sin_ref[here, :]
            for j in range(q_ref.shape[1] // PAIR):
                lanes = slice(j * PAIR, j * PAIR + PAIR)
                group = 2 * j // GROUP
                query, grad = q_ref[:, lanes], grad_ref[there, lanes]
                dq = jnp.zeros((rows, PAIR), F32)
                for p in range(2):
                    index, head = group * 2 + p, 2 * j + p
                    scores = dot_nt(keys[index, :width, :], query) + bias[:width, :]
                    probs = jnp.exp(scores - lse_rows[head : head + 1, :])
                    probs_grad = dot_nt(values[index, :width, :], grad)
                    value_sum[index, :width, :] += dot_nn(probs.astype(BF16), grad)
                    weighted = probs * probs_grad
                    delta = jnp.sum(weighted, axis=0, keepdims=True)
                    score_grad = (weighted - probs * delta).astype(BF16)
                    key_sum[index, :width, :] += dot_nn(score_grad, query)
                    dq = dq + dot_tn(score_grad, keys[index, :width, :])
                dq_ref[there, lanes] = turn(dq * ATTN_SCALE, cosine, -sine).astype(BF16)

    @pl.when(step == blocks - 1)
    def _():
        for b in range(blocks):
            here = pl.ds(b * rows, rows)
            there = pl.ds(pl.multiple_of(place(b) * rows, rows), rows)
            cosine, sine = cos_ref[here, :], sin_ref[here, :]
            lane = lax.broadcasted_iota(jnp.int32, (rows, PAIR), 1)
            lower = lane < HEAD_DIM
            for c in range(0, kv_heads, 2):
                halves = []
                for acc in (key_sum, value_sum):
                    own, other = [], []
                    for g in range(c, min(c + 2, kv_heads)):
                        low, high = acc[g * 2, here, :], acc[g * 2 + 1, here, :]
                        own.append(low)
                        other.append(high)
                    first = own[0] + pltpu.roll(other[0], HEAD_DIM, 1)
                    if len(own) == 2:
                        second = other[1] + pltpu.roll(own[1], HEAD_DIM, 1)
                    else:
                        second = first
                    halves.append(jnp.where(lower, first, second))
                turned = turn(halves[0], cosine, -sine)
                if kv_width >= PAIR:
                    lanes = slice(c * HEAD_DIM, c * HEAD_DIM + PAIR)
                    dkv_ref[there, lanes] = turned.astype(BF16)
                    lanes = slice(kv_width + c * HEAD_DIM, kv_width + c * HEAD_DIM + PAIR)
                    dkv_ref[there, lanes] = halves[1].astype(BF16)
                else:
                    moved = pltpu.roll(halves[1], HEAD_DIM, 1)
                    dkv_ref[there, :] = jnp.where(lower, turned, moved).astype(BF16)

    comm.finish(step == blocks - 1)


def attention_backward(place, grad, query, kv, lse, cosine, sine, member, sees, blocks, comm):
    tree, q_width = query.shape
    rows = tree // blocks
    kv_width = kv.shape[1] // 2
    kv_heads = kv_width // HEAD_DIM
    whole = lambda width: pl.BlockSpec((tree, width), lambda i: (0, 0))
    natural = lambda width: pl.BlockSpec((rows, width), lambda i: (i, 0))
    out = pl.pallas_call(
        functools.partial(attention_backward_kernel, kv_heads, blocks, place, comm),
        grid_spec=pl.GridSpec(
            grid=(blocks,),
            in_specs=[
                whole(q_width),
                natural(q_width),
                whole(2 * kv_width),
                natural(PAIR),
                whole(PAIR),
                whole(PAIR),
                whole(PAIR),
                whole(PAIR),
                *comm.in_specs,
            ],
            out_specs=[whole(q_width), whole(2 * kv_width), *comm.out_specs],
            scratch_shapes=[
                pltpu.VMEM((2 * kv_heads, tree, PAIR), BF16),
                pltpu.VMEM((2 * kv_heads, tree, PAIR), BF16),
                pltpu.VMEM((tree, rows), F32),
                pltpu.VMEM((2 * kv_heads, tree, PAIR), F32),
                pltpu.VMEM((2 * kv_heads, tree, PAIR), F32),
                *comm.scratch,
            ],
        ),
        out_shape=[
            jax.ShapeDtypeStruct((tree, q_width), BF16),
            jax.ShapeDtypeStruct((tree, 2 * kv_width), BF16),
            *comm.out_shapes,
        ],
        compiler_params=comm_params(comm, 56),
        cost_estimate=pl.CostEstimate(
            flops=20_000_000_000, bytes_accessed=12_000_000, transcendentals=5_000_000
        ),
        name="attention_backward",
    )(grad, query, kv, lse, cosine, sine, member, sees, *comm.operands)
    return out[:2], out[2:]


def sync(*values):
    return lax.optimization_barrier(values)


def assemble(where, chunks):
    rows, width = chunks[0][0].shape
    block = math.gcd(rows, 128)
    each = rows // block
    half = each * len(chunks)

    def source(c, k):
        def index(i, where):
            local = jnp.clip(i - (k // 2) * half - c * each, 0, each - 1)
            chosen = where[1] == (1 if k % 2 == 0 else 0)
            return (jnp.where(chosen, local, 0), 0)

        return pl.BlockSpec((block, width), index)

    def target(i, where):
        own = i < half
        return (jnp.where(own, where[0] * half + i, (1 - where[0]) * half + i - half), 0)

    def kernel(where_ref, *refs):
        i = pl.program_id(0)
        out = refs[-1]
        for c in range(len(chunks)):
            for k in range(4):
                begin = (k // 2) * half + c * each

                @pl.when(
                    (i >= begin)
                    & (i < begin + each)
                    & (where_ref[1] == (1 if k % 2 == 0 else 0))
                )
                def _(ref=refs[4 * c + k]):
                    out[...] = ref[...].astype(F32)

    return pl.pallas_call(
        kernel,
        grid_spec=pltpu.PrefetchScalarGridSpec(
            num_scalar_prefetch=1,
            grid=(2 * half,),
            in_specs=[source(c, k) for c in range(len(chunks)) for k in range(4)],
            out_specs=pl.BlockSpec((block, width), target),
        ),
        out_shape=jax.ShapeDtypeStruct((2 * half * block, width), F32),
        compiler_params=pltpu.CompilerParams(vmem_limit_bytes=40 << 20),
        cost_estimate=pl.CostEstimate(
            flops=0, bytes_accessed=12 * half * block * width, transcendentals=0
        ),
        name="assemble",
    )(where, *[array for chunk in chunks for array in chunk])


class Square:
    def __init__(self, shard, replica):
        self.shard, self.replica = shard, replica
        self.x = [(i, i ^ 1) for i in range(shard)]
        self.y = [(i, i ^ 2) for i in range(shard)]
        self.d = [(i, i ^ 3) for i in range(shard)]
        self.core = [(i, i ^ 1) for i in range(replica)]
        both = lambda pairs: [(2 * a + c, 2 * b + c) for a, b in pairs for c in range(2)]
        self.inward = both([(0, 1), (3, 2)])
        self.outward = both([(1, 0), (2, 3)])
        self.middle = both([(1, 2), (2, 1)])

    def place(self, block):
        shard = lax.axis_index("shard")
        return (block + shard) % 2 + 2 * ((block // 2 + shard // 2) % 2)

    def reorder(self, blocks, axis):
        me = lax.axis_index("shard")
        return jnp.concatenate(
            [lax.dynamic_slice_in_dim(blocks, n ^ me, 1, axis) for n in range(self.shard)], axis=axis
        )

    def gather_small(self, own):
        parts = [
            own,
            lax.ppermute(own, "shard", self.x),
            lax.ppermute(own, "shard", self.y),
            lax.ppermute(own, "shard", self.d),
        ]
        return self.reorder(jnp.stack(parts), 0)

    def sum_small(self, values):
        share = values.shape[1] // self.shard
        blocks = values.reshape(values.shape[0], self.shard, share)
        blocks = self.reorder(blocks, 1)
        total = blocks[:, 0]
        for k, perm in ((1, self.x), (2, self.y), (3, self.d)):
            total = total + lax.ppermute(blocks[:, k], "shard", perm)
        for step in (1, 2, 4):
            perm = [(i, i ^ step) for i in range(self.replica)]
            total = total + lax.ppermute(total, "replica", perm)
        return total

    def gather_start(self, own):
        return lax.ppermute(own, "shard", self.x), lax.ppermute(own, "shard", self.y)

    def gather_more(self, own, got):
        from_x, from_y = got
        half = own.shape[0] // 2
        first = lax.ppermute(from_y[:half], "shard", self.x)
        second = lax.ppermute(from_x[half:], "shard", self.y)
        return [own, from_x, from_y, first, second]

    def carry(self, compute, gathers=(), sums=()):
        jobs = [GatherJob(own) for own in gathers] + [SumJob(part) for part in sums]
        self.kernels += 1
        comm = Comm(jobs, self.kernels)
        if compute is None:
            results, moved = None, transfer(comm)
        else:
            results, moved = compute(comm)
        return results, list(moved[: len(gathers)]), list(moved[len(gathers) :])

    def start_line(self):
        self.kernels = 0
        self.waiting = []
        self.inward_flight = None
        self.middle_flight = None
        self.outward_flight = None
        self.finals = {}

    def feed(self, name, grad, chunks):
        half = grad.shape[0] // 2
        core = lax.axis_index("replica") % 2
        send = lax.dynamic_slice_in_dim(grad, (1 - core) * half, half, 0)
        got = lax.ppermute(send, "replica", self.core)
        rows = half // chunks
        self.finals[name] = [None] * chunks
        for c in range(chunks):
            keep = lax.dynamic_slice_in_dim(grad, core * half + c * rows, rows, 0)
            mine = keep.astype(F32) + got[c * rows : (c + 1) * rows].astype(F32)
            self.waiting.append(((name, c), mine.astype(BF16)))

    def tick(self, *values):
        flying = (self.inward_flight, self.middle_flight, self.outward_flight)
        chunk = self.waiting.pop(0) if self.waiting else None
        landed, mine, values = sync(
            tuple(f and f[-1] for f in flying), None if chunk is None else chunk[1], values
        )
        add = lambda a, b: (a.astype(F32) + b.astype(F32)).astype(BF16)
        move = lambda v, perm: lax.ppermute(v, "replica", perm)
        self.inward_flight = self.middle_flight = self.outward_flight = None
        if flying[0] is not None:
            pair = add(flying[0][1], landed[0])
            self.middle_flight = (flying[0][0], pair, move(pair, self.middle))
        if flying[1] is not None:
            whole = add(flying[1][1], landed[1])
            self.outward_flight = (flying[1][0], whole, move(whole, self.outward))
        if flying[2] is not None:
            (name, c), whole, _ = flying[2]
            self.finals[name][c] = (
                whole,
                landed[2],
                move(whole, self.core),
                move(landed[2], self.core),
            )
        if chunk is not None:
            self.inward_flight = (chunk[0], mine, move(mine, self.inward))
        return values

    def finish(self, name):
        place = lax.axis_index("replica")
        z = place // 2
        inner = ((z == 1) | (z == 2)).astype(jnp.int32)
        return assemble(jnp.stack([place % 2, inner]), self.finals[name])

    def drain(self):
        while self.waiting or self.inward_flight or self.middle_flight or self.outward_flight:
            self.tick()


class General:
    def __init__(self, shard, replica):
        self.shard, self.replica = shard, replica

    def place(self, block):
        return block

    def gather_small(self, own):
        return lax.all_gather(own, "shard", axis=0, tiled=False)

    def carry(self, compute, gathers=(), sums=()):
        results = None if compute is None else compute(NoComm())[0]
        gathered = [lax.all_gather(own, "shard", axis=0, tiled=True) for own in gathers]
        summed = [
            lax.psum_scatter(part, "shard", scatter_dimension=0, tiled=True).astype(F32)
            for part in sums
        ]
        return results, gathered, summed

    def gather_start(self, own):
        return lax.all_gather(own, "shard", axis=0, tiled=True)

    def gather_more(self, own, got):
        return [got]

    def sum_small(self, values):
        share = lax.psum_scatter(values, "shard", scatter_dimension=1, tiled=True)
        return lax.psum(share, "replica")

    def start_line(self):
        self.finals = {}

    def feed(self, name, grad, chunks):
        self.finals[name] = lax.psum(grad, "replica").astype(F32)

    def tick(self, *values):
        return values

    def drain(self):
        pass

    def finish(self, name):
        return self.finals[name]


def rms_scale(values):
    return lax.rsqrt(jnp.mean(values * values, axis=-1, keepdims=True) + EPSILON)


def normalized(piece, gain):
    values = piece.astype(F32)
    return (values * rms_scale(values) * gain).astype(BF16)


def norm_back(values, scale, gain, grad_in):
    scaled = values * scale
    weighted = grad_in * gain
    back = scale * (weighted - scaled * jnp.mean(weighted * scaled, axis=-1, keepdims=True))
    return back, jnp.sum(grad_in * scaled, axis=0)


def body(
    links,
    tokens,
    gain_attn,
    w_query,
    w_key,
    w_value,
    w_out,
    gain_ff,
    w_gate,
    w_up,
    w_down,
    cotangent,
    segment_ids,
    parents,
):
    trees, _, own_rows, width = tokens.shape
    shard = links.shard
    q_width, kv_width = w_query.shape[0], w_key.shape[0]
    tree_rows = own_rows * shard
    links.start_line()
    share = gain_attn.shape[0]
    w_qkv = jnp.concatenate([w_query, w_key, w_value], axis=0)
    token_rows = [tokens[t, 0] for t in range(trees)]
    cot_rows = [cotangent[t, 0] for t in range(trees)]

    small = jnp.concatenate(
        [gain_attn, gain_ff] + [segment_ids[t, 0].astype(BF16) for t in range(trees)]
    )
    smalls = links.gather_small(small)
    _, (rows_0,), _ = links.carry(None, gathers=[token_rows[0]])
    gain_first = smalls[:, :share].reshape(width).astype(F32)
    gain_second = smalls[:, share : 2 * share].reshape(width).astype(F32)
    masks, tables = [], []
    for t in range(trees):
        begin = 2 * share + t * own_rows
        segments = smalls[:, begin : begin + own_rows].reshape(tree_rows).astype(jnp.int32)
        position, member, sees = tree_layout(segments, parents[t, 0])
        masks.append((member, sees))
        tables.append(rope_tables(position))

    def attention(t, qkv):
        return lambda comm: attention_forward(
            links.place, qkv, *tables[t], *masks[t], q_width, shard, comm
        )

    def after_attention(t, branch):
        value = token_rows[t].astype(F32) + RESIDUAL * branch
        scale = rms_scale(value)
        return value, scale, (value * scale * gain_second).astype(BF16)

    normed_0 = normalized(rows_0, gain_first)
    saved_0, (rows_1,), _ = links.carry(
        attention(0, dot_nt(normed_0, w_qkv)), gathers=[token_rows[1]]
    )
    part_0 = dot_nn(saved_0[0], w_out).astype(BF16)
    normed_1 = normalized(rows_1, gain_first)
    saved_1, _, (branch_0,) = links.carry(attention(1, dot_nt(normed_1, w_qkv)), sums=[part_0])
    part_1 = dot_nn(saved_1[0], w_out).astype(BF16)
    middle_0, scale_0, own_0 = after_attention(0, branch_0)
    _, (ff_rows_0,), (branch_1,) = links.carry(None, gathers=[own_0], sums=[part_1])
    middle_1, scale_1, own_1 = after_attention(1, branch_1)
    _, (ff_rows_1,), _ = links.carry(None, gathers=[own_1])
    ff_rows_0, ff_rows_1, cot_rows = sync(ff_rows_0, ff_rows_1, cot_rows)

    cot_got = [links.gather_start(cot) for cot in cot_rows]
    rows_all = jnp.concatenate([ff_rows_0, ff_rows_1], axis=0)
    gate = dot_nt(rows_all, w_gate).astype(BF16)
    gate, cot_got, rows_all = sync(gate, cot_got, rows_all)
    cot_pieces = [links.gather_more(cot, got) for cot, got in zip(cot_rows, cot_got)]
    upper = dot_nt(rows_all, w_up)
    wide = gate.astype(F32)
    hidden = (wide * jax.nn.sigmoid(wide) * upper).astype(BF16)
    upper = upper.astype(BF16)
    hidden, upper, gate, cot_pieces = sync(hidden, upper, gate, cot_pieces)
    cot_all = jnp.concatenate(
        [(RESIDUAL * piece.astype(F32)).astype(BF16) for pieces in cot_pieces for piece in pieces],
        axis=0,
    )
    grad_down = dot_tn(hidden, cot_all).astype(BF16)
    grad_down, hidden, cot_all, gate, upper = sync(grad_down, hidden, cot_all, gate, upper)
    links.feed("down", grad_down, 1)
    cot_all, gate, upper, hidden = links.tick(cot_all, gate, upper, hidden)
    hidden_grad = dot_nt(cot_all, w_down)
    wide = gate.astype(F32)
    sigma = jax.nn.sigmoid(wide)
    gate_grad = (
        hidden_grad * upper.astype(F32) * sigma * (1.0 + wide * (1.0 - sigma))
    ).astype(BF16)
    up_grad = (hidden_grad * wide * sigma).astype(BF16)
    ff_part = (dot_nn(gate_grad, w_gate) + dot_nn(up_grad, w_up)).astype(BF16)
    ff_part, gate_grad, up_grad, hidden = links.tick(ff_part, gate_grad, up_grad, hidden)

    parts = lambda whole: [whole[t * tree_rows : (t + 1) * tree_rows] for t in range(trees)]
    (grad_gate, grad_up), _, ff_grad = links.carry(
        lambda comm: products([(gate_grad, rows_all, True), (up_grad, rows_all, True)], 512, comm),
        sums=parts(ff_part),
    )
    links.feed("gate", grad_gate, 1)
    links.feed("up", grad_up, 1)
    (hidden, ff_grad) = links.tick(hidden, ff_grad)
    out_own, middle_grads = [], []
    gain_ff_sum = jnp.zeros((width,), F32)
    for t, (middle, scale) in enumerate(((middle_0, scale_0), (middle_1, scale_1))):
        middle_back, term = norm_back(middle, scale, gain_second, ff_grad[t])
        gain_ff_sum = gain_ff_sum + term
        middle_grads.append(cot_rows[t].astype(F32) + middle_back)
        out_own.append((RESIDUAL * middle_grads[t]).astype(BF16))
    (down_part,), out_alls, _ = links.carry(
        lambda comm: products([(hidden, w_down, False)], 512, comm), gathers=out_own
    )
    down_part, out_alls = links.tick(down_part, out_alls)

    def attention_back(t, saved):
        _, query, kv, lse = saved
        attended_grad = dot_nt(out_alls[t], w_out).astype(BF16)
        return lambda comm: attention_backward(
            links.place, attended_grad, query, kv, lse, *tables[t], *masks[t], shard, comm
        )

    down_parts = parts(down_part)
    back_0, _, (down_0,) = links.carry(attention_back(0, saved_0), sums=[down_parts[0]])
    back_1, _, (down_1,) = links.carry(attention_back(1, saved_1), sums=[down_parts[1]])
    results = [
        (middle + RESIDUAL * down).astype(BF16)
        for middle, down in ((middle_0, down_0), (middle_1, down_1))
    ]
    qkv_grad = jnp.concatenate(
        [jnp.concatenate(back_0, axis=1), jnp.concatenate(back_1, axis=1)], axis=0
    )
    normed_part = dot_nn(qkv_grad, w_qkv).astype(BF16)
    qkv_grad, normed_part, results = links.tick(qkv_grad, normed_part, results)
    attended_all = jnp.concatenate([saved_0[0], saved_1[0]], axis=0)
    out_all = jnp.concatenate(out_alls, axis=0)
    normed_all = jnp.concatenate([normed_0, normed_1], axis=0)
    (grad_out, grad_qkv), _, normed_grads = links.carry(
        lambda comm: products(
            [(attended_all, out_all, True), (qkv_grad, normed_all, True)], 128 if shard > 4 else 256, comm
        ),
        sums=parts(normed_part),
    )
    grad_out, grad_qkv, normed_grads = links.tick(grad_out, grad_qkv, normed_grads)
    links.feed("out", grad_out, 1)
    links.feed("qkv", grad_qkv, 1)
    input_grads = []
    gain_attn_sum = jnp.zeros((width,), F32)
    for t in range(trees):
        inputs = token_rows[t].astype(F32)
        input_back, term = norm_back(inputs, rms_scale(inputs), gain_first, normed_grads[t])
        gain_attn_sum = gain_attn_sum + term
        input_grads.append(middle_grads[t] + input_back)
    gains = links.sum_small(jnp.stack([gain_attn_sum, gain_ff_sum]))
    links.drain()
    grad_qkv = links.finish("qkv")
    return (
        jnp.stack(results)[:, None],
        jnp.stack(input_grads)[:, None],
        gains[0],
        grad_qkv[:q_width],
        grad_qkv[q_width : q_width + kv_width],
        grad_qkv[q_width + kv_width :],
        links.finish("out"),
        gains[1],
        links.finish("gate"),
        links.finish("up"),
        links.finish("down"),
    )


def solution(mesh):
    shard, replica = mesh.shape["shard"], mesh.shape["replica"]
    links = (Square if (shard, replica) == (4, 8) else General)(shard, replica)
    in_specs = (
        P(None, "replica", "shard", None),
        P("shard"),
        P("shard", None),
        P("shard", None),
        P("shard", None),
        P("shard", None),
        P("shard"),
        P("shard", None),
        P("shard", None),
        P("shard", None),
        P(None, "replica", "shard", None),
        P(None, "replica", "shard"),
        P(None, "replica", None),
    )
    out_specs = (
        P(None, "replica", "shard", None),
        P(None, "replica", "shard", None),
        P("shard"),
        P("shard", None),
        P("shard", None),
        P("shard", None),
        P("shard", None),
        P("shard"),
        P("shard", None),
        P("shard", None),
        P("shard", None),
    )
    return jax.shard_map(
        functools.partial(body, links),
        mesh=mesh,
        in_specs=in_specs,
        out_specs=out_specs,
        check_vma=False,
    )
```

```python
import functools
import math

import jax
import jax.numpy as jnp
from jax import lax
from jax.experimental import pallas as pl
from jax.experimental.pallas import tpu as pltpu
from jax.sharding import PartitionSpec as P

HEADS = 32
KV_HEADS = 8
HEAD_DIM = 64
PAIR = 2 * HEAD_DIM
GROUP = HEADS // KV_HEADS

EPSILON = 1e-05
RESIDUAL = 0.22
ATTN_SCALE = 0.015625
ROPE_BASE = 10000000.0
NEGATIVE = -1e30
BF16 = jnp.bfloat16
F32 = jnp.float32


def dot_nt(left, right):
    return lax.dot_general(left, right, (((1,), (1,)), ((), ())), preferred_element_type=F32)


def dot_nn(left, right):
    return lax.dot_general(left, right, (((1,), (0,)), ((), ())), preferred_element_type=F32)


def dot_tn(left, right):
    return lax.dot_general(left, right, (((0,), (0,)), ((), ())), preferred_element_type=F32)


def tree_layout(segment_row, parent_row):
    seg_numbers = jnp.arange(parent_row.shape[0], dtype=jnp.int32)
    member = (segment_row[:, None] == seg_numbers[None, :]).astype(jnp.int32)
    lengths = jnp.sum(member, axis=0)
    earlier = seg_numbers[None, :] < seg_numbers[:, None]
    starts = jnp.sum(jnp.where(earlier, lengths[None, :], 0), axis=1)
    parent_hit = parent_row[:, None] == seg_numbers[None, :]
    grandparent = jnp.sum(jnp.where(parent_hit, parent_row[None, :], 0), axis=1)
    itself = seg_numbers[:, None] == seg_numbers[None, :]
    related = itself | parent_hit | (grandparent[:, None] == seg_numbers[None, :])
    before = jnp.sum(jnp.where(related & jnp.logical_not(itself), lengths[None, :], 0), axis=1)
    shift = jnp.sum(member * (before - starts)[None, :], axis=1)
    position = jnp.arange(segment_row.shape[0], dtype=jnp.int32) + shift
    pad = ((0, 0), (0, PAIR - parent_row.shape[0]))
    sees = dot_nn(member.astype(BF16), related.astype(BF16)).astype(BF16)
    return position, jnp.pad(member.astype(BF16), pad), jnp.pad(sees, pad)


def rope_tables(position):
    lane = jnp.arange(PAIR, dtype=jnp.int32) % HEAD_DIM
    half = HEAD_DIM // 2
    fraction = (lane % half).astype(F32) * (2.0 / HEAD_DIM)
    freq = jnp.exp(-math.log(ROPE_BASE) * fraction)
    angle = position.astype(F32)[:, None] * freq[None, :]
    return jnp.cos(angle), jnp.sin(angle) * jnp.where(lane < half, -1.0, 1.0)[None, :]


MESH = pl.DeviceIdType.MESH
CHUNK = 64


def remote(source, target, sems, index, device):
    return pltpu.make_async_remote_copy(
        source, target, sems.at[0, index], sems.at[1, index], device_id=device, device_id_type=MESH
    )


class GatherJob:
    def __init__(self, own):
        self.operand = own
        self.rows, self.width = own.shape
        self.chunks = self.rows // CHUNK
        self.out_shape = jax.ShapeDtypeStruct((4 * self.rows, self.width), own.dtype)
        self.out_spec = pl.BlockSpec(memory_space=pl.ANY)

    def scratch(self):
        return [pltpu.SemaphoreType.DMA((2, 3 * self.chunks)), pltpu.SemaphoreType.DMA(())]

    def bind(self, operand, out, scratch, x, y):
        sems, local = scratch
        n, rows = self.chunks, self.rows
        at = lambda block, j: out.at[pl.ds(block * rows + j * CHUNK, CHUNK), :]
        own = lambda j: operand.at[pl.ds(j * CHUNK, CHUNK), :]
        self.local = pltpu.make_async_copy(operand, out.at[pl.ds(0, rows), :], local)
        self.to_x = [remote(own(j), at(1, j), sems, j, x) for j in range(n)]
        self.to_y = [remote(own(j), at(2, j), sems, n + j, y) for j in range(n)]
        self.on_x = [remote(at(2, j), at(3, j), sems, 2 * n + j, x) for j in range(n // 2)]
        self.on_y = [remote(at(1, j), at(3, j), sems, 2 * n + j, y) for j in range(n // 2, n)]

    def begin(self):
        n = self.chunks
        half = n // 2
        for k in range(n):
            self.to_x[(k + half) % n].start()
            self.to_y[k].start()
        self.local.start()

    def stages(self):
        def stage(k):
            half = self.chunks // 2
            self.to_y[k].wait_recv()
            self.on_x[k].start()
            self.to_x[half + k].wait_recv()
            self.on_y[k].start()

        return [functools.partial(stage, k) for k in range(self.chunks // 2)]

    def finish(self):
        half = self.chunks // 2
        for copy in self.to_x[:half] + self.to_y[half:] + self.on_x + self.on_y:
            copy.wait_recv()
        for copy in self.to_x + self.to_y + self.on_x + self.on_y:
            copy.wait_send()
        self.local.wait()


class SumJob:
    def __init__(self, part):
        self.operand = part
        self.rows, self.width = part.shape[0] // 4, part.shape[1]
        self.half = self.rows // 2
        self.chunks = self.half // CHUNK
        self.out_shape = jax.ShapeDtypeStruct((self.rows, self.width), F32)
        self.out_spec = pl.BlockSpec((self.rows, self.width), lambda *_: (0, 0))

    def scratch(self):
        return [
            pltpu.VMEM((4, self.half, self.width), BF16),
            pltpu.VMEM((6, self.half, self.width), BF16),
            pltpu.SemaphoreType.DMA((2, 6 * self.chunks)),
            pltpu.SemaphoreType.DMA((4,)),
        ]

    def bind(self, part, out, scratch, x, y):
        self.out = out
        self.mine, self.got, sems, local = scratch
        n, half = self.chunks, self.half
        rows = lambda block, second: pl.ds(block * self.rows + second * half, half)
        piece = lambda block, second, j: part.at[
            pl.ds(block * self.rows + second * half + j * CHUNK, CHUNK), :
        ]
        here = lambda ref, k, j: ref.at[k, pl.ds(j * CHUNK, CHUNK), :]
        self.loads = [
            pltpu.make_async_copy(part.at[rows(block, second), :], self.mine.at[k], local.at[k])
            for k, (block, second) in enumerate(((0, 0), (0, 1), (2, 0), (1, 1)))
        ]
        send = lambda k, source, device: [
            remote(source(j), here(self.got, k, j), sems, k * n + j, device) for j in range(n)
        ]
        self.sends = [
            send(0, lambda j: piece(1, 0, j), x),
            send(1, lambda j: piece(3, 0, j), x),
            send(2, lambda j: here(self.mine, 2, j), y),
            send(3, lambda j: piece(2, 1, j), y),
            send(4, lambda j: piece(3, 1, j), y),
            send(5, lambda j: here(self.mine, 3, j), x),
        ]

    def begin(self):
        for j in range(self.chunks):
            self.sends[1][j].start()
            self.sends[4][j].start()
        for load in self.loads:
            load.start()
        for j in range(self.chunks):
            self.sends[0][j].start()
            self.sends[3][j].start()

    def stages(self):
        def stage(j):
            if j == 0:
                for load in self.loads:
                    load.wait()
            rows = pl.ds(j * CHUNK, CHUNK)
            for first, second, own in ((1, 2, 2), (4, 5, 3)):
                self.sends[first][j].wait_recv()
                total = self.mine[own, rows, :].astype(F32) + self.got[first, rows, :].astype(F32)
                self.mine[own, rows, :] = total.astype(BF16)
                self.sends[second][j].start()

        return [functools.partial(stage, j) for j in range(self.chunks)]

    def finish(self):
        for j in range(self.chunks):
            rows = pl.ds(j * CHUNK, CHUNK)
            for own, one, two in ((0, 0, 2), (1, 3, 5)):
                self.sends[one][j].wait_recv()
                self.sends[two][j].wait_recv()
                self.out[pl.ds(own * self.half + j * CHUNK, CHUNK), :] = (
                    self.mine[own, rows, :].astype(F32)
                    + self.got[one, rows, :].astype(F32)
                    + self.got[two, rows, :].astype(F32)
                )
        for copies in self.sends:
            for copy in copies:
                copy.wait_send()


class LineJob:
    LINE_ROWS = 32
    LAG = 2

    def __init__(self, grad):
        self.operand = grad
        self.half, self.width = grad.shape[0] // 2, grad.shape[1]
        self.chunks = self.half // self.LINE_ROWS
        self.steps = self.chunks + 1 + 3 * self.LAG
        self.out_shape = jax.ShapeDtypeStruct(grad.shape, BF16)
        self.out_spec = pl.BlockSpec(memory_space=pl.ANY)

    def scratch(self):
        place = lambda: pltpu.VMEM((self.half, self.width), BF16)
        return [place(), place(), place(), place(), pltpu.SemaphoreType.DMA((9, self.chunks))]

    def bind(self, grad, out, scratch, x, y):
        self.grad, self.out = grad, out
        self.from_core, self.own, self.from_line, self.from_inner, self.sems = scratch
        shard, place = lax.axis_index("shard"), lax.axis_index("replica")
        self.core, z = place % 2, place // 2
        self.inner = (z == 1) | (z == 2)
        self.outer = (z == 0) | (z == 3)
        self.twin = (shard, z * 2 + 1 - self.core)
        self.pair = (shard, (z + 1 - 2 * (z % 2)) * 2 + self.core)
        self.across = (shard, (3 - z) * 2 + self.core)

    def chunk(self, c):
        return pl.ds(pl.multiple_of(c * self.LINE_ROWS, self.LINE_ROWS), self.LINE_ROWS)

    def at(self, core, c):
        return pl.ds(
            pl.multiple_of(core * self.half + c * self.LINE_ROWS, self.LINE_ROWS), self.LINE_ROWS
        )

    def send(self, source, target, index, arrival, device, c):
        return pltpu.make_async_remote_copy(
            source,
            target,
            self.sems.at[index, c],
            self.sems.at[arrival, c],
            device_id=device,
            device_id_type=MESH,
        )

    def to_twin(self, c):
        source = self.grad.at[self.at(1 - self.core, c), :]
        return self.send(source, self.from_core.at[self.chunk(c), :], 0, 1, self.twin, c)

    def load(self, c):
        source = self.grad.at[self.at(self.core, c), :]
        return pltpu.make_async_copy(source, self.own.at[self.chunk(c), :], self.sems.at[2, c])

    def inward(self, c):
        rows = self.chunk(c)
        return self.send(self.own.at[rows, :], self.from_line.at[rows, :], 3, 4, self.pair, c)

    def between(self, c):
        rows = self.chunk(c)
        return self.send(self.own.at[rows, :], self.from_inner.at[rows, :], 3, 5, self.across, c)

    def outward(self, c):
        rows = self.chunk(c)
        return self.send(self.from_core.at[rows, :], self.from_line.at[rows, :], 6, 4, self.pair, c)

    def store(self, source, c):
        target = self.out.at[self.at(self.core, c), :]
        return pltpu.make_async_copy(source.at[self.chunk(c), :], target, self.sems.at[2, c])

    def give(self, source, c):
        target = self.out.at[self.at(self.core, c), :]
        return self.send(source.at[self.chunk(c), :], target, 7, 8, self.twin, c)

    def begin(self):
        pass

    def stages(self):
        return []

    def step(self, s):
        n, lag = self.chunks, self.LAG
        live = lambda begin: (s >= begin) & (s < n + begin)
        add = lambda a, b: (a.astype(F32) + b.astype(F32)).astype(BF16)

        @pl.when(live(0))
        def _():
            self.to_twin(s).start()
            self.load(s).start()

        @pl.when(live(1))
        def _():
            c = s - 1
            rows = self.chunk(c)
            self.to_twin(c).wait()
            self.load(c).wait()
            self.own[rows, :] = add(self.own[rows, :], self.from_core[rows, :])
            pl.when(self.outer)(lambda: self.inward(c).start())

        @pl.when(live(1 + lag) & self.inner)
        def _():
            c = s - 1 - lag
            rows = self.chunk(c)
            self.inward(c).wait_recv()
            self.own[rows, :] = add(self.own[rows, :], self.from_line[rows, :])
            self.between(c).start()

        @pl.when(live(1 + 2 * lag) & self.inner)
        def _():
            c = s - 1 - 2 * lag
            rows = self.chunk(c)
            self.between(c).wait_recv()
            self.from_core[rows, :] = add(self.own[rows, :], self.from_inner[rows, :])
            self.outward(c).start()
            self.store(self.from_core, c).start()
            self.give(self.from_core, c).start()

        @pl.when(live(1 + 3 * lag) & self.outer)
        def _():
            c = s - 1 - 3 * lag
            self.outward(c).wait_recv()
            self.store(self.from_line, c).start()
            self.give(self.from_line, c).start()

    def finish(self):
        def body(c, carry):
            self.store(self.from_line, c).wait()
            self.give(self.from_line, c).wait()

            @pl.when(self.inner)
            def _():
                self.between(c).wait_send()
                self.outward(c).wait_send()

            pl.when(self.outer)(lambda: self.inward(c).wait_send())
            return carry

        lax.fori_loop(0, self.chunks, body, 0)


class Comm:
    def __init__(self, jobs, number):
        self.jobs, self.number = jobs, number
        self.operands = [job.operand for job in jobs]
        self.in_specs = [pl.BlockSpec(memory_space=pl.ANY) for _ in jobs]
        self.out_specs = [job.out_spec for job in jobs]
        self.out_shapes = [job.out_shape for job in jobs]
        self.scratch = [entry for job in jobs for entry in job.scratch()]

    def enter(self, operands, outs, scratch, now):
        shard, replica = lax.axis_index("shard"), lax.axis_index("replica")
        x = (shard + 1 - 2 * (shard % 2), replica)
        y = ((shard + 2) % 4, replica)
        scratch = list(scratch)
        for job, operand, out in zip(self.jobs, operands, outs):
            count = len(job.scratch())
            job.bind(operand, out, scratch[:count], x, y)
            scratch = scratch[count:]

        lines = [job for job in self.jobs if isinstance(job, LineJob)]
        square = len(lines) < len(self.jobs)

        @pl.when(now)
        def _():
            barrier = pltpu.get_barrier_semaphore()

            def greet(device):
                pl.semaphore_signal(barrier, inc=1, device_id=device, device_id_type=MESH)

            near = ([x, y] if square else []) + ([lines[0].twin, lines[0].pair] if lines else [])
            for device in near:
                greet(device)
            if lines:

                @pl.when(lines[0].inner)
                def _():
                    greet(lines[0].across)
                    pl.semaphore_wait(barrier, len(near) + 1)

                @pl.when(lines[0].outer)
                def _():
                    pl.semaphore_wait(barrier, len(near))

            else:
                pl.semaphore_wait(barrier, len(near))
            for job in self.jobs:
                job.begin()

    def stages(self):
        return [stage for job in self.jobs for stage in job.stages()]

    def advance(self, step, steps):
        stages = self.stages()
        for job in self.jobs:
            if isinstance(job, LineJob):
                each = -(-job.steps // steps)

                def body(k, carry, job=job, each=each):
                    job.step(step * each + k)
                    return carry

                lax.fori_loop(0, each, body, 0)
        for index, stage in enumerate(stages):
            if steps <= 4:
                due = min(steps - 1, steps // 2 + index * (steps - steps // 2) // len(stages))
            else:
                due = min(steps - 1, max(1, int(steps * (0.25 + 0.5 * index / len(stages)))))
            pl.when(step == due)(stage)

    def finish(self, now):
        @pl.when(now)
        def _():
            for job in self.jobs:
                job.finish()


class NoComm:
    operands = in_specs = out_specs = out_shapes = scratch = ()
    number = None

    def enter(self, *_):
        pass

    def advance(self, *_):
        pass

    def finish(self, *_):
        pass


def comm_params(comm, vmem):
    if comm.number is None:
        return pltpu.CompilerParams(vmem_limit_bytes=vmem << 20)
    return pltpu.CompilerParams(
        vmem_limit_bytes=vmem << 20, collective_id=comm.number, has_side_effects=True
    )


def split_refs(refs, *counts):
    parts, begin = [], 0
    for count in counts:
        parts.append(refs[begin : begin + count])
        begin += count
    return parts


def transfer(comm):
    count = len(comm.operands)
    steps = 9 if any(isinstance(job, LineJob) for job in comm.jobs) else 1

    def kernel(*refs):
        operands, outs, scratch = split_refs(refs, count, count, len(comm.scratch))
        step = pl.program_id(0)
        comm.enter(operands, outs, scratch, step == 0)
        if steps == 1:
            for stage in comm.stages():
                stage()
        else:
            comm.advance(step, steps)
        comm.finish(step == steps - 1)

    return pl.pallas_call(
        kernel,
        grid=(steps,),
        in_specs=comm.in_specs,
        out_specs=comm.out_specs,
        out_shape=comm.out_shapes,
        scratch_shapes=comm.scratch,
        compiler_params=comm_params(comm, 48),
        name="transfer",
    )(*comm.operands)


def products(items, block, comm, joined=False):
    specs, shapes, out_specs, steps, rights = [], [], [], [], []
    total = sum((l.shape[1] if t else l.shape[0]) // block for l, _, t in items)
    begin = 0
    for left, right, transposed in items:
        size = left.shape[1] if transposed else left.shape[0]
        count = size // block

        def place(i, begin=begin, count=count):
            return jnp.clip(i - begin, 0, count - 1)

        if transposed:
            specs.append(pl.BlockSpec((left.shape[0], block), lambda i, p=place: (0, p(i))))
        else:
            specs.append(pl.BlockSpec((block, left.shape[1]), lambda i, p=place: (p(i), 0)))
        if not joined:
            out_specs.append(pl.BlockSpec((block, right.shape[1]), lambda i, p=place: (p(i), 0)))
            shapes.append(jax.ShapeDtypeStruct((size, right.shape[1]), BF16))
        if not any(right is r for r in rights):
            rights.append(right)
        steps.append((begin, count))
        begin += count
    right_specs = [
        pl.BlockSpec(r.shape, lambda i: (0, 0), pipeline_mode=pl.Buffered(1)) for r in rights
    ]
    which = [next(k for k, r in enumerate(rights) if r is right) for _, right, _ in items]
    n = len(items)
    if joined:
        width = items[0][1].shape[1]
        out_specs = [pl.BlockSpec((block, width), lambda i: (i, 0))]
        shapes = [jax.ShapeDtypeStruct((total * block, width), BF16)]
    made = len(shapes)

    def kernel(*refs):
        lefts, held, operands, outs, comm_outs, scratch = split_refs(
            refs, n, len(rights), len(comm.operands), made, len(comm.operands), len(comm.scratch)
        )
        step = pl.program_id(0)
        comm.enter(operands, comm_outs, scratch, step == 0)
        comm.advance(step, total)
        for k, (_, _, transposed) in enumerate(items):
            begin, count = steps[k]

            @pl.when((step >= begin) & (step < begin + count))
            def _(k=k, transposed=transposed):
                dot = dot_tn if transposed else dot_nn
                outs[0 if joined else k][...] = dot(lefts[k][...], held[which[k]][...]).astype(BF16)

        comm.finish(step == total - 1)

    flops = 2 * sum(math.prod(l.shape) * r.shape[1] for l, r, _ in items)
    out = pl.pallas_call(
        kernel,
        grid=(total,),
        in_specs=specs + right_specs + list(comm.in_specs),
        out_specs=out_specs + list(comm.out_specs),
        out_shape=shapes + list(comm.out_shapes),
        scratch_shapes=list(comm.scratch),
        compiler_params=comm_params(comm, 58),
        cost_estimate=pl.CostEstimate(flops=flops, bytes_accessed=30_000_000, transcendentals=0),
        name="products",
    )(*[l for l, _, _ in items], *rights, *comm.operands)
    return out[:made], out[made:]


def swap_halves(block):
    lane = lax.broadcasted_iota(jnp.int32, block.shape, 1)
    half = HEAD_DIM // 2
    up = pltpu.roll(block, PAIR - half, 1)
    down = pltpu.roll(block, half, 1)
    return jnp.where(lane % HEAD_DIM < half, up, down)


def turn(block, cosine, sine):
    return block * cosine + swap_halves(block) * sine


def place_heads(wide, kv_heads, fill):
    placed = []
    for g in range(kv_heads):
        base = wide[:, (g // 2) * PAIR : (g // 2) * PAIR + PAIR] if wide.shape[1] >= PAIR else wide
        lane = lax.broadcasted_iota(jnp.int32, base.shape, 1)
        moved = pltpu.roll(base, HEAD_DIM, 1)
        for p in range(2):
            source = base if g % 2 == p else moved
            inside = (lane // HEAD_DIM) == p
            placed.append(jnp.where(inside, source, jnp.full_like(source, fill)))
    return placed


def attention_forward_kernel(kv_heads, blocks, place, comm, *refs):
    jobs = len(comm.operands)
    inputs, operands, outs, comm_outs, own, scratch = split_refs(
        refs, 6, jobs, 4, jobs, 3, len(comm.scratch)
    )
    q_ref, kv_ref, cos_ref, sin_ref, member_ref, sees_ref = inputs
    out_ref, q_out_ref, kv_out_ref, lse_ref = outs
    keys, values, bias = own
    step = pl.program_id(0)
    comm.enter(operands, comm_outs, scratch, step == 0)
    comm.advance(step, blocks)
    tree = q_ref.shape[0]
    rows = tree // blocks
    kv_width = kv_heads * HEAD_DIM

    @pl.when(step == 0)
    def _():
        for b in range(blocks):
            here = pl.ds(b * rows, rows)
            raw = kv_ref[pl.ds(pl.multiple_of(place(b) * rows, rows), rows), :]
            cosine, sine = cos_ref[here, :], sin_ref[here, :]
            if kv_width >= PAIR:
                turned = jnp.concatenate(
                    [
                        turn(raw[:, c : c + PAIR], cosine, sine)
                        for c in range(0, kv_width, PAIR)
                    ],
                    axis=1,
                )
                plain = raw[:, kv_width:]
            else:
                lane = lax.broadcasted_iota(jnp.int32, raw.shape, 1)
                turned = turn(raw, cosine, sine)
                plain = pltpu.roll(raw, HEAD_DIM, 1)
                both = jnp.where(lane < HEAD_DIM, turned, raw)
            if kv_width >= PAIR:
                both = jnp.concatenate([turned, plain], axis=1)
            kv_out_ref[here, :] = both.astype(BF16)
            for index, placed in enumerate(place_heads(turned, kv_heads, 0.0)):
                keys[index, here, :] = placed.astype(BF16)
            for index, placed in enumerate(place_heads(plain, kv_heads, 1.0)):
                values[index, here, :] = placed.astype(BF16)

    here = pl.ds(pl.multiple_of(step * rows, rows), rows)
    there = pl.ds(pl.multiple_of(place(step) * rows, rows), rows)
    cosine, sine = cos_ref[here, :], sin_ref[here, :]
    for j in range(q_ref.shape[1] // PAIR):
        lanes = slice(j * PAIR, j * PAIR + PAIR)
        turned = turn(q_ref[there, lanes], cosine, sine).astype(BF16)
        q_out_ref[:, lanes] = turned * BF16(ATTN_SCALE)

    link = dot_nt(sees_ref[here, :], member_ref[...])
    row_index = lax.broadcasted_iota(jnp.int32, (rows, tree), 0) + step * rows
    col_index = lax.broadcasted_iota(jnp.int32, (rows, tree), 1)
    bias[...] = jnp.where((link > 0.5) & (col_index <= row_index), 0.0, NEGATIVE)

    lane = lax.broadcasted_iota(jnp.int32, (rows, PAIR), 1)
    for block in range(blocks):
        width = (block + 1) * rows

        @pl.when(step == block)
        def _(width=width):
            lse = jnp.zeros((rows, PAIR), F32)
            for j in range(q_ref.shape[1] // PAIR):
                lanes = slice(j * PAIR, j * PAIR + PAIR)
                group = 2 * j // GROUP
                mixed, tops = [], []
                for p in range(2):
                    scores = dot_nt(q_out_ref[:, lanes], keys[group * 2 + p, :width, :])
                    scores = scores + bias[:, :width]
                    top = jnp.max(scores, axis=1, keepdims=True)
                    expo = jnp.exp(scores - top).astype(BF16)
                    mixed.append(dot_nn(expo, values[group * 2 + p, :width, :]))
                    tops.append(top)
                upper = lane >= HEAD_DIM
                total = pltpu.roll(jnp.where(upper, mixed[0], mixed[1]), HEAD_DIM, 1)
                out_ref[there, lanes] = (jnp.where(upper, mixed[1], mixed[0]) / total).astype(BF16)
                logs = jnp.log(total)
                lse = jnp.where(lane == 2 * j, tops[0] + logs[:, :1], lse)
                lse = jnp.where(lane == 2 * j + 1, tops[1] + logs[:, HEAD_DIM : HEAD_DIM + 1], lse)
            lse_ref[...] = lse

    comm.finish(step == blocks - 1)


def attention_forward(place, qkv, cosine, sine, member, sees, q_width, blocks, comm):
    tree = qkv.shape[0]
    rows = tree // blocks
    kv_width = (qkv.shape[1] - q_width) // 2
    kv_heads = kv_width // HEAD_DIM
    whole = lambda width: pl.BlockSpec((tree, width), lambda i: (0, 0))
    natural = lambda width: pl.BlockSpec((rows, width), lambda i: (i, 0))
    out = pl.pallas_call(
        functools.partial(attention_forward_kernel, kv_heads, blocks, place, comm),
        grid_spec=pl.GridSpec(
            grid=(blocks,),
            in_specs=[
                whole(q_width),
                pl.BlockSpec((tree, 2 * kv_width), lambda i: (0, q_width // (2 * kv_width))),
                whole(PAIR),
                whole(PAIR),
                whole(PAIR),
                whole(PAIR),
                *comm.in_specs,
            ],
            out_specs=[
                whole(q_width),
                natural(q_width),
                whole(2 * kv_width),
                natural(PAIR),
                *comm.out_specs,
            ],
            scratch_shapes=[
                pltpu.VMEM((2 * kv_heads, tree, PAIR), BF16),
                pltpu.VMEM((2 * kv_heads, tree, PAIR), BF16),
                pltpu.VMEM((rows, tree), F32),
                *comm.scratch,
            ],
        ),
        out_shape=[
            jax.ShapeDtypeStruct((tree, q_width), BF16),
            jax.ShapeDtypeStruct((tree, q_width), BF16),
            jax.ShapeDtypeStruct((tree, 2 * kv_width), BF16),
            jax.ShapeDtypeStruct((tree, PAIR), F32),
            *comm.out_shapes,
        ],
        compiler_params=comm_params(comm, 40),
        cost_estimate=pl.CostEstimate(
            flops=10_000_000_000, bytes_accessed=12_000_000, transcendentals=5_000_000
        ),
        name="attention_forward",
    )(qkv, qkv, cosine, sine, member, sees, *comm.operands)
    return out[:4], out[4:]


def attention_backward_kernel(kv_heads, blocks, trees, place, comm, *refs):
    jobs = len(comm.operands)
    inputs, operands, outs, comm_outs, own, scratch = split_refs(
        refs, 8 * trees, jobs, 2 * trees, jobs, 5, len(comm.scratch)
    )
    step = pl.program_id(0)
    comm.enter(operands, comm_outs, scratch, step == 0)
    comm.advance(step, blocks * trees)
    for t in range(trees):

        @pl.when((step >= t * blocks) & (step < (t + 1) * blocks))
        def _(t=t):
            attention_backward_step(
                kv_heads,
                blocks,
                place,
                step - t * blocks,
                inputs[8 * t : 8 * t + 8],
                outs[2 * t : 2 * t + 2],
                own,
            )

    comm.finish(step == blocks * trees - 1)


def attention_backward_step(kv_heads, blocks, place, step, inputs, outs, own):
    grad_ref, q_ref, kv_ref, lse_ref, cos_ref, sin_ref, member_ref, sees_ref = inputs
    dq_ref, dkv_ref = outs
    keys, values, bias, key_sum, value_sum = own
    tree, rows = grad_ref.shape[0], q_ref.shape[0]
    kv_width = kv_heads * HEAD_DIM

    @pl.when(step == 0)
    def _():
        for b in range(blocks):
            here = pl.ds(b * rows, rows)
            both = kv_ref[here, :].astype(F32)
            if kv_width >= PAIR:
                turned, plain = both[:, :kv_width], both[:, kv_width:]
            else:
                turned, plain = both, pltpu.roll(both, HEAD_DIM, 1)
            for index, placed in enumerate(place_heads(turned, kv_heads, 0.0)):
                keys[index, here, :] = placed.astype(BF16)
            for index, placed in enumerate(place_heads(plain, kv_heads, 0.0)):
                values[index, here, :] = placed.astype(BF16)
        key_sum[...] = jnp.zeros_like(key_sum)
        value_sum[...] = jnp.zeros_like(value_sum)

    here = pl.ds(pl.multiple_of(step * rows, rows), rows)
    there = pl.ds(pl.multiple_of(place(step) * rows, rows), rows)
    link = dot_nt(member_ref[...], sees_ref[here, :])
    key_index = lax.broadcasted_iota(jnp.int32, (tree, rows), 0)
    query_index = lax.broadcasted_iota(jnp.int32, (tree, rows), 1) + step * rows
    bias[...] = jnp.where((link > 0.5) & (key_index <= query_index), 0.0, NEGATIVE)
    lse_rows = jnp.transpose(lse_ref[...])

    for block in range(blocks):
        width = (block + 1) * rows

        @pl.when(step == block)
        def _(width=width):
            cosine, sine = cos_ref[here, :], sin_ref[here, :]
            for j in range(q_ref.shape[1] // PAIR):
                lanes = slice(j * PAIR, j * PAIR + PAIR)
                group = 2 * j // GROUP
                query, grad = q_ref[:, lanes], grad_ref[there, lanes]
                dq = jnp.zeros((rows, PAIR), F32)
                for p in range(2):
                    index, head = group * 2 + p, 2 * j + p
                    scores = dot_nt(keys[index, :width, :], query) + bias[:width, :]
                    probs = jnp.exp(scores - lse_rows[head : head + 1, :])
                    probs_grad = dot_nt(values[index, :width, :], grad)
                    value_sum[index, :width, :] += dot_nn(probs.astype(BF16), grad)
                    weighted = probs * probs_grad
                    delta = jnp.sum(weighted, axis=0, keepdims=True)
                    score_grad = (weighted - probs * delta).astype(BF16)
                    key_sum[index, :width, :] += dot_nn(score_grad, query)
                    dq = dq + dot_tn(score_grad, keys[index, :width, :])
                dq_ref[there, lanes] = turn(dq * ATTN_SCALE, cosine, -sine).astype(BF16)

    @pl.when(step == blocks - 1)
    def _():
        for b in range(blocks):
            here = pl.ds(b * rows, rows)
            there = pl.ds(pl.multiple_of(place(b) * rows, rows), rows)
            cosine, sine = cos_ref[here, :], sin_ref[here, :]
            lane = lax.broadcasted_iota(jnp.int32, (rows, PAIR), 1)
            lower = lane < HEAD_DIM
            for c in range(0, kv_heads, 2):
                halves = []
                for acc in (key_sum, value_sum):
                    own, other = [], []
                    for g in range(c, min(c + 2, kv_heads)):
                        low, high = acc[g * 2, here, :], acc[g * 2 + 1, here, :]
                        own.append(low)
                        other.append(high)
                    first = own[0] + pltpu.roll(other[0], HEAD_DIM, 1)
                    if len(own) == 2:
                        second = other[1] + pltpu.roll(own[1], HEAD_DIM, 1)
                    else:
                        second = first
                    halves.append(jnp.where(lower, first, second))
                turned = turn(halves[0], cosine, -sine)
                if kv_width >= PAIR:
                    lanes = slice(c * HEAD_DIM, c * HEAD_DIM + PAIR)
                    dkv_ref[there, lanes] = turned.astype(BF16)
                    lanes = slice(kv_width + c * HEAD_DIM, kv_width + c * HEAD_DIM + PAIR)
                    dkv_ref[there, lanes] = halves[1].astype(BF16)
                else:
                    moved = pltpu.roll(halves[1], HEAD_DIM, 1)
                    dkv_ref[there, :] = jnp.where(lower, turned, moved).astype(BF16)


def attention_backward(place, arrays, blocks, comm):
    trees = len(arrays)
    tree, q_width = arrays[0][1].shape
    rows = tree // blocks
    kv_width = arrays[0][2].shape[1] // 2
    kv_heads = kv_width // HEAD_DIM
    whole = lambda width: pl.BlockSpec((tree, width), lambda i: (0, 0))

    def natural(width, t):
        return pl.BlockSpec((rows, width), lambda i: (jnp.clip(i - t * blocks, 0, blocks - 1), 0))

    in_specs, out_specs, out_shapes = [], [], []
    for t in range(trees):
        in_specs += [whole(q_width), natural(q_width, t), whole(2 * kv_width), natural(PAIR, t)]
        in_specs += [whole(PAIR)] * 4
        out_specs += [whole(q_width), whole(2 * kv_width)]
        out_shapes += [
            jax.ShapeDtypeStruct((tree, q_width), BF16),
            jax.ShapeDtypeStruct((tree, 2 * kv_width), BF16),
        ]
    out = pl.pallas_call(
        functools.partial(attention_backward_kernel, kv_heads, blocks, trees, place, comm),
        grid=(blocks * trees,),
        in_specs=in_specs + list(comm.in_specs),
        out_specs=out_specs + list(comm.out_specs),
        out_shape=out_shapes + list(comm.out_shapes),
        scratch_shapes=[
            pltpu.VMEM((2 * kv_heads, tree, PAIR), BF16),
            pltpu.VMEM((2 * kv_heads, tree, PAIR), BF16),
            pltpu.VMEM((tree, rows), F32),
            pltpu.VMEM((2 * kv_heads, tree, PAIR), F32),
            pltpu.VMEM((2 * kv_heads, tree, PAIR), F32),
            *comm.scratch,
        ],
        compiler_params=comm_params(comm, 60),
        cost_estimate=pl.CostEstimate(
            flops=40_000_000_000, bytes_accessed=24_000_000, transcendentals=10_000_000
        ),
        name="attention_backward",
    )(*[array for per_tree in arrays for array in per_tree], *comm.operands)
    return out[: 2 * trees], out[2 * trees :]


def sync(*values):
    return lax.optimization_barrier(values)


class Square:
    def __init__(self, shard, replica):
        self.shard, self.replica = shard, replica
        self.x = [(i, i ^ 1) for i in range(shard)]
        self.y = [(i, i ^ 2) for i in range(shard)]
        self.d = [(i, i ^ 3) for i in range(shard)]

    def place(self, block):
        shard = lax.axis_index("shard")
        return (block + shard) % 2 + 2 * ((block // 2 + shard // 2) % 2)

    def reorder(self, blocks, axis):
        me = lax.axis_index("shard")
        return jnp.concatenate(
            [lax.dynamic_slice_in_dim(blocks, n ^ me, 1, axis) for n in range(self.shard)], axis=axis
        )

    def gather_small(self, own):
        parts = [
            own,
            lax.ppermute(own, "shard", self.x),
            lax.ppermute(own, "shard", self.y),
            lax.ppermute(own, "shard", self.d),
        ]
        return self.reorder(jnp.stack(parts), 0)

    def sum_small(self, values):
        share = values.shape[1] // self.shard
        blocks = values.reshape(values.shape[0], self.shard, share)
        blocks = self.reorder(blocks, 1)
        total = blocks[:, 0]
        for k, perm in ((1, self.x), (2, self.y), (3, self.d)):
            total = total + lax.ppermute(blocks[:, k], "shard", perm)
        for step in (1, 2, 4):
            perm = [(i, i ^ step) for i in range(self.replica)]
            total = total + lax.ppermute(total, "replica", perm)
        return total

    def gather_start(self, own):
        return lax.ppermute(own, "shard", self.x), lax.ppermute(own, "shard", self.y)

    def gather_more(self, own, got):
        from_x, from_y = got
        half = own.shape[0] // 2
        first = lax.ppermute(from_y[:half], "shard", self.x)
        second = lax.ppermute(from_x[half:], "shard", self.y)
        return [own, from_x, from_y, first, second]

    def carry(self, compute, gathers=(), sums=(), totals=()):
        jobs = [GatherJob(own) for own in gathers] + [SumJob(part) for part in sums]
        jobs += [LineJob(grad) for grad in totals]
        self.kernels += 1
        comm = Comm(jobs, self.kernels)
        if compute is None:
            results, moved = None, transfer(comm)
        else:
            results, moved = compute(comm)
        return (results, *map(list, split_refs(moved, len(gathers), len(sums), len(totals))))

    def start(self):
        self.kernels = 0


class General:
    def __init__(self, shard, replica):
        self.shard, self.replica = shard, replica

    def place(self, block):
        return block

    def gather_small(self, own):
        return lax.all_gather(own, "shard", axis=0, tiled=False)

    def carry(self, compute, gathers=(), sums=(), totals=()):
        results = None if compute is None else compute(NoComm())[0]
        gathered = [lax.all_gather(own, "shard", axis=0, tiled=True) for own in gathers]
        summed = [
            lax.psum_scatter(part, "shard", scatter_dimension=0, tiled=True).astype(F32)
            for part in sums
        ]
        return results, gathered, summed, [lax.psum(grad, "replica") for grad in totals]

    def gather_start(self, own):
        return lax.all_gather(own, "shard", axis=0, tiled=True)

    def gather_more(self, own, got):
        return [got]

    def sum_small(self, values):
        share = lax.psum_scatter(values, "shard", scatter_dimension=1, tiled=True)
        return lax.psum(share, "replica")

    def start(self):
        pass


def rms_scale(values):
    return lax.rsqrt(jnp.mean(values * values, axis=-1, keepdims=True) + EPSILON)


def normalized(piece, gain):
    values = piece.astype(F32)
    return (values * rms_scale(values) * gain).astype(BF16)


def norm_back(values, scale, gain, grad_in):
    scaled = values * scale
    weighted = grad_in * gain
    back = scale * (weighted - scaled * jnp.mean(weighted * scaled, axis=-1, keepdims=True))
    return back, jnp.sum(grad_in * scaled, axis=0)


def body(
    links,
    tokens,
    gain_attn,
    w_query,
    w_key,
    w_value,
    w_out,
    gain_ff,
    w_gate,
    w_up,
    w_down,
    cotangent,
    segment_ids,
    parents,
):
    trees, _, own_rows, width = tokens.shape
    shard = links.shard
    q_width, kv_width = w_query.shape[0], w_key.shape[0]
    tree_rows = own_rows * shard
    links.start()
    share = gain_attn.shape[0]
    w_qkv = jnp.concatenate([w_query, w_key, w_value], axis=0)
    token_rows = [tokens[t, 0] for t in range(trees)]
    cot_rows = [cotangent[t, 0] for t in range(trees)]

    small = jnp.concatenate(
        [gain_attn, gain_ff] + [segment_ids[t, 0].astype(BF16) for t in range(trees)]
    )
    smalls = links.gather_small(small)
    _, (rows_0,), _, _ = links.carry(None, gathers=[token_rows[0]])
    gain_first = smalls[:, :share].reshape(width).astype(F32)
    gain_second = smalls[:, share : 2 * share].reshape(width).astype(F32)
    masks, tables = [], []
    for t in range(trees):
        begin = 2 * share + t * own_rows
        segments = smalls[:, begin : begin + own_rows].reshape(tree_rows).astype(jnp.int32)
        position, member, sees = tree_layout(segments, parents[t, 0])
        masks.append((member, sees))
        tables.append(rope_tables(position))

    def attention(t, qkv):
        return lambda comm: attention_forward(
            links.place, qkv, *tables[t], *masks[t], q_width, shard, comm
        )

    def after_attention(t, branch):
        value = token_rows[t].astype(F32) + RESIDUAL * branch
        scale = rms_scale(value)
        return value, scale, (value * scale * gain_second).astype(BF16)

    normed_0 = normalized(rows_0, gain_first)
    saved_0, (rows_1,), _, _ = links.carry(
        attention(0, dot_nt(normed_0, w_qkv)), gathers=[token_rows[1]]
    )
    part_0 = dot_nn(saved_0[0], w_out).astype(BF16)
    normed_1 = normalized(rows_1, gain_first)
    saved_1, _, (branch_0,), _ = links.carry(attention(1, dot_nt(normed_1, w_qkv)), sums=[part_0])
    part_1 = dot_nn(saved_1[0], w_out).astype(BF16)
    middle_0, scale_0, own_0 = after_attention(0, branch_0)
    _, (ff_rows_0,), (branch_1,), _ = links.carry(None, gathers=[own_0], sums=[part_1])
    middle_1, scale_1, own_1 = after_attention(1, branch_1)
    _, (ff_rows_1,), _, _ = links.carry(None, gathers=[own_1])
    ff_rows_0, ff_rows_1, cot_rows = sync(ff_rows_0, ff_rows_1, cot_rows)

    cot_got = [links.gather_start(cot) for cot in cot_rows]
    rows_all = jnp.concatenate([ff_rows_0, ff_rows_1], axis=0)
    gate = dot_nt(rows_all, w_gate).astype(BF16)
    gate, cot_got, rows_all = sync(gate, cot_got, rows_all)
    cot_pieces = [links.gather_more(cot, got) for cot, got in zip(cot_rows, cot_got)]
    upper = dot_nt(rows_all, w_up)
    wide = gate.astype(F32)
    hidden = (wide * jax.nn.sigmoid(wide) * upper).astype(BF16)
    upper = upper.astype(BF16)
    hidden, upper, gate, cot_pieces = sync(hidden, upper, gate, cot_pieces)
    cot_all = jnp.concatenate(
        [(RESIDUAL * piece.astype(F32)).astype(BF16) for pieces in cot_pieces for piece in pieces],
        axis=0,
    )
    grad_down = dot_tn(hidden, cot_all).astype(BF16)
    hidden_grad = dot_nt(cot_all, w_down)
    wide = gate.astype(F32)
    sigma = jax.nn.sigmoid(wide)
    gate_grad = (
        hidden_grad * upper.astype(F32) * sigma * (1.0 + wide * (1.0 - sigma))
    ).astype(BF16)
    up_grad = (hidden_grad * wide * sigma).astype(BF16)
    ff_part = (dot_nn(gate_grad, w_gate) + dot_nn(up_grad, w_up)).astype(BF16)
    parts = lambda whole: [whole[t * tree_rows : (t + 1) * tree_rows] for t in range(trees)]
    (grad_gate, grad_up), _, ff_grad, (total_down,) = links.carry(
        lambda comm: products([(gate_grad, rows_all, True), (up_grad, rows_all, True)], 256, comm),
        sums=parts(ff_part),
        totals=[grad_down],
    )
    out_own, middle_grads = [], []
    gain_ff_sum = jnp.zeros((width,), F32)
    for t, (middle, scale) in enumerate(((middle_0, scale_0), (middle_1, scale_1))):
        middle_back, term = norm_back(middle, scale, gain_second, ff_grad[t])
        gain_ff_sum = gain_ff_sum + term
        middle_grads.append(cot_rows[t].astype(F32) + middle_back)
        out_own.append((RESIDUAL * middle_grads[t]).astype(BF16))
    (down_part,), out_alls, _, (total_gate,) = links.carry(
        lambda comm: products([(hidden, w_down, False)], 256, comm),
        gathers=out_own,
        totals=[grad_gate],
    )
    arrays = []
    for t, (_, query, kv, lse) in enumerate((saved_0, saved_1)):
        attended_grad = dot_nt(out_alls[t], w_out).astype(BF16)
        arrays.append((attended_grad, query, kv, lse, *tables[t], *masks[t]))
    back, _, downs, (total_up,) = links.carry(
        lambda comm: attention_backward(links.place, arrays, shard, comm),
        sums=parts(down_part),
        totals=[grad_up],
    )
    results = [
        (middle + RESIDUAL * down).astype(BF16) for middle, down in zip((middle_0, middle_1), downs)
    ]
    qkv_grad = jnp.concatenate(
        [jnp.concatenate(back[2 * t : 2 * t + 2], axis=1) for t in range(trees)], axis=0
    )
    normed_part = dot_nn(qkv_grad, w_qkv).astype(BF16)
    attended_all = jnp.concatenate([saved_0[0], saved_1[0]], axis=0)
    out_all = jnp.concatenate(out_alls, axis=0)
    normed_all = jnp.concatenate([normed_0, normed_1], axis=0)
    (grad_attn,), _ = products(
        [(attended_all, out_all, True), (qkv_grad, normed_all, True)],
        128 if shard > 4 else 256,
        NoComm(),
        joined=True,
    )
    _, _, normed_grads, (total_attn,) = links.carry(
        None, sums=parts(normed_part), totals=[grad_attn]
    )
    input_grads = []
    gain_attn_sum = jnp.zeros((width,), F32)
    for t in range(trees):
        inputs = token_rows[t].astype(F32)
        input_back, term = norm_back(inputs, rms_scale(inputs), gain_first, normed_grads[t])
        gain_attn_sum = gain_attn_sum + term
        input_grads.append(middle_grads[t] + input_back)
    gains = links.sum_small(jnp.stack([gain_attn_sum, gain_ff_sum]))
    rows = lambda begin, count: total_attn[begin : begin + count].astype(F32)
    return (
        jnp.stack(results)[:, None],
        jnp.stack(input_grads)[:, None],
        gains[0],
        rows(q_width, q_width),
        rows(2 * q_width, kv_width),
        rows(2 * q_width + kv_width, kv_width),
        rows(0, q_width),
        gains[1],
        total_gate.astype(F32),
        total_up.astype(F32),
        total_down.astype(F32),
    )


def solution(mesh):
    shard, replica = mesh.shape["shard"], mesh.shape["replica"]
    links = (Square if (shard, replica) == (4, 8) else General)(shard, replica)
    in_specs = (
        P(None, "replica", "shard", None),
        P("shard"),
        P("shard", None),
        P("shard", None),
        P("shard", None),
        P("shard", None),
        P("shard"),
        P("shard", None),
        P("shard", None),
        P("shard", None),
        P(None, "replica", "shard", None),
        P(None, "replica", "shard"),
        P(None, "replica", None),
    )
    out_specs = (
        P(None, "replica", "shard", None),
        P(None, "replica", "shard", None),
        P("shard"),
        P("shard", None),
        P("shard", None),
        P("shard", None),
        P("shard", None),
        P("shard"),
        P("shard", None),
        P("shard", None),
        P("shard", None),
    )
    return jax.shard_map(
        functools.partial(body, links),
        mesh=mesh,
        in_specs=in_specs,
        out_specs=out_specs,
        check_vma=False,
    )
```

```python
import functools
import math

import jax
import jax.numpy as jnp
from jax import lax
from jax.experimental import pallas as pl
from jax.experimental.pallas import tpu as pltpu
from jax.sharding import PartitionSpec as P

HEADS = 32
KV_HEADS = 8
HEAD_DIM = 64
PAIR = 2 * HEAD_DIM
GROUP = HEADS // KV_HEADS

EPSILON = 1e-05
RESIDUAL = 0.22
ATTN_SCALE = 0.015625
ROPE_BASE = 10000000.0
NEGATIVE = -1e30
BF16 = jnp.bfloat16
F32 = jnp.float32


def dot_nt(left, right):
    return lax.dot_general(left, right, (((1,), (1,)), ((), ())), preferred_element_type=F32)


def dot_nn(left, right):
    return lax.dot_general(left, right, (((1,), (0,)), ((), ())), preferred_element_type=F32)


def dot_tn(left, right):
    return lax.dot_general(left, right, (((0,), (0,)), ((), ())), preferred_element_type=F32)


def tree_layout(segment_row, parent_row):
    seg_numbers = jnp.arange(parent_row.shape[0], dtype=jnp.int32)
    member = (segment_row[:, None] == seg_numbers[None, :]).astype(jnp.int32)
    lengths = jnp.sum(member, axis=0)
    earlier = seg_numbers[None, :] < seg_numbers[:, None]
    starts = jnp.sum(jnp.where(earlier, lengths[None, :], 0), axis=1)
    parent_hit = parent_row[:, None] == seg_numbers[None, :]
    grandparent = jnp.sum(jnp.where(parent_hit, parent_row[None, :], 0), axis=1)
    itself = seg_numbers[:, None] == seg_numbers[None, :]
    related = itself | parent_hit | (grandparent[:, None] == seg_numbers[None, :])
    before = jnp.sum(jnp.where(related & jnp.logical_not(itself), lengths[None, :], 0), axis=1)
    shift = jnp.sum(member * (before - starts)[None, :], axis=1)
    position = jnp.arange(segment_row.shape[0], dtype=jnp.int32) + shift
    pad = ((0, 0), (0, PAIR - parent_row.shape[0]))
    sees = dot_nn(member.astype(BF16), related.astype(BF16)).astype(BF16)
    return position, jnp.pad(member.astype(BF16), pad), jnp.pad(sees, pad)


def rope_tables(position):
    lane = jnp.arange(PAIR, dtype=jnp.int32) % HEAD_DIM
    half = HEAD_DIM // 2
    fraction = (lane % half).astype(F32) * (2.0 / HEAD_DIM)
    freq = jnp.exp(-math.log(ROPE_BASE) * fraction)
    angle = position.astype(F32)[:, None] * freq[None, :]
    return jnp.cos(angle), jnp.sin(angle) * jnp.where(lane < half, -1.0, 1.0)[None, :]


MESH = pl.DeviceIdType.MESH
CHUNK = 64
SLOTS = 4


def remote(source, target, sems, index, device):
    return pltpu.make_async_remote_copy(
        source, target, sems.at[0, index], sems.at[1, index], device_id=device, device_id_type=MESH
    )


class GatherJob:
    def __init__(self, own, trees):
        self.operand = own
        self.trees = trees
        self.rows, self.width = own.shape[0] // trees, own.shape[1]
        self.chunks = self.rows // CHUNK
        self.out_shape = jax.ShapeDtypeStruct((4 * own.shape[0], self.width), own.dtype)
        self.out_spec = pl.BlockSpec(memory_space=pl.ANY)

    def scratch(self):
        return [
            pltpu.SemaphoreType.DMA((2, 3 * self.chunks * self.trees)),
            pltpu.SemaphoreType.DMA((self.trees,)),
        ]

    def bind(self, operand, out, scratch, x, y):
        sems, local = scratch
        n, rows = self.chunks, self.rows
        self.local, self.to_x, self.to_y, self.on_x, self.on_y = [], [], [], [], []
        for t in range(self.trees):
            at = lambda block, j: out.at[pl.ds((4 * t + block) * rows + j * CHUNK, CHUNK), :]
            own = lambda j: operand.at[pl.ds(t * rows + j * CHUNK, CHUNK), :]
            sem = 3 * n * t
            self.local.append(
                pltpu.make_async_copy(
                    operand.at[pl.ds(t * rows, rows), :],
                    out.at[pl.ds(4 * t * rows, rows), :],
                    local.at[t],
                )
            )
            self.to_x.append([remote(own(j), at(1, j), sems, sem + j, x) for j in range(n)])
            self.to_y.append([remote(own(j), at(2, j), sems, sem + n + j, y) for j in range(n)])
            on = lambda block, j, to: remote(at(block, j), at(3, j), sems, sem + 2 * n + j, to)
            self.on_x.append([on(2, j, x) for j in range(n // 2)])
            self.on_y.append([on(1, j, y) for j in range(n // 2, n)])

    def begin(self):
        n = self.chunks
        half = n // 2
        for t in range(self.trees):
            for k in range(n):
                self.to_x[t][(k + half) % n].start()
                self.to_y[t][k].start()
            self.local[t].start()

    def stages(self):
        def stage(t, k):
            half = self.chunks // 2
            self.to_y[t][k].wait_recv()
            self.on_x[t][k].start()
            self.to_x[t][half + k].wait_recv()
            self.on_y[t][k].start()

        return [
            functools.partial(stage, t, k)
            for t in range(self.trees)
            for k in range(self.chunks // 2)
        ]

    def finish(self):
        half = self.chunks // 2
        for t in range(self.trees):
            for copy in self.to_x[t][:half] + self.to_y[t][half:] + self.on_x[t] + self.on_y[t]:
                copy.wait_recv()
            for copy in self.to_x[t] + self.to_y[t] + self.on_x[t] + self.on_y[t]:
                copy.wait_send()
            self.local[t].wait()


class SumJob:
    def __init__(self, part, trees, tree):
        self.operand = part
        self.rows, self.width = part.shape[0] // 4 // trees, part.shape[1]
        self.base = 4 * self.rows * tree
        self.half = self.rows // 2
        self.chunks = self.half // CHUNK
        self.out_shape = jax.ShapeDtypeStruct((self.rows, self.width), F32)
        self.out_spec = pl.BlockSpec((self.rows, self.width), lambda *_: (0, 0))

    def scratch(self):
        return [
            pltpu.VMEM((4, self.half, self.width), BF16),
            pltpu.VMEM((6, self.half, self.width), BF16),
            pltpu.SemaphoreType.DMA((2, 6 * self.chunks)),
            pltpu.SemaphoreType.DMA((4,)),
        ]

    def bind(self, part, out, scratch, x, y):
        self.out = out
        self.mine, self.got, sems, local = scratch
        n, half = self.chunks, self.half
        rows = lambda block, second: pl.ds(self.base + block * self.rows + second * half, half)
        piece = lambda block, second, j: part.at[
            pl.ds(self.base + block * self.rows + second * half + j * CHUNK, CHUNK), :
        ]
        here = lambda ref, k, j: ref.at[k, pl.ds(j * CHUNK, CHUNK), :]
        self.loads = [
            pltpu.make_async_copy(part.at[rows(block, second), :], self.mine.at[k], local.at[k])
            for k, (block, second) in enumerate(((0, 0), (0, 1), (2, 0), (1, 1)))
        ]
        send = lambda k, source, device: [
            remote(source(j), here(self.got, k, j), sems, k * n + j, device) for j in range(n)
        ]
        self.sends = [
            send(0, lambda j: piece(1, 0, j), x),
            send(1, lambda j: piece(3, 0, j), x),
            send(2, lambda j: here(self.mine, 2, j), y),
            send(3, lambda j: piece(2, 1, j), y),
            send(4, lambda j: piece(3, 1, j), y),
            send(5, lambda j: here(self.mine, 3, j), x),
        ]

    def begin(self):
        for j in range(self.chunks):
            self.sends[1][j].start()
            self.sends[4][j].start()
        for load in self.loads:
            load.start()
        for j in range(self.chunks):
            self.sends[0][j].start()
            self.sends[3][j].start()

    def stages(self):
        def stage(j):
            if j == 0:
                for load in self.loads:
                    load.wait()
            rows = pl.ds(j * CHUNK, CHUNK)
            for first, second, own in ((1, 2, 2), (4, 5, 3)):
                self.sends[first][j].wait_recv()
                total = self.mine[own, rows, :].astype(F32) + self.got[first, rows, :].astype(F32)
                self.mine[own, rows, :] = total.astype(BF16)
                self.sends[second][j].start()

        return [functools.partial(stage, j) for j in range(self.chunks)]

    def finish(self):
        for j in range(self.chunks):
            rows = pl.ds(j * CHUNK, CHUNK)
            for own, one, two in ((0, 0, 2), (1, 3, 5)):
                self.sends[one][j].wait_recv()
                self.sends[two][j].wait_recv()
                self.out[pl.ds(own * self.half + j * CHUNK, CHUNK), :] = (
                    self.mine[own, rows, :].astype(F32)
                    + self.got[one, rows, :].astype(F32)
                    + self.got[two, rows, :].astype(F32)
                )
        for copies in self.sends:
            for copy in copies:
                copy.wait_send()


class LineJob:
    LINE_ROWS = 32
    LAG = 2

    def __init__(self, grad):
        self.operand = grad
        self.half, self.width = grad.shape[0] // 2, grad.shape[1]
        self.chunks = self.half // self.LINE_ROWS
        self.steps = self.chunks + 1 + 3 * self.LAG
        self.out_shape = jax.ShapeDtypeStruct(grad.shape, BF16)
        self.out_spec = pl.BlockSpec(memory_space=pl.ANY)

    def scratch(self):
        place = lambda: pltpu.VMEM((self.half, self.width), BF16)
        return [place(), place(), place(), place(), pltpu.SemaphoreType.DMA((9, self.chunks))]

    def bind(self, grad, out, scratch, x, y):
        self.grad, self.out = grad, out
        self.from_core, self.own, self.from_line, self.from_inner, self.sems = scratch
        shard, place = lax.axis_index("shard"), lax.axis_index("replica")
        self.core, z = place % 2, place // 2
        self.inner = (z == 1) | (z == 2)
        self.outer = (z == 0) | (z == 3)
        self.twin = (shard, z * 2 + 1 - self.core)
        self.pair = (shard, (z + 1 - 2 * (z % 2)) * 2 + self.core)
        self.across = (shard, (3 - z) * 2 + self.core)

    def chunk(self, c):
        return pl.ds(pl.multiple_of(c * self.LINE_ROWS, self.LINE_ROWS), self.LINE_ROWS)

    def at(self, core, c):
        return pl.ds(
            pl.multiple_of(core * self.half + c * self.LINE_ROWS, self.LINE_ROWS), self.LINE_ROWS
        )

    def send(self, source, target, index, arrival, device, c):
        return pltpu.make_async_remote_copy(
            source,
            target,
            self.sems.at[index, c],
            self.sems.at[arrival, c],
            device_id=device,
            device_id_type=MESH,
        )

    def to_twin(self, c):
        source = self.grad.at[self.at(1 - self.core, c), :]
        return self.send(source, self.from_core.at[self.chunk(c), :], 0, 1, self.twin, c)

    def load(self, c):
        source = self.grad.at[self.at(self.core, c), :]
        return pltpu.make_async_copy(source, self.own.at[self.chunk(c), :], self.sems.at[2, c])

    def inward(self, c):
        rows = self.chunk(c)
        return self.send(self.own.at[rows, :], self.from_line.at[rows, :], 3, 4, self.pair, c)

    def between(self, c):
        rows = self.chunk(c)
        return self.send(self.own.at[rows, :], self.from_inner.at[rows, :], 3, 5, self.across, c)

    def outward(self, c):
        rows = self.chunk(c)
        return self.send(self.from_core.at[rows, :], self.from_line.at[rows, :], 6, 4, self.pair, c)

    def store(self, source, c):
        target = self.out.at[self.at(self.core, c), :]
        return pltpu.make_async_copy(source.at[self.chunk(c), :], target, self.sems.at[2, c])

    def give(self, source, c):
        target = self.out.at[self.at(self.core, c), :]
        return self.send(source.at[self.chunk(c), :], target, 7, 8, self.twin, c)

    def begin(self):
        pass

    def stages(self):
        return []

    def step(self, s):
        n, lag = self.chunks, self.LAG
        live = lambda begin: (s >= begin) & (s < n + begin)
        add = lambda a, b: (a.astype(F32) + b.astype(F32)).astype(BF16)

        @pl.when(live(0))
        def _():
            self.to_twin(s).start()
            self.load(s).start()

        @pl.when(live(1))
        def _():
            c = s - 1
            rows = self.chunk(c)
            self.to_twin(c).wait()
            self.load(c).wait()
            self.own[rows, :] = add(self.own[rows, :], self.from_core[rows, :])
            pl.when(self.outer)(lambda: self.inward(c).start())

        @pl.when(live(1 + lag) & self.inner)
        def _():
            c = s - 1 - lag
            rows = self.chunk(c)
            self.inward(c).wait_recv()
            self.own[rows, :] = add(self.own[rows, :], self.from_line[rows, :])
            self.between(c).start()

        @pl.when(live(1 + 2 * lag) & self.inner)
        def _():
            c = s - 1 - 2 * lag
            rows = self.chunk(c)
            self.between(c).wait_recv()
            self.from_core[rows, :] = add(self.own[rows, :], self.from_inner[rows, :])
            self.outward(c).start()
            self.store(self.from_core, c).start()
            self.give(self.from_core, c).start()

        @pl.when(live(1 + 3 * lag) & self.outer)
        def _():
            c = s - 1 - 3 * lag
            self.outward(c).wait_recv()
            self.store(self.from_line, c).start()
            self.give(self.from_line, c).start()

    def finish(self):
        def body(c, carry):
            self.store(self.from_line, c).wait()
            self.give(self.from_line, c).wait()

            @pl.when(self.inner)
            def _():
                self.between(c).wait_send()
                self.outward(c).wait_send()

            pl.when(self.outer)(lambda: self.inward(c).wait_send())
            return carry

        lax.fori_loop(0, self.chunks, body, 0)


class Comm:
    def __init__(self, jobs, number):
        self.jobs, self.number = jobs, number
        self.operands = [job.operand for job in jobs]
        self.in_specs = [pl.BlockSpec(memory_space=pl.ANY) for _ in jobs]
        self.out_specs = [job.out_spec for job in jobs]
        self.out_shapes = [job.out_shape for job in jobs]
        self.scratch = [entry for job in jobs for entry in job.scratch()]

    def enter(self, operands, outs, scratch, now):
        shard, replica = lax.axis_index("shard"), lax.axis_index("replica")
        x = (shard + 1 - 2 * (shard % 2), replica)
        y = ((shard + 2) % 4, replica)
        scratch = list(scratch)
        for job, operand, out in zip(self.jobs, operands, outs):
            count = len(job.scratch())
            job.bind(operand, out, scratch[:count], x, y)
            scratch = scratch[count:]

        lines = [job for job in self.jobs if isinstance(job, LineJob)]
        square = len(lines) < len(self.jobs)

        @pl.when(now)
        def _():
            barrier = pltpu.get_barrier_semaphore()

            def greet(device):
                pl.semaphore_signal(barrier, inc=1, device_id=device, device_id_type=MESH)

            near = ([x, y] if square else []) + ([lines[0].twin, lines[0].pair] if lines else [])
            for device in near:
                greet(device)
            if lines:

                @pl.when(lines[0].inner)
                def _():
                    greet(lines[0].across)
                    pl.semaphore_wait(barrier, len(near) + 1)

                @pl.when(lines[0].outer)
                def _():
                    pl.semaphore_wait(barrier, len(near))

            else:
                pl.semaphore_wait(barrier, len(near))
            for job in self.jobs:
                job.begin()

    def stages(self):
        return [stage for job in self.jobs for stage in job.stages()]

    def advance(self, slot, slots):
        stages = self.stages()
        for job in self.jobs:
            if isinstance(job, LineJob):

                def body(k, carry, job=job):
                    job.step(k)
                    return carry

                lax.fori_loop(slot * job.steps // slots, (slot + 1) * job.steps // slots, body, 0)
        for index, stage in enumerate(stages):
            if slots <= 4:
                due = min(slots - 1, slots // 2 + index * (slots - slots // 2) // len(stages))
            else:
                due = min(slots - 1, max(1, int(slots * (0.25 + 0.5 * index / len(stages)))))
            pl.when(slot == due)(stage)

    def finish(self, now):
        @pl.when(now)
        def _():
            for job in self.jobs:
                job.finish()


class NoComm:
    operands = in_specs = out_specs = out_shapes = scratch = ()
    number = None

    def enter(self, *_):
        pass

    def advance(self, *_):
        pass

    def finish(self, *_):
        pass


def comm_params(comm, vmem):
    if comm.number is None:
        return pltpu.CompilerParams(vmem_limit_bytes=vmem << 20)
    return pltpu.CompilerParams(
        vmem_limit_bytes=vmem << 20, collective_id=comm.number, has_side_effects=True
    )


def split_refs(refs, *counts):
    parts, begin = [], 0
    for count in counts:
        parts.append(refs[begin : begin + count])
        begin += count
    return parts


def transfer(comm):
    count = len(comm.operands)
    steps = max([1] + [job.steps for job in comm.jobs if isinstance(job, LineJob)])

    def kernel(*refs):
        operands, outs, scratch = split_refs(refs, count, count, len(comm.scratch))
        step = pl.program_id(0)
        comm.enter(operands, outs, scratch, step == 0)
        if steps == 1:
            for stage in comm.stages():
                stage()
        else:
            comm.advance(step, steps)
        comm.finish(step == steps - 1)

    return pl.pallas_call(
        kernel,
        grid=(steps,),
        in_specs=comm.in_specs,
        out_specs=comm.out_specs,
        out_shape=comm.out_shapes,
        scratch_shapes=comm.scratch,
        compiler_params=comm_params(comm, 48),
        name="transfer",
    )(*comm.operands)


def products(items, block, comm, joined=False):
    specs, shapes, out_specs, steps, rights = [], [], [], [], []
    total = sum((l.shape[1] if t else l.shape[0]) // block for l, _, t in items)
    begin = 0
    for left, right, transposed in items:
        size = left.shape[1] if transposed else left.shape[0]
        count = size // block

        def place(i, begin=begin, count=count):
            return jnp.clip(i - begin, 0, count - 1)

        if transposed:
            specs.append(pl.BlockSpec((left.shape[0], block), lambda i, p=place: (0, p(i))))
        else:
            specs.append(pl.BlockSpec((block, left.shape[1]), lambda i, p=place: (p(i), 0)))
        if not joined:
            out_specs.append(pl.BlockSpec((block, right.shape[1]), lambda i, p=place: (p(i), 0)))
            shapes.append(jax.ShapeDtypeStruct((size, right.shape[1]), BF16))
        if not any(right is r for r in rights):
            rights.append(right)
        steps.append((begin, count))
        begin += count
    right_specs = [
        pl.BlockSpec(r.shape, lambda i: (0, 0), pipeline_mode=pl.Buffered(1)) for r in rights
    ]
    which = [next(k for k, r in enumerate(rights) if r is right) for _, right, _ in items]
    n = len(items)
    if joined:
        width = items[0][1].shape[1]
        out_specs = [pl.BlockSpec((block, width), lambda i: (i, 0))]
        shapes = [jax.ShapeDtypeStruct((total * block, width), BF16)]
    made = len(shapes)

    def kernel(*refs):
        lefts, held, operands, outs, comm_outs, scratch = split_refs(
            refs, n, len(rights), len(comm.operands), made, len(comm.operands), len(comm.scratch)
        )
        step = pl.program_id(0)
        comm.enter(operands, comm_outs, scratch, step == 0)
        width = items[0][1].shape[1] // SLOTS

        def part(slot, carry):
            comm.advance(step * SLOTS + slot, total * SLOTS)
            columns = pl.ds(pl.multiple_of(slot * width, width), width)
            for k, (_, _, transposed) in enumerate(items):
                begin, count = steps[k]

                @pl.when((step >= begin) & (step < begin + count))
                def _(k=k, transposed=transposed):
                    dot = dot_tn if transposed else dot_nn
                    result = dot(lefts[k][...], held[which[k]][:, columns])
                    outs[0 if joined else k][:, columns] = result.astype(BF16)

            return carry

        lax.fori_loop(0, SLOTS, part, 0)

        comm.finish(step == total - 1)

    flops = 2 * sum(math.prod(l.shape) * r.shape[1] for l, r, _ in items)
    out = pl.pallas_call(
        kernel,
        grid=(total,),
        in_specs=specs + right_specs + list(comm.in_specs),
        out_specs=out_specs + list(comm.out_specs),
        out_shape=shapes + list(comm.out_shapes),
        scratch_shapes=list(comm.scratch),
        compiler_params=comm_params(comm, 58),
        cost_estimate=pl.CostEstimate(flops=flops, bytes_accessed=30_000_000, transcendentals=0),
        name="products",
    )(*[l for l, _, _ in items], *rights, *comm.operands)
    return out[:made], out[made:]


def feed_forward(rows_all, w_gate, w_up, block, comm):
    rows, width = rows_all.shape
    units = w_gate.shape[0]
    steps = units // block
    part = rows // SLOTS

    def kernel(*refs):
        inputs, operands, outs, comm_outs, scratch = split_refs(
            refs, 3, len(comm.operands), 3, len(comm.operands), len(comm.scratch)
        )
        x_ref, gate_w, up_w = inputs
        gate_ref, upper_ref, hidden_ref = outs
        step = pl.program_id(0)
        comm.enter(operands, comm_outs, scratch, step == 0)
        comm.advance(step, steps)
        for slot in range(SLOTS):
            here = pl.ds(slot * part, part)
            gate = dot_nt(x_ref[here, :], gate_w[...])
            upper = dot_nt(x_ref[here, :], up_w[...])
            gate_ref[here, :] = gate.astype(BF16)
            upper_ref[here, :] = upper.astype(BF16)
            hidden_ref[here, :] = (gate * jax.nn.sigmoid(gate) * upper).astype(BF16)
        comm.finish(step == steps - 1)

    out = pl.pallas_call(
        kernel,
        grid=(steps,),
        in_specs=[
            pl.BlockSpec((rows, width), lambda i: (0, 0), pipeline_mode=pl.Buffered(1)),
            pl.BlockSpec((block, width), lambda i: (i, 0)),
            pl.BlockSpec((block, width), lambda i: (i, 0)),
            *comm.in_specs,
        ],
        out_specs=[pl.BlockSpec((rows, block), lambda i: (0, i))] * 3 + list(comm.out_specs),
        out_shape=[jax.ShapeDtypeStruct((rows, units), BF16)] * 3 + list(comm.out_shapes),
        scratch_shapes=list(comm.scratch),
        compiler_params=comm_params(comm, 56),
        cost_estimate=pl.CostEstimate(
            flops=4 * rows * width * units, bytes_accessed=48_000_000, transcendentals=rows * units
        ),
        name="feed_forward",
    )(rows_all, w_gate, w_up, *comm.operands)
    return out[:3], out[3:]


def swap_halves(block):
    lane = lax.broadcasted_iota(jnp.int32, block.shape, 1)
    half = HEAD_DIM // 2
    up = pltpu.roll(block, PAIR - half, 1)
    down = pltpu.roll(block, half, 1)
    return jnp.where(lane % HEAD_DIM < half, up, down)


def turn(block, cosine, sine):
    return block * cosine + swap_halves(block) * sine


def place_heads(wide, kv_heads, fill):
    placed = []
    for g in range(kv_heads):
        base = wide[:, (g // 2) * PAIR : (g // 2) * PAIR + PAIR] if wide.shape[1] >= PAIR else wide
        lane = lax.broadcasted_iota(jnp.int32, base.shape, 1)
        moved = pltpu.roll(base, HEAD_DIM, 1)
        for p in range(2):
            source = base if g % 2 == p else moved
            inside = (lane // HEAD_DIM) == p
            placed.append(jnp.where(inside, source, jnp.full_like(source, fill)))
    return placed


def attention_forward_kernel(kv_heads, blocks, place, comm, *refs):
    jobs = len(comm.operands)
    inputs, operands, outs, comm_outs, own, scratch = split_refs(
        refs, 6, jobs, 4, jobs, 3, len(comm.scratch)
    )
    q_ref, kv_ref, cos_ref, sin_ref, member_ref, sees_ref = inputs
    out_ref, q_out_ref, kv_out_ref, lse_ref = outs
    keys, values, bias = own
    step = pl.program_id(0)
    comm.enter(operands, comm_outs, scratch, step == 0)
    comm.advance(step, blocks)
    tree = q_ref.shape[0]
    rows = tree // blocks
    kv_width = kv_heads * HEAD_DIM

    @pl.when(step == 0)
    def _():
        for b in range(blocks):
            here = pl.ds(b * rows, rows)
            raw = kv_ref[pl.ds(pl.multiple_of(place(b) * rows, rows), rows), :]
            cosine, sine = cos_ref[here, :], sin_ref[here, :]
            if kv_width >= PAIR:
                turned = jnp.concatenate(
                    [
                        turn(raw[:, c : c + PAIR], cosine, sine)
                        for c in range(0, kv_width, PAIR)
                    ],
                    axis=1,
                )
                plain = raw[:, kv_width:]
            else:
                lane = lax.broadcasted_iota(jnp.int32, raw.shape, 1)
                turned = turn(raw, cosine, sine)
                plain = pltpu.roll(raw, HEAD_DIM, 1)
                both = jnp.where(lane < HEAD_DIM, turned, raw)
            if kv_width >= PAIR:
                both = jnp.concatenate([turned, plain], axis=1)
            kv_out_ref[here, :] = both.astype(BF16)
            for index, placed in enumerate(place_heads(turned, kv_heads, 0.0)):
                keys[index, here, :] = placed.astype(BF16)
            for index, placed in enumerate(place_heads(plain, kv_heads, 1.0)):
                values[index, here, :] = placed.astype(BF16)

    here = pl.ds(pl.multiple_of(step * rows, rows), rows)
    there = pl.ds(pl.multiple_of(place(step) * rows, rows), rows)
    cosine, sine = cos_ref[here, :], sin_ref[here, :]
    for j in range(q_ref.shape[1] // PAIR):
        lanes = slice(j * PAIR, j * PAIR + PAIR)
        turned = turn(q_ref[there, lanes], cosine, sine).astype(BF16)
        q_out_ref[:, lanes] = turned * BF16(ATTN_SCALE)

    link = dot_nt(sees_ref[here, :], member_ref[...])
    row_index = lax.broadcasted_iota(jnp.int32, (rows, tree), 0) + step * rows
    col_index = lax.broadcasted_iota(jnp.int32, (rows, tree), 1)
    bias[...] = jnp.where((link > 0.5) & (col_index <= row_index), 0.0, NEGATIVE)

    lane = lax.broadcasted_iota(jnp.int32, (rows, PAIR), 1)
    for block in range(blocks):
        width = (block + 1) * rows

        @pl.when(step == block)
        def _(width=width):
            lse = jnp.zeros((rows, PAIR), F32)
            for j in range(q_ref.shape[1] // PAIR):
                lanes = slice(j * PAIR, j * PAIR + PAIR)
                group = 2 * j // GROUP
                mixed, tops = [], []
                for p in range(2):
                    scores = dot_nt(q_out_ref[:, lanes], keys[group * 2 + p, :width, :])
                    scores = scores + bias[:, :width]
                    top = jnp.max(scores, axis=1, keepdims=True)
                    expo = jnp.exp(scores - top).astype(BF16)
                    mixed.append(dot_nn(expo, values[group * 2 + p, :width, :]))
                    tops.append(top)
                upper = lane >= HEAD_DIM
                total = pltpu.roll(jnp.where(upper, mixed[0], mixed[1]), HEAD_DIM, 1)
                out_ref[there, lanes] = (jnp.where(upper, mixed[1], mixed[0]) / total).astype(BF16)
                logs = jnp.log(total)
                lse = jnp.where(lane == 2 * j, tops[0] + logs[:, :1], lse)
                lse = jnp.where(lane == 2 * j + 1, tops[1] + logs[:, HEAD_DIM : HEAD_DIM + 1], lse)
            lse_ref[...] = lse

    comm.finish(step == blocks - 1)


def attention_forward(place, qkv, cosine, sine, member, sees, q_width, blocks, comm):
    tree = qkv.shape[0]
    rows = tree // blocks
    kv_width = (qkv.shape[1] - q_width) // 2
    kv_heads = kv_width // HEAD_DIM
    whole = lambda width: pl.BlockSpec((tree, width), lambda i: (0, 0))
    natural = lambda width: pl.BlockSpec((rows, width), lambda i: (i, 0))
    out = pl.pallas_call(
        functools.partial(attention_forward_kernel, kv_heads, blocks, place, comm),
        grid_spec=pl.GridSpec(
            grid=(blocks,),
            in_specs=[
                whole(q_width),
                pl.BlockSpec((tree, 2 * kv_width), lambda i: (0, q_width // (2 * kv_width))),
                whole(PAIR),
                whole(PAIR),
                whole(PAIR),
                whole(PAIR),
                *comm.in_specs,
            ],
            out_specs=[
                whole(q_width),
                natural(q_width),
                whole(2 * kv_width),
                natural(PAIR),
                *comm.out_specs,
            ],
            scratch_shapes=[
                pltpu.VMEM((2 * kv_heads, tree, PAIR), BF16),
                pltpu.VMEM((2 * kv_heads, tree, PAIR), BF16),
                pltpu.VMEM((rows, tree), F32),
                *comm.scratch,
            ],
        ),
        out_shape=[
            jax.ShapeDtypeStruct((tree, q_width), BF16),
            jax.ShapeDtypeStruct((tree, q_width), BF16),
            jax.ShapeDtypeStruct((tree, 2 * kv_width), BF16),
            jax.ShapeDtypeStruct((tree, PAIR), F32),
            *comm.out_shapes,
        ],
        compiler_params=comm_params(comm, 40),
        cost_estimate=pl.CostEstimate(
            flops=10_000_000_000, bytes_accessed=12_000_000, transcendentals=5_000_000
        ),
        name="attention_forward",
    )(qkv, qkv, cosine, sine, member, sees, *comm.operands)
    return out[:4], out[4:]


def attention_backward_kernel(kv_heads, blocks, trees, place, comm, *refs):
    jobs = len(comm.operands)
    inputs, operands, outs, comm_outs, own, scratch = split_refs(
        refs, 8 * trees, jobs, 1, jobs, 6, len(comm.scratch)
    )
    pairs = inputs[1].shape[1] // PAIR
    each = blocks * pairs
    step = pl.program_id(0)
    comm.enter(operands, comm_outs, scratch, step == 0)
    comm.advance(step, each * trees)
    for t in range(trees):

        @pl.when((step >= t * each) & (step < (t + 1) * each))
        def _(t=t):
            local = step - t * each
            attention_backward_step(
                kv_heads,
                blocks,
                pairs,
                place,
                local // pairs,
                local % pairs,
                t,
                inputs[8 * t : 8 * t + 8],
                outs[0],
                own,
            )

    comm.finish(step == each * trees - 1)


def attention_backward_step(kv_heads, blocks, pairs, place, step, j, t, inputs, out_ref, own):
    grad_ref, q_ref, kv_ref, lse_ref, cos_ref, sin_ref, member_ref, sees_ref = inputs
    keys, values, bias, lse_rows, key_sum, value_sum = own
    tree, rows = grad_ref.shape[0], q_ref.shape[0]
    kv_width = kv_heads * HEAD_DIM
    q_width = q_ref.shape[1]
    base = t * tree

    @pl.when((step == 0) & (j == 0))
    def _():
        for b in range(blocks):
            here = pl.ds(b * rows, rows)
            both = kv_ref[here, :].astype(F32)
            if kv_width >= PAIR:
                turned, plain = both[:, :kv_width], both[:, kv_width:]
            else:
                turned, plain = both, pltpu.roll(both, HEAD_DIM, 1)
            for index, placed in enumerate(place_heads(turned, kv_heads, 0.0)):
                keys[index, here, :] = placed.astype(BF16)
            for index, placed in enumerate(place_heads(plain, kv_heads, 0.0)):
                values[index, here, :] = placed.astype(BF16)
        key_sum[...] = jnp.zeros_like(key_sum)
        value_sum[...] = jnp.zeros_like(value_sum)

    here = pl.ds(pl.multiple_of(step * rows, rows), rows)

    @pl.when(j == 0)
    def _():
        link = dot_nt(member_ref[...], sees_ref[here, :])
        key_index = lax.broadcasted_iota(jnp.int32, (tree, rows), 0)
        query_index = lax.broadcasted_iota(jnp.int32, (tree, rows), 1) + step * rows
        bias[...] = jnp.where((link > 0.5) & (key_index <= query_index), 0.0, NEGATIVE)
        lse_rows[...] = jnp.transpose(lse_ref[...])

    there = pl.ds(pl.multiple_of(place(step) * rows, rows), rows)
    out_rows = pl.ds(pl.multiple_of(base + place(step) * rows, rows), rows)
    lanes = pl.ds(pl.multiple_of(j * PAIR, PAIR), PAIR)
    group = 2 * j // GROUP
    for block in range(blocks):
        width = (block + 1) * rows

        @pl.when(step == block)
        def _(width=width):
            cosine, sine = cos_ref[here, :], sin_ref[here, :]
            query, grad = q_ref[:, lanes], grad_ref[there, lanes]
            dq = jnp.zeros((rows, PAIR), F32)
            for p in range(2):
                index = group * 2 + p
                scores = dot_nt(keys[index, :width, :], query) + bias[:width, :]
                probs = jnp.exp(scores - lse_rows[pl.ds(2 * j + p, 1), :])
                probs_grad = dot_nt(values[index, :width, :], grad)
                value_sum[index, :width, :] += dot_nn(probs.astype(BF16), grad)
                weighted = probs * probs_grad
                delta = jnp.sum(weighted, axis=0, keepdims=True)
                score_grad = (weighted - probs * delta).astype(BF16)
                key_sum[index, :width, :] += dot_nn(score_grad, query)
                dq = dq + dot_tn(score_grad, keys[index, :width, :])
            out_ref[out_rows, lanes] = turn(dq * ATTN_SCALE, cosine, -sine).astype(BF16)

    @pl.when((step == blocks - 1) & (j == pairs - 1))
    def _():
        for b in range(blocks):
            here = pl.ds(b * rows, rows)
            there = pl.ds(pl.multiple_of(base + place(b) * rows, rows), rows)
            cosine, sine = cos_ref[here, :], sin_ref[here, :]
            lane = lax.broadcasted_iota(jnp.int32, (rows, PAIR), 1)
            lower = lane < HEAD_DIM
            for c in range(0, kv_heads, 2):
                halves = []
                for acc in (key_sum, value_sum):
                    own, other = [], []
                    for g in range(c, min(c + 2, kv_heads)):
                        own.append(acc[g * 2, here, :])
                        other.append(acc[g * 2 + 1, here, :])
                    first = own[0] + pltpu.roll(other[0], HEAD_DIM, 1)
                    if len(own) == 2:
                        second = other[1] + pltpu.roll(own[1], HEAD_DIM, 1)
                    else:
                        second = first
                    halves.append(jnp.where(lower, first, second))
                turned = turn(halves[0], cosine, -sine)
                if kv_width >= PAIR:
                    begin = q_width + c * HEAD_DIM
                    out_ref[there, begin : begin + PAIR] = turned.astype(BF16)
                    begin += kv_width
                    out_ref[there, begin : begin + PAIR] = halves[1].astype(BF16)
                else:
                    moved = pltpu.roll(halves[1], HEAD_DIM, 1)
                    both = jnp.where(lower, turned, moved)
                    out_ref[there, q_width : q_width + PAIR] = both.astype(BF16)


def attention_backward(place, arrays, blocks, comm):
    trees = len(arrays)
    tree, q_width = arrays[0][1].shape
    rows = tree // blocks
    kv_width = arrays[0][2].shape[1] // 2
    kv_heads = kv_width // HEAD_DIM
    each = blocks * (q_width // PAIR)
    whole = lambda width: pl.BlockSpec((tree, width), lambda i: (0, 0))

    def natural(width, t):
        return pl.BlockSpec(
            (rows, width),
            lambda i: (jnp.clip((i - t * each) // (q_width // PAIR), 0, blocks - 1), 0),
        )

    in_specs = []
    for t in range(trees):
        in_specs += [whole(q_width), natural(q_width, t), whole(2 * kv_width), natural(PAIR, t)]
        in_specs += [whole(PAIR)] * 4
    total = q_width + 2 * kv_width
    out = pl.pallas_call(
        functools.partial(attention_backward_kernel, kv_heads, blocks, trees, place, comm),
        grid=(each * trees,),
        in_specs=in_specs + list(comm.in_specs),
        out_specs=[pl.BlockSpec((trees * tree, total), lambda i: (0, 0))] + list(comm.out_specs),
        out_shape=[jax.ShapeDtypeStruct((trees * tree, total), BF16)] + list(comm.out_shapes),
        scratch_shapes=[
            pltpu.VMEM((2 * kv_heads, tree, PAIR), BF16),
            pltpu.VMEM((2 * kv_heads, tree, PAIR), BF16),
            pltpu.VMEM((tree, rows), F32),
            pltpu.VMEM((PAIR, rows), F32),
            pltpu.VMEM((2 * kv_heads, tree, PAIR), F32),
            pltpu.VMEM((2 * kv_heads, tree, PAIR), F32),
            *comm.scratch,
        ],
        compiler_params=comm_params(comm, 60),
        cost_estimate=pl.CostEstimate(
            flops=40_000_000_000, bytes_accessed=24_000_000, transcendentals=10_000_000
        ),
        name="attention_backward",
    )(*[array for per_tree in arrays for array in per_tree], *comm.operands)
    return out[:1], out[1:]


def sync(*values):
    return lax.optimization_barrier(values)


class Square:
    def __init__(self, shard, replica):
        self.shard, self.replica = shard, replica
        self.x = [(i, i ^ 1) for i in range(shard)]
        self.y = [(i, i ^ 2) for i in range(shard)]
        self.d = [(i, i ^ 3) for i in range(shard)]

    def place(self, block):
        shard = lax.axis_index("shard")
        return (block + shard) % 2 + 2 * ((block // 2 + shard // 2) % 2)

    def reorder(self, blocks, axis):
        me = lax.axis_index("shard")
        return jnp.concatenate(
            [lax.dynamic_slice_in_dim(blocks, n ^ me, 1, axis) for n in range(self.shard)], axis=axis
        )

    def gather_small(self, own):
        parts = [
            own,
            lax.ppermute(own, "shard", self.x),
            lax.ppermute(own, "shard", self.y),
            lax.ppermute(own, "shard", self.d),
        ]
        return self.reorder(jnp.stack(parts), 0)

    def sum_small(self, values):
        share = values.shape[1] // self.shard
        blocks = values.reshape(values.shape[0], self.shard, share)
        blocks = self.reorder(blocks, 1)
        total = blocks[:, 0]
        for k, perm in ((1, self.x), (2, self.y), (3, self.d)):
            total = total + lax.ppermute(blocks[:, k], "shard", perm)
        for step in (1, 2, 4):
            perm = [(i, i ^ step) for i in range(self.replica)]
            total = total + lax.ppermute(total, "replica", perm)
        return total

    def carry(self, compute, gathers=(), sums=(), totals=()):
        jobs = [GatherJob(*own) for own in gathers] + [SumJob(*part) for part in sums]
        jobs += [LineJob(grad) for grad in totals]
        self.kernels += 1
        comm = Comm(jobs, self.kernels)
        if compute is None:
            results, moved = None, transfer(comm)
        else:
            results, moved = compute(comm)
        return (results, *map(list, split_refs(moved, len(gathers), len(sums), len(totals))))

    def start(self):
        self.kernels = 0


class General:
    def __init__(self, shard, replica):
        self.shard, self.replica = shard, replica

    def place(self, block):
        return block

    def gather_small(self, own):
        return lax.all_gather(own, "shard", axis=0, tiled=False)

    def carry(self, compute, gathers=(), sums=(), totals=()):
        results = None if compute is None else compute(NoComm())[0]
        rows = lambda array, trees: array.reshape(trees, -1, array.shape[1])
        gathered = [
            lax.all_gather(rows(own, trees), "shard", axis=1, tiled=True).reshape(-1, own.shape[1])
            for own, trees in gathers
        ]
        summed = [
            lax.psum_scatter(
                rows(part, trees)[tree], "shard", scatter_dimension=0, tiled=True
            ).astype(F32)
            for part, trees, tree in sums
        ]
        return results, gathered, summed, [lax.psum(grad, "replica") for grad in totals]

    def sum_small(self, values):
        share = lax.psum_scatter(values, "shard", scatter_dimension=1, tiled=True)
        return lax.psum(share, "replica")

    def start(self):
        pass


def rms_scale(values):
    return lax.rsqrt(jnp.mean(values * values, axis=-1, keepdims=True) + EPSILON)


def normalized(piece, gain):
    values = piece.astype(F32)
    return (values * rms_scale(values) * gain).astype(BF16)


def norm_back(values, scale, gain, grad_in):
    scaled = values * scale
    weighted = grad_in * gain
    back = scale * (weighted - scaled * jnp.mean(weighted * scaled, axis=-1, keepdims=True))
    return back, jnp.sum(grad_in * scaled, axis=0)


def body(
    links,
    tokens,
    gain_attn,
    w_query,
    w_key,
    w_value,
    w_out,
    gain_ff,
    w_gate,
    w_up,
    w_down,
    cotangent,
    segment_ids,
    parents,
):
    trees, _, own_rows, width = tokens.shape
    shard = links.shard
    q_width, kv_width = w_query.shape[0], w_key.shape[0]
    tree_rows = own_rows * shard
    links.start()
    share = gain_attn.shape[0]
    w_qkv = jnp.concatenate([w_query, w_key, w_value], axis=0)
    token_rows = [tokens[t, 0] for t in range(trees)]
    cot_rows = [cotangent[t, 0] for t in range(trees)]

    small = jnp.concatenate(
        [gain_attn, gain_ff] + [segment_ids[t, 0].astype(BF16) for t in range(trees)]
    )
    smalls = links.gather_small(small)
    _, (rows_0,), _, _ = links.carry(None, gathers=[(token_rows[0], 1)])
    gain_first = smalls[:, :share].reshape(width).astype(F32)
    gain_second = smalls[:, share : 2 * share].reshape(width).astype(F32)
    masks, tables = [], []
    for t in range(trees):
        begin = 2 * share + t * own_rows
        segments = smalls[:, begin : begin + own_rows].reshape(tree_rows).astype(jnp.int32)
        position, member, sees = tree_layout(segments, parents[t, 0])
        masks.append((member, sees))
        tables.append(rope_tables(position))

    def attention(t, qkv):
        return lambda comm: attention_forward(
            links.place, qkv, *tables[t], *masks[t], q_width, shard, comm
        )

    def after_attention(t, branch):
        value = token_rows[t].astype(F32) + RESIDUAL * branch
        scale = rms_scale(value)
        return value, scale, (value * scale * gain_second).astype(BF16)

    normed_0 = normalized(rows_0, gain_first)
    saved_0, (rows_1,), _, _ = links.carry(
        attention(0, dot_nt(normed_0, w_qkv)), gathers=[(token_rows[1], 1)]
    )
    part_0 = dot_nn(saved_0[0], w_out).astype(BF16)
    normed_1 = normalized(rows_1, gain_first)
    saved_1, _, (branch_0,), _ = links.carry(attention(1, dot_nt(normed_1, w_qkv)), sums=[(part_0, 1, 0)])
    part_1 = dot_nn(saved_1[0], w_out).astype(BF16)
    middle_0, scale_0, own_0 = after_attention(0, branch_0)
    _, _, (branch_1,), _ = links.carry(None, sums=[(part_1, 1, 0)])
    middle_1, scale_1, own_1 = after_attention(1, branch_1)
    own_all = jnp.concatenate([own_0, own_1], axis=0)
    _, (rows_all,), _, _ = links.carry(None, gathers=[(own_all, trees)])

    cot_own = jnp.concatenate([(RESIDUAL * cot.astype(F32)).astype(BF16) for cot in cot_rows], axis=0)
    (gate, upper, hidden), (cot_all,), _, _ = links.carry(
        lambda comm: feed_forward(rows_all, w_gate, w_up, 256, comm), gathers=[(cot_own, trees)]
    )
    grad_down = dot_tn(hidden, cot_all).astype(BF16)
    hidden_grad = dot_nt(cot_all, w_down)
    wide = gate.astype(F32)
    sigma = jax.nn.sigmoid(wide)
    gate_grad = (
        hidden_grad * upper.astype(F32) * sigma * (1.0 + wide * (1.0 - sigma))
    ).astype(BF16)
    up_grad = (hidden_grad * wide * sigma).astype(BF16)
    ff_part = (dot_nn(gate_grad, w_gate) + dot_nn(up_grad, w_up)).astype(BF16)
    parts = lambda whole: [(whole, trees, t) for t in range(trees)]
    (grad_gate, grad_up), _, ff_grad, (total_down,) = links.carry(
        lambda comm: products([(gate_grad, rows_all, True), (up_grad, rows_all, True)], 256, comm),
        sums=parts(ff_part),
        totals=[grad_down],
    )
    out_own, middle_grads = [], []
    gain_ff_sum = jnp.zeros((width,), F32)
    for t, (middle, scale) in enumerate(((middle_0, scale_0), (middle_1, scale_1))):
        middle_back, term = norm_back(middle, scale, gain_second, ff_grad[t])
        gain_ff_sum = gain_ff_sum + term
        middle_grads.append(cot_rows[t].astype(F32) + middle_back)
        out_own.append((RESIDUAL * middle_grads[t]).astype(BF16))
    (down_part,), (out_all,), _, (total_gate,) = links.carry(
        lambda comm: products([(hidden, w_down, False)], 256, comm),
        gathers=[(jnp.concatenate(out_own, axis=0), trees)],
        totals=[grad_gate],
    )
    arrays = []
    for t, (_, query, kv, lse) in enumerate((saved_0, saved_1)):
        attended_grad = dot_nt(out_all[t * tree_rows : (t + 1) * tree_rows], w_out).astype(BF16)
        arrays.append((attended_grad, query, kv, lse, *tables[t], *masks[t]))
    (qkv_grad,), _, downs, (total_up,) = links.carry(
        lambda comm: attention_backward(links.place, arrays, shard, comm),
        sums=parts(down_part),
        totals=[grad_up],
    )
    results = [
        (middle + RESIDUAL * down).astype(BF16) for middle, down in zip((middle_0, middle_1), downs)
    ]
    normed_part = dot_nn(qkv_grad, w_qkv).astype(BF16)
    attended_all = jnp.concatenate([saved_0[0], saved_1[0]], axis=0)
    normed_all = jnp.concatenate([normed_0, normed_1], axis=0)
    (grad_attn,), _ = products(
        [(attended_all, out_all, True), (qkv_grad, normed_all, True)],
        128 if shard > 4 else 256,
        NoComm(),
        joined=True,
    )
    _, _, normed_grads, (total_attn,) = links.carry(
        None, sums=parts(normed_part), totals=[grad_attn]
    )
    input_grads = []
    gain_attn_sum = jnp.zeros((width,), F32)
    for t in range(trees):
        inputs = token_rows[t].astype(F32)
        input_back, term = norm_back(inputs, rms_scale(inputs), gain_first, normed_grads[t])
        gain_attn_sum = gain_attn_sum + term
        input_grads.append(middle_grads[t] + input_back)
    gains = links.sum_small(jnp.stack([gain_attn_sum, gain_ff_sum]))
    rows = lambda begin, count: total_attn[begin : begin + count].astype(F32)
    return (
        jnp.stack(results)[:, None],
        jnp.stack(input_grads)[:, None],
        gains[0],
        rows(q_width, q_width),
        rows(2 * q_width, kv_width),
        rows(2 * q_width + kv_width, kv_width),
        rows(0, q_width),
        gains[1],
        total_gate.astype(F32),
        total_up.astype(F32),
        total_down.astype(F32),
    )


def solution(mesh):
    shard, replica = mesh.shape["shard"], mesh.shape["replica"]
    links = (Square if (shard, replica) == (4, 8) else General)(shard, replica)
    in_specs = (
        P(None, "replica", "shard", None),
        P("shard"),
        P("shard", None),
        P("shard", None),
        P("shard", None),
        P("shard", None),
        P("shard"),
        P("shard", None),
        P("shard", None),
        P("shard", None),
        P(None, "replica", "shard", None),
        P(None, "replica", "shard"),
        P(None, "replica", None),
    )
    out_specs = (
        P(None, "replica", "shard", None),
        P(None, "replica", "shard", None),
        P("shard"),
        P("shard", None),
        P("shard", None),
        P("shard", None),
        P("shard", None),
        P("shard"),
        P("shard", None),
        P("shard", None),
        P("shard", None),
    )
    return jax.shard_map(
        functools.partial(body, links),
        mesh=mesh,
        in_specs=in_specs,
        out_specs=out_specs,
        check_vma=False,
    )
```

```python
import functools
import math

import jax
import jax.numpy as jnp
from jax import lax
from jax.experimental import pallas as pl
from jax.experimental.pallas import tpu as pltpu
from jax.sharding import PartitionSpec as P

HEADS = 32
KV_HEADS = 8
HEAD_DIM = 64
PAIR = 2 * HEAD_DIM
GROUP = HEADS // KV_HEADS

EPSILON = 1e-05
RESIDUAL = 0.22
ATTN_SCALE = 0.015625
ROPE_BASE = 10000000.0
NEGATIVE = -1e30
BF16 = jnp.bfloat16
F32 = jnp.float32


def dot_nt(left, right):
    return lax.dot_general(left, right, (((1,), (1,)), ((), ())), preferred_element_type=F32)


def dot_nn(left, right):
    return lax.dot_general(left, right, (((1,), (0,)), ((), ())), preferred_element_type=F32)


def dot_tn(left, right):
    return lax.dot_general(left, right, (((0,), (0,)), ((), ())), preferred_element_type=F32)


def tree_layout(segment_row, parent_row):
    seg_numbers = jnp.arange(parent_row.shape[0], dtype=jnp.int32)
    member = (segment_row[:, None] == seg_numbers[None, :]).astype(jnp.int32)
    lengths = jnp.sum(member, axis=0)
    earlier = seg_numbers[None, :] < seg_numbers[:, None]
    starts = jnp.sum(jnp.where(earlier, lengths[None, :], 0), axis=1)
    parent_hit = parent_row[:, None] == seg_numbers[None, :]
    grandparent = jnp.sum(jnp.where(parent_hit, parent_row[None, :], 0), axis=1)
    itself = seg_numbers[:, None] == seg_numbers[None, :]
    related = itself | parent_hit | (grandparent[:, None] == seg_numbers[None, :])
    before = jnp.sum(jnp.where(related & jnp.logical_not(itself), lengths[None, :], 0), axis=1)
    shift = jnp.sum(member * (before - starts)[None, :], axis=1)
    position = jnp.arange(segment_row.shape[0], dtype=jnp.int32) + shift
    pad = ((0, 0), (0, PAIR - parent_row.shape[0]))
    sees = dot_nn(member.astype(BF16), related.astype(BF16)).astype(BF16)
    return position, jnp.pad(member.astype(BF16), pad), jnp.pad(sees, pad)


def rope_tables(position):
    lane = jnp.arange(PAIR, dtype=jnp.int32) % HEAD_DIM
    half = HEAD_DIM // 2
    fraction = (lane % half).astype(F32) * (2.0 / HEAD_DIM)
    freq = jnp.exp(-math.log(ROPE_BASE) * fraction)
    angle = position.astype(F32)[:, None] * freq[None, :]
    return jnp.cos(angle), jnp.sin(angle) * jnp.where(lane < half, -1.0, 1.0)[None, :]


MESH = pl.DeviceIdType.MESH
CHUNK = 64
SLOTS = 4


def remote(source, target, sems, index, device):
    return pltpu.make_async_remote_copy(
        source, target, sems.at[0, index], sems.at[1, index], device_id=device, device_id_type=MESH
    )


class GatherJob:
    def __init__(self, own, trees):
        self.operand = own
        self.trees = trees
        self.rows, self.width = own.shape[0] // trees, own.shape[1]
        self.chunks = self.rows // CHUNK
        self.out_shape = jax.ShapeDtypeStruct((4 * own.shape[0], self.width), own.dtype)
        self.out_spec = pl.BlockSpec(memory_space=pl.ANY)

    def scratch(self):
        return [
            pltpu.SemaphoreType.DMA((2, 3 * self.chunks * self.trees)),
            pltpu.SemaphoreType.DMA((self.trees,)),
        ]

    def bind(self, operand, out, scratch, x, y):
        sems, local = scratch
        n, rows = self.chunks, self.rows
        self.local, self.to_x, self.to_y, self.on_x, self.on_y = [], [], [], [], []
        for t in range(self.trees):
            at = lambda block, j: out.at[pl.ds((4 * t + block) * rows + j * CHUNK, CHUNK), :]
            own = lambda j: operand.at[pl.ds(t * rows + j * CHUNK, CHUNK), :]
            sem = 3 * n * t
            self.local.append(
                pltpu.make_async_copy(
                    operand.at[pl.ds(t * rows, rows), :],
                    out.at[pl.ds(4 * t * rows, rows), :],
                    local.at[t],
                )
            )
            self.to_x.append([remote(own(j), at(1, j), sems, sem + j, x) for j in range(n)])
            self.to_y.append([remote(own(j), at(2, j), sems, sem + n + j, y) for j in range(n)])
            on = lambda block, j, to: remote(at(block, j), at(3, j), sems, sem + 2 * n + j, to)
            self.on_x.append([on(2, j, x) for j in range(n // 2)])
            self.on_y.append([on(1, j, y) for j in range(n // 2, n)])

    def begin(self):
        n = self.chunks
        half = n // 2
        for t in range(self.trees):
            for k in range(n):
                self.to_x[t][(k + half) % n].start()
                self.to_y[t][k].start()
            self.local[t].start()

    def stages(self):
        def stage(t, k):
            half = self.chunks // 2
            self.to_y[t][k].wait_recv()
            self.on_x[t][k].start()
            self.to_x[t][half + k].wait_recv()
            self.on_y[t][k].start()

        return [
            functools.partial(stage, t, k)
            for t in range(self.trees)
            for k in range(self.chunks // 2)
        ]

    def finish(self):
        half = self.chunks // 2
        for t in range(self.trees):
            for copy in self.to_x[t][:half] + self.to_y[t][half:] + self.on_x[t] + self.on_y[t]:
                copy.wait_recv()
            for copy in self.to_x[t] + self.to_y[t] + self.on_x[t] + self.on_y[t]:
                copy.wait_send()
            self.local[t].wait()


class SmallJob:
    def __init__(self, own):
        self.operand = own
        self.rows, self.width = own.shape
        self.out_shape = jax.ShapeDtypeStruct((4 * self.rows, self.width), own.dtype)
        self.out_spec = pl.BlockSpec(memory_space=pl.ANY)

    def scratch(self):
        return [pltpu.SemaphoreType.DMA((2, 3)), pltpu.SemaphoreType.DMA(())]

    def bind(self, operand, out, scratch, x, y):
        sems, local = scratch
        shard = lax.axis_index("shard")
        mine = out.at[pl.ds(pl.multiple_of(shard * self.rows, self.rows), self.rows), :]
        self.local = pltpu.make_async_copy(operand, mine, local)
        self.sends = [
            remote(operand, mine, sems, k, device)
            for k, device in enumerate((x, y, (3 - shard, x[1])))
        ]

    def begin(self):
        for send in self.sends:
            send.start()
        self.local.start()

    def stages(self):
        return []

    def finish(self):
        for send in self.sends:
            send.wait()
        self.local.wait()


class SumJob:
    def __init__(self, part, trees, tree):
        self.operand = part
        self.rows, self.width = part.shape[0] // 4 // trees, part.shape[1]
        self.base = 4 * self.rows * tree
        self.half = self.rows // 2
        self.chunks = self.half // CHUNK
        self.out_shape = jax.ShapeDtypeStruct((self.rows, self.width), F32)
        self.out_spec = pl.BlockSpec((self.rows, self.width), lambda *_: (0, 0))

    def scratch(self):
        return [
            pltpu.VMEM((4, self.half, self.width), BF16),
            pltpu.VMEM((6, self.half, self.width), BF16),
            pltpu.SemaphoreType.DMA((2, 6 * self.chunks)),
            pltpu.SemaphoreType.DMA((4,)),
        ]

    def bind(self, part, out, scratch, x, y):
        self.out = out
        self.mine, self.got, sems, local = scratch
        n, half = self.chunks, self.half
        rows = lambda block, second: pl.ds(self.base + block * self.rows + second * half, half)
        piece = lambda block, second, j: part.at[
            pl.ds(self.base + block * self.rows + second * half + j * CHUNK, CHUNK), :
        ]
        here = lambda ref, k, j: ref.at[k, pl.ds(j * CHUNK, CHUNK), :]
        self.loads = [
            pltpu.make_async_copy(part.at[rows(block, second), :], self.mine.at[k], local.at[k])
            for k, (block, second) in enumerate(((0, 0), (0, 1), (2, 0), (1, 1)))
        ]
        send = lambda k, source, device: [
            remote(source(j), here(self.got, k, j), sems, k * n + j, device) for j in range(n)
        ]
        self.sends = [
            send(0, lambda j: piece(1, 0, j), x),
            send(1, lambda j: piece(3, 0, j), x),
            send(2, lambda j: here(self.mine, 2, j), y),
            send(3, lambda j: piece(2, 1, j), y),
            send(4, lambda j: piece(3, 1, j), y),
            send(5, lambda j: here(self.mine, 3, j), x),
        ]

    def begin(self):
        for j in range(self.chunks):
            self.sends[1][j].start()
            self.sends[4][j].start()
        for load in self.loads:
            load.start()
        for j in range(self.chunks):
            self.sends[0][j].start()
            self.sends[3][j].start()

    def stages(self):
        def stage(j):
            if j == 0:
                for load in self.loads:
                    load.wait()
            rows = pl.ds(j * CHUNK, CHUNK)
            for first, second, own in ((1, 2, 2), (4, 5, 3)):
                self.sends[first][j].wait_recv()
                total = self.mine[own, rows, :].astype(F32) + self.got[first, rows, :].astype(F32)
                self.mine[own, rows, :] = total.astype(BF16)
                self.sends[second][j].start()

        return [functools.partial(stage, j) for j in range(self.chunks)]

    def finish(self):
        for j in range(self.chunks):
            rows = pl.ds(j * CHUNK, CHUNK)
            for own, one, two in ((0, 0, 2), (1, 3, 5)):
                self.sends[one][j].wait_recv()
                self.sends[two][j].wait_recv()
                self.out[pl.ds(own * self.half + j * CHUNK, CHUNK), :] = (
                    self.mine[own, rows, :].astype(F32)
                    + self.got[one, rows, :].astype(F32)
                    + self.got[two, rows, :].astype(F32)
                )
        for copies in self.sends:
            for copy in copies:
                copy.wait_send()


class LineJob:
    LINE_ROWS = 32
    LAG = 2

    def __init__(self, grad):
        self.operand = grad
        self.half, self.width = grad.shape[0] // 2, grad.shape[1]
        self.chunks = self.half // self.LINE_ROWS
        self.steps = self.chunks + 1 + 3 * self.LAG
        self.out_shape = jax.ShapeDtypeStruct(grad.shape, BF16)
        self.out_spec = pl.BlockSpec(memory_space=pl.ANY)

    def scratch(self):
        place = lambda: pltpu.VMEM((self.half, self.width), BF16)
        return [place(), place(), place(), place(), pltpu.SemaphoreType.DMA((9, self.chunks))]

    def bind(self, grad, out, scratch, x, y):
        self.grad, self.out = grad, out
        self.from_core, self.own, self.from_line, self.from_inner, self.sems = scratch
        shard, place = lax.axis_index("shard"), lax.axis_index("replica")
        self.core, z = place % 2, place // 2
        self.inner = (z == 1) | (z == 2)
        self.outer = (z == 0) | (z == 3)
        self.twin = (shard, z * 2 + 1 - self.core)
        self.pair = (shard, (z + 1 - 2 * (z % 2)) * 2 + self.core)
        self.across = (shard, (3 - z) * 2 + self.core)

    def chunk(self, c):
        return pl.ds(pl.multiple_of(c * self.LINE_ROWS, self.LINE_ROWS), self.LINE_ROWS)

    def at(self, core, c):
        return pl.ds(
            pl.multiple_of(core * self.half + c * self.LINE_ROWS, self.LINE_ROWS), self.LINE_ROWS
        )

    def send(self, source, target, index, arrival, device, c):
        return pltpu.make_async_remote_copy(
            source,
            target,
            self.sems.at[index, c],
            self.sems.at[arrival, c],
            device_id=device,
            device_id_type=MESH,
        )

    def to_twin(self, c):
        source = self.grad.at[self.at(1 - self.core, c), :]
        return self.send(source, self.from_core.at[self.chunk(c), :], 0, 1, self.twin, c)

    def load(self, c):
        source = self.grad.at[self.at(self.core, c), :]
        return pltpu.make_async_copy(source, self.own.at[self.chunk(c), :], self.sems.at[2, c])

    def inward(self, c):
        rows = self.chunk(c)
        return self.send(self.own.at[rows, :], self.from_line.at[rows, :], 3, 4, self.pair, c)

    def between(self, c):
        rows = self.chunk(c)
        return self.send(self.own.at[rows, :], self.from_inner.at[rows, :], 3, 5, self.across, c)

    def outward(self, c):
        rows = self.chunk(c)
        return self.send(self.from_core.at[rows, :], self.from_line.at[rows, :], 6, 4, self.pair, c)

    def store(self, source, c):
        target = self.out.at[self.at(self.core, c), :]
        return pltpu.make_async_copy(source.at[self.chunk(c), :], target, self.sems.at[2, c])

    def give(self, source, c):
        target = self.out.at[self.at(self.core, c), :]
        return self.send(source.at[self.chunk(c), :], target, 7, 8, self.twin, c)

    def begin(self):
        pass

    def stages(self):
        return []

    def step(self, s):
        n, lag = self.chunks, self.LAG
        live = lambda begin: (s >= begin) & (s < n + begin)
        add = lambda a, b: (a.astype(F32) + b.astype(F32)).astype(BF16)

        @pl.when(live(0))
        def _():
            self.to_twin(s).start()
            self.load(s).start()

        @pl.when(live(1))
        def _():
            c = s - 1
            rows = self.chunk(c)
            self.to_twin(c).wait()
            self.load(c).wait()
            self.own[rows, :] = add(self.own[rows, :], self.from_core[rows, :])
            pl.when(self.outer)(lambda: self.inward(c).start())

        @pl.when(live(1 + lag) & self.inner)
        def _():
            c = s - 1 - lag
            rows = self.chunk(c)
            self.inward(c).wait_recv()
            self.own[rows, :] = add(self.own[rows, :], self.from_line[rows, :])
            self.between(c).start()

        @pl.when(live(1 + 2 * lag) & self.inner)
        def _():
            c = s - 1 - 2 * lag
            rows = self.chunk(c)
            self.between(c).wait_recv()
            self.from_core[rows, :] = add(self.own[rows, :], self.from_inner[rows, :])
            self.outward(c).start()
            self.store(self.from_core, c).start()
            self.give(self.from_core, c).start()

        @pl.when(live(1 + 3 * lag) & self.outer)
        def _():
            c = s - 1 - 3 * lag
            self.outward(c).wait_recv()
            self.store(self.from_line, c).start()
            self.give(self.from_line, c).start()

    def finish(self):
        def body(c, carry):
            self.store(self.from_line, c).wait()
            self.give(self.from_line, c).wait()

            @pl.when(self.inner)
            def _():
                self.between(c).wait_send()
                self.outward(c).wait_send()

            pl.when(self.outer)(lambda: self.inward(c).wait_send())
            return carry

        lax.fori_loop(0, self.chunks, body, 0)


class Comm:
    def __init__(self, jobs, number):
        self.jobs, self.number = jobs, number
        self.operands = [job.operand for job in jobs]
        self.in_specs = [pl.BlockSpec(memory_space=pl.ANY) for _ in jobs]
        self.out_specs = [job.out_spec for job in jobs]
        self.out_shapes = [job.out_shape for job in jobs]
        self.scratch = [entry for job in jobs for entry in job.scratch()]

    def enter(self, operands, outs, scratch, now):
        shard, replica = lax.axis_index("shard"), lax.axis_index("replica")
        x = (shard + 1 - 2 * (shard % 2), replica)
        y = ((shard + 2) % 4, replica)
        scratch = list(scratch)
        for job, operand, out in zip(self.jobs, operands, outs):
            count = len(job.scratch())
            job.bind(operand, out, scratch[:count], x, y)
            scratch = scratch[count:]

        lines = [job for job in self.jobs if isinstance(job, LineJob)]
        square = len(lines) < len(self.jobs)

        @pl.when(now)
        def _():
            barrier = pltpu.get_barrier_semaphore()

            def greet(device):
                pl.semaphore_signal(barrier, inc=1, device_id=device, device_id_type=MESH)

            near = ([x, y] if square else []) + ([lines[0].twin, lines[0].pair] if lines else [])
            if any(isinstance(job, SmallJob) for job in self.jobs):
                near.append((3 - shard, replica))
            for device in near:
                greet(device)
            if lines:

                @pl.when(lines[0].inner)
                def _():
                    greet(lines[0].across)
                    pl.semaphore_wait(barrier, len(near) + 1)

                @pl.when(lines[0].outer)
                def _():
                    pl.semaphore_wait(barrier, len(near))

            else:
                pl.semaphore_wait(barrier, len(near))
            for job in self.jobs:
                job.begin()

    def stages(self):
        return [stage for job in self.jobs for stage in job.stages()]

    def advance(self, slot, slots):
        stages = self.stages()
        for job in self.jobs:
            if isinstance(job, LineJob):

                def body(k, carry, job=job):
                    job.step(k)
                    return carry

                lax.fori_loop(slot * job.steps // slots, (slot + 1) * job.steps // slots, body, 0)
        for index, stage in enumerate(stages):
            if slots <= 4:
                due = min(slots - 1, slots // 2 + index * (slots - slots // 2) // len(stages))
            else:
                due = min(slots - 1, max(1, int(slots * (0.25 + 0.5 * index / len(stages)))))
            pl.when(slot == due)(stage)

    def finish(self, now):
        @pl.when(now)
        def _():
            for job in self.jobs:
                job.finish()


class NoComm:
    operands = in_specs = out_specs = out_shapes = scratch = ()
    number = None

    def enter(self, *_):
        pass

    def advance(self, *_):
        pass

    def finish(self, *_):
        pass


def comm_params(comm, vmem):
    if comm.number is None:
        return pltpu.CompilerParams(vmem_limit_bytes=vmem << 20)
    return pltpu.CompilerParams(
        vmem_limit_bytes=vmem << 20, collective_id=comm.number, has_side_effects=True
    )


def split_refs(refs, *counts):
    parts, begin = [], 0
    for count in counts:
        parts.append(refs[begin : begin + count])
        begin += count
    return parts


def transfer(comm):
    count = len(comm.operands)
    steps = max([1] + [job.steps for job in comm.jobs if isinstance(job, LineJob)])

    def kernel(*refs):
        operands, outs, scratch = split_refs(refs, count, count, len(comm.scratch))
        step = pl.program_id(0)
        comm.enter(operands, outs, scratch, step == 0)
        if steps == 1:
            for stage in comm.stages():
                stage()
        else:
            comm.advance(step, steps)
        comm.finish(step == steps - 1)

    return pl.pallas_call(
        kernel,
        grid=(steps,),
        in_specs=comm.in_specs,
        out_specs=comm.out_specs,
        out_shape=comm.out_shapes,
        scratch_shapes=comm.scratch,
        compiler_params=comm_params(comm, 48),
        name="transfer",
    )(*comm.operands)


def products(items, block, comm, joined=False):
    specs, shapes, out_specs, steps, rights = [], [], [], [], []
    begin = 0
    items = [
        (l if isinstance(l, tuple) else (l,), r if isinstance(r, tuple) else (r,), t)
        for l, r, t in items
    ]
    total = sum((l[0].shape[1] if t else l[0].shape[0]) // block for l, _, t in items)
    for left, right, transposed in items:
        size = left[0].shape[1] if transposed else left[0].shape[0]
        count = size // block

        def place(i, begin=begin, count=count):
            return jnp.clip(i - begin, 0, count - 1)

        for l in left:
            if transposed:
                specs.append(pl.BlockSpec((l.shape[0], block), lambda i, p=place: (0, p(i))))
            else:
                specs.append(pl.BlockSpec((block, l.shape[1]), lambda i, p=place: (p(i), 0)))
        columns = right[0].shape[1]
        if not joined:
            out_specs.append(pl.BlockSpec((block, columns), lambda i, p=place: (p(i), 0)))
            shapes.append(jax.ShapeDtypeStruct((size, columns), BF16))
        for r in right:
            if not any(r is other for other in rights):
                rights.append(r)
        steps.append((begin, count))
        begin += count
    right_specs = [
        pl.BlockSpec(r.shape, lambda i: (0, 0), pipeline_mode=pl.Buffered(1)) for r in rights
    ]
    which = [
        [next(k for k, other in enumerate(rights) if other is r) for r in right]
        for _, right, _ in items
    ]
    firsts = [sum(len(l) for l, _, _ in items[:k]) for k in range(len(items))]
    n = sum(len(l) for l, _, _ in items)
    if joined:
        width = items[0][1][0].shape[1]
        out_specs = [pl.BlockSpec((block, width), lambda i: (i, 0))]
        shapes = [jax.ShapeDtypeStruct((total * block, width), BF16)]
    made = len(shapes)

    def kernel(*refs):
        lefts, held, operands, outs, comm_outs, scratch = split_refs(
            refs, n, len(rights), len(comm.operands), made, len(comm.operands), len(comm.scratch)
        )
        step = pl.program_id(0)
        comm.enter(operands, comm_outs, scratch, step == 0)
        width = items[0][1][0].shape[1] // SLOTS

        def part(slot, carry):
            comm.advance(step * SLOTS + slot, total * SLOTS)
            columns = pl.ds(pl.multiple_of(slot * width, width), width)
            for k, (left, right, transposed) in enumerate(items):
                begin, count = steps[k]

                @pl.when((step >= begin) & (step < begin + count))
                def _(k=k, left=left, right=right, transposed=transposed):
                    dot = dot_tn if transposed else dot_nn
                    result, pieces = 0.0, max(len(left), len(right))
                    for piece in range(pieces):
                        l, r = lefts[firsts[k] + piece % len(left)], held[which[k][piece % len(right)]]
                        share = pl.ds(piece * (r.shape[0] // pieces), r.shape[0] // pieces)
                        ours = pl.ds(piece * (l.shape[0] // pieces), l.shape[0] // pieces)
                        result += dot(
                            l[ours, :] if len(left) < pieces else l[...],
                            r[share, columns] if len(right) < pieces else r[:, columns],
                        )
                    outs[0 if joined else k][:, columns] = result.astype(BF16)

            return carry

        lax.fori_loop(0, SLOTS, part, 0)

        comm.finish(step == total - 1)

    flops = 2 * sum(math.prod(l.shape) * right[0].shape[1] for left, right, _ in items for l in left)
    out = pl.pallas_call(
        kernel,
        grid=(total,),
        in_specs=specs + right_specs + list(comm.in_specs),
        out_specs=out_specs + list(comm.out_specs),
        out_shape=shapes + list(comm.out_shapes),
        scratch_shapes=list(comm.scratch),
        compiler_params=comm_params(comm, 58),
        cost_estimate=pl.CostEstimate(flops=flops, bytes_accessed=30_000_000, transcendentals=0),
        name="products",
    )(*[l for left, _, _ in items for l in left], *rights, *comm.operands)
    return out[:made], out[made:]


def feed_forward(rows_all, w_gate, w_up, block, comm):
    rows, width = rows_all.shape
    units = w_gate.shape[0]
    steps = units // block
    part = rows // SLOTS

    def kernel(*refs):
        inputs, operands, outs, comm_outs, scratch = split_refs(
            refs, 3, len(comm.operands), 3, len(comm.operands), len(comm.scratch)
        )
        x_ref, gate_w, up_w = inputs
        gate_ref, upper_ref, hidden_ref = outs
        step = pl.program_id(0)
        comm.enter(operands, comm_outs, scratch, step == 0)
        comm.advance(step, steps)
        for slot in range(SLOTS):
            here = pl.ds(slot * part, part)
            gate = dot_nt(x_ref[here, :], gate_w[...])
            upper = dot_nt(x_ref[here, :], up_w[...])
            gate_ref[here, :] = gate.astype(BF16)
            upper_ref[here, :] = upper.astype(BF16)
            hidden_ref[here, :] = (gate * jax.nn.sigmoid(gate) * upper).astype(BF16)
        comm.finish(step == steps - 1)

    out = pl.pallas_call(
        kernel,
        grid=(steps,),
        in_specs=[
            pl.BlockSpec((rows, width), lambda i: (0, 0), pipeline_mode=pl.Buffered(1)),
            pl.BlockSpec((block, width), lambda i: (i, 0)),
            pl.BlockSpec((block, width), lambda i: (i, 0)),
            *comm.in_specs,
        ],
        out_specs=[pl.BlockSpec((rows, block), lambda i: (0, i))] * 3 + list(comm.out_specs),
        out_shape=[jax.ShapeDtypeStruct((rows, units), BF16)] * 3 + list(comm.out_shapes),
        scratch_shapes=list(comm.scratch),
        compiler_params=comm_params(comm, 56),
        cost_estimate=pl.CostEstimate(
            flops=4 * rows * width * units, bytes_accessed=48_000_000, transcendentals=rows * units
        ),
        name="feed_forward",
    )(rows_all, w_gate, w_up, *comm.operands)
    return out[:3], out[3:]


def swap_halves(block):
    lane = lax.broadcasted_iota(jnp.int32, block.shape, 1)
    half = HEAD_DIM // 2
    up = pltpu.roll(block, PAIR - half, 1)
    down = pltpu.roll(block, half, 1)
    return jnp.where(lane % HEAD_DIM < half, up, down)


def turn(block, cosine, sine):
    return block * cosine + swap_halves(block) * sine


def place_heads(wide, kv_heads, fill):
    placed = []
    for g in range(kv_heads):
        base = wide[:, (g // 2) * PAIR : (g // 2) * PAIR + PAIR] if wide.shape[1] >= PAIR else wide
        lane = lax.broadcasted_iota(jnp.int32, base.shape, 1)
        moved = pltpu.roll(base, HEAD_DIM, 1)
        for p in range(2):
            source = base if g % 2 == p else moved
            inside = (lane // HEAD_DIM) == p
            placed.append(jnp.where(inside, source, jnp.full_like(source, fill)))
    return placed


def attention_forward_kernel(kv_heads, blocks, place, comm, *refs):
    jobs = len(comm.operands)
    inputs, operands, outs, comm_outs, own, scratch = split_refs(
        refs, 6, jobs, 4, jobs, 3, len(comm.scratch)
    )
    q_ref, kv_ref, cos_ref, sin_ref, member_ref, sees_ref = inputs
    out_ref, q_out_ref, kv_out_ref, lse_ref = outs
    keys, values, bias = own
    step = pl.program_id(0)
    comm.enter(operands, comm_outs, scratch, step == 0)
    comm.advance(step, blocks)
    tree = q_ref.shape[0]
    rows = tree // blocks
    kv_width = kv_heads * HEAD_DIM

    @pl.when(step == 0)
    def _():
        for b in range(blocks):
            here = pl.ds(b * rows, rows)
            raw = kv_ref[pl.ds(pl.multiple_of(place(b) * rows, rows), rows), :]
            cosine, sine = cos_ref[here, :], sin_ref[here, :]
            if kv_width >= PAIR:
                turned = jnp.concatenate(
                    [
                        turn(raw[:, c : c + PAIR], cosine, sine)
                        for c in range(0, kv_width, PAIR)
                    ],
                    axis=1,
                )
                plain = raw[:, kv_width:]
            else:
                lane = lax.broadcasted_iota(jnp.int32, raw.shape, 1)
                turned = turn(raw, cosine, sine)
                plain = pltpu.roll(raw, HEAD_DIM, 1)
                both = jnp.where(lane < HEAD_DIM, turned, raw)
            if kv_width >= PAIR:
                both = jnp.concatenate([turned, plain], axis=1)
            kv_out_ref[here, :] = both.astype(BF16)
            for index, placed in enumerate(place_heads(turned, kv_heads, 0.0)):
                keys[index, here, :] = placed.astype(BF16)
            for index, placed in enumerate(place_heads(plain, kv_heads, 1.0)):
                values[index, here, :] = placed.astype(BF16)

    here = pl.ds(pl.multiple_of(step * rows, rows), rows)
    there = pl.ds(pl.multiple_of(place(step) * rows, rows), rows)
    cosine, sine = cos_ref[here, :], sin_ref[here, :]
    for j in range(q_ref.shape[1] // PAIR):
        lanes = slice(j * PAIR, j * PAIR + PAIR)
        turned = turn(q_ref[there, lanes], cosine, sine).astype(BF16)
        q_out_ref[:, lanes] = turned * BF16(ATTN_SCALE)

    link = dot_nt(sees_ref[here, :], member_ref[...])
    row_index = lax.broadcasted_iota(jnp.int32, (rows, tree), 0) + step * rows
    col_index = lax.broadcasted_iota(jnp.int32, (rows, tree), 1)
    bias[...] = jnp.where((link > 0.5) & (col_index <= row_index), 0.0, NEGATIVE)

    lane = lax.broadcasted_iota(jnp.int32, (rows, PAIR), 1)
    for block in range(blocks):
        width = (block + 1) * rows

        @pl.when(step == block)
        def _(width=width):
            lse = jnp.zeros((rows, PAIR), F32)
            for j in range(q_ref.shape[1] // PAIR):
                lanes = slice(j * PAIR, j * PAIR + PAIR)
                group = 2 * j // GROUP
                mixed, tops = [], []
                for p in range(2):
                    scores = dot_nt(q_out_ref[:, lanes], keys[group * 2 + p, :width, :])
                    scores = scores + bias[:, :width]
                    top = jnp.max(scores, axis=1, keepdims=True)
                    expo = jnp.exp(scores - top).astype(BF16)
                    mixed.append(dot_nn(expo, values[group * 2 + p, :width, :]))
                    tops.append(top)
                upper = lane >= HEAD_DIM
                total = pltpu.roll(jnp.where(upper, mixed[0], mixed[1]), HEAD_DIM, 1)
                out_ref[there, lanes] = (jnp.where(upper, mixed[1], mixed[0]) / total).astype(BF16)
                logs = jnp.log(total)
                lse = jnp.where(lane == 2 * j, tops[0] + logs[:, :1], lse)
                lse = jnp.where(lane == 2 * j + 1, tops[1] + logs[:, HEAD_DIM : HEAD_DIM + 1], lse)
            lse_ref[...] = lse

    comm.finish(step == blocks - 1)


def attention_forward(place, qkv, cosine, sine, member, sees, q_width, blocks, comm):
    tree = qkv.shape[0]
    rows = tree // blocks
    kv_width = (qkv.shape[1] - q_width) // 2
    kv_heads = kv_width // HEAD_DIM
    whole = lambda width: pl.BlockSpec((tree, width), lambda i: (0, 0))
    natural = lambda width: pl.BlockSpec((rows, width), lambda i: (i, 0))
    out = pl.pallas_call(
        functools.partial(attention_forward_kernel, kv_heads, blocks, place, comm),
        grid_spec=pl.GridSpec(
            grid=(blocks,),
            in_specs=[
                whole(q_width),
                pl.BlockSpec((tree, 2 * kv_width), lambda i: (0, q_width // (2 * kv_width))),
                whole(PAIR),
                whole(PAIR),
                whole(PAIR),
                whole(PAIR),
                *comm.in_specs,
            ],
            out_specs=[
                whole(q_width),
                natural(q_width),
                whole(2 * kv_width),
                natural(PAIR),
                *comm.out_specs,
            ],
            scratch_shapes=[
                pltpu.VMEM((2 * kv_heads, tree, PAIR), BF16),
                pltpu.VMEM((2 * kv_heads, tree, PAIR), BF16),
                pltpu.VMEM((rows, tree), F32),
                *comm.scratch,
            ],
        ),
        out_shape=[
            jax.ShapeDtypeStruct((tree, q_width), BF16),
            jax.ShapeDtypeStruct((tree, q_width), BF16),
            jax.ShapeDtypeStruct((tree, 2 * kv_width), BF16),
            jax.ShapeDtypeStruct((tree, PAIR), F32),
            *comm.out_shapes,
        ],
        compiler_params=comm_params(comm, 40),
        cost_estimate=pl.CostEstimate(
            flops=10_000_000_000, bytes_accessed=12_000_000, transcendentals=5_000_000
        ),
        name="attention_forward",
    )(qkv, qkv, cosine, sine, member, sees, *comm.operands)
    return out[:4], out[4:]


def attention_backward_kernel(kv_heads, blocks, trees, place, comm, *refs):
    jobs = len(comm.operands)
    inputs, operands, outs, comm_outs, own, scratch = split_refs(
        refs, 8 * trees, jobs, 1, jobs, 6, len(comm.scratch)
    )
    pairs = inputs[1].shape[1] // PAIR
    each = blocks * pairs
    step = pl.program_id(0)
    comm.enter(operands, comm_outs, scratch, step == 0)
    comm.advance(step, each * trees)
    for t in range(trees):

        @pl.when((step >= t * each) & (step < (t + 1) * each))
        def _(t=t):
            local = step - t * each
            attention_backward_step(
                kv_heads,
                blocks,
                pairs,
                place,
                local // pairs,
                local % pairs,
                t,
                inputs[8 * t : 8 * t + 8],
                outs[0],
                own,
            )

    comm.finish(step == each * trees - 1)


def attention_backward_step(kv_heads, blocks, pairs, place, step, j, t, inputs, out_ref, own):
    grad_ref, q_ref, kv_ref, lse_ref, cos_ref, sin_ref, member_ref, sees_ref = inputs
    keys, values, bias, lse_rows, key_sum, value_sum = own
    tree, rows = grad_ref.shape[0], q_ref.shape[0]
    kv_width = kv_heads * HEAD_DIM
    q_width = q_ref.shape[1]
    base = t * tree

    @pl.when((step == 0) & (j == 0))
    def _():
        for b in range(blocks):
            here = pl.ds(b * rows, rows)
            both = kv_ref[here, :].astype(F32)
            if kv_width >= PAIR:
                turned, plain = both[:, :kv_width], both[:, kv_width:]
            else:
                turned, plain = both, pltpu.roll(both, HEAD_DIM, 1)
            for index, placed in enumerate(place_heads(turned, kv_heads, 0.0)):
                keys[index, here, :] = placed.astype(BF16)
            for index, placed in enumerate(place_heads(plain, kv_heads, 0.0)):
                values[index, here, :] = placed.astype(BF16)
        key_sum[...] = jnp.zeros_like(key_sum)
        value_sum[...] = jnp.zeros_like(value_sum)

    here = pl.ds(pl.multiple_of(step * rows, rows), rows)

    @pl.when(j == 0)
    def _():
        link = dot_nt(member_ref[...], sees_ref[here, :])
        key_index = lax.broadcasted_iota(jnp.int32, (tree, rows), 0)
        query_index = lax.broadcasted_iota(jnp.int32, (tree, rows), 1) + step * rows
        bias[...] = jnp.where((link > 0.5) & (key_index <= query_index), 0.0, NEGATIVE)
        lse_rows[...] = jnp.transpose(lse_ref[...])

    there = pl.ds(pl.multiple_of(place(step) * rows, rows), rows)
    out_rows = pl.ds(pl.multiple_of(base + place(step) * rows, rows), rows)
    lanes = pl.ds(pl.multiple_of(j * PAIR, PAIR), PAIR)
    group = 2 * j // GROUP
    for block in range(blocks):
        width = (block + 1) * rows

        @pl.when(step == block)
        def _(width=width):
            cosine, sine = cos_ref[here, :], sin_ref[here, :]
            query, grad = q_ref[:, lanes], grad_ref[there, lanes]
            dq = jnp.zeros((rows, PAIR), F32)
            for p in range(2):
                index = group * 2 + p
                scores = dot_nt(keys[index, :width, :], query) + bias[:width, :]
                probs = jnp.exp(scores - lse_rows[pl.ds(2 * j + p, 1), :])
                probs_grad = dot_nt(values[index, :width, :], grad)
                value_sum[index, :width, :] += dot_nn(probs.astype(BF16), grad)
                weighted = probs * probs_grad
                delta = jnp.sum(weighted, axis=0, keepdims=True)
                score_grad = (weighted - probs * delta).astype(BF16)
                key_sum[index, :width, :] += dot_nn(score_grad, query)
                dq = dq + dot_tn(score_grad, keys[index, :width, :])
            out_ref[out_rows, lanes] = turn(dq * ATTN_SCALE, cosine, -sine).astype(BF16)

    @pl.when((step == blocks - 1) & (j == pairs - 1))
    def _():
        for b in range(blocks):
            here = pl.ds(b * rows, rows)
            there = pl.ds(pl.multiple_of(base + place(b) * rows, rows), rows)
            cosine, sine = cos_ref[here, :], sin_ref[here, :]
            lane = lax.broadcasted_iota(jnp.int32, (rows, PAIR), 1)
            lower = lane < HEAD_DIM
            for c in range(0, kv_heads, 2):
                halves = []
                for acc in (key_sum, value_sum):
                    own, other = [], []
                    for g in range(c, min(c + 2, kv_heads)):
                        own.append(acc[g * 2, here, :])
                        other.append(acc[g * 2 + 1, here, :])
                    first = own[0] + pltpu.roll(other[0], HEAD_DIM, 1)
                    if len(own) == 2:
                        second = other[1] + pltpu.roll(own[1], HEAD_DIM, 1)
                    else:
                        second = first
                    halves.append(jnp.where(lower, first, second))
                turned = turn(halves[0], cosine, -sine)
                if kv_width >= PAIR:
                    begin = q_width + c * HEAD_DIM
                    out_ref[there, begin : begin + PAIR] = turned.astype(BF16)
                    begin += kv_width
                    out_ref[there, begin : begin + PAIR] = halves[1].astype(BF16)
                else:
                    moved = pltpu.roll(halves[1], HEAD_DIM, 1)
                    both = jnp.where(lower, turned, moved)
                    out_ref[there, q_width : q_width + PAIR] = both.astype(BF16)


def attention_backward(place, arrays, blocks, comm):
    trees = len(arrays)
    tree, q_width = arrays[0][1].shape
    rows = tree // blocks
    kv_width = arrays[0][2].shape[1] // 2
    kv_heads = kv_width // HEAD_DIM
    each = blocks * (q_width // PAIR)
    whole = lambda width: pl.BlockSpec((tree, width), lambda i: (0, 0))

    def natural(width, t):
        return pl.BlockSpec(
            (rows, width),
            lambda i: (jnp.clip((i - t * each) // (q_width // PAIR), 0, blocks - 1), 0),
        )

    in_specs = []
    for t in range(trees):
        in_specs += [whole(q_width), natural(q_width, t), whole(2 * kv_width), natural(PAIR, t)]
        in_specs += [whole(PAIR)] * 4
    total = q_width + 2 * kv_width
    out = pl.pallas_call(
        functools.partial(attention_backward_kernel, kv_heads, blocks, trees, place, comm),
        grid=(each * trees,),
        in_specs=in_specs + list(comm.in_specs),
        out_specs=[pl.BlockSpec((trees * tree, total), lambda i: (0, 0))] + list(comm.out_specs),
        out_shape=[jax.ShapeDtypeStruct((trees * tree, total), BF16)] + list(comm.out_shapes),
        scratch_shapes=[
            pltpu.VMEM((2 * kv_heads, tree, PAIR), BF16),
            pltpu.VMEM((2 * kv_heads, tree, PAIR), BF16),
            pltpu.VMEM((tree, rows), F32),
            pltpu.VMEM((PAIR, rows), F32),
            pltpu.VMEM((2 * kv_heads, tree, PAIR), F32),
            pltpu.VMEM((2 * kv_heads, tree, PAIR), F32),
            *comm.scratch,
        ],
        compiler_params=comm_params(comm, 60),
        cost_estimate=pl.CostEstimate(
            flops=40_000_000_000, bytes_accessed=24_000_000, transcendentals=10_000_000
        ),
        name="attention_backward",
    )(*[array for per_tree in arrays for array in per_tree], *comm.operands)
    return out[:1], out[1:]


def sync(*values):
    return lax.optimization_barrier(values)


def sum_beside(part, trees):
    return lax.psum_scatter(
        part.reshape(trees, -1, part.shape[1]), "shard", scatter_dimension=1, tiled=True
    )


class Square:
    def __init__(self, shard, replica):
        self.shard, self.replica = shard, replica
        self.x = [(i, i ^ 1) for i in range(shard)]
        self.y = [(i, i ^ 2) for i in range(shard)]
        self.d = [(i, i ^ 3) for i in range(shard)]

    def natural(self, rows, trees):
        blocks = rows.reshape(trees, self.shard, -1, rows.shape[1])
        return self.reorder(blocks, 1).reshape(rows.shape)

    def place(self, block):
        shard = lax.axis_index("shard")
        return (block + shard) % 2 + 2 * ((block // 2 + shard // 2) % 2)

    def reorder(self, blocks, axis):
        me = lax.axis_index("shard")
        return jnp.concatenate(
            [lax.dynamic_slice_in_dim(blocks, n ^ me, 1, axis) for n in range(self.shard)], axis=axis
        )

    def first(self, small, own):
        padded = jnp.pad(small, (0, -small.shape[0] % 2048)).reshape(16, -1)
        self.kernels += 1
        smalls, rows = transfer(Comm([SmallJob(padded), GatherJob(own, 1)], self.kernels))
        return smalls.reshape(self.shard, -1)[:, : small.shape[0]], rows

    def sum_small(self, values):
        share = values.shape[1] // self.shard
        blocks = values.reshape(values.shape[0], self.shard, share)
        blocks = self.reorder(blocks, 1)
        total = blocks[:, 0]
        for k, perm in ((1, self.x), (2, self.y), (3, self.d)):
            total = total + lax.ppermute(blocks[:, k], "shard", perm)
        for step in (1, 2, 4):
            perm = [(i, i ^ step) for i in range(self.replica)]
            total = total + lax.ppermute(total, "replica", perm)
        return total

    def carry(self, compute, gathers=(), sums=(), totals=()):
        jobs = [GatherJob(*own) for own in gathers] + [SumJob(*part) for part in sums]
        jobs += [LineJob(grad) for grad in totals]
        self.kernels += 1
        comm = Comm(jobs, self.kernels)
        if compute is None:
            results, moved = None, transfer(comm)
        else:
            results, moved = compute(comm)
        return (results, *map(list, split_refs(moved, len(gathers), len(sums), len(totals))))

    def start(self):
        self.kernels = 0


class General:
    def __init__(self, shard, replica):
        self.shard, self.replica = shard, replica

    def place(self, block):
        return block

    def natural(self, rows, trees):
        return rows

    def first(self, small, own):
        rows = lax.all_gather(own, "shard", axis=0, tiled=True)
        return lax.all_gather(small, "shard", axis=0, tiled=False), rows

    def carry(self, compute, gathers=(), sums=(), totals=()):
        results = None if compute is None else compute(NoComm())[0]
        rows = lambda array, trees: array.reshape(trees, -1, array.shape[1])
        gathered = [
            lax.all_gather(rows(own, trees), "shard", axis=1, tiled=True).reshape(-1, own.shape[1])
            for own, trees in gathers
        ]
        summed = [
            lax.psum_scatter(
                rows(part, trees)[tree], "shard", scatter_dimension=0, tiled=True
            ).astype(F32)
            for part, trees, tree in sums
        ]
        return results, gathered, summed, [lax.psum(grad, "replica") for grad in totals]

    def sum_small(self, values):
        share = lax.psum_scatter(values, "shard", scatter_dimension=1, tiled=True)
        return lax.psum(share, "replica")

    def start(self):
        pass


def rms_scale(values):
    return lax.rsqrt(jnp.mean(values * values, axis=-1, keepdims=True) + EPSILON)


def normalized(piece, gain):
    values = piece.astype(F32)
    return (values * rms_scale(values) * gain).astype(BF16)


def norm_back(values, scale, gain, grad_in):
    scaled = values * scale
    weighted = grad_in * gain
    back = scale * (weighted - scaled * jnp.mean(weighted * scaled, axis=-1, keepdims=True))
    return back, jnp.sum(grad_in * scaled, axis=0)


def body(
    links,
    tokens,
    gain_attn,
    w_query,
    w_key,
    w_value,
    w_out,
    gain_ff,
    w_gate,
    w_up,
    w_down,
    cotangent,
    segment_ids,
    parents,
):
    trees, _, own_rows, width = tokens.shape
    shard = links.shard
    q_width, kv_width = w_query.shape[0], w_key.shape[0]
    tree_rows = own_rows * shard
    links.start()
    share = gain_attn.shape[0]
    w_qkv = jnp.concatenate([w_query, w_key, w_value], axis=0)
    token_rows = [tokens[t, 0] for t in range(trees)]
    cot_rows = [cotangent[t, 0] for t in range(trees)]

    small = jnp.concatenate(
        [gain_attn, gain_ff] + [segment_ids[t, 0].astype(BF16) for t in range(trees)]
    )
    smalls, rows_0 = links.first(small, token_rows[0])
    gain_first = smalls[:, :share].reshape(width).astype(F32)
    gain_second = smalls[:, share : 2 * share].reshape(width).astype(F32)
    masks, tables = [], []
    for t in range(trees):
        begin = 2 * share + t * own_rows
        segments = smalls[:, begin : begin + own_rows].reshape(tree_rows).astype(jnp.int32)
        position, member, sees = tree_layout(segments, parents[t, 0])
        masks.append((member, sees))
        tables.append(rope_tables(position))

    def attention(t, qkv):
        return lambda comm: attention_forward(
            links.place, qkv, *tables[t], *masks[t], q_width, shard, comm
        )

    def after_attention(t, branch):
        value = token_rows[t].astype(F32) + RESIDUAL * branch
        scale = rms_scale(value)
        return value, scale, (value * scale * gain_second).astype(BF16)

    normed_0 = normalized(rows_0, gain_first)
    saved_0, (rows_1,), _, _ = links.carry(
        attention(0, dot_nt(normed_0, w_qkv)), gathers=[(token_rows[1], 1)]
    )
    part_0 = dot_nn(saved_0[0], w_out).astype(BF16)
    normed_1 = normalized(rows_1, gain_first)
    saved_1, _, (branch_0,), _ = links.carry(attention(1, dot_nt(normed_1, w_qkv)), sums=[(part_0, 1, 0)])
    part_1 = dot_nn(saved_1[0], w_out).astype(BF16)
    middle_0, scale_0, own_0 = after_attention(0, branch_0)
    _, _, (branch_1,), _ = links.carry(None, sums=[(part_1, 1, 0)])
    middle_1, scale_1, own_1 = after_attention(1, branch_1)
    own_all = jnp.concatenate([own_0, own_1], axis=0)
    _, (rows_all,), _, _ = links.carry(None, gathers=[(own_all, trees)])

    cot_own = jnp.concatenate([(RESIDUAL * cot.astype(F32)).astype(BF16) for cot in cot_rows], axis=0)
    (gate, upper, hidden), (cot_all,), _, _ = links.carry(
        lambda comm: feed_forward(rows_all, w_gate, w_up, 256, comm), gathers=[(cot_own, trees)]
    )
    grad_down = dot_tn(hidden, cot_all).astype(BF16)
    hidden_grad = dot_nt(cot_all, w_down)
    wide = gate.astype(F32)
    sigma = jax.nn.sigmoid(wide)
    gate_grad = (
        hidden_grad * upper.astype(F32) * sigma * (1.0 + wide * (1.0 - sigma))
    ).astype(BF16)
    up_grad = (hidden_grad * wide * sigma).astype(BF16)
    ff_part = (dot_nn(gate_grad, w_gate) + dot_nn(up_grad, w_up)).astype(BF16)
    parts = lambda whole: [(whole, trees, t) for t in range(trees)]
    (grad_gate, grad_up), _, ff_grad, (total_down,) = links.carry(
        lambda comm: products([(gate_grad, rows_all, True), (up_grad, rows_all, True)], 256, comm),
        sums=parts(ff_part),
        totals=[grad_down],
    )
    out_own, middle_grads = [], []
    gain_ff_sum = jnp.zeros((width,), F32)
    for t, (middle, scale) in enumerate(((middle_0, scale_0), (middle_1, scale_1))):
        middle_back, term = norm_back(middle, scale, gain_second, ff_grad[t])
        gain_ff_sum = gain_ff_sum + term
        middle_grads.append(cot_rows[t].astype(F32) + middle_back)
        out_own.append((RESIDUAL * middle_grads[t]).astype(BF16))
    (down_part,), (out_all,), _, (total_gate,) = links.carry(
        lambda comm: products([(hidden, w_down, False)], 256, comm),
        gathers=[(jnp.concatenate(out_own, axis=0), trees)],
        totals=[grad_gate],
    )
    arrays = []
    for t, (_, query, kv, lse) in enumerate((saved_0, saved_1)):
        attended_grad = dot_nt(out_all[t * tree_rows : (t + 1) * tree_rows], w_out).astype(BF16)
        arrays.append((attended_grad, query, kv, lse, *tables[t], *masks[t]))
    (qkv_grad,), _, downs, (total_up,) = links.carry(
        lambda comm: attention_backward(links.place, arrays, shard, comm),
        sums=parts(down_part),
        totals=[grad_up],
    )
    results = [
        (middle + RESIDUAL * down).astype(BF16) for middle, down in zip((middle_0, middle_1), downs)
    ]
    normed_part = dot_nn(links.natural(qkv_grad, trees), w_qkv).astype(BF16)
    normed_sums = sum_beside(normed_part, trees)
    (grad_attn,), _ = products(
        [
            ((saved_0[0], saved_1[0]), out_all, True),
            (qkv_grad, (normed_0, normed_1), True),
        ],
        128 if shard > 4 else 256,
        NoComm(),
        joined=True,
    )
    _, _, _, (total_attn,) = links.carry(None, totals=[grad_attn])
    normed_grads = [normed_sums[t].astype(F32) for t in range(trees)]
    input_grads = []
    gain_attn_sum = jnp.zeros((width,), F32)
    for t in range(trees):
        inputs = token_rows[t].astype(F32)
        input_back, term = norm_back(inputs, rms_scale(inputs), gain_first, normed_grads[t])
        gain_attn_sum = gain_attn_sum + term
        input_grads.append(middle_grads[t] + input_back)
    gains = links.sum_small(jnp.stack([gain_attn_sum, gain_ff_sum]))
    rows = lambda begin, count: total_attn[begin : begin + count].astype(F32)
    return (
        jnp.stack(results)[:, None],
        jnp.stack(input_grads)[:, None],
        gains[0],
        rows(q_width, q_width),
        rows(2 * q_width, kv_width),
        rows(2 * q_width + kv_width, kv_width),
        rows(0, q_width),
        gains[1],
        total_gate.astype(F32),
        total_up.astype(F32),
        total_down.astype(F32),
    )


def solution(mesh):
    shard, replica = mesh.shape["shard"], mesh.shape["replica"]
    links = (Square if (shard, replica) == (4, 8) else General)(shard, replica)
    in_specs = (
        P(None, "replica", "shard", None),
        P("shard"),
        P("shard", None),
        P("shard", None),
        P("shard", None),
        P("shard", None),
        P("shard"),
        P("shard", None),
        P("shard", None),
        P("shard", None),
        P(None, "replica", "shard", None),
        P(None, "replica", "shard"),
        P(None, "replica", None),
    )
    out_specs = (
        P(None, "replica", "shard", None),
        P(None, "replica", "shard", None),
        P("shard"),
        P("shard", None),
        P("shard", None),
        P("shard", None),
        P("shard", None),
        P("shard"),
        P("shard", None),
        P("shard", None),
        P("shard", None),
    )
    return jax.shard_map(
        functools.partial(body, links),
        mesh=mesh,
        in_specs=in_specs,
        out_specs=out_specs,
        check_vma=False,
    )
```

```python
import functools
import math

import jax
import jax.numpy as jnp
from jax import lax
from jax.experimental import pallas as pl
from jax.experimental.pallas import tpu as pltpu
from jax.sharding import PartitionSpec as P

HEADS = 32
KV_HEADS = 8
HEAD_DIM = 64
PAIR = 2 * HEAD_DIM
GROUP = HEADS // KV_HEADS

EPSILON = 1e-05
RESIDUAL = 0.22
ATTN_SCALE = 0.015625
ROPE_BASE = 10000000.0
NEGATIVE = -1e30
BF16 = jnp.bfloat16
F32 = jnp.float32


def dot_nt(left, right):
    return lax.dot_general(left, right, (((1,), (1,)), ((), ())), preferred_element_type=F32)


def dot_nn(left, right):
    return lax.dot_general(left, right, (((1,), (0,)), ((), ())), preferred_element_type=F32)


def dot_tn(left, right):
    return lax.dot_general(left, right, (((0,), (0,)), ((), ())), preferred_element_type=F32)


def tree_layout(segment_row, parent_row):
    seg_numbers = jnp.arange(parent_row.shape[0], dtype=jnp.int32)
    member = (segment_row[:, None] == seg_numbers[None, :]).astype(jnp.int32)
    lengths = jnp.sum(member, axis=0)
    earlier = seg_numbers[None, :] < seg_numbers[:, None]
    starts = jnp.sum(jnp.where(earlier, lengths[None, :], 0), axis=1)
    parent_hit = parent_row[:, None] == seg_numbers[None, :]
    grandparent = jnp.sum(jnp.where(parent_hit, parent_row[None, :], 0), axis=1)
    itself = seg_numbers[:, None] == seg_numbers[None, :]
    related = itself | parent_hit | (grandparent[:, None] == seg_numbers[None, :])
    before = jnp.sum(jnp.where(related & jnp.logical_not(itself), lengths[None, :], 0), axis=1)
    shift = jnp.sum(member * (before - starts)[None, :], axis=1)
    position = jnp.arange(segment_row.shape[0], dtype=jnp.int32) + shift
    pad = ((0, 0), (0, PAIR - parent_row.shape[0]))
    sees = dot_nn(member.astype(BF16), related.astype(BF16)).astype(BF16)
    return position, jnp.pad(member.astype(BF16), pad), jnp.pad(sees, pad)


def rope_tables(position):
    lane = jnp.arange(PAIR, dtype=jnp.int32) % HEAD_DIM
    half = HEAD_DIM // 2
    fraction = (lane % half).astype(F32) * (2.0 / HEAD_DIM)
    freq = jnp.exp(-math.log(ROPE_BASE) * fraction)
    angle = position.astype(F32)[:, None] * freq[None, :]
    return jnp.cos(angle), jnp.sin(angle) * jnp.where(lane < half, -1.0, 1.0)[None, :]


MESH = pl.DeviceIdType.MESH
CHUNK = 64
SLOTS = 4


def remote(source, target, sems, index, device):
    return pltpu.make_async_remote_copy(
        source, target, sems.at[0, index], sems.at[1, index], device_id=device, device_id_type=MESH
    )


class GatherJob:
    def __init__(self, own, trees):
        self.operand = own
        self.trees = trees
        self.rows, self.width = own.shape[0] // trees, own.shape[1]
        self.chunks = self.rows // CHUNK
        self.out_shape = jax.ShapeDtypeStruct((4 * own.shape[0], self.width), own.dtype)
        self.out_spec = pl.BlockSpec(memory_space=pl.ANY)

    def scratch(self):
        return [
            pltpu.SemaphoreType.DMA((2, 3 * self.chunks * self.trees)),
            pltpu.SemaphoreType.DMA((self.trees,)),
        ]

    def bind(self, operand, out, scratch, x, y):
        sems, local = scratch
        n, rows = self.chunks, self.rows
        self.local, self.to_x, self.to_y, self.on_x, self.on_y = [], [], [], [], []
        for t in range(self.trees):
            at = lambda block, j: out.at[pl.ds((4 * t + block) * rows + j * CHUNK, CHUNK), :]
            own = lambda j: operand.at[pl.ds(t * rows + j * CHUNK, CHUNK), :]
            sem = 3 * n * t
            self.local.append(
                pltpu.make_async_copy(
                    operand.at[pl.ds(t * rows, rows), :],
                    out.at[pl.ds(4 * t * rows, rows), :],
                    local.at[t],
                )
            )
            self.to_x.append([remote(own(j), at(1, j), sems, sem + j, x) for j in range(n)])
            self.to_y.append([remote(own(j), at(2, j), sems, sem + n + j, y) for j in range(n)])
            on = lambda block, j, to: remote(at(block, j), at(3, j), sems, sem + 2 * n + j, to)
            self.on_x.append([on(2, j, x) for j in range(n // 2)])
            self.on_y.append([on(1, j, y) for j in range(n // 2, n)])

    def begin(self):
        n = self.chunks
        half = n // 2
        for t in range(self.trees):
            for k in range(n):
                self.to_x[t][(k + half) % n].start()
                self.to_y[t][k].start()
            self.local[t].start()

    def stages(self):
        def stage(t, k):
            half = self.chunks // 2
            self.to_y[t][k].wait_recv()
            self.on_x[t][k].start()
            self.to_x[t][half + k].wait_recv()
            self.on_y[t][k].start()

        return [
            functools.partial(stage, t, k)
            for t in range(self.trees)
            for k in range(self.chunks // 2)
        ]

    def finish(self):
        half = self.chunks // 2
        for t in range(self.trees):
            for copy in self.to_x[t][:half] + self.to_y[t][half:] + self.on_x[t] + self.on_y[t]:
                copy.wait_recv()
            for copy in self.to_x[t] + self.to_y[t] + self.on_x[t] + self.on_y[t]:
                copy.wait_send()
            self.local[t].wait()


class SmallJob:
    def __init__(self, own):
        self.operand = own
        self.rows, self.width = own.shape
        self.out_shape = jax.ShapeDtypeStruct((4 * self.rows, self.width), own.dtype)
        self.out_spec = pl.BlockSpec(memory_space=pl.ANY)

    def scratch(self):
        return [pltpu.SemaphoreType.DMA((2, 3)), pltpu.SemaphoreType.DMA(())]

    def bind(self, operand, out, scratch, x, y):
        sems, local = scratch
        shard = lax.axis_index("shard")
        mine = out.at[pl.ds(pl.multiple_of(shard * self.rows, self.rows), self.rows), :]
        self.local = pltpu.make_async_copy(operand, mine, local)
        self.sends = [
            remote(operand, mine, sems, k, device)
            for k, device in enumerate((x, y, (3 - shard, x[1])))
        ]

    def begin(self):
        for send in self.sends:
            send.start()
        self.local.start()

    def stages(self):
        return []

    def finish(self):
        for send in self.sends:
            send.wait()
        self.local.wait()


class SumJob:
    def __init__(self, part, trees, tree):
        self.operand = part
        self.rows, self.width = part.shape[0] // 4 // trees, part.shape[1]
        self.base = 4 * self.rows * tree
        self.half = self.rows // 2
        self.chunks = self.half // CHUNK
        self.out_shape = jax.ShapeDtypeStruct((self.rows, self.width), F32)
        self.out_spec = pl.BlockSpec((self.rows, self.width), lambda *_: (0, 0))

    def scratch(self):
        return [
            pltpu.VMEM((4, self.half, self.width), BF16),
            pltpu.VMEM((6, self.half, self.width), BF16),
            pltpu.SemaphoreType.DMA((2, 6 * self.chunks)),
            pltpu.SemaphoreType.DMA((4,)),
        ]

    def bind(self, part, out, scratch, x, y):
        self.out = out
        self.mine, self.got, sems, local = scratch
        n, half = self.chunks, self.half
        rows = lambda block, second: pl.ds(self.base + block * self.rows + second * half, half)
        piece = lambda block, second, j: part.at[
            pl.ds(self.base + block * self.rows + second * half + j * CHUNK, CHUNK), :
        ]
        here = lambda ref, k, j: ref.at[k, pl.ds(j * CHUNK, CHUNK), :]
        self.loads = [
            pltpu.make_async_copy(part.at[rows(block, second), :], self.mine.at[k], local.at[k])
            for k, (block, second) in enumerate(((0, 0), (0, 1), (2, 0), (1, 1)))
        ]
        send = lambda k, source, device: [
            remote(source(j), here(self.got, k, j), sems, k * n + j, device) for j in range(n)
        ]
        self.sends = [
            send(0, lambda j: piece(1, 0, j), x),
            send(1, lambda j: piece(3, 0, j), x),
            send(2, lambda j: here(self.mine, 2, j), y),
            send(3, lambda j: piece(2, 1, j), y),
            send(4, lambda j: piece(3, 1, j), y),
            send(5, lambda j: here(self.mine, 3, j), x),
        ]

    def begin(self):
        for j in range(self.chunks):
            self.sends[1][j].start()
            self.sends[4][j].start()
        for load in self.loads:
            load.start()
        for j in range(self.chunks):
            self.sends[0][j].start()
            self.sends[3][j].start()

    def stages(self):
        def stage(j):
            if j == 0:
                for load in self.loads:
                    load.wait()
            rows = pl.ds(j * CHUNK, CHUNK)
            for first, second, own in ((1, 2, 2), (4, 5, 3)):
                self.sends[first][j].wait_recv()
                total = self.mine[own, rows, :].astype(F32) + self.got[first, rows, :].astype(F32)
                self.mine[own, rows, :] = total.astype(BF16)
                self.sends[second][j].start()

        return [functools.partial(stage, j) for j in range(self.chunks)]

    def finish(self):
        for j in range(self.chunks):
            rows = pl.ds(j * CHUNK, CHUNK)
            for own, one, two in ((0, 0, 2), (1, 3, 5)):
                self.sends[one][j].wait_recv()
                self.sends[two][j].wait_recv()
                self.out[pl.ds(own * self.half + j * CHUNK, CHUNK), :] = (
                    self.mine[own, rows, :].astype(F32)
                    + self.got[one, rows, :].astype(F32)
                    + self.got[two, rows, :].astype(F32)
                )
        for copies in self.sends:
            for copy in copies:
                copy.wait_send()


class LineJob:
    def __init__(self, grad, rows, lag):
        self.operand = grad
        self.LINE_ROWS, self.LAG = rows, lag
        self.half, self.width = grad.shape[0] // 2, grad.shape[1]
        self.chunks = self.half // self.LINE_ROWS
        self.steps = self.chunks + 1 + 3 * self.LAG
        self.out_shape = jax.ShapeDtypeStruct(grad.shape, BF16)
        self.out_spec = pl.BlockSpec(memory_space=pl.ANY)

    def scratch(self):
        place = lambda: pltpu.VMEM((self.half, self.width), BF16)
        return [place(), place(), place(), place(), pltpu.SemaphoreType.DMA((9, self.chunks))]

    def bind(self, grad, out, scratch, x, y):
        self.grad, self.out = grad, out
        self.from_core, self.own, self.from_line, self.from_inner, self.sems = scratch
        shard, place = lax.axis_index("shard"), lax.axis_index("replica")
        self.core, z = place % 2, place // 2
        self.inner = (z == 1) | (z == 2)
        self.outer = (z == 0) | (z == 3)
        self.twin = (shard, z * 2 + 1 - self.core)
        self.pair = (shard, (z + 1 - 2 * (z % 2)) * 2 + self.core)
        self.across = (shard, (3 - z) * 2 + self.core)

    def chunk(self, c):
        return pl.ds(pl.multiple_of(c * self.LINE_ROWS, self.LINE_ROWS), self.LINE_ROWS)

    def at(self, core, c):
        return pl.ds(
            pl.multiple_of(core * self.half + c * self.LINE_ROWS, self.LINE_ROWS), self.LINE_ROWS
        )

    def send(self, source, target, index, arrival, device, c):
        return pltpu.make_async_remote_copy(
            source,
            target,
            self.sems.at[index, c],
            self.sems.at[arrival, c],
            device_id=device,
            device_id_type=MESH,
        )

    def to_twin(self, c):
        source = self.grad.at[self.at(1 - self.core, c), :]
        return self.send(source, self.from_core.at[self.chunk(c), :], 0, 1, self.twin, c)

    def load(self, c):
        source = self.grad.at[self.at(self.core, c), :]
        return pltpu.make_async_copy(source, self.own.at[self.chunk(c), :], self.sems.at[2, c])

    def inward(self, c):
        rows = self.chunk(c)
        return self.send(self.own.at[rows, :], self.from_line.at[rows, :], 3, 4, self.pair, c)

    def between(self, c):
        rows = self.chunk(c)
        return self.send(self.own.at[rows, :], self.from_inner.at[rows, :], 3, 5, self.across, c)

    def outward(self, c):
        rows = self.chunk(c)
        return self.send(self.from_core.at[rows, :], self.from_line.at[rows, :], 6, 4, self.pair, c)

    def store(self, source, c):
        target = self.out.at[self.at(self.core, c), :]
        return pltpu.make_async_copy(source.at[self.chunk(c), :], target, self.sems.at[2, c])

    def give(self, source, c):
        target = self.out.at[self.at(self.core, c), :]
        return self.send(source.at[self.chunk(c), :], target, 7, 8, self.twin, c)

    def begin(self):
        pass

    def stages(self):
        return []

    def step(self, s):
        n, lag = self.chunks, self.LAG
        live = lambda begin: (s >= begin) & (s < n + begin)
        add = lambda a, b: (a.astype(F32) + b.astype(F32)).astype(BF16)

        @pl.when(live(0))
        def _():
            self.to_twin(s).start()
            self.load(s).start()

        @pl.when(live(1))
        def _():
            c = s - 1
            rows = self.chunk(c)
            self.to_twin(c).wait()
            self.load(c).wait()
            self.own[rows, :] = add(self.own[rows, :], self.from_core[rows, :])
            pl.when(self.outer)(lambda: self.inward(c).start())

        @pl.when(live(1 + lag) & self.inner)
        def _():
            c = s - 1 - lag
            rows = self.chunk(c)
            self.inward(c).wait_recv()
            self.own[rows, :] = add(self.own[rows, :], self.from_line[rows, :])
            self.between(c).start()

        @pl.when(live(1 + 2 * lag) & self.inner)
        def _():
            c = s - 1 - 2 * lag
            rows = self.chunk(c)
            self.between(c).wait_recv()
            self.from_core[rows, :] = add(self.own[rows, :], self.from_inner[rows, :])
            self.outward(c).start()
            self.store(self.from_core, c).start()
            self.give(self.from_core, c).start()

        @pl.when(live(1 + 3 * lag) & self.outer)
        def _():
            c = s - 1 - 3 * lag
            self.outward(c).wait_recv()
            self.store(self.from_line, c).start()
            self.give(self.from_line, c).start()

    def finish(self):
        def body(c, carry):
            self.store(self.from_line, c).wait()
            self.give(self.from_line, c).wait()

            @pl.when(self.inner)
            def _():
                self.between(c).wait_send()
                self.outward(c).wait_send()

            pl.when(self.outer)(lambda: self.inward(c).wait_send())
            return carry

        lax.fori_loop(0, self.chunks, body, 0)


class Comm:
    def __init__(self, jobs, number):
        self.jobs, self.number = jobs, number
        self.operands = [job.operand for job in jobs]
        self.in_specs = [pl.BlockSpec(memory_space=pl.ANY) for _ in jobs]
        self.out_specs = [job.out_spec for job in jobs]
        self.out_shapes = [job.out_shape for job in jobs]
        self.scratch = [entry for job in jobs for entry in job.scratch()]

    def enter(self, operands, outs, scratch, now):
        shard, replica = lax.axis_index("shard"), lax.axis_index("replica")
        x = (shard + 1 - 2 * (shard % 2), replica)
        y = ((shard + 2) % 4, replica)
        scratch = list(scratch)
        for job, operand, out in zip(self.jobs, operands, outs):
            count = len(job.scratch())
            job.bind(operand, out, scratch[:count], x, y)
            scratch = scratch[count:]

        lines = [job for job in self.jobs if isinstance(job, LineJob)]
        square = len(lines) < len(self.jobs)

        @pl.when(now)
        def _():
            barrier = pltpu.get_barrier_semaphore()

            def greet(device):
                pl.semaphore_signal(barrier, inc=1, device_id=device, device_id_type=MESH)

            near = ([x, y] if square else []) + ([lines[0].twin, lines[0].pair] if lines else [])
            if any(isinstance(job, SmallJob) for job in self.jobs):
                near.append((3 - shard, replica))
            for device in near:
                greet(device)
            if lines:

                @pl.when(lines[0].inner)
                def _():
                    greet(lines[0].across)
                    pl.semaphore_wait(barrier, len(near) + 1)

                @pl.when(lines[0].outer)
                def _():
                    pl.semaphore_wait(barrier, len(near))

            else:
                pl.semaphore_wait(barrier, len(near))
            for job in self.jobs:
                job.begin()

    def stages(self):
        return [stage for job in self.jobs for stage in job.stages()]

    def advance(self, slot, slots):
        stages = self.stages()
        for job in self.jobs:
            if isinstance(job, LineJob):

                def body(k, carry, job=job):
                    job.step(k)
                    return carry

                lax.fori_loop(slot * job.steps // slots, (slot + 1) * job.steps // slots, body, 0)
        for index, stage in enumerate(stages):
            if slots <= 4:
                due = min(slots - 1, slots // 2 + index * (slots - slots // 2) // len(stages))
            else:
                due = min(slots - 1, max(1, int(slots * (0.25 + 0.5 * index / len(stages)))))
            pl.when(slot == due)(stage)

    def finish(self, now):
        @pl.when(now)
        def _():
            for job in self.jobs:
                job.finish()


class NoComm:
    operands = in_specs = out_specs = out_shapes = scratch = ()
    number = None

    def enter(self, *_):
        pass

    def advance(self, *_):
        pass

    def finish(self, *_):
        pass


def comm_params(comm, vmem):
    if comm.number is None:
        return pltpu.CompilerParams(vmem_limit_bytes=vmem << 20)
    return pltpu.CompilerParams(
        vmem_limit_bytes=vmem << 20, collective_id=comm.number, has_side_effects=True
    )


def split_refs(refs, *counts):
    parts, begin = [], 0
    for count in counts:
        parts.append(refs[begin : begin + count])
        begin += count
    return parts


def transfer(comm):
    count = len(comm.operands)
    steps = max([1] + [job.steps for job in comm.jobs if isinstance(job, LineJob)])

    def kernel(*refs):
        operands, outs, scratch = split_refs(refs, count, count, len(comm.scratch))
        step = pl.program_id(0)
        comm.enter(operands, outs, scratch, step == 0)
        if steps == 1:
            for stage in comm.stages():
                stage()
        else:
            comm.advance(step, steps)
        comm.finish(step == steps - 1)

    return pl.pallas_call(
        kernel,
        grid=(steps,),
        in_specs=comm.in_specs,
        out_specs=comm.out_specs,
        out_shape=comm.out_shapes,
        scratch_shapes=comm.scratch,
        compiler_params=comm_params(comm, 48),
        name="transfer",
    )(*comm.operands)


def products(items, block, comm, joined=False):
    specs, shapes, out_specs, steps, rights = [], [], [], [], []
    begin = 0
    items = [
        (l if isinstance(l, tuple) else (l,), r if isinstance(r, tuple) else (r,), t)
        for l, r, t in items
    ]
    total = sum((l[0].shape[1] if t else l[0].shape[0]) // block for l, _, t in items)
    for left, right, transposed in items:
        size = left[0].shape[1] if transposed else left[0].shape[0]
        count = size // block

        def place(i, begin=begin, count=count):
            return jnp.clip(i - begin, 0, count - 1)

        for l in left:
            if transposed:
                specs.append(pl.BlockSpec((l.shape[0], block), lambda i, p=place: (0, p(i))))
            else:
                specs.append(pl.BlockSpec((block, l.shape[1]), lambda i, p=place: (p(i), 0)))
        columns = right[0].shape[1]
        if not joined:
            out_specs.append(pl.BlockSpec((block, columns), lambda i, p=place: (p(i), 0)))
            shapes.append(jax.ShapeDtypeStruct((size, columns), BF16))
        for r in right:
            if not any(r is other for other in rights):
                rights.append(r)
        steps.append((begin, count))
        begin += count
    right_specs = [
        pl.BlockSpec(r.shape, lambda i: (0, 0), pipeline_mode=pl.Buffered(1)) for r in rights
    ]
    which = [
        [next(k for k, other in enumerate(rights) if other is r) for r in right]
        for _, right, _ in items
    ]
    firsts = [sum(len(l) for l, _, _ in items[:k]) for k in range(len(items))]
    n = sum(len(l) for l, _, _ in items)
    if joined:
        width = items[0][1][0].shape[1]
        out_specs = [pl.BlockSpec((block, width), lambda i: (i, 0))]
        shapes = [jax.ShapeDtypeStruct((total * block, width), BF16)]
    made = len(shapes)

    def kernel(*refs):
        lefts, held, operands, outs, comm_outs, scratch = split_refs(
            refs, n, len(rights), len(comm.operands), made, len(comm.operands), len(comm.scratch)
        )
        step = pl.program_id(0)
        comm.enter(operands, comm_outs, scratch, step == 0)
        width = items[0][1][0].shape[1] // SLOTS

        def part(slot, carry):
            comm.advance(step * SLOTS + slot, total * SLOTS)
            columns = pl.ds(pl.multiple_of(slot * width, width), width)
            for k, (left, right, transposed) in enumerate(items):
                begin, count = steps[k]

                @pl.when((step >= begin) & (step < begin + count))
                def _(k=k, left=left, right=right, transposed=transposed):
                    dot = dot_tn if transposed else dot_nn
                    result, pieces = 0.0, max(len(left), len(right))
                    for piece in range(pieces):
                        l, r = lefts[firsts[k] + piece % len(left)], held[which[k][piece % len(right)]]
                        share = pl.ds(piece * (r.shape[0] // pieces), r.shape[0] // pieces)
                        ours = pl.ds(piece * (l.shape[0] // pieces), l.shape[0] // pieces)
                        result += dot(
                            l[ours, :] if len(left) < pieces else l[...],
                            r[share, columns] if len(right) < pieces else r[:, columns],
                        )
                    outs[0 if joined else k][:, columns] = result.astype(BF16)

            return carry

        lax.fori_loop(0, SLOTS, part, 0)

        comm.finish(step == total - 1)

    flops = 2 * sum(math.prod(l.shape) * right[0].shape[1] for left, right, _ in items for l in left)
    out = pl.pallas_call(
        kernel,
        grid=(total,),
        in_specs=specs + right_specs + list(comm.in_specs),
        out_specs=out_specs + list(comm.out_specs),
        out_shape=shapes + list(comm.out_shapes),
        scratch_shapes=list(comm.scratch),
        compiler_params=comm_params(comm, 58),
        cost_estimate=pl.CostEstimate(flops=flops, bytes_accessed=30_000_000, transcendentals=0),
        name="products",
    )(*[l for left, _, _ in items for l in left], *rights, *comm.operands)
    return out[:made], out[made:]


def feed_forward(rows_all, w_gate, w_up, block, comm):
    rows, width = rows_all.shape
    units = w_gate.shape[0]
    steps = units // block
    part = rows // SLOTS

    def kernel(*refs):
        inputs, operands, outs, comm_outs, scratch = split_refs(
            refs, 3, len(comm.operands), 3, len(comm.operands), len(comm.scratch)
        )
        x_ref, gate_w, up_w = inputs
        gate_ref, upper_ref, hidden_ref = outs
        step = pl.program_id(0)
        comm.enter(operands, comm_outs, scratch, step == 0)
        comm.advance(step, steps)
        for slot in range(SLOTS):
            here = pl.ds(slot * part, part)
            gate = dot_nt(x_ref[here, :], gate_w[...])
            upper = dot_nt(x_ref[here, :], up_w[...])
            gate_ref[here, :] = gate.astype(BF16)
            upper_ref[here, :] = upper.astype(BF16)
            hidden_ref[here, :] = (gate * jax.nn.sigmoid(gate) * upper).astype(BF16)
        comm.finish(step == steps - 1)

    out = pl.pallas_call(
        kernel,
        grid=(steps,),
        in_specs=[
            pl.BlockSpec((rows, width), lambda i: (0, 0), pipeline_mode=pl.Buffered(1)),
            pl.BlockSpec((block, width), lambda i: (i, 0)),
            pl.BlockSpec((block, width), lambda i: (i, 0)),
            *comm.in_specs,
        ],
        out_specs=[pl.BlockSpec((rows, block), lambda i: (0, i))] * 3 + list(comm.out_specs),
        out_shape=[jax.ShapeDtypeStruct((rows, units), BF16)] * 3 + list(comm.out_shapes),
        scratch_shapes=list(comm.scratch),
        compiler_params=comm_params(comm, 56),
        cost_estimate=pl.CostEstimate(
            flops=4 * rows * width * units, bytes_accessed=48_000_000, transcendentals=rows * units
        ),
        name="feed_forward",
    )(rows_all, w_gate, w_up, *comm.operands)
    return out[:3], out[3:]


def swap_halves(block):
    lane = lax.broadcasted_iota(jnp.int32, block.shape, 1)
    half = HEAD_DIM // 2
    up = pltpu.roll(block, PAIR - half, 1)
    down = pltpu.roll(block, half, 1)
    return jnp.where(lane % HEAD_DIM < half, up, down)


def turn(block, cosine, sine):
    return block * cosine + swap_halves(block) * sine


def place_heads(wide, kv_heads, fill):
    placed = []
    for g in range(kv_heads):
        base = wide[:, (g // 2) * PAIR : (g // 2) * PAIR + PAIR] if wide.shape[1] >= PAIR else wide
        lane = lax.broadcasted_iota(jnp.int32, base.shape, 1)
        moved = pltpu.roll(base, HEAD_DIM, 1)
        for p in range(2):
            source = base if g % 2 == p else moved
            inside = (lane // HEAD_DIM) == p
            placed.append(jnp.where(inside, source, jnp.full_like(source, fill)))
    return placed


def attention_forward_kernel(kv_heads, blocks, place, comm, *refs):
    jobs = len(comm.operands)
    inputs, operands, outs, comm_outs, own, scratch = split_refs(
        refs, 6, jobs, 4, jobs, 3, len(comm.scratch)
    )
    q_ref, kv_ref, cos_ref, sin_ref, member_ref, sees_ref = inputs
    out_ref, q_out_ref, kv_out_ref, lse_ref = outs
    keys, values, bias = own
    step = pl.program_id(0)
    comm.enter(operands, comm_outs, scratch, step == 0)
    comm.advance(step, blocks)
    tree = q_ref.shape[0]
    rows = tree // blocks
    kv_width = kv_heads * HEAD_DIM

    @pl.when(step == 0)
    def _():
        for b in range(blocks):
            here = pl.ds(b * rows, rows)
            raw = kv_ref[pl.ds(pl.multiple_of(place(b) * rows, rows), rows), :]
            cosine, sine = cos_ref[here, :], sin_ref[here, :]
            if kv_width >= PAIR:
                turned = jnp.concatenate(
                    [
                        turn(raw[:, c : c + PAIR], cosine, sine)
                        for c in range(0, kv_width, PAIR)
                    ],
                    axis=1,
                )
                plain = raw[:, kv_width:]
            else:
                lane = lax.broadcasted_iota(jnp.int32, raw.shape, 1)
                turned = turn(raw, cosine, sine)
                plain = pltpu.roll(raw, HEAD_DIM, 1)
                both = jnp.where(lane < HEAD_DIM, turned, raw)
            if kv_width >= PAIR:
                both = jnp.concatenate([turned, plain], axis=1)
            kv_out_ref[here, :] = both.astype(BF16)
            for index, placed in enumerate(place_heads(turned, kv_heads, 0.0)):
                keys[index, here, :] = placed.astype(BF16)
            for index, placed in enumerate(place_heads(plain, kv_heads, 1.0)):
                values[index, here, :] = placed.astype(BF16)

    here = pl.ds(pl.multiple_of(step * rows, rows), rows)
    there = pl.ds(pl.multiple_of(place(step) * rows, rows), rows)
    cosine, sine = cos_ref[here, :], sin_ref[here, :]
    for j in range(q_ref.shape[1] // PAIR):
        lanes = slice(j * PAIR, j * PAIR + PAIR)
        turned = turn(q_ref[there, lanes], cosine, sine).astype(BF16)
        q_out_ref[:, lanes] = turned * BF16(ATTN_SCALE)

    link = dot_nt(sees_ref[here, :], member_ref[...])
    row_index = lax.broadcasted_iota(jnp.int32, (rows, tree), 0) + step * rows
    col_index = lax.broadcasted_iota(jnp.int32, (rows, tree), 1)
    bias[...] = jnp.where((link > 0.5) & (col_index <= row_index), 0.0, NEGATIVE)

    lane = lax.broadcasted_iota(jnp.int32, (rows, PAIR), 1)
    for block in range(blocks):
        width = (block + 1) * rows

        @pl.when(step == block)
        def _(width=width):
            lse = jnp.zeros((rows, PAIR), F32)
            for j in range(q_ref.shape[1] // PAIR):
                lanes = slice(j * PAIR, j * PAIR + PAIR)
                group = 2 * j // GROUP
                mixed, tops = [], []
                for p in range(2):
                    scores = dot_nt(q_out_ref[:, lanes], keys[group * 2 + p, :width, :])
                    scores = scores + bias[:, :width]
                    top = jnp.max(scores, axis=1, keepdims=True)
                    expo = jnp.exp(scores - top).astype(BF16)
                    mixed.append(dot_nn(expo, values[group * 2 + p, :width, :]))
                    tops.append(top)
                upper = lane >= HEAD_DIM
                total = pltpu.roll(jnp.where(upper, mixed[0], mixed[1]), HEAD_DIM, 1)
                out_ref[there, lanes] = (jnp.where(upper, mixed[1], mixed[0]) / total).astype(BF16)
                logs = jnp.log(total)
                lse = jnp.where(lane == 2 * j, tops[0] + logs[:, :1], lse)
                lse = jnp.where(lane == 2 * j + 1, tops[1] + logs[:, HEAD_DIM : HEAD_DIM + 1], lse)
            lse_ref[...] = lse

    comm.finish(step == blocks - 1)


def attention_forward(place, qkv, cosine, sine, member, sees, q_width, blocks, comm):
    tree = qkv.shape[0]
    rows = tree // blocks
    kv_width = (qkv.shape[1] - q_width) // 2
    kv_heads = kv_width // HEAD_DIM
    whole = lambda width: pl.BlockSpec((tree, width), lambda i: (0, 0))
    natural = lambda width: pl.BlockSpec((rows, width), lambda i: (i, 0))
    out = pl.pallas_call(
        functools.partial(attention_forward_kernel, kv_heads, blocks, place, comm),
        grid_spec=pl.GridSpec(
            grid=(blocks,),
            in_specs=[
                whole(q_width),
                pl.BlockSpec((tree, 2 * kv_width), lambda i: (0, q_width // (2 * kv_width))),
                whole(PAIR),
                whole(PAIR),
                whole(PAIR),
                whole(PAIR),
                *comm.in_specs,
            ],
            out_specs=[
                whole(q_width),
                natural(q_width),
                whole(2 * kv_width),
                natural(PAIR),
                *comm.out_specs,
            ],
            scratch_shapes=[
                pltpu.VMEM((2 * kv_heads, tree, PAIR), BF16),
                pltpu.VMEM((2 * kv_heads, tree, PAIR), BF16),
                pltpu.VMEM((rows, tree), F32),
                *comm.scratch,
            ],
        ),
        out_shape=[
            jax.ShapeDtypeStruct((tree, q_width), BF16),
            jax.ShapeDtypeStruct((tree, q_width), BF16),
            jax.ShapeDtypeStruct((tree, 2 * kv_width), BF16),
            jax.ShapeDtypeStruct((tree, PAIR), F32),
            *comm.out_shapes,
        ],
        compiler_params=comm_params(comm, 40),
        cost_estimate=pl.CostEstimate(
            flops=10_000_000_000, bytes_accessed=12_000_000, transcendentals=5_000_000
        ),
        name="attention_forward",
    )(qkv, qkv, cosine, sine, member, sees, *comm.operands)
    return out[:4], out[4:]


def attention_backward_kernel(kv_heads, blocks, trees, place, comm, *refs):
    jobs = len(comm.operands)
    inputs, operands, outs, comm_outs, own, scratch = split_refs(
        refs, 8 * trees, jobs, 1, jobs, 6, len(comm.scratch)
    )
    pairs = inputs[1].shape[1] // PAIR
    each = blocks * pairs
    step = pl.program_id(0)
    comm.enter(operands, comm_outs, scratch, step == 0)
    comm.advance(step, each * trees)
    for t in range(trees):

        @pl.when((step >= t * each) & (step < (t + 1) * each))
        def _(t=t):
            local = step - t * each
            attention_backward_step(
                kv_heads,
                blocks,
                pairs,
                place,
                local // pairs,
                local % pairs,
                t,
                inputs[8 * t : 8 * t + 8],
                outs[0],
                own,
            )

    comm.finish(step == each * trees - 1)


def attention_backward_step(kv_heads, blocks, pairs, place, step, j, t, inputs, out_ref, own):
    grad_ref, q_ref, kv_ref, lse_ref, cos_ref, sin_ref, member_ref, sees_ref = inputs
    keys, values, bias, lse_rows, key_sum, value_sum = own
    tree, rows = grad_ref.shape[0], q_ref.shape[0]
    kv_width = kv_heads * HEAD_DIM
    q_width = q_ref.shape[1]
    base = t * tree

    @pl.when((step == 0) & (j == 0))
    def _():
        for b in range(blocks):
            here = pl.ds(b * rows, rows)
            both = kv_ref[here, :].astype(F32)
            if kv_width >= PAIR:
                turned, plain = both[:, :kv_width], both[:, kv_width:]
            else:
                turned, plain = both, pltpu.roll(both, HEAD_DIM, 1)
            for index, placed in enumerate(place_heads(turned, kv_heads, 0.0)):
                keys[index, here, :] = placed.astype(BF16)
            for index, placed in enumerate(place_heads(plain, kv_heads, 0.0)):
                values[index, here, :] = placed.astype(BF16)
        key_sum[...] = jnp.zeros_like(key_sum)
        value_sum[...] = jnp.zeros_like(value_sum)

    here = pl.ds(pl.multiple_of(step * rows, rows), rows)

    @pl.when(j == 0)
    def _():
        link = dot_nt(member_ref[...], sees_ref[here, :])
        key_index = lax.broadcasted_iota(jnp.int32, (tree, rows), 0)
        query_index = lax.broadcasted_iota(jnp.int32, (tree, rows), 1) + step * rows
        bias[...] = jnp.where((link > 0.5) & (key_index <= query_index), 0.0, NEGATIVE)
        lse_rows[...] = jnp.transpose(lse_ref[...])

    there = pl.ds(pl.multiple_of(place(step) * rows, rows), rows)
    out_rows = pl.ds(pl.multiple_of(base + place(step) * rows, rows), rows)
    lanes = pl.ds(pl.multiple_of(j * PAIR, PAIR), PAIR)
    group = 2 * j // GROUP
    for block in range(blocks):
        width = (block + 1) * rows

        @pl.when(step == block)
        def _(width=width):
            cosine, sine = cos_ref[here, :], sin_ref[here, :]
            query, grad = q_ref[:, lanes], grad_ref[there, lanes]
            dq = jnp.zeros((rows, PAIR), F32)
            for p in range(2):
                index = group * 2 + p
                scores = dot_nt(keys[index, :width, :], query) + bias[:width, :]
                probs = jnp.exp(scores - lse_rows[pl.ds(2 * j + p, 1), :])
                probs_grad = dot_nt(values[index, :width, :], grad)
                value_sum[index, :width, :] += dot_nn(probs.astype(BF16), grad)
                weighted = probs * probs_grad
                delta = jnp.sum(weighted, axis=0, keepdims=True)
                score_grad = (weighted - probs * delta).astype(BF16)
                key_sum[index, :width, :] += dot_nn(score_grad, query)
                dq = dq + dot_tn(score_grad, keys[index, :width, :])
            out_ref[out_rows, lanes] = turn(dq * ATTN_SCALE, cosine, -sine).astype(BF16)

    @pl.when((step == blocks - 1) & (j == pairs - 1))
    def _():
        for b in range(blocks):
            here = pl.ds(b * rows, rows)
            there = pl.ds(pl.multiple_of(base + place(b) * rows, rows), rows)
            cosine, sine = cos_ref[here, :], sin_ref[here, :]
            lane = lax.broadcasted_iota(jnp.int32, (rows, PAIR), 1)
            lower = lane < HEAD_DIM
            for c in range(0, kv_heads, 2):
                halves = []
                for acc in (key_sum, value_sum):
                    own, other = [], []
                    for g in range(c, min(c + 2, kv_heads)):
                        own.append(acc[g * 2, here, :])
                        other.append(acc[g * 2 + 1, here, :])
                    first = own[0] + pltpu.roll(other[0], HEAD_DIM, 1)
                    if len(own) == 2:
                        second = other[1] + pltpu.roll(own[1], HEAD_DIM, 1)
                    else:
                        second = first
                    halves.append(jnp.where(lower, first, second))
                turned = turn(halves[0], cosine, -sine)
                if kv_width >= PAIR:
                    begin = q_width + c * HEAD_DIM
                    out_ref[there, begin : begin + PAIR] = turned.astype(BF16)
                    begin += kv_width
                    out_ref[there, begin : begin + PAIR] = halves[1].astype(BF16)
                else:
                    moved = pltpu.roll(halves[1], HEAD_DIM, 1)
                    both = jnp.where(lower, turned, moved)
                    out_ref[there, q_width : q_width + PAIR] = both.astype(BF16)


def attention_backward(place, arrays, blocks, comm):
    trees = len(arrays)
    tree, q_width = arrays[0][1].shape
    rows = tree // blocks
    kv_width = arrays[0][2].shape[1] // 2
    kv_heads = kv_width // HEAD_DIM
    each = blocks * (q_width // PAIR)
    whole = lambda width: pl.BlockSpec((tree, width), lambda i: (0, 0))

    def natural(width, t):
        return pl.BlockSpec(
            (rows, width),
            lambda i: (jnp.clip((i - t * each) // (q_width // PAIR), 0, blocks - 1), 0),
        )

    in_specs = []
    for t in range(trees):
        in_specs += [whole(q_width), natural(q_width, t), whole(2 * kv_width), natural(PAIR, t)]
        in_specs += [whole(PAIR)] * 4
    total = q_width + 2 * kv_width
    out = pl.pallas_call(
        functools.partial(attention_backward_kernel, kv_heads, blocks, trees, place, comm),
        grid=(each * trees,),
        in_specs=in_specs + list(comm.in_specs),
        out_specs=[pl.BlockSpec((trees * tree, total), lambda i: (0, 0))] + list(comm.out_specs),
        out_shape=[jax.ShapeDtypeStruct((trees * tree, total), BF16)] + list(comm.out_shapes),
        scratch_shapes=[
            pltpu.VMEM((2 * kv_heads, tree, PAIR), BF16),
            pltpu.VMEM((2 * kv_heads, tree, PAIR), BF16),
            pltpu.VMEM((tree, rows), F32),
            pltpu.VMEM((PAIR, rows), F32),
            pltpu.VMEM((2 * kv_heads, tree, PAIR), F32),
            pltpu.VMEM((2 * kv_heads, tree, PAIR), F32),
            *comm.scratch,
        ],
        compiler_params=comm_params(comm, 60),
        cost_estimate=pl.CostEstimate(
            flops=40_000_000_000, bytes_accessed=24_000_000, transcendentals=10_000_000
        ),
        name="attention_backward",
    )(*[array for per_tree in arrays for array in per_tree], *comm.operands)
    return out[:1], out[1:]


def sync(*values):
    return lax.optimization_barrier(values)


def sum_beside(part, trees):
    return lax.psum_scatter(
        part.reshape(trees, -1, part.shape[1]), "shard", scatter_dimension=1, tiled=True
    )


class Square:
    def __init__(self, shard, replica):
        self.shard, self.replica = shard, replica
        self.x = [(i, i ^ 1) for i in range(shard)]
        self.y = [(i, i ^ 2) for i in range(shard)]
        self.d = [(i, i ^ 3) for i in range(shard)]

    def natural(self, rows, trees):
        blocks = rows.reshape(trees, self.shard, -1, rows.shape[1])
        return self.reorder(blocks, 1).reshape(rows.shape)

    def place(self, block):
        shard = lax.axis_index("shard")
        return (block + shard) % 2 + 2 * ((block // 2 + shard // 2) % 2)

    def reorder(self, blocks, axis):
        me = lax.axis_index("shard")
        return jnp.concatenate(
            [lax.dynamic_slice_in_dim(blocks, n ^ me, 1, axis) for n in range(self.shard)], axis=axis
        )

    def first(self, small, own):
        padded = jnp.pad(small, (0, -small.shape[0] % 2048)).reshape(16, -1)
        self.kernels += 1
        smalls, rows = transfer(Comm([SmallJob(padded), GatherJob(own, 1)], self.kernels))
        return smalls.reshape(self.shard, -1)[:, : small.shape[0]], rows

    def sum_small(self, values, beside):
        share = values.shape[1] // self.shard
        blocks = values.reshape(values.shape[0], self.shard, share)
        blocks = self.reorder(blocks, 1)
        hops = [[("shard", perm) for perm in (self.x, self.y, self.d)]]
        hops += [[("replica", [(i, i ^ k) for i in range(self.replica)])] for k in (1, 2, 4)]
        total, done = blocks[:, 0], []
        for number, hop in enumerate(hops):
            got = [
                lax.ppermute(blocks[:, k + 1] if number == 0 else total, axis, perm)
                for k, (axis, perm) in enumerate(hop)
            ]
            if number < len(beside):
                done.append(beside[number](total))
                got, done[-1] = sync(got, done[-1])
            total = total + sum(got)
        return total, done + [f(total) for f in beside[len(hops) :]]

    def carry(self, compute, gathers=(), sums=(), totals=()):
        jobs = [GatherJob(*own) for own in gathers] + [SumJob(*part) for part in sums]
        jobs += [LineJob(grad, *((32, 2) if compute is None else (64, 1))) for grad in totals]
        self.kernels += 1
        comm = Comm(jobs, self.kernels)
        if compute is None:
            results, moved = None, transfer(comm)
        else:
            results, moved = compute(comm)
        return (results, *map(list, split_refs(moved, len(gathers), len(sums), len(totals))))

    def start(self):
        self.kernels = 0


class General:
    def __init__(self, shard, replica):
        self.shard, self.replica = shard, replica

    def place(self, block):
        return block

    def natural(self, rows, trees):
        return rows

    def first(self, small, own):
        rows = lax.all_gather(own, "shard", axis=0, tiled=True)
        return lax.all_gather(small, "shard", axis=0, tiled=False), rows

    def carry(self, compute, gathers=(), sums=(), totals=()):
        results = None if compute is None else compute(NoComm())[0]
        rows = lambda array, trees: array.reshape(trees, -1, array.shape[1])
        gathered = [
            lax.all_gather(rows(own, trees), "shard", axis=1, tiled=True).reshape(-1, own.shape[1])
            for own, trees in gathers
        ]
        summed = [
            lax.psum_scatter(
                rows(part, trees)[tree], "shard", scatter_dimension=0, tiled=True
            ).astype(F32)
            for part, trees, tree in sums
        ]
        return results, gathered, summed, [lax.psum(grad, "replica") for grad in totals]

    def sum_small(self, values, beside):
        share = lax.psum_scatter(values, "shard", scatter_dimension=1, tiled=True)
        return lax.psum(share, "replica"), [f(share) for f in beside]

    def start(self):
        pass


def rms_scale(values):
    return lax.rsqrt(jnp.mean(values * values, axis=-1, keepdims=True) + EPSILON)


def normalized(piece, gain):
    values = piece.astype(F32)
    return (values * rms_scale(values) * gain).astype(BF16)


def norm_back(values, scale, gain, grad_in):
    scaled = values * scale
    weighted = grad_in * gain
    back = scale * (weighted - scaled * jnp.mean(weighted * scaled, axis=-1, keepdims=True))
    return back, jnp.sum(grad_in * scaled, axis=0)


def body(
    links,
    tokens,
    gain_attn,
    w_query,
    w_key,
    w_value,
    w_out,
    gain_ff,
    w_gate,
    w_up,
    w_down,
    cotangent,
    segment_ids,
    parents,
):
    trees, _, own_rows, width = tokens.shape
    shard = links.shard
    q_width, kv_width = w_query.shape[0], w_key.shape[0]
    tree_rows = own_rows * shard
    links.start()
    share = gain_attn.shape[0]
    w_qkv = jnp.concatenate([w_query, w_key, w_value], axis=0)
    token_rows = [tokens[t, 0] for t in range(trees)]
    cot_rows = [cotangent[t, 0] for t in range(trees)]

    small = jnp.concatenate(
        [gain_attn, gain_ff] + [segment_ids[t, 0].astype(BF16) for t in range(trees)]
    )
    smalls, rows_0 = links.first(small, token_rows[0])
    gain_first = smalls[:, :share].reshape(width).astype(F32)
    gain_second = smalls[:, share : 2 * share].reshape(width).astype(F32)
    masks, tables = [], []
    for t in range(trees):
        begin = 2 * share + t * own_rows
        segments = smalls[:, begin : begin + own_rows].reshape(tree_rows).astype(jnp.int32)
        position, member, sees = tree_layout(segments, parents[t, 0])
        masks.append((member, sees))
        tables.append(rope_tables(position))

    def attention(t, qkv):
        return lambda comm: attention_forward(
            links.place, qkv, *tables[t], *masks[t], q_width, shard, comm
        )

    def after_attention(t, branch):
        value = token_rows[t].astype(F32) + RESIDUAL * branch
        scale = rms_scale(value)
        return value, scale, (value * scale * gain_second).astype(BF16)

    normed_0 = normalized(rows_0, gain_first)
    saved_0, (rows_1,), _, _ = links.carry(
        attention(0, dot_nt(normed_0, w_qkv)), gathers=[(token_rows[1], 1)]
    )
    part_0 = dot_nn(saved_0[0], w_out).astype(BF16)
    normed_1 = normalized(rows_1, gain_first)
    saved_1, _, (branch_0,), _ = links.carry(attention(1, dot_nt(normed_1, w_qkv)), sums=[(part_0, 1, 0)])
    part_1 = dot_nn(saved_1[0], w_out).astype(BF16)
    middle_0, scale_0, own_0 = after_attention(0, branch_0)
    _, _, (branch_1,), _ = links.carry(None, sums=[(part_1, 1, 0)])
    middle_1, scale_1, own_1 = after_attention(1, branch_1)
    own_all = jnp.concatenate([own_0, own_1], axis=0)
    _, (rows_all,), _, _ = links.carry(None, gathers=[(own_all, trees)])

    cot_own = jnp.concatenate([(RESIDUAL * cot.astype(F32)).astype(BF16) for cot in cot_rows], axis=0)
    (gate, upper, hidden), (cot_all,), _, _ = links.carry(
        lambda comm: feed_forward(rows_all, w_gate, w_up, 256, comm), gathers=[(cot_own, trees)]
    )
    grad_down = dot_tn(hidden, cot_all).astype(BF16)
    hidden_grad = dot_nt(cot_all, w_down)
    wide = gate.astype(F32)
    sigma = jax.nn.sigmoid(wide)
    gate_grad = (
        hidden_grad * upper.astype(F32) * sigma * (1.0 + wide * (1.0 - sigma))
    ).astype(BF16)
    up_grad = (hidden_grad * wide * sigma).astype(BF16)
    ff_part = (dot_nn(gate_grad, w_gate) + dot_nn(up_grad, w_up)).astype(BF16)
    parts = lambda whole: [(whole, trees, t) for t in range(trees)]
    (grad_gate, grad_up), _, ff_grad, (total_down,) = links.carry(
        lambda comm: products([(gate_grad, rows_all, True), (up_grad, rows_all, True)], 256, comm),
        sums=parts(ff_part),
        totals=[grad_down],
    )
    out_own, middle_grads = [], []
    gain_ff_sum = jnp.zeros((width,), F32)
    for t, (middle, scale) in enumerate(((middle_0, scale_0), (middle_1, scale_1))):
        middle_back, term = norm_back(middle, scale, gain_second, ff_grad[t])
        gain_ff_sum = gain_ff_sum + term
        middle_grads.append(cot_rows[t].astype(F32) + middle_back)
        out_own.append((RESIDUAL * middle_grads[t]).astype(BF16))
    (down_part,), (out_all,), _, (total_gate,) = links.carry(
        lambda comm: products([(hidden, w_down, False)], 256, comm),
        gathers=[(jnp.concatenate(out_own, axis=0), trees)],
        totals=[grad_gate],
    )
    arrays = []
    for t, (_, query, kv, lse) in enumerate((saved_0, saved_1)):
        attended_grad = dot_nt(out_all[t * tree_rows : (t + 1) * tree_rows], w_out).astype(BF16)
        arrays.append((attended_grad, query, kv, lse, *tables[t], *masks[t]))
    (qkv_grad,), _, downs, (total_up,) = links.carry(
        lambda comm: attention_backward(links.place, arrays, shard, comm),
        sums=parts(down_part),
        totals=[grad_up],
    )
    results = [
        (middle + RESIDUAL * down).astype(BF16) for middle, down in zip((middle_0, middle_1), downs)
    ]
    normed_part = dot_nn(links.natural(qkv_grad, trees), w_qkv).astype(BF16)
    normed_sums = sum_beside(normed_part, trees)
    (grad_attn,), _ = products(
        [
            ((saved_0[0], saved_1[0]), out_all, True),
            (qkv_grad, (normed_0, normed_1), True),
        ],
        128 if shard > 4 else 256,
        NoComm(),
        joined=True,
    )
    _, _, _, (total_attn,) = links.carry(None, totals=[grad_attn])
    normed_sums, total_attn = sync(normed_sums, total_attn)
    normed_grads = [normed_sums[t].astype(F32) for t in range(trees)]
    input_grads = []
    gain_attn_sum = jnp.zeros((width,), F32)
    for t in range(trees):
        inputs = token_rows[t].astype(F32)
        input_back, term = norm_back(inputs, rms_scale(inputs), gain_first, normed_grads[t])
        gain_attn_sum = gain_attn_sum + term
        input_grads.append(middle_grads[t] + input_back)
    totals = (total_down, total_gate, total_up)

    def convert(index):
        return lambda after: sync(totals[index], after)[0].astype(F32)

    gains, converted = links.sum_small(
        jnp.stack([gain_attn_sum, gain_ff_sum]), [convert(0), convert(1), convert(2)]
    )
    rows = lambda begin, count: total_attn[begin : begin + count].astype(F32)
    return (
        jnp.stack(results)[:, None],
        jnp.stack(input_grads)[:, None],
        gains[0],
        rows(q_width, q_width),
        rows(2 * q_width, kv_width),
        rows(2 * q_width + kv_width, kv_width),
        rows(0, q_width),
        gains[1],
        converted[1],
        converted[2],
        converted[0],
    )


def solution(mesh):
    shard, replica = mesh.shape["shard"], mesh.shape["replica"]
    links = (Square if (shard, replica) == (4, 8) else General)(shard, replica)
    in_specs = (
        P(None, "replica", "shard", None),
        P("shard"),
        P("shard", None),
        P("shard", None),
        P("shard", None),
        P("shard", None),
        P("shard"),
        P("shard", None),
        P("shard", None),
        P("shard", None),
        P(None, "replica", "shard", None),
        P(None, "replica", "shard"),
        P(None, "replica", None),
    )
    out_specs = (
        P(None, "replica", "shard", None),
        P(None, "replica", "shard", None),
        P("shard"),
        P("shard", None),
        P("shard", None),
        P("shard", None),
        P("shard", None),
        P("shard"),
        P("shard", None),
        P("shard", None),
        P("shard", None),
    )
    return jax.shard_map(
        functools.partial(body, links),
        mesh=mesh,
        in_specs=in_specs,
        out_specs=out_specs,
        check_vma=False,
    )
```

```python
import functools
import math

import jax
import jax.numpy as jnp
from jax import lax
from jax.experimental import pallas as pl
from jax.experimental.pallas import tpu as pltpu
from jax.sharding import PartitionSpec as P

HEADS = 32
KV_HEADS = 8
HEAD_DIM = 64
PAIR = 2 * HEAD_DIM
GROUP = HEADS // KV_HEADS

EPSILON = 1e-05
RESIDUAL = 0.22
ATTN_SCALE = 0.015625
ROPE_BASE = 10000000.0
NEGATIVE = -1e30
BF16 = jnp.bfloat16
F32 = jnp.float32


def dot_nt(left, right):
    return lax.dot_general(left, right, (((1,), (1,)), ((), ())), preferred_element_type=F32)


def dot_nn(left, right):
    return lax.dot_general(left, right, (((1,), (0,)), ((), ())), preferred_element_type=F32)


def dot_tn(left, right):
    return lax.dot_general(left, right, (((0,), (0,)), ((), ())), preferred_element_type=F32)


def tree_layout(segment_row, parent_row):
    seg_numbers = jnp.arange(parent_row.shape[0], dtype=jnp.int32)
    member = (segment_row[:, None] == seg_numbers[None, :]).astype(jnp.int32)
    lengths = jnp.sum(member, axis=0)
    earlier = seg_numbers[None, :] < seg_numbers[:, None]
    starts = jnp.sum(jnp.where(earlier, lengths[None, :], 0), axis=1)
    parent_hit = parent_row[:, None] == seg_numbers[None, :]
    grandparent = jnp.sum(jnp.where(parent_hit, parent_row[None, :], 0), axis=1)
    itself = seg_numbers[:, None] == seg_numbers[None, :]
    related = itself | parent_hit | (grandparent[:, None] == seg_numbers[None, :])
    before = jnp.sum(jnp.where(related & jnp.logical_not(itself), lengths[None, :], 0), axis=1)
    shift = jnp.sum(member * (before - starts)[None, :], axis=1)
    position = jnp.arange(segment_row.shape[0], dtype=jnp.int32) + shift
    pad = ((0, 0), (0, PAIR - parent_row.shape[0]))
    sees = dot_nn(member.astype(BF16), related.astype(BF16)).astype(BF16)
    return position, jnp.pad(member.astype(BF16), pad), jnp.pad(sees, pad)


def rope_tables(position):
    lane = jnp.arange(PAIR, dtype=jnp.int32) % HEAD_DIM
    half = HEAD_DIM // 2
    fraction = (lane % half).astype(F32) * (2.0 / HEAD_DIM)
    freq = jnp.exp(-math.log(ROPE_BASE) * fraction)
    angle = position.astype(F32)[:, None] * freq[None, :]
    return jnp.cos(angle), jnp.sin(angle) * jnp.where(lane < half, -1.0, 1.0)[None, :]


MESH = pl.DeviceIdType.MESH
CHUNK = 64
SLOTS = 4


def remote(source, target, sems, index, device):
    return pltpu.make_async_remote_copy(
        source, target, sems.at[0, index], sems.at[1, index], device_id=device, device_id_type=MESH
    )


class GatherJob:
    def __init__(self, own, trees):
        self.operand = own
        self.trees = trees
        self.rows, self.width = own.shape[0] // trees, own.shape[1]
        self.chunks = self.rows // CHUNK
        self.out_shape = jax.ShapeDtypeStruct((4 * own.shape[0], self.width), own.dtype)
        self.out_spec = pl.BlockSpec(memory_space=pl.ANY)

    def scratch(self):
        return [
            pltpu.SemaphoreType.DMA((2, 3 * self.chunks * self.trees)),
            pltpu.SemaphoreType.DMA((self.trees,)),
        ]

    def bind(self, operand, out, scratch, x, y):
        sems, local = scratch
        n, rows = self.chunks, self.rows
        self.local, self.to_x, self.to_y, self.on_x, self.on_y = [], [], [], [], []
        for t in range(self.trees):
            at = lambda block, j: out.at[pl.ds((4 * t + block) * rows + j * CHUNK, CHUNK), :]
            own = lambda j: operand.at[pl.ds(t * rows + j * CHUNK, CHUNK), :]
            sem = 3 * n * t
            self.local.append(
                pltpu.make_async_copy(
                    operand.at[pl.ds(t * rows, rows), :],
                    out.at[pl.ds(4 * t * rows, rows), :],
                    local.at[t],
                )
            )
            self.to_x.append([remote(own(j), at(1, j), sems, sem + j, x) for j in range(n)])
            self.to_y.append([remote(own(j), at(2, j), sems, sem + n + j, y) for j in range(n)])
            on = lambda block, j, to: remote(at(block, j), at(3, j), sems, sem + 2 * n + j, to)
            self.on_x.append([on(2, j, x) for j in range(n // 2)])
            self.on_y.append([on(1, j, y) for j in range(n // 2, n)])

    def begin(self):
        n = self.chunks
        half = n // 2
        for t in range(self.trees):
            for k in range(n):
                self.to_x[t][(k + half) % n].start()
                self.to_y[t][k].start()
            self.local[t].start()

    def stages(self):
        def stage(t, k):
            half = self.chunks // 2
            self.to_y[t][k].wait_recv()
            self.on_x[t][k].start()
            self.to_x[t][half + k].wait_recv()
            self.on_y[t][k].start()

        return [
            functools.partial(stage, t, k)
            for t in range(self.trees)
            for k in range(self.chunks // 2)
        ]

    def finish(self):
        half = self.chunks // 2
        for t in range(self.trees):
            for copy in self.to_x[t][:half] + self.to_y[t][half:] + self.on_x[t] + self.on_y[t]:
                copy.wait_recv()
            for copy in self.to_x[t] + self.to_y[t] + self.on_x[t] + self.on_y[t]:
                copy.wait_send()
            self.local[t].wait()


class SumJob:
    def __init__(self, part, trees, tree):
        self.operand = part
        self.rows, self.width = part.shape[0] // 4 // trees, part.shape[1]
        self.base = 4 * self.rows * tree
        self.half = self.rows // 2
        self.chunks = self.half // CHUNK
        self.out_shape = jax.ShapeDtypeStruct((self.rows, self.width), F32)
        self.out_spec = pl.BlockSpec((self.rows, self.width), lambda *_: (0, 0))

    def scratch(self):
        return [
            pltpu.VMEM((4, self.half, self.width), BF16),
            pltpu.VMEM((6, self.half, self.width), BF16),
            pltpu.SemaphoreType.DMA((2, 6 * self.chunks)),
            pltpu.SemaphoreType.DMA((4,)),
        ]

    def bind(self, part, out, scratch, x, y):
        self.out = out
        self.mine, self.got, sems, local = scratch
        n, half = self.chunks, self.half
        rows = lambda block, second: pl.ds(self.base + block * self.rows + second * half, half)
        piece = lambda block, second, j: part.at[
            pl.ds(self.base + block * self.rows + second * half + j * CHUNK, CHUNK), :
        ]
        here = lambda ref, k, j: ref.at[k, pl.ds(j * CHUNK, CHUNK), :]
        self.loads = [
            pltpu.make_async_copy(part.at[rows(block, second), :], self.mine.at[k], local.at[k])
            for k, (block, second) in enumerate(((0, 0), (0, 1), (2, 0), (1, 1)))
        ]
        send = lambda k, source, device: [
            remote(source(j), here(self.got, k, j), sems, k * n + j, device) for j in range(n)
        ]
        self.sends = [
            send(0, lambda j: piece(1, 0, j), x),
            send(1, lambda j: piece(3, 0, j), x),
            send(2, lambda j: here(self.mine, 2, j), y),
            send(3, lambda j: piece(2, 1, j), y),
            send(4, lambda j: piece(3, 1, j), y),
            send(5, lambda j: here(self.mine, 3, j), x),
        ]

    def begin(self):
        for j in range(self.chunks):
            self.sends[1][j].start()
            self.sends[4][j].start()
        for load in self.loads:
            load.start()
        for j in range(self.chunks):
            self.sends[0][j].start()
            self.sends[3][j].start()

    def stages(self):
        def stage(j):
            if j == 0:
                for load in self.loads:
                    load.wait()
            rows = pl.ds(j * CHUNK, CHUNK)
            for first, second, own in ((1, 2, 2), (4, 5, 3)):
                self.sends[first][j].wait_recv()
                total = self.mine[own, rows, :].astype(F32) + self.got[first, rows, :].astype(F32)
                self.mine[own, rows, :] = total.astype(BF16)
                self.sends[second][j].start()

        return [functools.partial(stage, j) for j in range(self.chunks)]

    def finish(self):
        for j in range(self.chunks):
            rows = pl.ds(j * CHUNK, CHUNK)
            for own, one, two in ((0, 0, 2), (1, 3, 5)):
                self.sends[one][j].wait_recv()
                self.sends[two][j].wait_recv()
                self.out[pl.ds(own * self.half + j * CHUNK, CHUNK), :] = (
                    self.mine[own, rows, :].astype(F32)
                    + self.got[one, rows, :].astype(F32)
                    + self.got[two, rows, :].astype(F32)
                )
        for copies in self.sends:
            for copy in copies:
                copy.wait_send()


class LineJob:
    LINE_ROWS = 32
    BATCH = 4
    LAG = 2

    def __init__(self, grad):
        self.operand = grad
        self.half, self.width = grad.shape[0] // 2, grad.shape[1]
        self.chunks = self.half // self.LINE_ROWS
        self.batches = self.chunks // self.BATCH
        self.steps = self.chunks + 1 + 3 * self.LAG
        self.out_shape = jax.ShapeDtypeStruct(grad.shape, BF16)
        self.out_spec = pl.BlockSpec(memory_space=pl.ANY)

    def scratch(self):
        place = lambda: pltpu.VMEM((self.half, self.width), BF16)
        return [place(), place(), place(), place(), pltpu.SemaphoreType.DMA((9, self.chunks))]

    def bind(self, grad, out, scratch, x, y):
        self.grad, self.out = grad, out
        self.from_core, self.own, self.from_line, self.from_inner, self.sems = scratch
        shard, place = lax.axis_index("shard"), lax.axis_index("replica")
        self.core, z = place % 2, place // 2
        self.inner = (z == 1) | (z == 2)
        self.outer = (z == 0) | (z == 3)
        self.twin = (shard, z * 2 + 1 - self.core)
        self.pair = (shard, (z + 1 - 2 * (z % 2)) * 2 + self.core)
        self.across = (shard, (3 - z) * 2 + self.core)

    def chunk(self, c):
        return pl.ds(pl.multiple_of(c * self.LINE_ROWS, self.LINE_ROWS), self.LINE_ROWS)

    def batch(self, b):
        size = self.BATCH * self.LINE_ROWS
        return pl.ds(pl.multiple_of(b * size, size), size)

    def at(self, core, b):
        size = self.BATCH * self.LINE_ROWS
        return pl.ds(pl.multiple_of(core * self.half + b * size, size), size)

    def send(self, source, target, index, arrival, device, c):
        return pltpu.make_async_remote_copy(
            source,
            target,
            self.sems.at[index, c],
            self.sems.at[arrival, c],
            device_id=device,
            device_id_type=MESH,
        )

    def to_twin(self, b):
        source = self.grad.at[self.at(1 - self.core, b), :]
        return self.send(source, self.from_core.at[self.batch(b), :], 0, 1, self.twin, b)

    def load(self, b):
        source = self.grad.at[self.at(self.core, b), :]
        return pltpu.make_async_copy(source, self.own.at[self.batch(b), :], self.sems.at[2, b])

    def inward(self, c):
        rows = self.chunk(c)
        return self.send(self.own.at[rows, :], self.from_line.at[rows, :], 3, 4, self.pair, c)

    def between(self, c):
        rows = self.chunk(c)
        return self.send(self.own.at[rows, :], self.from_inner.at[rows, :], 3, 5, self.across, c)

    def outward(self, c):
        rows = self.chunk(c)
        return self.send(self.from_core.at[rows, :], self.from_line.at[rows, :], 6, 4, self.pair, c)

    def store(self, source, b):
        target = self.out.at[self.at(self.core, b), :]
        return pltpu.make_async_copy(source.at[self.batch(b), :], target, self.sems.at[2, b])

    def give(self, source, b):
        target = self.out.at[self.at(self.core, b), :]
        return self.send(source.at[self.batch(b), :], target, 7, 8, self.twin, b)

    def hand_out(self, source, c):
        @pl.when(c % self.BATCH == self.BATCH - 1)
        def _():
            self.store(source, c // self.BATCH).start()
            self.give(source, c // self.BATCH).start()

    def begin(self):
        pass

    def stages(self):
        return []

    def step(self, s):
        n, lag = self.chunks, self.LAG
        live = lambda begin: (s >= begin) & (s < n + begin)
        add = lambda a, b: (a.astype(F32) + b.astype(F32)).astype(BF16)

        @pl.when(live(0) & (s % self.BATCH == 0))
        def _():
            self.to_twin(s // self.BATCH).start()
            self.load(s // self.BATCH).start()

        @pl.when(live(1))
        def _():
            c = s - 1
            rows = self.chunk(c)

            @pl.when(c % self.BATCH == 0)
            def _():
                self.to_twin(c // self.BATCH).wait()
                self.load(c // self.BATCH).wait()

            self.own[rows, :] = add(self.own[rows, :], self.from_core[rows, :])
            pl.when(self.outer)(lambda: self.inward(c).start())

        @pl.when(live(1 + lag) & self.inner)
        def _():
            c = s - 1 - lag
            rows = self.chunk(c)
            self.inward(c).wait_recv()
            self.own[rows, :] = add(self.own[rows, :], self.from_line[rows, :])
            self.between(c).start()

        @pl.when(live(1 + 2 * lag) & self.inner)
        def _():
            c = s - 1 - 2 * lag
            rows = self.chunk(c)
            self.between(c).wait_recv()
            self.from_core[rows, :] = add(self.own[rows, :], self.from_inner[rows, :])
            self.outward(c).start()
            self.hand_out(self.from_core, c)

        @pl.when(live(1 + 3 * lag) & self.outer)
        def _():
            c = s - 1 - 3 * lag
            self.outward(c).wait_recv()
            self.hand_out(self.from_line, c)

    def finish(self):
        def inside(b, carry):
            self.store(self.from_line, b).wait()
            self.give(self.from_line, b).wait()
            return carry

        def body(c, carry):
            @pl.when(self.inner)
            def _():
                self.between(c).wait_send()
                self.outward(c).wait_send()

            pl.when(self.outer)(lambda: self.inward(c).wait_send())
            return carry

        lax.fori_loop(0, self.batches, inside, 0)
        lax.fori_loop(0, self.chunks, body, 0)


class Comm:
    def __init__(self, jobs, number):
        self.jobs, self.number = jobs, number
        self.operands = [job.operand for job in jobs]
        self.in_specs = [pl.BlockSpec(memory_space=pl.ANY) for _ in jobs]
        self.out_specs = [job.out_spec for job in jobs]
        self.out_shapes = [job.out_shape for job in jobs]
        self.scratch = [entry for job in jobs for entry in job.scratch()]

    def enter(self, operands, outs, scratch, now):
        shard, replica = lax.axis_index("shard"), lax.axis_index("replica")
        x = (shard + 1 - 2 * (shard % 2), replica)
        y = ((shard + 2) % 4, replica)
        scratch = list(scratch)
        for job, operand, out in zip(self.jobs, operands, outs):
            count = len(job.scratch())
            job.bind(operand, out, scratch[:count], x, y)
            scratch = scratch[count:]

        lines = [job for job in self.jobs if isinstance(job, LineJob)]
        square = len(lines) < len(self.jobs)

        @pl.when(now)
        def _():
            barrier = pltpu.get_barrier_semaphore()

            def greet(device):
                pl.semaphore_signal(barrier, inc=1, device_id=device, device_id_type=MESH)

            near = ([x, y] if square else []) + ([lines[0].twin, lines[0].pair] if lines else [])
            for device in near:
                greet(device)
            if lines:

                @pl.when(lines[0].inner)
                def _():
                    greet(lines[0].across)
                    pl.semaphore_wait(barrier, len(near) + 1)

                @pl.when(lines[0].outer)
                def _():
                    pl.semaphore_wait(barrier, len(near))

            else:
                pl.semaphore_wait(barrier, len(near))
            for job in self.jobs:
                job.begin()

    def stages(self):
        return [stage for job in self.jobs for stage in job.stages()]

    def advance(self, slot, slots):
        stages = self.stages()
        for job in self.jobs:
            if isinstance(job, LineJob):

                def body(k, carry, job=job):
                    job.step(k)
                    return carry

                lax.fori_loop(slot * job.steps // slots, (slot + 1) * job.steps // slots, body, 0)
        for index, stage in enumerate(stages):
            if slots <= 4:
                due = min(slots - 1, slots // 2 + index * (slots - slots // 2) // len(stages))
            else:
                due = min(slots - 1, max(1, int(slots * (0.25 + 0.5 * index / len(stages)))))
            pl.when(slot == due)(stage)

    def finish(self, now):
        @pl.when(now)
        def _():
            for job in self.jobs:
                job.finish()


class NoComm:
    operands = in_specs = out_specs = out_shapes = scratch = ()
    number = None

    def enter(self, *_):
        pass

    def advance(self, *_):
        pass

    def finish(self, *_):
        pass


def comm_params(comm, vmem):
    if comm.number is None:
        return pltpu.CompilerParams(vmem_limit_bytes=vmem << 20)
    return pltpu.CompilerParams(
        vmem_limit_bytes=vmem << 20, collective_id=comm.number, has_side_effects=True
    )


def split_refs(refs, *counts):
    parts, begin = [], 0
    for count in counts:
        parts.append(refs[begin : begin + count])
        begin += count
    return parts


def transfer(comm):
    count = len(comm.operands)
    steps = max([1] + [job.steps for job in comm.jobs if isinstance(job, LineJob)])

    def kernel(*refs):
        operands, outs, scratch = split_refs(refs, count, count, len(comm.scratch))
        step = pl.program_id(0)
        comm.enter(operands, outs, scratch, step == 0)
        if steps == 1:
            for stage in comm.stages():
                stage()
        else:
            comm.advance(step, steps)
        comm.finish(step == steps - 1)

    return pl.pallas_call(
        kernel,
        grid=(steps,),
        in_specs=comm.in_specs,
        out_specs=comm.out_specs,
        out_shape=comm.out_shapes,
        scratch_shapes=comm.scratch,
        compiler_params=comm_params(comm, 48),
        name="transfer",
    )(*comm.operands)


def products(items, block, comm, joined=False):
    specs, shapes, out_specs, steps, rights = [], [], [], [], []
    begin = 0
    items = [
        (l if isinstance(l, tuple) else (l,), r if isinstance(r, tuple) else (r,), t)
        for l, r, t in items
    ]
    total = sum((l[0].shape[1] if t else l[0].shape[0]) // block for l, _, t in items)
    for left, right, transposed in items:
        size = left[0].shape[1] if transposed else left[0].shape[0]
        count = size // block

        def place(i, begin=begin, count=count):
            return jnp.clip(i - begin, 0, count - 1)

        for l in left:
            if transposed:
                specs.append(pl.BlockSpec((l.shape[0], block), lambda i, p=place: (0, p(i))))
            else:
                specs.append(pl.BlockSpec((block, l.shape[1]), lambda i, p=place: (p(i), 0)))
        columns = right[0].shape[1]
        if not joined:
            out_specs.append(pl.BlockSpec((block, columns), lambda i, p=place: (p(i), 0)))
            shapes.append(jax.ShapeDtypeStruct((size, columns), BF16))
        for r in right:
            if not any(r is other for other in rights):
                rights.append(r)
        steps.append((begin, count))
        begin += count
    right_specs = [
        pl.BlockSpec(r.shape, lambda i: (0, 0), pipeline_mode=pl.Buffered(1)) for r in rights
    ]
    which = [
        [next(k for k, other in enumerate(rights) if other is r) for r in right]
        for _, right, _ in items
    ]
    firsts = [sum(len(l) for l, _, _ in items[:k]) for k in range(len(items))]
    n = sum(len(l) for l, _, _ in items)
    if joined:
        width = items[0][1][0].shape[1]
        out_specs = [pl.BlockSpec((block, width), lambda i: (i, 0))]
        shapes = [jax.ShapeDtypeStruct((total * block, width), BF16)]
    made = len(shapes)

    def kernel(*refs):
        lefts, held, operands, outs, comm_outs, scratch = split_refs(
            refs, n, len(rights), len(comm.operands), made, len(comm.operands), len(comm.scratch)
        )
        step = pl.program_id(0)
        comm.enter(operands, comm_outs, scratch, step == 0)
        width = items[0][1][0].shape[1] // SLOTS

        def part(slot, carry):
            comm.advance(step * SLOTS + slot, total * SLOTS)
            columns = pl.ds(pl.multiple_of(slot * width, width), width)
            for k, (left, right, transposed) in enumerate(items):
                begin, count = steps[k]

                @pl.when((step >= begin) & (step < begin + count))
                def _(k=k, left=left, right=right, transposed=transposed):
                    dot = dot_tn if transposed else dot_nn
                    result, pieces = 0.0, max(len(left), len(right))
                    for piece in range(pieces):
                        l, r = lefts[firsts[k] + piece % len(left)], held[which[k][piece % len(right)]]
                        share = pl.ds(piece * (r.shape[0] // pieces), r.shape[0] // pieces)
                        ours = pl.ds(piece * (l.shape[0] // pieces), l.shape[0] // pieces)
                        result += dot(
                            l[ours, :] if len(left) < pieces else l[...],
                            r[share, columns] if len(right) < pieces else r[:, columns],
                        )
                    outs[0 if joined else k][:, columns] = result.astype(BF16)

            return carry

        lax.fori_loop(0, SLOTS, part, 0)

        comm.finish(step == total - 1)

    flops = 2 * sum(math.prod(l.shape) * right[0].shape[1] for left, right, _ in items for l in left)
    out = pl.pallas_call(
        kernel,
        grid=(total,),
        in_specs=specs + right_specs + list(comm.in_specs),
        out_specs=out_specs + list(comm.out_specs),
        out_shape=shapes + list(comm.out_shapes),
        scratch_shapes=list(comm.scratch),
        compiler_params=comm_params(comm, 58),
        cost_estimate=pl.CostEstimate(flops=flops, bytes_accessed=30_000_000, transcendentals=0),
        name="products",
    )(*[l for left, _, _ in items for l in left], *rights, *comm.operands)
    return out[:made], out[made:]


def feed_forward(rows_all, w_gate, w_up, block, comm):
    rows, width = rows_all.shape
    units = w_gate.shape[0]
    steps = units // block
    part = rows // SLOTS

    def kernel(*refs):
        inputs, operands, outs, comm_outs, scratch = split_refs(
            refs, 3, len(comm.operands), 3, len(comm.operands), len(comm.scratch)
        )
        x_ref, gate_w, up_w = inputs
        gate_ref, upper_ref, hidden_ref = outs
        step = pl.program_id(0)
        comm.enter(operands, comm_outs, scratch, step == 0)
        comm.advance(step, steps)
        for slot in range(SLOTS):
            here = pl.ds(slot * part, part)
            gate = dot_nt(x_ref[here, :], gate_w[...])
            upper = dot_nt(x_ref[here, :], up_w[...])
            gate_ref[here, :] = gate.astype(BF16)
            upper_ref[here, :] = upper.astype(BF16)
            hidden_ref[here, :] = (gate * jax.nn.sigmoid(gate) * upper).astype(BF16)
        comm.finish(step == steps - 1)

    out = pl.pallas_call(
        kernel,
        grid=(steps,),
        in_specs=[
            pl.BlockSpec((rows, width), lambda i: (0, 0), pipeline_mode=pl.Buffered(1)),
            pl.BlockSpec((block, width), lambda i: (i, 0)),
            pl.BlockSpec((block, width), lambda i: (i, 0)),
            *comm.in_specs,
        ],
        out_specs=[pl.BlockSpec((rows, block), lambda i: (0, i))] * 3 + list(comm.out_specs),
        out_shape=[jax.ShapeDtypeStruct((rows, units), BF16)] * 3 + list(comm.out_shapes),
        scratch_shapes=list(comm.scratch),
        compiler_params=comm_params(comm, 56),
        cost_estimate=pl.CostEstimate(
            flops=4 * rows * width * units, bytes_accessed=48_000_000, transcendentals=rows * units
        ),
        name="feed_forward",
    )(rows_all, w_gate, w_up, *comm.operands)
    return out[:3], out[3:]


def swap_halves(block):
    lane = lax.broadcasted_iota(jnp.int32, block.shape, 1)
    half = HEAD_DIM // 2
    up = pltpu.roll(block, PAIR - half, 1)
    down = pltpu.roll(block, half, 1)
    return jnp.where(lane % HEAD_DIM < half, up, down)


def turn(block, cosine, sine):
    return block * cosine + swap_halves(block) * sine


def place_heads(wide, kv_heads, fill):
    placed = []
    for g in range(kv_heads):
        base = wide[:, (g // 2) * PAIR : (g // 2) * PAIR + PAIR] if wide.shape[1] >= PAIR else wide
        lane = lax.broadcasted_iota(jnp.int32, base.shape, 1)
        moved = pltpu.roll(base, HEAD_DIM, 1)
        for p in range(2):
            source = base if g % 2 == p else moved
            inside = (lane // HEAD_DIM) == p
            placed.append(jnp.where(inside, source, jnp.full_like(source, fill)))
    return placed


def attention_forward_kernel(kv_heads, blocks, place, comm, *refs):
    jobs = len(comm.operands)
    inputs, operands, outs, comm_outs, own, scratch = split_refs(
        refs, 6, jobs, 4, jobs, 3, len(comm.scratch)
    )
    q_ref, kv_ref, cos_ref, sin_ref, member_ref, sees_ref = inputs
    out_ref, q_out_ref, kv_out_ref, lse_ref = outs
    keys, values, bias = own
    step = pl.program_id(0)
    comm.enter(operands, comm_outs, scratch, step == 0)
    comm.advance(step, blocks)
    tree = q_ref.shape[0]
    rows = tree // blocks
    kv_width = kv_heads * HEAD_DIM

    @pl.when(step == 0)
    def _():
        for b in range(blocks):
            here = pl.ds(b * rows, rows)
            raw = kv_ref[pl.ds(pl.multiple_of(place(b) * rows, rows), rows), :]
            cosine, sine = cos_ref[here, :], sin_ref[here, :]
            if kv_width >= PAIR:
                turned = jnp.concatenate(
                    [
                        turn(raw[:, c : c + PAIR], cosine, sine)
                        for c in range(0, kv_width, PAIR)
                    ],
                    axis=1,
                )
                plain = raw[:, kv_width:]
            else:
                lane = lax.broadcasted_iota(jnp.int32, raw.shape, 1)
                turned = turn(raw, cosine, sine)
                plain = pltpu.roll(raw, HEAD_DIM, 1)
                both = jnp.where(lane < HEAD_DIM, turned, raw)
            if kv_width >= PAIR:
                both = jnp.concatenate([turned, plain], axis=1)
            kv_out_ref[here, :] = both.astype(BF16)
            for index, placed in enumerate(place_heads(turned, kv_heads, 0.0)):
                keys[index, here, :] = placed.astype(BF16)
            for index, placed in enumerate(place_heads(plain, kv_heads, 1.0)):
                values[index, here, :] = placed.astype(BF16)

    here = pl.ds(pl.multiple_of(step * rows, rows), rows)
    there = pl.ds(pl.multiple_of(place(step) * rows, rows), rows)
    cosine, sine = cos_ref[here, :], sin_ref[here, :]
    for j in range(q_ref.shape[1] // PAIR):
        lanes = slice(j * PAIR, j * PAIR + PAIR)
        turned = turn(q_ref[there, lanes], cosine, sine).astype(BF16)
        q_out_ref[:, lanes] = turned * BF16(ATTN_SCALE)

    link = dot_nt(sees_ref[here, :], member_ref[...])
    row_index = lax.broadcasted_iota(jnp.int32, (rows, tree), 0) + step * rows
    col_index = lax.broadcasted_iota(jnp.int32, (rows, tree), 1)
    bias[...] = jnp.where((link > 0.5) & (col_index <= row_index), 0.0, NEGATIVE)

    lane = lax.broadcasted_iota(jnp.int32, (rows, PAIR), 1)
    for block in range(blocks):
        width = (block + 1) * rows

        @pl.when(step == block)
        def _(width=width):
            lse = jnp.zeros((rows, PAIR), F32)
            for j in range(q_ref.shape[1] // PAIR):
                lanes = slice(j * PAIR, j * PAIR + PAIR)
                group = 2 * j // GROUP
                mixed, tops = [], []
                for p in range(2):
                    scores = dot_nt(q_out_ref[:, lanes], keys[group * 2 + p, :width, :])
                    scores = scores + bias[:, :width]
                    top = jnp.max(scores, axis=1, keepdims=True)
                    expo = jnp.exp(scores - top).astype(BF16)
                    mixed.append(dot_nn(expo, values[group * 2 + p, :width, :]))
                    tops.append(top)
                upper = lane >= HEAD_DIM
                total = pltpu.roll(jnp.where(upper, mixed[0], mixed[1]), HEAD_DIM, 1)
                out_ref[there, lanes] = (jnp.where(upper, mixed[1], mixed[0]) / total).astype(BF16)
                logs = jnp.log(total)
                lse = jnp.where(lane == 2 * j, tops[0] + logs[:, :1], lse)
                lse = jnp.where(lane == 2 * j + 1, tops[1] + logs[:, HEAD_DIM : HEAD_DIM + 1], lse)
            lse_ref[...] = lse

    comm.finish(step == blocks - 1)


def attention_forward(place, qkv, cosine, sine, member, sees, q_width, blocks, comm):
    tree = qkv.shape[0]
    rows = tree // blocks
    kv_width = (qkv.shape[1] - q_width) // 2
    kv_heads = kv_width // HEAD_DIM
    whole = lambda width: pl.BlockSpec((tree, width), lambda i: (0, 0))
    natural = lambda width: pl.BlockSpec((rows, width), lambda i: (i, 0))
    out = pl.pallas_call(
        functools.partial(attention_forward_kernel, kv_heads, blocks, place, comm),
        grid_spec=pl.GridSpec(
            grid=(blocks,),
            in_specs=[
                whole(q_width),
                pl.BlockSpec((tree, 2 * kv_width), lambda i: (0, q_width // (2 * kv_width))),
                whole(PAIR),
                whole(PAIR),
                whole(PAIR),
                whole(PAIR),
                *comm.in_specs,
            ],
            out_specs=[
                whole(q_width),
                natural(q_width),
                whole(2 * kv_width),
                natural(PAIR),
                *comm.out_specs,
            ],
            scratch_shapes=[
                pltpu.VMEM((2 * kv_heads, tree, PAIR), BF16),
                pltpu.VMEM((2 * kv_heads, tree, PAIR), BF16),
                pltpu.VMEM((rows, tree), F32),
                *comm.scratch,
            ],
        ),
        out_shape=[
            jax.ShapeDtypeStruct((tree, q_width), BF16),
            jax.ShapeDtypeStruct((tree, q_width), BF16),
            jax.ShapeDtypeStruct((tree, 2 * kv_width), BF16),
            jax.ShapeDtypeStruct((tree, PAIR), F32),
            *comm.out_shapes,
        ],
        compiler_params=comm_params(comm, 40),
        cost_estimate=pl.CostEstimate(
            flops=10_000_000_000, bytes_accessed=12_000_000, transcendentals=5_000_000
        ),
        name="attention_forward",
    )(qkv, qkv, cosine, sine, member, sees, *comm.operands)
    return out[:4], out[4:]


def attention_backward_kernel(kv_heads, blocks, trees, place, comm, *refs):
    jobs = len(comm.operands)
    inputs, operands, outs, comm_outs, own, scratch = split_refs(
        refs, 8 * trees, jobs, 1, jobs, 6, len(comm.scratch)
    )
    pairs = inputs[1].shape[1] // PAIR
    each = blocks * pairs
    step = pl.program_id(0)
    comm.enter(operands, comm_outs, scratch, step == 0)
    comm.advance(step, each * trees)
    for t in range(trees):

        @pl.when((step >= t * each) & (step < (t + 1) * each))
        def _(t=t):
            local = step - t * each
            attention_backward_step(
                kv_heads,
                blocks,
                pairs,
                place,
                local // pairs,
                local % pairs,
                t,
                inputs[8 * t : 8 * t + 8],
                outs[0],
                own,
            )

    comm.finish(step == each * trees - 1)


def attention_backward_step(kv_heads, blocks, pairs, place, step, j, t, inputs, out_ref, own):
    grad_ref, q_ref, kv_ref, lse_ref, cos_ref, sin_ref, member_ref, sees_ref = inputs
    keys, values, bias, lse_rows, key_sum, value_sum = own
    tree, rows = grad_ref.shape[0], q_ref.shape[0]
    kv_width = kv_heads * HEAD_DIM
    q_width = q_ref.shape[1]
    base = t * tree

    @pl.when((step == 0) & (j == 0))
    def _():
        for b in range(blocks):
            here = pl.ds(b * rows, rows)
            both = kv_ref[here, :].astype(F32)
            if kv_width >= PAIR:
                turned, plain = both[:, :kv_width], both[:, kv_width:]
            else:
                turned, plain = both, pltpu.roll(both, HEAD_DIM, 1)
            for index, placed in enumerate(place_heads(turned, kv_heads, 0.0)):
                keys[index, here, :] = placed.astype(BF16)
            for index, placed in enumerate(place_heads(plain, kv_heads, 0.0)):
                values[index, here, :] = placed.astype(BF16)
        key_sum[...] = jnp.zeros_like(key_sum)
        value_sum[...] = jnp.zeros_like(value_sum)

    here = pl.ds(pl.multiple_of(step * rows, rows), rows)

    @pl.when(j == 0)
    def _():
        link = dot_nt(member_ref[...], sees_ref[here, :])
        key_index = lax.broadcasted_iota(jnp.int32, (tree, rows), 0)
        query_index = lax.broadcasted_iota(jnp.int32, (tree, rows), 1) + step * rows
        bias[...] = jnp.where((link > 0.5) & (key_index <= query_index), 0.0, NEGATIVE)
        lse_rows[...] = jnp.transpose(lse_ref[...])

    there = pl.ds(pl.multiple_of(place(step) * rows, rows), rows)
    out_rows = pl.ds(pl.multiple_of(base + place(step) * rows, rows), rows)
    lanes = pl.ds(pl.multiple_of(j * PAIR, PAIR), PAIR)
    group = 2 * j // GROUP
    for block in range(blocks):
        width = (block + 1) * rows

        @pl.when(step == block)
        def _(width=width):
            cosine, sine = cos_ref[here, :], sin_ref[here, :]
            query, grad = q_ref[:, lanes], grad_ref[there, lanes]
            dq = jnp.zeros((rows, PAIR), F32)
            for p in range(2):
                index = group * 2 + p
                scores = dot_nt(keys[index, :width, :], query) + bias[:width, :]
                probs = jnp.exp(scores - lse_rows[pl.ds(2 * j + p, 1), :])
                probs_grad = dot_nt(values[index, :width, :], grad)
                value_sum[index, :width, :] += dot_nn(probs.astype(BF16), grad)
                weighted = probs * probs_grad
                delta = jnp.sum(weighted, axis=0, keepdims=True)
                score_grad = (weighted - probs * delta).astype(BF16)
                key_sum[index, :width, :] += dot_nn(score_grad, query)
                dq = dq + dot_tn(score_grad, keys[index, :width, :])
            out_ref[out_rows, lanes] = turn(dq * ATTN_SCALE, cosine, -sine).astype(BF16)

    @pl.when((step == blocks - 1) & (j == pairs - 1))
    def _():
        for b in range(blocks):
            here = pl.ds(b * rows, rows)
            there = pl.ds(pl.multiple_of(base + place(b) * rows, rows), rows)
            cosine, sine = cos_ref[here, :], sin_ref[here, :]
            lane = lax.broadcasted_iota(jnp.int32, (rows, PAIR), 1)
            lower = lane < HEAD_DIM
            for c in range(0, kv_heads, 2):
                halves = []
                for acc in (key_sum, value_sum):
                    own, other = [], []
                    for g in range(c, min(c + 2, kv_heads)):
                        own.append(acc[g * 2, here, :])
                        other.append(acc[g * 2 + 1, here, :])
                    first = own[0] + pltpu.roll(other[0], HEAD_DIM, 1)
                    if len(own) == 2:
                        second = other[1] + pltpu.roll(own[1], HEAD_DIM, 1)
                    else:
                        second = first
                    halves.append(jnp.where(lower, first, second))
                turned = turn(halves[0], cosine, -sine)
                if kv_width >= PAIR:
                    begin = q_width + c * HEAD_DIM
                    out_ref[there, begin : begin + PAIR] = turned.astype(BF16)
                    begin += kv_width
                    out_ref[there, begin : begin + PAIR] = halves[1].astype(BF16)
                else:
                    moved = pltpu.roll(halves[1], HEAD_DIM, 1)
                    both = jnp.where(lower, turned, moved)
                    out_ref[there, q_width : q_width + PAIR] = both.astype(BF16)


def attention_backward(place, arrays, blocks, comm):
    trees = len(arrays)
    tree, q_width = arrays[0][1].shape
    rows = tree // blocks
    kv_width = arrays[0][2].shape[1] // 2
    kv_heads = kv_width // HEAD_DIM
    each = blocks * (q_width // PAIR)
    whole = lambda width: pl.BlockSpec((tree, width), lambda i: (0, 0))

    def natural(width, t):
        return pl.BlockSpec(
            (rows, width),
            lambda i: (jnp.clip((i - t * each) // (q_width // PAIR), 0, blocks - 1), 0),
        )

    in_specs = []
    for t in range(trees):
        in_specs += [whole(q_width), natural(q_width, t), whole(2 * kv_width), natural(PAIR, t)]
        in_specs += [whole(PAIR)] * 4
    total = q_width + 2 * kv_width
    out = pl.pallas_call(
        functools.partial(attention_backward_kernel, kv_heads, blocks, trees, place, comm),
        grid=(each * trees,),
        in_specs=in_specs + list(comm.in_specs),
        out_specs=[pl.BlockSpec((trees * tree, total), lambda i: (0, 0))] + list(comm.out_specs),
        out_shape=[jax.ShapeDtypeStruct((trees * tree, total), BF16)] + list(comm.out_shapes),
        scratch_shapes=[
            pltpu.VMEM((2 * kv_heads, tree, PAIR), BF16),
            pltpu.VMEM((2 * kv_heads, tree, PAIR), BF16),
            pltpu.VMEM((tree, rows), F32),
            pltpu.VMEM((PAIR, rows), F32),
            pltpu.VMEM((2 * kv_heads, tree, PAIR), F32),
            pltpu.VMEM((2 * kv_heads, tree, PAIR), F32),
            *comm.scratch,
        ],
        compiler_params=comm_params(comm, 60),
        cost_estimate=pl.CostEstimate(
            flops=40_000_000_000, bytes_accessed=24_000_000, transcendentals=10_000_000
        ),
        name="attention_backward",
    )(*[array for per_tree in arrays for array in per_tree], *comm.operands)
    return out[:1], out[1:]


def sync(*values):
    return lax.optimization_barrier(values)


class Square:
    def __init__(self, shard, replica):
        self.shard, self.replica = shard, replica
        self.x = [(i, i ^ 1) for i in range(shard)]
        self.y = [(i, i ^ 2) for i in range(shard)]
        self.d = [(i, i ^ 3) for i in range(shard)]

    def place(self, block):
        shard = lax.axis_index("shard")
        return (block + shard) % 2 + 2 * ((block // 2 + shard // 2) % 2)

    def reorder(self, blocks, axis):
        me = lax.axis_index("shard")
        return jnp.concatenate(
            [lax.dynamic_slice_in_dim(blocks, n ^ me, 1, axis) for n in range(self.shard)], axis=axis
        )

    def gather_small(self, own):
        parts = [
            own,
            lax.ppermute(own, "shard", self.x),
            lax.ppermute(own, "shard", self.y),
            lax.ppermute(own, "shard", self.d),
        ]
        return self.reorder(jnp.stack(parts), 0)

    def sum_small(self, values, beside):
        share = values.shape[1] // self.shard
        blocks = values.reshape(values.shape[0], self.shard, share)
        blocks = self.reorder(blocks, 1)
        hops = [[("shard", perm) for perm in (self.x, self.y, self.d)]]
        hops += [[("replica", [(i, i ^ k) for i in range(self.replica)])] for k in (1, 2, 4)]
        total, done = blocks[:, 0], []
        for number, hop in enumerate(hops):
            got = [
                lax.ppermute(blocks[:, k + 1] if number == 0 else total, axis, perm)
                for k, (axis, perm) in enumerate(hop)
            ]
            if number < len(beside):
                done.append(beside[number](total))
                got, done[-1] = sync(got, done[-1])
            total = total + sum(got)
        return total, done

    def carry(self, compute, gathers=(), sums=(), totals=()):
        jobs = [GatherJob(*own) for own in gathers] + [SumJob(*part) for part in sums]
        jobs += [LineJob(grad) for grad in totals]
        self.kernels += 1
        comm = Comm(jobs, self.kernels)
        if compute is None:
            results, moved = None, transfer(comm)
        else:
            results, moved = compute(comm)
        return (results, *map(list, split_refs(moved, len(gathers), len(sums), len(totals))))

    def start(self):
        self.kernels = 0


class General:
    def __init__(self, shard, replica):
        self.shard, self.replica = shard, replica

    def place(self, block):
        return block

    def gather_small(self, own):
        return lax.all_gather(own, "shard", axis=0, tiled=False)

    def carry(self, compute, gathers=(), sums=(), totals=()):
        results = None if compute is None else compute(NoComm())[0]
        rows = lambda array, trees: array.reshape(trees, -1, array.shape[1])
        gathered = [
            lax.all_gather(rows(own, trees), "shard", axis=1, tiled=True).reshape(-1, own.shape[1])
            for own, trees in gathers
        ]
        summed = [
            lax.psum_scatter(
                rows(part, trees)[tree], "shard", scatter_dimension=0, tiled=True
            ).astype(F32)
            for part, trees, tree in sums
        ]
        return results, gathered, summed, [lax.psum(grad, "replica") for grad in totals]

    def sum_small(self, values, beside):
        share = lax.psum_scatter(values, "shard", scatter_dimension=1, tiled=True)
        return lax.psum(share, "replica"), [f(share) for f in beside]

    def start(self):
        pass


def rms_scale(values):
    return lax.rsqrt(jnp.mean(values * values, axis=-1, keepdims=True) + EPSILON)


def normalized(piece, gain):
    values = piece.astype(F32)
    return (values * rms_scale(values) * gain).astype(BF16)


def norm_back(values, scale, gain, grad_in):
    scaled = values * scale
    weighted = grad_in * gain
    back = scale * (weighted - scaled * jnp.mean(weighted * scaled, axis=-1, keepdims=True))
    return back, jnp.sum(grad_in * scaled, axis=0)


def body(
    links,
    tokens,
    gain_attn,
    w_query,
    w_key,
    w_value,
    w_out,
    gain_ff,
    w_gate,
    w_up,
    w_down,
    cotangent,
    segment_ids,
    parents,
):
    trees, _, own_rows, width = tokens.shape
    shard = links.shard
    q_width, kv_width = w_query.shape[0], w_key.shape[0]
    tree_rows = own_rows * shard
    links.start()
    share = gain_attn.shape[0]
    w_qkv = jnp.concatenate([w_query, w_key, w_value], axis=0)
    token_rows = [tokens[t, 0] for t in range(trees)]
    cot_rows = [cotangent[t, 0] for t in range(trees)]

    small = jnp.concatenate(
        [gain_attn, gain_ff] + [segment_ids[t, 0].astype(BF16) for t in range(trees)]
    )
    smalls = links.gather_small(small)
    _, (rows_0,), _, _ = links.carry(None, gathers=[(token_rows[0], 1)])
    gain_first = smalls[:, :share].reshape(width).astype(F32)
    gain_second = smalls[:, share : 2 * share].reshape(width).astype(F32)
    masks, tables = [], []
    for t in range(trees):
        begin = 2 * share + t * own_rows
        segments = smalls[:, begin : begin + own_rows].reshape(tree_rows).astype(jnp.int32)
        position, member, sees = tree_layout(segments, parents[t, 0])
        masks.append((member, sees))
        tables.append(rope_tables(position))

    def attention(t, qkv):
        return lambda comm: attention_forward(
            links.place, qkv, *tables[t], *masks[t], q_width, shard, comm
        )

    def after_attention(t, branch):
        value = token_rows[t].astype(F32) + RESIDUAL * branch
        scale = rms_scale(value)
        return value, scale, (value * scale * gain_second).astype(BF16)

    normed_0 = normalized(rows_0, gain_first)
    saved_0, (rows_1,), _, _ = links.carry(
        attention(0, dot_nt(normed_0, w_qkv)), gathers=[(token_rows[1], 1)]
    )
    part_0 = dot_nn(saved_0[0], w_out).astype(BF16)
    normed_1 = normalized(rows_1, gain_first)
    saved_1, _, (branch_0,), _ = links.carry(attention(1, dot_nt(normed_1, w_qkv)), sums=[(part_0, 1, 0)])
    part_1 = dot_nn(saved_1[0], w_out).astype(BF16)
    middle_0, scale_0, own_0 = after_attention(0, branch_0)
    _, _, (branch_1,), _ = links.carry(None, sums=[(part_1, 1, 0)])
    middle_1, scale_1, own_1 = after_attention(1, branch_1)
    own_all = jnp.concatenate([own_0, own_1], axis=0)
    _, (rows_all,), _, _ = links.carry(None, gathers=[(own_all, trees)])

    cot_own = jnp.concatenate([(RESIDUAL * cot.astype(F32)).astype(BF16) for cot in cot_rows], axis=0)
    (gate, upper, hidden), (cot_all,), _, _ = links.carry(
        lambda comm: feed_forward(rows_all, w_gate, w_up, 256, comm), gathers=[(cot_own, trees)]
    )
    grad_down = dot_tn(hidden, cot_all).astype(BF16)
    hidden_grad = dot_nt(cot_all, w_down)
    wide = gate.astype(F32)
    sigma = jax.nn.sigmoid(wide)
    gate_grad = (
        hidden_grad * upper.astype(F32) * sigma * (1.0 + wide * (1.0 - sigma))
    ).astype(BF16)
    up_grad = (hidden_grad * wide * sigma).astype(BF16)
    ff_part = (dot_nn(gate_grad, w_gate) + dot_nn(up_grad, w_up)).astype(BF16)
    parts = lambda whole: [(whole, trees, t) for t in range(trees)]
    (grad_gate, grad_up), _, ff_grad, (total_down,) = links.carry(
        lambda comm: products([(gate_grad, rows_all, True), (up_grad, rows_all, True)], 256, comm),
        sums=parts(ff_part),
        totals=[grad_down],
    )
    out_own, middle_grads = [], []
    gain_ff_sum = jnp.zeros((width,), F32)
    for t, (middle, scale) in enumerate(((middle_0, scale_0), (middle_1, scale_1))):
        middle_back, term = norm_back(middle, scale, gain_second, ff_grad[t])
        gain_ff_sum = gain_ff_sum + term
        middle_grads.append(cot_rows[t].astype(F32) + middle_back)
        out_own.append((RESIDUAL * middle_grads[t]).astype(BF16))
    (down_part,), (out_all,), _, (total_gate,) = links.carry(
        lambda comm: products([(hidden, w_down, False)], 256, comm),
        gathers=[(jnp.concatenate(out_own, axis=0), trees)],
        totals=[grad_gate],
    )
    arrays = []
    for t, (_, query, kv, lse) in enumerate((saved_0, saved_1)):
        attended_grad = dot_nt(out_all[t * tree_rows : (t + 1) * tree_rows], w_out).astype(BF16)
        arrays.append((attended_grad, query, kv, lse, *tables[t], *masks[t]))
    (qkv_grad,), _, downs, (total_up,) = links.carry(
        lambda comm: attention_backward(links.place, arrays, shard, comm),
        sums=parts(down_part),
        totals=[grad_up],
    )
    results = [
        (middle + RESIDUAL * down).astype(BF16) for middle, down in zip((middle_0, middle_1), downs)
    ]
    normed_part = dot_nn(qkv_grad, w_qkv).astype(BF16)
    (grad_attn,), _ = products(
        [
            ((saved_0[0], saved_1[0]), out_all, True),
            (qkv_grad, (normed_0, normed_1), True),
        ],
        128 if shard > 4 else 256,
        NoComm(),
        joined=True,
    )
    _, _, normed_grads, (total_attn,) = links.carry(
        None, sums=parts(normed_part), totals=[grad_attn]
    )
    input_grads = []
    gain_attn_sum = jnp.zeros((width,), F32)
    for t in range(trees):
        inputs = token_rows[t].astype(F32)
        input_back, term = norm_back(inputs, rms_scale(inputs), gain_first, normed_grads[t])
        gain_attn_sum = gain_attn_sum + term
        input_grads.append(middle_grads[t] + input_back)
    totals = (total_down, total_gate, total_up)

    def convert(index):
        return lambda after: sync(totals[index], after)[0].astype(F32)

    gains, converted = links.sum_small(
        jnp.stack([gain_attn_sum, gain_ff_sum]), [convert(0), convert(1), convert(2)]
    )
    rows = lambda begin, count: total_attn[begin : begin + count].astype(F32)
    return (
        jnp.stack(results)[:, None],
        jnp.stack(input_grads)[:, None],
        gains[0],
        rows(q_width, q_width),
        rows(2 * q_width, kv_width),
        rows(2 * q_width + kv_width, kv_width),
        rows(0, q_width),
        gains[1],
        converted[1],
        converted[2],
        converted[0],
    )


def solution(mesh):
    shard, replica = mesh.shape["shard"], mesh.shape["replica"]
    links = (Square if (shard, replica) == (4, 8) else General)(shard, replica)
    in_specs = (
        P(None, "replica", "shard", None),
        P("shard"),
        P("shard", None),
        P("shard", None),
        P("shard", None),
        P("shard", None),
        P("shard"),
        P("shard", None),
        P("shard", None),
        P("shard", None),
        P(None, "replica", "shard", None),
        P(None, "replica", "shard"),
        P(None, "replica", None),
    )
    out_specs = (
        P(None, "replica", "shard", None),
        P(None, "replica", "shard", None),
        P("shard"),
        P("shard", None),
        P("shard", None),
        P("shard", None),
        P("shard", None),
        P("shard"),
        P("shard", None),
        P("shard", None),
        P("shard", None),
    )
    return jax.shard_map(
        functools.partial(body, links),
        mesh=mesh,
        in_specs=in_specs,
        out_specs=out_specs,
        check_vma=False,
    )
```

```python
import functools
import math

import jax
import jax.numpy as jnp
from jax import lax
from jax.experimental import pallas as pl
from jax.experimental.pallas import tpu as pltpu
from jax.sharding import PartitionSpec as P

HEADS = 32
KV_HEADS = 8
HEAD_DIM = 64
PAIR = 2 * HEAD_DIM
GROUP = HEADS // KV_HEADS

EPSILON = 1e-05
RESIDUAL = 0.22
ATTN_SCALE = 0.015625
ROPE_BASE = 10000000.0
NEGATIVE = -1e30
BF16 = jnp.bfloat16
F32 = jnp.float32


def dot_nt(left, right):
    return lax.dot_general(left, right, (((1,), (1,)), ((), ())), preferred_element_type=F32)


def dot_nn(left, right):
    return lax.dot_general(left, right, (((1,), (0,)), ((), ())), preferred_element_type=F32)


def dot_tn(left, right):
    return lax.dot_general(left, right, (((0,), (0,)), ((), ())), preferred_element_type=F32)


def tree_layout(segment_row, parent_row):
    seg_numbers = jnp.arange(parent_row.shape[0], dtype=jnp.int32)
    member = (segment_row[:, None] == seg_numbers[None, :]).astype(jnp.int32)
    lengths = jnp.sum(member, axis=0)
    earlier = seg_numbers[None, :] < seg_numbers[:, None]
    starts = jnp.sum(jnp.where(earlier, lengths[None, :], 0), axis=1)
    parent_hit = parent_row[:, None] == seg_numbers[None, :]
    grandparent = jnp.sum(jnp.where(parent_hit, parent_row[None, :], 0), axis=1)
    itself = seg_numbers[:, None] == seg_numbers[None, :]
    related = itself | parent_hit | (grandparent[:, None] == seg_numbers[None, :])
    before = jnp.sum(jnp.where(related & jnp.logical_not(itself), lengths[None, :], 0), axis=1)
    shift = jnp.sum(member * (before - starts)[None, :], axis=1)
    position = jnp.arange(segment_row.shape[0], dtype=jnp.int32) + shift
    pad = ((0, 0), (0, PAIR - parent_row.shape[0]))
    sees = dot_nn(member.astype(BF16), related.astype(BF16)).astype(BF16)
    return position, jnp.pad(member.astype(BF16), pad), jnp.pad(sees, pad)


def rope_tables(position):
    lane = jnp.arange(PAIR, dtype=jnp.int32) % HEAD_DIM
    half = HEAD_DIM // 2
    fraction = (lane % half).astype(F32) * (2.0 / HEAD_DIM)
    freq = jnp.exp(-math.log(ROPE_BASE) * fraction)
    angle = position.astype(F32)[:, None] * freq[None, :]
    return jnp.cos(angle), jnp.sin(angle) * jnp.where(lane < half, -1.0, 1.0)[None, :]


MESH = pl.DeviceIdType.MESH
CHUNK = 64
SLOTS = 4


def remote(source, target, sems, index, device):
    return pltpu.make_async_remote_copy(
        source, target, sems.at[0, index], sems.at[1, index], device_id=device, device_id_type=MESH
    )


class GatherJob:
    def __init__(self, own, trees):
        self.operand = own
        self.trees = trees
        self.rows, self.width = own.shape[0] // trees, own.shape[1]
        self.chunks = self.rows // CHUNK
        self.out_shape = jax.ShapeDtypeStruct((4 * own.shape[0], self.width), own.dtype)
        self.out_spec = pl.BlockSpec(memory_space=pl.ANY)

    def scratch(self):
        return [
            pltpu.SemaphoreType.DMA((2, 3 * self.chunks * self.trees)),
            pltpu.SemaphoreType.DMA((self.trees,)),
        ]

    def bind(self, operand, out, scratch, x, y):
        sems, local = scratch
        n, rows = self.chunks, self.rows
        self.local, self.to_x, self.to_y, self.on_x, self.on_y = [], [], [], [], []
        for t in range(self.trees):
            at = lambda block, j: out.at[pl.ds((4 * t + block) * rows + j * CHUNK, CHUNK), :]
            own = lambda j: operand.at[pl.ds(t * rows + j * CHUNK, CHUNK), :]
            sem = 3 * n * t
            self.local.append(
                pltpu.make_async_copy(
                    operand.at[pl.ds(t * rows, rows), :],
                    out.at[pl.ds(4 * t * rows, rows), :],
                    local.at[t],
                )
            )
            self.to_x.append([remote(own(j), at(1, j), sems, sem + j, x) for j in range(n)])
            self.to_y.append([remote(own(j), at(2, j), sems, sem + n + j, y) for j in range(n)])
            on = lambda block, j, to: remote(at(block, j), at(3, j), sems, sem + 2 * n + j, to)
            self.on_x.append([on(2, j, x) for j in range(n // 2)])
            self.on_y.append([on(1, j, y) for j in range(n // 2, n)])

    def begin(self):
        n = self.chunks
        half = n // 2
        for t in range(self.trees):
            for k in range(n):
                self.to_x[t][(k + half) % n].start()
                self.to_y[t][k].start()
            self.local[t].start()

    def stages(self):
        def stage(t, k):
            half = self.chunks // 2
            self.to_y[t][k].wait_recv()
            self.on_x[t][k].start()
            self.to_x[t][half + k].wait_recv()
            self.on_y[t][k].start()

        return [
            functools.partial(stage, t, k)
            for t in range(self.trees)
            for k in range(self.chunks // 2)
        ]

    def finish(self):
        half = self.chunks // 2
        for t in range(self.trees):
            for copy in self.to_x[t][:half] + self.to_y[t][half:] + self.on_x[t] + self.on_y[t]:
                copy.wait_recv()
            for copy in self.to_x[t] + self.to_y[t] + self.on_x[t] + self.on_y[t]:
                copy.wait_send()
            self.local[t].wait()


class SmallJob:
    def __init__(self, own):
        self.operand = own
        self.rows, self.width = own.shape
        self.out_shape = jax.ShapeDtypeStruct((4 * self.rows, self.width), own.dtype)
        self.out_spec = pl.BlockSpec(memory_space=pl.ANY)

    def scratch(self):
        return [pltpu.SemaphoreType.DMA((2, 3)), pltpu.SemaphoreType.DMA(())]

    def bind(self, operand, out, scratch, x, y):
        sems, local = scratch
        shard = lax.axis_index("shard")
        mine = out.at[pl.ds(pl.multiple_of(shard * self.rows, self.rows), self.rows), :]
        self.local = pltpu.make_async_copy(operand, mine, local)
        self.sends = [
            remote(operand, mine, sems, k, device)
            for k, device in enumerate((x, y, (3 - shard, x[1])))
        ]

    def begin(self):
        for send in self.sends:
            send.start()
        self.local.start()

    def stages(self):
        return []

    def finish(self):
        for send in self.sends:
            send.wait()
        self.local.wait()


class SumJob:
    def __init__(self, part, trees, tree):
        self.operand = part
        self.rows, self.width = part.shape[0] // 4 // trees, part.shape[1]
        self.base = 4 * self.rows * tree
        self.half = self.rows // 2
        self.chunks = self.half // CHUNK
        self.out_shape = jax.ShapeDtypeStruct((self.rows, self.width), F32)
        self.out_spec = pl.BlockSpec((self.rows, self.width), lambda *_: (0, 0))

    def scratch(self):
        return [
            pltpu.VMEM((4, self.half, self.width), BF16),
            pltpu.VMEM((6, self.half, self.width), BF16),
            pltpu.SemaphoreType.DMA((2, 6 * self.chunks)),
            pltpu.SemaphoreType.DMA((4,)),
        ]

    def bind(self, part, out, scratch, x, y):
        self.out = out
        self.mine, self.got, sems, local = scratch
        n, half = self.chunks, self.half
        rows = lambda block, second: pl.ds(self.base + block * self.rows + second * half, half)
        piece = lambda block, second, j: part.at[
            pl.ds(self.base + block * self.rows + second * half + j * CHUNK, CHUNK), :
        ]
        here = lambda ref, k, j: ref.at[k, pl.ds(j * CHUNK, CHUNK), :]
        self.loads = [
            pltpu.make_async_copy(part.at[rows(block, second), :], self.mine.at[k], local.at[k])
            for k, (block, second) in enumerate(((0, 0), (0, 1), (2, 0), (1, 1)))
        ]
        send = lambda k, source, device: [
            remote(source(j), here(self.got, k, j), sems, k * n + j, device) for j in range(n)
        ]
        self.sends = [
            send(0, lambda j: piece(1, 0, j), x),
            send(1, lambda j: piece(3, 0, j), x),
            send(2, lambda j: here(self.mine, 2, j), y),
            send(3, lambda j: piece(2, 1, j), y),
            send(4, lambda j: piece(3, 1, j), y),
            send(5, lambda j: here(self.mine, 3, j), x),
        ]

    def begin(self):
        for j in range(self.chunks):
            self.sends[1][j].start()
            self.sends[4][j].start()
        for load in self.loads:
            load.start()
        for j in range(self.chunks):
            self.sends[0][j].start()
            self.sends[3][j].start()

    def stages(self):
        def stage(j):
            if j == 0:
                for load in self.loads:
                    load.wait()
            rows = pl.ds(j * CHUNK, CHUNK)
            for first, second, own in ((1, 2, 2), (4, 5, 3)):
                self.sends[first][j].wait_recv()
                total = self.mine[own, rows, :].astype(F32) + self.got[first, rows, :].astype(F32)
                self.mine[own, rows, :] = total.astype(BF16)
                self.sends[second][j].start()

        return [functools.partial(stage, j) for j in range(self.chunks)]

    def finish(self):
        for j in range(self.chunks):
            rows = pl.ds(j * CHUNK, CHUNK)
            for own, one, two in ((0, 0, 2), (1, 3, 5)):
                self.sends[one][j].wait_recv()
                self.sends[two][j].wait_recv()
                self.out[pl.ds(own * self.half + j * CHUNK, CHUNK), :] = (
                    self.mine[own, rows, :].astype(F32)
                    + self.got[one, rows, :].astype(F32)
                    + self.got[two, rows, :].astype(F32)
                )
        for copies in self.sends:
            for copy in copies:
                copy.wait_send()


class LineJob:
    LINE_ROWS = 32
    BATCH = 4
    LAG = 2

    def __init__(self, grad):
        self.operand = grad
        self.half, self.width = grad.shape[0] // 2, grad.shape[1]
        self.chunks = self.half // self.LINE_ROWS
        self.batches = self.chunks // self.BATCH
        self.steps = self.chunks + 1 + 3 * self.LAG
        self.out_shape = jax.ShapeDtypeStruct(grad.shape, BF16)
        self.out_spec = pl.BlockSpec(memory_space=pl.ANY)

    def scratch(self):
        place = lambda: pltpu.VMEM((self.half, self.width), BF16)
        return [place(), place(), place(), place(), pltpu.SemaphoreType.DMA((9, self.chunks))]

    def bind(self, grad, out, scratch, x, y):
        self.grad, self.out = grad, out
        self.from_core, self.own, self.from_line, self.from_inner, self.sems = scratch
        shard, place = lax.axis_index("shard"), lax.axis_index("replica")
        self.core, z = place % 2, place // 2
        self.inner = (z == 1) | (z == 2)
        self.outer = (z == 0) | (z == 3)
        self.twin = (shard, z * 2 + 1 - self.core)
        self.pair = (shard, (z + 1 - 2 * (z % 2)) * 2 + self.core)
        self.across = (shard, (3 - z) * 2 + self.core)

    def chunk(self, c):
        return pl.ds(pl.multiple_of(c * self.LINE_ROWS, self.LINE_ROWS), self.LINE_ROWS)

    def batch(self, b):
        size = self.BATCH * self.LINE_ROWS
        return pl.ds(pl.multiple_of(b * size, size), size)

    def at(self, core, b):
        size = self.BATCH * self.LINE_ROWS
        return pl.ds(pl.multiple_of(core * self.half + b * size, size), size)

    def send(self, source, target, index, arrival, device, c):
        return pltpu.make_async_remote_copy(
            source,
            target,
            self.sems.at[index, c],
            self.sems.at[arrival, c],
            device_id=device,
            device_id_type=MESH,
        )

    def to_twin(self, b):
        source = self.grad.at[self.at(1 - self.core, b), :]
        return self.send(source, self.from_core.at[self.batch(b), :], 0, 1, self.twin, b)

    def load(self, b):
        source = self.grad.at[self.at(self.core, b), :]
        return pltpu.make_async_copy(source, self.own.at[self.batch(b), :], self.sems.at[2, b])

    def inward(self, c):
        rows = self.chunk(c)
        return self.send(self.own.at[rows, :], self.from_line.at[rows, :], 3, 4, self.pair, c)

    def between(self, c):
        rows = self.chunk(c)
        return self.send(self.own.at[rows, :], self.from_inner.at[rows, :], 3, 5, self.across, c)

    def outward(self, c):
        rows = self.chunk(c)
        return self.send(self.from_core.at[rows, :], self.from_line.at[rows, :], 6, 4, self.pair, c)

    def store(self, source, b):
        target = self.out.at[self.at(self.core, b), :]
        return pltpu.make_async_copy(source.at[self.batch(b), :], target, self.sems.at[2, b])

    def give(self, source, b):
        target = self.out.at[self.at(self.core, b), :]
        return self.send(source.at[self.batch(b), :], target, 7, 8, self.twin, b)

    def hand_out(self, source, c):
        @pl.when(c % self.BATCH == self.BATCH - 1)
        def _():
            self.store(source, c // self.BATCH).start()
            self.give(source, c // self.BATCH).start()

    def begin(self):
        pass

    def stages(self):
        return []

    def step(self, s):
        n, lag = self.chunks, self.LAG
        live = lambda begin: (s >= begin) & (s < n + begin)
        add = lambda a, b: (a.astype(F32) + b.astype(F32)).astype(BF16)

        @pl.when(live(0) & (s % self.BATCH == 0))
        def _():
            self.to_twin(s // self.BATCH).start()
            self.load(s // self.BATCH).start()

        @pl.when(live(1))
        def _():
            c = s - 1
            rows = self.chunk(c)

            @pl.when(c % self.BATCH == 0)
            def _():
                self.to_twin(c // self.BATCH).wait()
                self.load(c // self.BATCH).wait()

            self.own[rows, :] = add(self.own[rows, :], self.from_core[rows, :])
            pl.when(self.outer)(lambda: self.inward(c).start())

        @pl.when(live(1 + lag) & self.inner)
        def _():
            c = s - 1 - lag
            rows = self.chunk(c)
            self.inward(c).wait_recv()
            self.own[rows, :] = add(self.own[rows, :], self.from_line[rows, :])
            self.between(c).start()

        @pl.when(live(1 + 2 * lag) & self.inner)
        def _():
            c = s - 1 - 2 * lag
            rows = self.chunk(c)
            self.between(c).wait_recv()
            self.from_core[rows, :] = add(self.own[rows, :], self.from_inner[rows, :])
            self.outward(c).start()
            self.hand_out(self.from_core, c)

        @pl.when(live(1 + 3 * lag) & self.outer)
        def _():
            c = s - 1 - 3 * lag
            self.outward(c).wait_recv()
            self.hand_out(self.from_line, c)

    def finish(self):
        def inside(b, carry):
            self.store(self.from_line, b).wait()
            self.give(self.from_line, b).wait()
            return carry

        def body(c, carry):
            @pl.when(self.inner)
            def _():
                self.between(c).wait_send()
                self.outward(c).wait_send()

            pl.when(self.outer)(lambda: self.inward(c).wait_send())
            return carry

        lax.fori_loop(0, self.batches, inside, 0)
        lax.fori_loop(0, self.chunks, body, 0)


class Comm:
    def __init__(self, jobs, number):
        self.jobs, self.number = jobs, number
        self.operands = [job.operand for job in jobs]
        self.in_specs = [pl.BlockSpec(memory_space=pl.ANY) for _ in jobs]
        self.out_specs = [job.out_spec for job in jobs]
        self.out_shapes = [job.out_shape for job in jobs]
        self.scratch = [entry for job in jobs for entry in job.scratch()]

    def enter(self, operands, outs, scratch, now):
        shard, replica = lax.axis_index("shard"), lax.axis_index("replica")
        x = (shard + 1 - 2 * (shard % 2), replica)
        y = ((shard + 2) % 4, replica)
        scratch = list(scratch)
        for job, operand, out in zip(self.jobs, operands, outs):
            count = len(job.scratch())
            job.bind(operand, out, scratch[:count], x, y)
            scratch = scratch[count:]

        lines = [job for job in self.jobs if isinstance(job, LineJob)]
        square = len(lines) < len(self.jobs)

        @pl.when(now)
        def _():
            barrier = pltpu.get_barrier_semaphore()

            def greet(device):
                pl.semaphore_signal(barrier, inc=1, device_id=device, device_id_type=MESH)

            near = ([x, y] if square else []) + ([lines[0].twin, lines[0].pair] if lines else [])
            if any(isinstance(job, SmallJob) for job in self.jobs):
                near.append((3 - shard, replica))
            for device in near:
                greet(device)
            if lines:

                @pl.when(lines[0].inner)
                def _():
                    greet(lines[0].across)
                    pl.semaphore_wait(barrier, len(near) + 1)

                @pl.when(lines[0].outer)
                def _():
                    pl.semaphore_wait(barrier, len(near))

            else:
                pl.semaphore_wait(barrier, len(near))
            for job in self.jobs:
                job.begin()

    def stages(self):
        return [stage for job in self.jobs for stage in job.stages()]

    def advance(self, slot, slots):
        stages = self.stages()
        for job in self.jobs:
            if isinstance(job, LineJob):

                def body(k, carry, job=job):
                    job.step(k)
                    return carry

                lax.fori_loop(slot * job.steps // slots, (slot + 1) * job.steps // slots, body, 0)
        for index, stage in enumerate(stages):
            if slots <= 4:
                due = slots - 1
            elif slots <= 8:
                due = slots * 3 // 4
            else:
                due = min(slots - 1, max(1, int(slots * (0.25 + 0.5 * index / len(stages)))))
            pl.when(slot == due)(stage)

    def finish(self, now):
        @pl.when(now)
        def _():
            for job in self.jobs:
                job.finish()


class NoComm:
    operands = in_specs = out_specs = out_shapes = scratch = ()
    number = None

    def enter(self, *_):
        pass

    def advance(self, *_):
        pass

    def finish(self, *_):
        pass


def comm_params(comm, vmem):
    if comm.number is None:
        return pltpu.CompilerParams(vmem_limit_bytes=vmem << 20)
    return pltpu.CompilerParams(
        vmem_limit_bytes=vmem << 20, collective_id=comm.number, has_side_effects=True
    )


def split_refs(refs, *counts):
    parts, begin = [], 0
    for count in counts:
        parts.append(refs[begin : begin + count])
        begin += count
    return parts


def transfer(comm):
    count = len(comm.operands)
    steps = max([1] + [job.steps for job in comm.jobs if isinstance(job, LineJob)])

    def kernel(*refs):
        operands, outs, scratch = split_refs(refs, count, count, len(comm.scratch))
        step = pl.program_id(0)
        comm.enter(operands, outs, scratch, step == 0)
        if steps == 1:
            for stage in comm.stages():
                stage()
        else:
            comm.advance(step, steps)
        comm.finish(step == steps - 1)

    return pl.pallas_call(
        kernel,
        grid=(steps,),
        in_specs=comm.in_specs,
        out_specs=comm.out_specs,
        out_shape=comm.out_shapes,
        scratch_shapes=comm.scratch,
        compiler_params=comm_params(comm, 48),
        name="transfer",
    )(*comm.operands)


def products(items, block, comm, joined=False):
    specs, shapes, out_specs, steps, rights = [], [], [], [], []
    begin = 0
    items = [
        (l if isinstance(l, tuple) else (l,), r if isinstance(r, tuple) else (r,), t)
        for l, r, t in items
    ]
    total = sum((l[0].shape[1] if t else l[0].shape[0]) // block for l, _, t in items)
    for left, right, transposed in items:
        size = left[0].shape[1] if transposed else left[0].shape[0]
        count = size // block

        def place(i, begin=begin, count=count):
            return jnp.clip(i - begin, 0, count - 1)

        for l in left:
            if transposed:
                specs.append(pl.BlockSpec((l.shape[0], block), lambda i, p=place: (0, p(i))))
            else:
                specs.append(pl.BlockSpec((block, l.shape[1]), lambda i, p=place: (p(i), 0)))
        columns = right[0].shape[1]
        if not joined:
            out_specs.append(pl.BlockSpec((block, columns), lambda i, p=place: (p(i), 0)))
            shapes.append(jax.ShapeDtypeStruct((size, columns), BF16))
        for r in right:
            if not any(r is other for other in rights):
                rights.append(r)
        steps.append((begin, count))
        begin += count
    right_specs = [
        pl.BlockSpec(r.shape, lambda i: (0, 0), pipeline_mode=pl.Buffered(1)) for r in rights
    ]
    which = [
        [next(k for k, other in enumerate(rights) if other is r) for r in right]
        for _, right, _ in items
    ]
    firsts = [sum(len(l) for l, _, _ in items[:k]) for k in range(len(items))]
    n = sum(len(l) for l, _, _ in items)
    slots = 1 if comm.number is None else SLOTS
    if joined:
        width = items[0][1][0].shape[1]
        out_specs = [pl.BlockSpec((block, width), lambda i: (i, 0))]
        shapes = [jax.ShapeDtypeStruct((total * block, width), BF16)]
    made = len(shapes)

    def kernel(*refs):
        lefts, held, operands, outs, comm_outs, scratch = split_refs(
            refs, n, len(rights), len(comm.operands), made, len(comm.operands), len(comm.scratch)
        )
        step = pl.program_id(0)
        comm.enter(operands, comm_outs, scratch, step == 0)
        width = items[0][1][0].shape[1] // slots

        def part(slot, carry):
            comm.advance(step * slots + slot, total * slots)
            columns = pl.ds(pl.multiple_of(slot * width, width), width)
            for k, (left, right, transposed) in enumerate(items):
                begin, count = steps[k]

                @pl.when((step >= begin) & (step < begin + count))
                def _(k=k, left=left, right=right, transposed=transposed):
                    dot = dot_tn if transposed else dot_nn
                    result, pieces = 0.0, max(len(left), len(right))
                    for piece in range(pieces):
                        l, r = lefts[firsts[k] + piece % len(left)], held[which[k][piece % len(right)]]
                        share = pl.ds(piece * (r.shape[0] // pieces), r.shape[0] // pieces)
                        ours = pl.ds(piece * (l.shape[0] // pieces), l.shape[0] // pieces)
                        result += dot(
                            l[ours, :] if len(left) < pieces else l[...],
                            r[share, columns] if len(right) < pieces else r[:, columns],
                        )
                    outs[0 if joined else k][:, columns] = result.astype(BF16)

            return carry

        lax.fori_loop(0, slots, part, 0)

        comm.finish(step == total - 1)

    flops = 2 * sum(math.prod(l.shape) * right[0].shape[1] for left, right, _ in items for l in left)
    out = pl.pallas_call(
        kernel,
        grid=(total,),
        in_specs=specs + right_specs + list(comm.in_specs),
        out_specs=out_specs + list(comm.out_specs),
        out_shape=shapes + list(comm.out_shapes),
        scratch_shapes=list(comm.scratch),
        compiler_params=comm_params(comm, 58),
        cost_estimate=pl.CostEstimate(flops=flops, bytes_accessed=30_000_000, transcendentals=0),
        name="products",
    )(*[l for left, _, _ in items for l in left], *rights, *comm.operands)
    return out[:made], out[made:]


def feed_forward(rows_all, w_gate, w_up, block, comm):
    rows, width = rows_all.shape
    units = w_gate.shape[0]
    steps = units // block
    part = rows // SLOTS

    def kernel(*refs):
        inputs, operands, outs, comm_outs, scratch = split_refs(
            refs, 3, len(comm.operands), 3, len(comm.operands), len(comm.scratch)
        )
        x_ref, gate_w, up_w = inputs
        gate_ref, upper_ref, hidden_ref = outs
        step = pl.program_id(0)
        comm.enter(operands, comm_outs, scratch, step == 0)
        comm.advance(step, steps)
        for slot in range(SLOTS):
            here = pl.ds(slot * part, part)
            gate = dot_nt(x_ref[here, :], gate_w[...])
            upper = dot_nt(x_ref[here, :], up_w[...])
            gate_ref[here, :] = gate.astype(BF16)
            upper_ref[here, :] = upper.astype(BF16)
            hidden_ref[here, :] = (gate * jax.nn.sigmoid(gate) * upper).astype(BF16)
        comm.finish(step == steps - 1)

    out = pl.pallas_call(
        kernel,
        grid=(steps,),
        in_specs=[
            pl.BlockSpec((rows, width), lambda i: (0, 0), pipeline_mode=pl.Buffered(1)),
            pl.BlockSpec((block, width), lambda i: (i, 0)),
            pl.BlockSpec((block, width), lambda i: (i, 0)),
            *comm.in_specs,
        ],
        out_specs=[pl.BlockSpec((rows, block), lambda i: (0, i))] * 3 + list(comm.out_specs),
        out_shape=[jax.ShapeDtypeStruct((rows, units), BF16)] * 3 + list(comm.out_shapes),
        scratch_shapes=list(comm.scratch),
        compiler_params=comm_params(comm, 56),
        cost_estimate=pl.CostEstimate(
            flops=4 * rows * width * units, bytes_accessed=48_000_000, transcendentals=rows * units
        ),
        name="feed_forward",
    )(rows_all, w_gate, w_up, *comm.operands)
    return out[:3], out[3:]


def swap_halves(block):
    lane = lax.broadcasted_iota(jnp.int32, block.shape, 1)
    half = HEAD_DIM // 2
    up = pltpu.roll(block, PAIR - half, 1)
    down = pltpu.roll(block, half, 1)
    return jnp.where(lane % HEAD_DIM < half, up, down)


def turn(block, cosine, sine):
    return block * cosine + swap_halves(block) * sine


def place_heads(wide, kv_heads, fill):
    placed = []
    for g in range(kv_heads):
        base = wide[:, (g // 2) * PAIR : (g // 2) * PAIR + PAIR] if wide.shape[1] >= PAIR else wide
        lane = lax.broadcasted_iota(jnp.int32, base.shape, 1)
        moved = pltpu.roll(base, HEAD_DIM, 1)
        for p in range(2):
            source = base if g % 2 == p else moved
            inside = (lane // HEAD_DIM) == p
            placed.append(jnp.where(inside, source, jnp.full_like(source, fill)))
    return placed


def attention_forward_kernel(kv_heads, blocks, place, comm, *refs):
    jobs = len(comm.operands)
    inputs, operands, outs, comm_outs, own, scratch = split_refs(
        refs, 6, jobs, 4, jobs, 3, len(comm.scratch)
    )
    q_ref, kv_ref, cos_ref, sin_ref, member_ref, sees_ref = inputs
    out_ref, q_out_ref, kv_out_ref, lse_ref = outs
    keys, values, bias = own
    step = pl.program_id(0)
    comm.enter(operands, comm_outs, scratch, step == 0)
    comm.advance(step, blocks)
    tree = q_ref.shape[0]
    rows = tree // blocks
    kv_width = kv_heads * HEAD_DIM

    @pl.when(step == 0)
    def _():
        for b in range(blocks):
            here = pl.ds(b * rows, rows)
            raw = kv_ref[pl.ds(pl.multiple_of(place(b) * rows, rows), rows), :]
            cosine, sine = cos_ref[here, :], sin_ref[here, :]
            if kv_width >= PAIR:
                turned = jnp.concatenate(
                    [
                        turn(raw[:, c : c + PAIR], cosine, sine)
                        for c in range(0, kv_width, PAIR)
                    ],
                    axis=1,
                )
                plain = raw[:, kv_width:]
            else:
                lane = lax.broadcasted_iota(jnp.int32, raw.shape, 1)
                turned = turn(raw, cosine, sine)
                plain = pltpu.roll(raw, HEAD_DIM, 1)
                both = jnp.where(lane < HEAD_DIM, turned, raw)
            if kv_width >= PAIR:
                both = jnp.concatenate([turned, plain], axis=1)
            kv_out_ref[here, :] = both.astype(BF16)
            for index, placed in enumerate(place_heads(turned, kv_heads, 0.0)):
                keys[index, here, :] = placed.astype(BF16)
            for index, placed in enumerate(place_heads(plain, kv_heads, 1.0)):
                values[index, here, :] = placed.astype(BF16)

    here = pl.ds(pl.multiple_of(step * rows, rows), rows)
    there = pl.ds(pl.multiple_of(place(step) * rows, rows), rows)
    cosine, sine = cos_ref[here, :], sin_ref[here, :]
    for j in range(q_ref.shape[1] // PAIR):
        lanes = slice(j * PAIR, j * PAIR + PAIR)
        turned = turn(q_ref[there, lanes], cosine, sine).astype(BF16)
        q_out_ref[:, lanes] = turned * BF16(ATTN_SCALE)

    link = dot_nt(sees_ref[here, :], member_ref[...])
    row_index = lax.broadcasted_iota(jnp.int32, (rows, tree), 0) + step * rows
    col_index = lax.broadcasted_iota(jnp.int32, (rows, tree), 1)
    bias[...] = jnp.where((link > 0.5) & (col_index <= row_index), 0.0, NEGATIVE)

    lane = lax.broadcasted_iota(jnp.int32, (rows, PAIR), 1)
    for block in range(blocks):
        width = (block + 1) * rows

        @pl.when(step == block)
        def _(width=width):
            lse = jnp.zeros((rows, PAIR), F32)
            for j in range(q_ref.shape[1] // PAIR):
                lanes = slice(j * PAIR, j * PAIR + PAIR)
                group = 2 * j // GROUP
                mixed, tops = [], []
                for p in range(2):
                    scores = dot_nt(q_out_ref[:, lanes], keys[group * 2 + p, :width, :])
                    scores = scores + bias[:, :width]
                    top = jnp.max(scores, axis=1, keepdims=True)
                    expo = jnp.exp(scores - top).astype(BF16)
                    mixed.append(dot_nn(expo, values[group * 2 + p, :width, :]))
                    tops.append(top)
                upper = lane >= HEAD_DIM
                total = pltpu.roll(jnp.where(upper, mixed[0], mixed[1]), HEAD_DIM, 1)
                out_ref[there, lanes] = (jnp.where(upper, mixed[1], mixed[0]) / total).astype(BF16)
                logs = jnp.log(total)
                lse = jnp.where(lane == 2 * j, tops[0] + logs[:, :1], lse)
                lse = jnp.where(lane == 2 * j + 1, tops[1] + logs[:, HEAD_DIM : HEAD_DIM + 1], lse)
            lse_ref[...] = lse

    comm.finish(step == blocks - 1)


def attention_forward(place, qkv, cosine, sine, member, sees, q_width, blocks, comm):
    tree = qkv.shape[0]
    rows = tree // blocks
    kv_width = (qkv.shape[1] - q_width) // 2
    kv_heads = kv_width // HEAD_DIM
    whole = lambda width: pl.BlockSpec((tree, width), lambda i: (0, 0))
    natural = lambda width: pl.BlockSpec((rows, width), lambda i: (i, 0))
    out = pl.pallas_call(
        functools.partial(attention_forward_kernel, kv_heads, blocks, place, comm),
        grid_spec=pl.GridSpec(
            grid=(blocks,),
            in_specs=[
                whole(q_width),
                pl.BlockSpec((tree, 2 * kv_width), lambda i: (0, q_width // (2 * kv_width))),
                whole(PAIR),
                whole(PAIR),
                whole(PAIR),
                whole(PAIR),
                *comm.in_specs,
            ],
            out_specs=[
                whole(q_width),
                natural(q_width),
                whole(2 * kv_width),
                natural(PAIR),
                *comm.out_specs,
            ],
            scratch_shapes=[
                pltpu.VMEM((2 * kv_heads, tree, PAIR), BF16),
                pltpu.VMEM((2 * kv_heads, tree, PAIR), BF16),
                pltpu.VMEM((rows, tree), F32),
                *comm.scratch,
            ],
        ),
        out_shape=[
            jax.ShapeDtypeStruct((tree, q_width), BF16),
            jax.ShapeDtypeStruct((tree, q_width), BF16),
            jax.ShapeDtypeStruct((tree, 2 * kv_width), BF16),
            jax.ShapeDtypeStruct((tree, PAIR), F32),
            *comm.out_shapes,
        ],
        compiler_params=comm_params(comm, 40),
        cost_estimate=pl.CostEstimate(
            flops=10_000_000_000, bytes_accessed=12_000_000, transcendentals=5_000_000
        ),
        name="attention_forward",
    )(qkv, qkv, cosine, sine, member, sees, *comm.operands)
    return out[:4], out[4:]


def attention_backward_kernel(kv_heads, blocks, trees, place, comm, *refs):
    jobs = len(comm.operands)
    inputs, operands, outs, comm_outs, own, scratch = split_refs(
        refs, 8 * trees, jobs, 1, jobs, 6, len(comm.scratch)
    )
    pairs = inputs[1].shape[1] // PAIR
    each = blocks * pairs
    step = pl.program_id(0)
    comm.enter(operands, comm_outs, scratch, step == 0)
    comm.advance(step, each * trees)
    for t in range(trees):

        @pl.when((step >= t * each) & (step < (t + 1) * each))
        def _(t=t):
            local = step - t * each
            attention_backward_step(
                kv_heads,
                blocks,
                pairs,
                place,
                local // pairs,
                local % pairs,
                t,
                inputs[8 * t : 8 * t + 8],
                outs[0],
                own,
            )

    comm.finish(step == each * trees - 1)


def attention_backward_step(kv_heads, blocks, pairs, place, step, j, t, inputs, out_ref, own):
    grad_ref, q_ref, kv_ref, lse_ref, cos_ref, sin_ref, member_ref, sees_ref = inputs
    keys, values, bias, lse_rows, key_sum, value_sum = own
    tree, rows = grad_ref.shape[0], q_ref.shape[0]
    kv_width = kv_heads * HEAD_DIM
    q_width = q_ref.shape[1]
    base = t * tree

    @pl.when((step == 0) & (j == 0))
    def _():
        for b in range(blocks):
            here = pl.ds(b * rows, rows)
            both = kv_ref[here, :].astype(F32)
            if kv_width >= PAIR:
                turned, plain = both[:, :kv_width], both[:, kv_width:]
            else:
                turned, plain = both, pltpu.roll(both, HEAD_DIM, 1)
            for index, placed in enumerate(place_heads(turned, kv_heads, 0.0)):
                keys[index, here, :] = placed.astype(BF16)
            for index, placed in enumerate(place_heads(plain, kv_heads, 0.0)):
                values[index, here, :] = placed.astype(BF16)
        key_sum[...] = jnp.zeros_like(key_sum)
        value_sum[...] = jnp.zeros_like(value_sum)

    here = pl.ds(pl.multiple_of(step * rows, rows), rows)

    @pl.when(j == 0)
    def _():
        link = dot_nt(member_ref[...], sees_ref[here, :])
        key_index = lax.broadcasted_iota(jnp.int32, (tree, rows), 0)
        query_index = lax.broadcasted_iota(jnp.int32, (tree, rows), 1) + step * rows
        bias[...] = jnp.where((link > 0.5) & (key_index <= query_index), 0.0, NEGATIVE)
        lse_rows[...] = jnp.transpose(lse_ref[...])

    there = pl.ds(pl.multiple_of(place(step) * rows, rows), rows)
    out_rows = pl.ds(pl.multiple_of(base + place(step) * rows, rows), rows)
    lanes = pl.ds(pl.multiple_of(j * PAIR, PAIR), PAIR)
    group = 2 * j // GROUP
    for block in range(blocks):
        width = (block + 1) * rows

        @pl.when(step == block)
        def _(width=width):
            cosine, sine = cos_ref[here, :], sin_ref[here, :]
            query, grad = q_ref[:, lanes], grad_ref[there, lanes]
            dq = jnp.zeros((rows, PAIR), F32)
            for p in range(2):
                index = group * 2 + p
                scores = dot_nt(keys[index, :width, :], query) + bias[:width, :]
                probs = jnp.exp(scores - lse_rows[pl.ds(2 * j + p, 1), :])
                probs_grad = dot_nt(values[index, :width, :], grad)
                value_sum[index, :width, :] += dot_nn(probs.astype(BF16), grad)
                weighted = probs * probs_grad
                delta = jnp.sum(weighted, axis=0, keepdims=True)
                score_grad = (weighted - probs * delta).astype(BF16)
                key_sum[index, :width, :] += dot_nn(score_grad, query)
                dq = dq + dot_tn(score_grad, keys[index, :width, :])
            out_ref[out_rows, lanes] = turn(dq * ATTN_SCALE, cosine, -sine).astype(BF16)

    @pl.when((step == blocks - 1) & (j == pairs - 1))
    def _():
        for b in range(blocks):
            here = pl.ds(b * rows, rows)
            there = pl.ds(pl.multiple_of(base + place(b) * rows, rows), rows)
            cosine, sine = cos_ref[here, :], sin_ref[here, :]
            lane = lax.broadcasted_iota(jnp.int32, (rows, PAIR), 1)
            lower = lane < HEAD_DIM
            for c in range(0, kv_heads, 2):
                halves = []
                for acc in (key_sum, value_sum):
                    own, other = [], []
                    for g in range(c, min(c + 2, kv_heads)):
                        own.append(acc[g * 2, here, :])
                        other.append(acc[g * 2 + 1, here, :])
                    first = own[0] + pltpu.roll(other[0], HEAD_DIM, 1)
                    if len(own) == 2:
                        second = other[1] + pltpu.roll(own[1], HEAD_DIM, 1)
                    else:
                        second = first
                    halves.append(jnp.where(lower, first, second))
                turned = turn(halves[0], cosine, -sine)
                if kv_width >= PAIR:
                    begin = q_width + c * HEAD_DIM
                    out_ref[there, begin : begin + PAIR] = turned.astype(BF16)
                    begin += kv_width
                    out_ref[there, begin : begin + PAIR] = halves[1].astype(BF16)
                else:
                    moved = pltpu.roll(halves[1], HEAD_DIM, 1)
                    both = jnp.where(lower, turned, moved)
                    out_ref[there, q_width : q_width + PAIR] = both.astype(BF16)


def attention_backward(place, arrays, blocks, comm):
    trees = len(arrays)
    tree, q_width = arrays[0][1].shape
    rows = tree // blocks
    kv_width = arrays[0][2].shape[1] // 2
    kv_heads = kv_width // HEAD_DIM
    each = blocks * (q_width // PAIR)
    whole = lambda width: pl.BlockSpec((tree, width), lambda i: (0, 0))

    def natural(width, t):
        return pl.BlockSpec(
            (rows, width),
            lambda i: (jnp.clip((i - t * each) // (q_width // PAIR), 0, blocks - 1), 0),
        )

    in_specs = []
    for t in range(trees):
        in_specs += [whole(q_width), natural(q_width, t), whole(2 * kv_width), natural(PAIR, t)]
        in_specs += [whole(PAIR)] * 4
    total = q_width + 2 * kv_width
    out = pl.pallas_call(
        functools.partial(attention_backward_kernel, kv_heads, blocks, trees, place, comm),
        grid=(each * trees,),
        in_specs=in_specs + list(comm.in_specs),
        out_specs=[pl.BlockSpec((trees * tree, total), lambda i: (0, 0))] + list(comm.out_specs),
        out_shape=[jax.ShapeDtypeStruct((trees * tree, total), BF16)] + list(comm.out_shapes),
        scratch_shapes=[
            pltpu.VMEM((2 * kv_heads, tree, PAIR), BF16),
            pltpu.VMEM((2 * kv_heads, tree, PAIR), BF16),
            pltpu.VMEM((tree, rows), F32),
            pltpu.VMEM((PAIR, rows), F32),
            pltpu.VMEM((2 * kv_heads, tree, PAIR), F32),
            pltpu.VMEM((2 * kv_heads, tree, PAIR), F32),
            *comm.scratch,
        ],
        compiler_params=comm_params(comm, 60),
        cost_estimate=pl.CostEstimate(
            flops=40_000_000_000, bytes_accessed=24_000_000, transcendentals=10_000_000
        ),
        name="attention_backward",
    )(*[array for per_tree in arrays for array in per_tree], *comm.operands)
    return out[:1], out[1:]


def sync(*values):
    return lax.optimization_barrier(values)


class Square:
    def __init__(self, shard, replica):
        self.shard, self.replica = shard, replica
        self.x = [(i, i ^ 1) for i in range(shard)]
        self.y = [(i, i ^ 2) for i in range(shard)]
        self.d = [(i, i ^ 3) for i in range(shard)]

    def place(self, block):
        shard = lax.axis_index("shard")
        return (block + shard) % 2 + 2 * ((block // 2 + shard // 2) % 2)

    def reorder(self, blocks, axis):
        me = lax.axis_index("shard")
        return jnp.concatenate(
            [lax.dynamic_slice_in_dim(blocks, n ^ me, 1, axis) for n in range(self.shard)], axis=axis
        )

    def first(self, small, own):
        padded = jnp.pad(small, (0, -small.shape[0] % 2048)).reshape(16, -1)
        self.kernels += 1
        smalls, rows = transfer(Comm([SmallJob(padded), GatherJob(own, 1)], self.kernels))
        return smalls.reshape(self.shard, -1)[:, : small.shape[0]], rows

    def sum_small(self, values, beside):
        share = values.shape[1] // self.shard
        blocks = values.reshape(values.shape[0], self.shard, share)
        blocks = self.reorder(blocks, 1)
        hops = [[("shard", perm) for perm in (self.x, self.y, self.d)]]
        hops += [[("replica", [(i, i ^ k) for i in range(self.replica)])] for k in (1, 2, 4)]
        total, done = blocks[:, 0], []
        for number, hop in enumerate(hops):
            got = [
                lax.ppermute(blocks[:, k + 1] if number == 0 else total, axis, perm)
                for k, (axis, perm) in enumerate(hop)
            ]
            if number < len(beside):
                done.append(beside[number](total))
                got, done[-1] = sync(got, done[-1])
            total = total + sum(got)
        return total, done

    def carry(self, compute, gathers=(), sums=(), totals=()):
        jobs = [GatherJob(*own) for own in gathers] + [SumJob(*part) for part in sums]
        jobs += [LineJob(grad) for grad in totals]
        self.kernels += 1
        comm = Comm(jobs, self.kernels)
        if compute is None:
            results, moved = None, transfer(comm)
        else:
            results, moved = compute(comm)
        return (results, *map(list, split_refs(moved, len(gathers), len(sums), len(totals))))

    def start(self):
        self.kernels = 0


class General:
    def __init__(self, shard, replica):
        self.shard, self.replica = shard, replica

    def place(self, block):
        return block

    def first(self, small, own):
        rows = lax.all_gather(own, "shard", axis=0, tiled=True)
        return lax.all_gather(small, "shard", axis=0, tiled=False), rows

    def carry(self, compute, gathers=(), sums=(), totals=()):
        results = None if compute is None else compute(NoComm())[0]
        rows = lambda array, trees: array.reshape(trees, -1, array.shape[1])
        gathered = [
            lax.all_gather(rows(own, trees), "shard", axis=1, tiled=True).reshape(-1, own.shape[1])
            for own, trees in gathers
        ]
        summed = [
            lax.psum_scatter(
                rows(part, trees)[tree], "shard", scatter_dimension=0, tiled=True
            ).astype(F32)
            for part, trees, tree in sums
        ]
        return results, gathered, summed, [lax.psum(grad, "replica") for grad in totals]

    def sum_small(self, values, beside):
        share = lax.psum_scatter(values, "shard", scatter_dimension=1, tiled=True)
        return lax.psum(share, "replica"), [f(share) for f in beside]

    def start(self):
        pass


def rms_scale(values):
    return lax.rsqrt(jnp.mean(values * values, axis=-1, keepdims=True) + EPSILON)


def normalized(piece, gain):
    values = piece.astype(F32)
    return (values * rms_scale(values) * gain).astype(BF16)


def norm_back(values, scale, gain, grad_in):
    scaled = values * scale
    weighted = grad_in * gain
    back = scale * (weighted - scaled * jnp.mean(weighted * scaled, axis=-1, keepdims=True))
    return back, jnp.sum(grad_in * scaled, axis=0)


def body(
    links,
    tokens,
    gain_attn,
    w_query,
    w_key,
    w_value,
    w_out,
    gain_ff,
    w_gate,
    w_up,
    w_down,
    cotangent,
    segment_ids,
    parents,
):
    trees, _, own_rows, width = tokens.shape
    shard = links.shard
    q_width, kv_width = w_query.shape[0], w_key.shape[0]
    tree_rows = own_rows * shard
    links.start()
    share = gain_attn.shape[0]
    w_qkv = jnp.concatenate([w_query, w_key, w_value], axis=0)
    token_rows = [tokens[t, 0] for t in range(trees)]
    cot_rows = [cotangent[t, 0] for t in range(trees)]

    small = jnp.concatenate(
        [gain_attn, gain_ff] + [segment_ids[t, 0].astype(BF16) for t in range(trees)]
    )
    smalls, rows_0 = links.first(small, token_rows[0])
    gain_first = smalls[:, :share].reshape(width).astype(F32)
    gain_second = smalls[:, share : 2 * share].reshape(width).astype(F32)
    masks, tables = [], []
    for t in range(trees):
        begin = 2 * share + t * own_rows
        segments = smalls[:, begin : begin + own_rows].reshape(tree_rows).astype(jnp.int32)
        position, member, sees = tree_layout(segments, parents[t, 0])
        masks.append((member, sees))
        tables.append(rope_tables(position))

    def attention(t, qkv):
        return lambda comm: attention_forward(
            links.place, qkv, *tables[t], *masks[t], q_width, shard, comm
        )

    def after_attention(t, branch):
        value = token_rows[t].astype(F32) + RESIDUAL * branch
        scale = rms_scale(value)
        return value, scale, (value * scale * gain_second).astype(BF16)

    normed_0 = normalized(rows_0, gain_first)
    saved_0, (rows_1,), _, _ = links.carry(
        attention(0, dot_nt(normed_0, w_qkv)), gathers=[(token_rows[1], 1)]
    )
    part_0 = dot_nn(saved_0[0], w_out).astype(BF16)
    normed_1 = normalized(rows_1, gain_first)
    saved_1, _, (branch_0,), _ = links.carry(attention(1, dot_nt(normed_1, w_qkv)), sums=[(part_0, 1, 0)])
    part_1 = dot_nn(saved_1[0], w_out).astype(BF16)
    middle_0, scale_0, own_0 = after_attention(0, branch_0)
    _, _, (branch_1,), _ = links.carry(None, sums=[(part_1, 1, 0)])
    middle_1, scale_1, own_1 = after_attention(1, branch_1)
    own_all = jnp.concatenate([own_0, own_1], axis=0)
    _, (rows_all,), _, _ = links.carry(None, gathers=[(own_all, trees)])

    cot_own = jnp.concatenate([(RESIDUAL * cot.astype(F32)).astype(BF16) for cot in cot_rows], axis=0)
    (gate, upper, hidden), (cot_all,), _, _ = links.carry(
        lambda comm: feed_forward(rows_all, w_gate, w_up, 256, comm), gathers=[(cot_own, trees)]
    )
    grad_down = dot_tn(hidden, cot_all).astype(BF16)
    hidden_grad = dot_nt(cot_all, w_down)
    wide = gate.astype(F32)
    sigma = jax.nn.sigmoid(wide)
    gate_grad = (
        hidden_grad * upper.astype(F32) * sigma * (1.0 + wide * (1.0 - sigma))
    ).astype(BF16)
    up_grad = (hidden_grad * wide * sigma).astype(BF16)
    ff_part = (dot_nn(gate_grad, w_gate) + dot_nn(up_grad, w_up)).astype(BF16)
    parts = lambda whole: [(whole, trees, t) for t in range(trees)]
    (grad_gate, grad_up), _, ff_grad, (total_down,) = links.carry(
        lambda comm: products([(gate_grad, rows_all, True), (up_grad, rows_all, True)], 256, comm),
        sums=parts(ff_part),
        totals=[grad_down],
    )
    out_own, middle_grads = [], []
    gain_ff_sum = jnp.zeros((width,), F32)
    for t, (middle, scale) in enumerate(((middle_0, scale_0), (middle_1, scale_1))):
        middle_back, term = norm_back(middle, scale, gain_second, ff_grad[t])
        gain_ff_sum = gain_ff_sum + term
        middle_grads.append(cot_rows[t].astype(F32) + middle_back)
        out_own.append((RESIDUAL * middle_grads[t]).astype(BF16))
    (down_part,), (out_all,), _, (total_gate,) = links.carry(
        lambda comm: products([(hidden, w_down, False)], 256, comm),
        gathers=[(jnp.concatenate(out_own, axis=0), trees)],
        totals=[grad_gate],
    )
    arrays = []
    for t, (_, query, kv, lse) in enumerate((saved_0, saved_1)):
        attended_grad = dot_nt(out_all[t * tree_rows : (t + 1) * tree_rows], w_out).astype(BF16)
        arrays.append((attended_grad, query, kv, lse, *tables[t], *masks[t]))
    (qkv_grad,), _, downs, (total_up,) = links.carry(
        lambda comm: attention_backward(links.place, arrays, shard, comm),
        sums=parts(down_part),
        totals=[grad_up],
    )
    results = [
        (middle + RESIDUAL * down).astype(BF16) for middle, down in zip((middle_0, middle_1), downs)
    ]
    normed_part = dot_nn(qkv_grad, w_qkv).astype(BF16)
    (grad_attn,), _ = products(
        [
            ((saved_0[0], saved_1[0]), out_all, True),
            (qkv_grad, (normed_0, normed_1), True),
        ],
        128 if shard > 4 else 256,
        NoComm(),
        joined=True,
    )
    _, _, normed_grads, (total_attn,) = links.carry(
        None, sums=parts(normed_part), totals=[grad_attn]
    )
    input_grads = []
    gain_attn_sum = jnp.zeros((width,), F32)
    for t in range(trees):
        inputs = token_rows[t].astype(F32)
        input_back, term = norm_back(inputs, rms_scale(inputs), gain_first, normed_grads[t])
        gain_attn_sum = gain_attn_sum + term
        input_grads.append(middle_grads[t] + input_back)
    totals = (total_down, total_gate, total_up)

    def convert(index):
        return lambda after: sync(totals[index], after)[0].astype(F32)

    gains, converted = links.sum_small(
        jnp.stack([gain_attn_sum, gain_ff_sum]), [convert(0), convert(1), convert(2)]
    )
    rows = lambda begin, count: total_attn[begin : begin + count].astype(F32)
    return (
        jnp.stack(results)[:, None],
        jnp.stack(input_grads)[:, None],
        gains[0],
        rows(q_width, q_width),
        rows(2 * q_width, kv_width),
        rows(2 * q_width + kv_width, kv_width),
        rows(0, q_width),
        gains[1],
        converted[1],
        converted[2],
        converted[0],
    )


def solution(mesh):
    shard, replica = mesh.shape["shard"], mesh.shape["replica"]
    links = (Square if (shard, replica) == (4, 8) else General)(shard, replica)
    in_specs = (
        P(None, "replica", "shard", None),
        P("shard"),
        P("shard", None),
        P("shard", None),
        P("shard", None),
        P("shard", None),
        P("shard"),
        P("shard", None),
        P("shard", None),
        P("shard", None),
        P(None, "replica", "shard", None),
        P(None, "replica", "shard"),
        P(None, "replica", None),
    )
    out_specs = (
        P(None, "replica", "shard", None),
        P(None, "replica", "shard", None),
        P("shard"),
        P("shard", None),
        P("shard", None),
        P("shard", None),
        P("shard", None),
        P("shard"),
        P("shard", None),
        P("shard", None),
        P("shard", None),
    )
    return jax.shard_map(
        functools.partial(body, links),
        mesh=mesh,
        in_specs=in_specs,
        out_specs=out_specs,
        check_vma=False,
    )
```

```python
import functools
import math

import jax
import jax.numpy as jnp
from jax import lax
from jax.experimental import pallas as pl
from jax.experimental.pallas import tpu as pltpu
from jax.sharding import PartitionSpec as P

HEADS = 32
KV_HEADS = 8
HEAD_DIM = 64
PAIR = 2 * HEAD_DIM
GROUP = HEADS // KV_HEADS

EPSILON = 1e-05
RESIDUAL = 0.22
ATTN_SCALE = 0.015625
ROPE_BASE = 10000000.0
NEGATIVE = -1e30
BF16 = jnp.bfloat16
F32 = jnp.float32


def dot_nt(left, right):
    return lax.dot_general(left, right, (((1,), (1,)), ((), ())), preferred_element_type=F32)


def dot_nn(left, right):
    return lax.dot_general(left, right, (((1,), (0,)), ((), ())), preferred_element_type=F32)


def dot_tn(left, right):
    return lax.dot_general(left, right, (((0,), (0,)), ((), ())), preferred_element_type=F32)


def tree_layout(segment_row, parent_row):
    seg_numbers = jnp.arange(parent_row.shape[0], dtype=jnp.int32)
    member = (segment_row[:, None] == seg_numbers[None, :]).astype(jnp.int32)
    lengths = jnp.sum(member, axis=0)
    earlier = seg_numbers[None, :] < seg_numbers[:, None]
    starts = jnp.sum(jnp.where(earlier, lengths[None, :], 0), axis=1)
    parent_hit = parent_row[:, None] == seg_numbers[None, :]
    grandparent = jnp.sum(jnp.where(parent_hit, parent_row[None, :], 0), axis=1)
    itself = seg_numbers[:, None] == seg_numbers[None, :]
    related = itself | parent_hit | (grandparent[:, None] == seg_numbers[None, :])
    before = jnp.sum(jnp.where(related & jnp.logical_not(itself), lengths[None, :], 0), axis=1)
    shift = jnp.sum(member * (before - starts)[None, :], axis=1)
    position = jnp.arange(segment_row.shape[0], dtype=jnp.int32) + shift
    pad = ((0, 0), (0, PAIR - parent_row.shape[0]))
    sees = dot_nn(member.astype(BF16), related.astype(BF16)).astype(BF16)
    return position, jnp.pad(member.astype(BF16), pad), jnp.pad(sees, pad)


def rope_tables(position):
    lane = jnp.arange(PAIR, dtype=jnp.int32) % HEAD_DIM
    half = HEAD_DIM // 2
    fraction = (lane % half).astype(F32) * (2.0 / HEAD_DIM)
    freq = jnp.exp(-math.log(ROPE_BASE) * fraction)
    angle = position.astype(F32)[:, None] * freq[None, :]
    return jnp.cos(angle), jnp.sin(angle) * jnp.where(lane < half, -1.0, 1.0)[None, :]


MESH = pl.DeviceIdType.MESH
CHUNK = 64
SLOTS = 4


def remote(source, target, sems, index, device):
    return pltpu.make_async_remote_copy(
        source, target, sems.at[0, index], sems.at[1, index], device_id=device, device_id_type=MESH
    )


class GatherJob:
    def __init__(self, own, trees):
        self.operand = own
        self.trees = trees
        self.rows, self.width = own.shape[0] // trees, own.shape[1]
        self.chunks = self.rows // CHUNK
        self.out_shape = jax.ShapeDtypeStruct((4 * own.shape[0], self.width), own.dtype)
        self.out_spec = pl.BlockSpec(memory_space=pl.ANY)

    def scratch(self):
        return [
            pltpu.SemaphoreType.DMA((2, 3 * self.chunks * self.trees)),
            pltpu.SemaphoreType.DMA((self.trees,)),
        ]

    def bind(self, operand, out, scratch, x, y):
        sems, local = scratch
        n, rows = self.chunks, self.rows
        self.local, self.to_x, self.to_y, self.on_x, self.on_y = [], [], [], [], []
        for t in range(self.trees):
            at = lambda block, j: out.at[pl.ds((4 * t + block) * rows + j * CHUNK, CHUNK), :]
            own = lambda j: operand.at[pl.ds(t * rows + j * CHUNK, CHUNK), :]
            sem = 3 * n * t
            self.local.append(
                pltpu.make_async_copy(
                    operand.at[pl.ds(t * rows, rows), :],
                    out.at[pl.ds(4 * t * rows, rows), :],
                    local.at[t],
                )
            )
            self.to_x.append([remote(own(j), at(1, j), sems, sem + j, x) for j in range(n)])
            self.to_y.append([remote(own(j), at(2, j), sems, sem + n + j, y) for j in range(n)])
            on = lambda block, j, to: remote(at(block, j), at(3, j), sems, sem + 2 * n + j, to)
            self.on_x.append([on(2, j, x) for j in range(n // 2)])
            self.on_y.append([on(1, j, y) for j in range(n // 2, n)])

    def begin(self):
        n = self.chunks
        half = n // 2
        for t in range(self.trees):
            for k in range(n):
                self.to_x[t][(k + half) % n].start()
                self.to_y[t][k].start()
            self.local[t].start()

    def stages(self):
        def stage(t, k):
            half = self.chunks // 2
            self.to_y[t][k].wait_recv()
            self.on_x[t][k].start()
            self.to_x[t][half + k].wait_recv()
            self.on_y[t][k].start()

        return [
            functools.partial(stage, t, k)
            for t in range(self.trees)
            for k in range(self.chunks // 2)
        ]

    def finish(self):
        half = self.chunks // 2
        for t in range(self.trees):
            for copy in self.to_x[t][:half] + self.to_y[t][half:] + self.on_x[t] + self.on_y[t]:
                copy.wait_recv()
            for copy in self.to_x[t] + self.to_y[t] + self.on_x[t] + self.on_y[t]:
                copy.wait_send()
            self.local[t].wait()


class SmallJob:
    def __init__(self, own):
        self.operand = own
        self.rows, self.width = own.shape
        self.out_shape = jax.ShapeDtypeStruct((4 * self.rows, self.width), own.dtype)
        self.out_spec = pl.BlockSpec(memory_space=pl.ANY)

    def scratch(self):
        return [pltpu.SemaphoreType.DMA((2, 3)), pltpu.SemaphoreType.DMA(())]

    def bind(self, operand, out, scratch, x, y):
        sems, local = scratch
        shard = lax.axis_index("shard")
        mine = out.at[pl.ds(pl.multiple_of(shard * self.rows, self.rows), self.rows), :]
        self.local = pltpu.make_async_copy(operand, mine, local)
        self.sends = [
            remote(operand, mine, sems, k, device)
            for k, device in enumerate((x, y, (3 - shard, x[1])))
        ]

    def begin(self):
        for send in self.sends:
            send.start()
        self.local.start()

    def stages(self):
        return []

    def finish(self):
        for send in self.sends:
            send.wait()
        self.local.wait()


class SumJob:
    def __init__(self, part, trees, tree):
        self.operand = part
        self.rows, self.width = part.shape[0] // 4 // trees, part.shape[1]
        self.base = 4 * self.rows * tree
        self.half = self.rows // 2
        self.chunks = self.half // CHUNK
        self.out_shape = jax.ShapeDtypeStruct((self.rows, self.width), F32)
        self.out_spec = pl.BlockSpec((self.rows, self.width), lambda *_: (0, 0))

    def scratch(self):
        return [
            pltpu.VMEM((4, self.half, self.width), BF16),
            pltpu.VMEM((6, self.half, self.width), BF16),
            pltpu.SemaphoreType.DMA((2, 6 * self.chunks)),
            pltpu.SemaphoreType.DMA((4,)),
        ]

    def bind(self, part, out, scratch, x, y):
        self.out = out
        self.mine, self.got, sems, local = scratch
        n, half = self.chunks, self.half
        rows = lambda block, second: pl.ds(self.base + block * self.rows + second * half, half)
        piece = lambda block, second, j: part.at[
            pl.ds(self.base + block * self.rows + second * half + j * CHUNK, CHUNK), :
        ]
        here = lambda ref, k, j: ref.at[k, pl.ds(j * CHUNK, CHUNK), :]
        self.loads = [
            pltpu.make_async_copy(part.at[rows(block, second), :], self.mine.at[k], local.at[k])
            for k, (block, second) in enumerate(((0, 0), (0, 1), (2, 0), (1, 1)))
        ]
        send = lambda k, source, device: [
            remote(source(j), here(self.got, k, j), sems, k * n + j, device) for j in range(n)
        ]
        self.sends = [
            send(0, lambda j: piece(1, 0, j), x),
            send(1, lambda j: piece(3, 0, j), x),
            send(2, lambda j: here(self.mine, 2, j), y),
            send(3, lambda j: piece(2, 1, j), y),
            send(4, lambda j: piece(3, 1, j), y),
            send(5, lambda j: here(self.mine, 3, j), x),
        ]

    def begin(self):
        for j in range(self.chunks):
            self.sends[1][j].start()
            self.sends[4][j].start()
        for load in self.loads:
            load.start()
        for j in range(self.chunks):
            self.sends[0][j].start()
            self.sends[3][j].start()

    def stages(self):
        def stage(j):
            if j == 0:
                for load in self.loads:
                    load.wait()
            rows = pl.ds(j * CHUNK, CHUNK)
            for first, second, own in ((1, 2, 2), (4, 5, 3)):
                self.sends[first][j].wait_recv()
                total = self.mine[own, rows, :].astype(F32) + self.got[first, rows, :].astype(F32)
                self.mine[own, rows, :] = total.astype(BF16)
                self.sends[second][j].start()

        return [functools.partial(stage, j) for j in range(self.chunks)]

    def finish(self):
        for j in range(self.chunks):
            rows = pl.ds(j * CHUNK, CHUNK)
            for own, one, two in ((0, 0, 2), (1, 3, 5)):
                self.sends[one][j].wait_recv()
                self.sends[two][j].wait_recv()
                self.out[pl.ds(own * self.half + j * CHUNK, CHUNK), :] = (
                    self.mine[own, rows, :].astype(F32)
                    + self.got[one, rows, :].astype(F32)
                    + self.got[two, rows, :].astype(F32)
                )
        for copies in self.sends:
            for copy in copies:
                copy.wait_send()


class LineJob:
    LINE_ROWS = 32
    BATCH = 4
    LAG = 2

    def __init__(self, grad):
        self.operand = grad
        self.half, self.width = grad.shape[0] // 2, grad.shape[1]
        self.chunks = self.half // self.LINE_ROWS
        self.batches = self.chunks // self.BATCH
        self.steps = self.chunks + 1 + 3 * self.LAG
        self.out_shape = jax.ShapeDtypeStruct(grad.shape, BF16)
        self.out_spec = pl.BlockSpec(memory_space=pl.ANY)

    def scratch(self):
        place = lambda: pltpu.VMEM((self.half, self.width), BF16)
        return [place(), place(), place(), place(), pltpu.SemaphoreType.DMA((9, self.chunks))]

    def bind(self, grad, out, scratch, x, y):
        self.grad, self.out = grad, out
        self.from_core, self.own, self.from_line, self.from_inner, self.sems = scratch
        shard, place = lax.axis_index("shard"), lax.axis_index("replica")
        self.core, z = place % 2, place // 2
        self.inner = (z == 1) | (z == 2)
        self.outer = (z == 0) | (z == 3)
        self.twin = (shard, z * 2 + 1 - self.core)
        self.pair = (shard, (z + 1 - 2 * (z % 2)) * 2 + self.core)
        self.across = (shard, (3 - z) * 2 + self.core)

    def chunk(self, c):
        return pl.ds(pl.multiple_of(c * self.LINE_ROWS, self.LINE_ROWS), self.LINE_ROWS)

    def batch(self, b):
        size = self.BATCH * self.LINE_ROWS
        return pl.ds(pl.multiple_of(b * size, size), size)

    def at(self, core, b):
        size = self.BATCH * self.LINE_ROWS
        return pl.ds(pl.multiple_of(core * self.half + b * size, size), size)

    def send(self, source, target, index, arrival, device, c):
        return pltpu.make_async_remote_copy(
            source,
            target,
            self.sems.at[index, c],
            self.sems.at[arrival, c],
            device_id=device,
            device_id_type=MESH,
        )

    def to_twin(self, b):
        source = self.grad.at[self.at(1 - self.core, b), :]
        return self.send(source, self.from_core.at[self.batch(b), :], 0, 1, self.twin, b)

    def load(self, b):
        source = self.grad.at[self.at(self.core, b), :]
        return pltpu.make_async_copy(source, self.own.at[self.batch(b), :], self.sems.at[2, b])

    def inward(self, c):
        rows = self.chunk(c)
        return self.send(self.own.at[rows, :], self.from_line.at[rows, :], 3, 4, self.pair, c)

    def between(self, c):
        rows = self.chunk(c)
        return self.send(self.own.at[rows, :], self.from_inner.at[rows, :], 3, 5, self.across, c)

    def outward(self, c):
        rows = self.chunk(c)
        return self.send(self.from_core.at[rows, :], self.from_line.at[rows, :], 6, 4, self.pair, c)

    def store(self, source, b):
        target = self.out.at[self.at(self.core, b), :]
        return pltpu.make_async_copy(source.at[self.batch(b), :], target, self.sems.at[2, b])

    def give(self, source, b):
        target = self.out.at[self.at(self.core, b), :]
        return self.send(source.at[self.batch(b), :], target, 7, 8, self.twin, b)

    def hand_out(self, source, c):
        @pl.when(c % self.BATCH == self.BATCH - 1)
        def _():
            self.store(source, c // self.BATCH).start()
            self.give(source, c // self.BATCH).start()

    def begin(self):
        pass

    def stages(self):
        return []

    def step(self, s):
        n, lag = self.chunks, self.LAG
        live = lambda begin: (s >= begin) & (s < n + begin)
        add = lambda a, b: (a.astype(F32) + b.astype(F32)).astype(BF16)

        @pl.when(live(0) & (s % self.BATCH == 0))
        def _():
            self.to_twin(s // self.BATCH).start()
            self.load(s // self.BATCH).start()

        @pl.when(live(1))
        def _():
            c = s - 1
            rows = self.chunk(c)

            @pl.when(c % self.BATCH == 0)
            def _():
                self.to_twin(c // self.BATCH).wait()
                self.load(c // self.BATCH).wait()

            self.own[rows, :] = add(self.own[rows, :], self.from_core[rows, :])
            pl.when(self.outer)(lambda: self.inward(c).start())

        @pl.when(live(1 + lag) & self.inner)
        def _():
            c = s - 1 - lag
            rows = self.chunk(c)
            self.inward(c).wait_recv()
            self.own[rows, :] = add(self.own[rows, :], self.from_line[rows, :])
            self.between(c).start()

        @pl.when(live(1 + 2 * lag) & self.inner)
        def _():
            c = s - 1 - 2 * lag
            rows = self.chunk(c)
            self.between(c).wait_recv()
            self.from_core[rows, :] = add(self.own[rows, :], self.from_inner[rows, :])
            self.outward(c).start()
            self.hand_out(self.from_core, c)

        @pl.when(live(1 + 3 * lag) & self.outer)
        def _():
            c = s - 1 - 3 * lag
            self.outward(c).wait_recv()
            self.hand_out(self.from_line, c)

    def finish(self):
        def inside(b, carry):
            self.store(self.from_line, b).wait()
            self.give(self.from_line, b).wait()
            return carry

        def body(c, carry):
            @pl.when(self.inner)
            def _():
                self.between(c).wait_send()
                self.outward(c).wait_send()

            pl.when(self.outer)(lambda: self.inward(c).wait_send())
            return carry

        lax.fori_loop(0, self.batches, inside, 0)
        lax.fori_loop(0, self.chunks, body, 0)


class Comm:
    def __init__(self, jobs, number):
        self.jobs, self.number = jobs, number
        self.operands = [job.operand for job in jobs]
        self.in_specs = [pl.BlockSpec(memory_space=pl.ANY) for _ in jobs]
        self.out_specs = [job.out_spec for job in jobs]
        self.out_shapes = [job.out_shape for job in jobs]
        self.scratch = [entry for job in jobs for entry in job.scratch()]

    def enter(self, operands, outs, scratch, now):
        shard, replica = lax.axis_index("shard"), lax.axis_index("replica")
        x = (shard + 1 - 2 * (shard % 2), replica)
        y = ((shard + 2) % 4, replica)
        scratch = list(scratch)
        for job, operand, out in zip(self.jobs, operands, outs):
            count = len(job.scratch())
            job.bind(operand, out, scratch[:count], x, y)
            scratch = scratch[count:]

        lines = [job for job in self.jobs if isinstance(job, LineJob)]
        square = len(lines) < len(self.jobs)

        @pl.when(now)
        def _():
            barrier = pltpu.get_barrier_semaphore()

            def greet(device):
                pl.semaphore_signal(barrier, inc=1, device_id=device, device_id_type=MESH)

            near = ([x, y] if square else []) + ([lines[0].twin, lines[0].pair] if lines else [])
            if any(isinstance(job, SmallJob) for job in self.jobs):
                near.append((3 - shard, replica))
            for device in near:
                greet(device)
            if lines:

                @pl.when(lines[0].inner)
                def _():
                    greet(lines[0].across)
                    pl.semaphore_wait(barrier, len(near) + 1)

                @pl.when(lines[0].outer)
                def _():
                    pl.semaphore_wait(barrier, len(near))

            else:
                pl.semaphore_wait(barrier, len(near))
            for job in self.jobs:
                job.begin()

    def stages(self):
        return [stage for job in self.jobs for stage in job.stages()]

    def advance(self, slot, slots):
        stages = self.stages()
        for job in self.jobs:
            if isinstance(job, LineJob):

                def body(k, carry, job=job):
                    job.step(k)
                    return carry

                lax.fori_loop(slot * job.steps // slots, (slot + 1) * job.steps // slots, body, 0)
        for index, stage in enumerate(stages):
            if slots <= 4:
                due = slots - 1
            elif slots <= 8:
                due = slots * 3 // 4
            else:
                due = min(slots - 1, max(1, int(slots * (0.25 + 0.5 * index / len(stages)))))
            pl.when(slot == due)(stage)

    def finish(self, now):
        @pl.when(now)
        def _():
            for job in self.jobs:
                job.finish()


class NoComm:
    operands = in_specs = out_specs = out_shapes = scratch = ()
    number = None

    def enter(self, *_):
        pass

    def advance(self, *_):
        pass

    def finish(self, *_):
        pass


def comm_params(comm, vmem):
    if comm.number is None:
        return pltpu.CompilerParams(vmem_limit_bytes=vmem << 20)
    return pltpu.CompilerParams(
        vmem_limit_bytes=vmem << 20, collective_id=comm.number, has_side_effects=True
    )


def split_refs(refs, *counts):
    parts, begin = [], 0
    for count in counts:
        parts.append(refs[begin : begin + count])
        begin += count
    return parts


def transfer(comm):
    count = len(comm.operands)
    steps = max([1] + [job.steps for job in comm.jobs if isinstance(job, LineJob)])

    def kernel(*refs):
        operands, outs, scratch = split_refs(refs, count, count, len(comm.scratch))
        step = pl.program_id(0)
        comm.enter(operands, outs, scratch, step == 0)
        if steps == 1:
            for stage in comm.stages():
                stage()
        else:
            comm.advance(step, steps)
        comm.finish(step == steps - 1)

    return pl.pallas_call(
        kernel,
        grid=(steps,),
        in_specs=comm.in_specs,
        out_specs=comm.out_specs,
        out_shape=comm.out_shapes,
        scratch_shapes=comm.scratch,
        compiler_params=comm_params(comm, 48),
        name="transfer",
    )(*comm.operands)


def products(items, block, comm, joined=False):
    specs, shapes, out_specs, steps, rights = [], [], [], [], []
    begin = 0
    items = [
        (l if isinstance(l, tuple) else (l,), r if isinstance(r, tuple) else (r,), t)
        for l, r, t in items
    ]
    total = sum((l[0].shape[1] if t else l[0].shape[0]) // block for l, _, t in items)
    for left, right, transposed in items:
        size = left[0].shape[1] if transposed else left[0].shape[0]
        count = size // block

        def place(i, begin=begin, count=count):
            return jnp.clip(i - begin, 0, count - 1)

        for l in left:
            if transposed:
                specs.append(pl.BlockSpec((l.shape[0], block), lambda i, p=place: (0, p(i))))
            else:
                specs.append(pl.BlockSpec((block, l.shape[1]), lambda i, p=place: (p(i), 0)))
        columns = right[0].shape[1]
        if not joined:
            out_specs.append(pl.BlockSpec((block, columns), lambda i, p=place: (p(i), 0)))
            shapes.append(jax.ShapeDtypeStruct((size, columns), BF16))
        for r in right:
            if not any(r is other for other in rights):
                rights.append(r)
        steps.append((begin, count))
        begin += count
    right_specs = [
        pl.BlockSpec(r.shape, lambda i: (0, 0), pipeline_mode=pl.Buffered(1)) for r in rights
    ]
    which = [
        [next(k for k, other in enumerate(rights) if other is r) for r in right]
        for _, right, _ in items
    ]
    firsts = [sum(len(l) for l, _, _ in items[:k]) for k in range(len(items))]
    n = sum(len(l) for l, _, _ in items)
    slots = 1 if comm.number is None else SLOTS
    if joined:
        width = items[0][1][0].shape[1]
        out_specs = [pl.BlockSpec((block, width), lambda i: (i, 0))]
        shapes = [jax.ShapeDtypeStruct((total * block, width), BF16)]
    made = len(shapes)

    def kernel(*refs):
        lefts, held, operands, outs, comm_outs, scratch = split_refs(
            refs, n, len(rights), len(comm.operands), made, len(comm.operands), len(comm.scratch)
        )
        step = pl.program_id(0)
        comm.enter(operands, comm_outs, scratch, step == 0)
        width = items[0][1][0].shape[1] // slots

        def part(slot, carry):
            comm.advance(step * slots + slot, total * slots)
            columns = pl.ds(pl.multiple_of(slot * width, width), width)
            for k, (left, right, transposed) in enumerate(items):
                begin, count = steps[k]

                @pl.when((step >= begin) & (step < begin + count))
                def _(k=k, left=left, right=right, transposed=transposed):
                    dot = dot_tn if transposed else dot_nn
                    result, pieces = 0.0, max(len(left), len(right))
                    for piece in range(pieces):
                        l, r = lefts[firsts[k] + piece % len(left)], held[which[k][piece % len(right)]]
                        share = pl.ds(piece * (r.shape[0] // pieces), r.shape[0] // pieces)
                        ours = pl.ds(piece * (l.shape[0] // pieces), l.shape[0] // pieces)
                        result += dot(
                            l[ours, :] if len(left) < pieces else l[...],
                            r[share, columns] if len(right) < pieces else r[:, columns],
                        )
                    outs[0 if joined else k][:, columns] = result.astype(BF16)

            return carry

        lax.fori_loop(0, slots, part, 0)

        comm.finish(step == total - 1)

    flops = 2 * sum(math.prod(l.shape) * right[0].shape[1] for left, right, _ in items for l in left)
    out = pl.pallas_call(
        kernel,
        grid=(total,),
        in_specs=specs + right_specs + list(comm.in_specs),
        out_specs=out_specs + list(comm.out_specs),
        out_shape=shapes + list(comm.out_shapes),
        scratch_shapes=list(comm.scratch),
        compiler_params=comm_params(comm, 58),
        cost_estimate=pl.CostEstimate(flops=flops, bytes_accessed=30_000_000, transcendentals=0),
        name="products",
    )(*[l for left, _, _ in items for l in left], *rights, *comm.operands)
    return out[:made], out[made:]


def feed_forward(rows_all, w_gate, w_up, block, comm):
    rows, width = rows_all.shape
    units = w_gate.shape[0]
    steps = units // block
    part = rows // SLOTS

    def kernel(*refs):
        inputs, operands, outs, comm_outs, scratch = split_refs(
            refs, 3, len(comm.operands), 3, len(comm.operands), len(comm.scratch)
        )
        x_ref, gate_w, up_w = inputs
        gate_ref, upper_ref, hidden_ref = outs
        step = pl.program_id(0)
        comm.enter(operands, comm_outs, scratch, step == 0)
        comm.advance(step, steps)
        for slot in range(SLOTS):
            here = pl.ds(slot * part, part)
            gate = dot_nt(x_ref[here, :], gate_w[...])
            upper = dot_nt(x_ref[here, :], up_w[...])
            gate_ref[here, :] = gate.astype(BF16)
            upper_ref[here, :] = upper.astype(BF16)
            hidden_ref[here, :] = (gate * jax.nn.sigmoid(gate) * upper).astype(BF16)
        comm.finish(step == steps - 1)

    out = pl.pallas_call(
        kernel,
        grid=(steps,),
        in_specs=[
            pl.BlockSpec((rows, width), lambda i: (0, 0), pipeline_mode=pl.Buffered(1)),
            pl.BlockSpec((block, width), lambda i: (i, 0)),
            pl.BlockSpec((block, width), lambda i: (i, 0)),
            *comm.in_specs,
        ],
        out_specs=[pl.BlockSpec((rows, block), lambda i: (0, i))] * 3 + list(comm.out_specs),
        out_shape=[jax.ShapeDtypeStruct((rows, units), BF16)] * 3 + list(comm.out_shapes),
        scratch_shapes=list(comm.scratch),
        compiler_params=comm_params(comm, 56),
        cost_estimate=pl.CostEstimate(
            flops=4 * rows * width * units, bytes_accessed=48_000_000, transcendentals=rows * units
        ),
        name="feed_forward",
    )(rows_all, w_gate, w_up, *comm.operands)
    return out[:3], out[3:]


def swap_halves(block):
    lane = lax.broadcasted_iota(jnp.int32, block.shape, 1)
    half = HEAD_DIM // 2
    up = pltpu.roll(block, PAIR - half, 1)
    down = pltpu.roll(block, half, 1)
    return jnp.where(lane % HEAD_DIM < half, up, down)


def turn(block, cosine, sine):
    return block * cosine + swap_halves(block) * sine


def place_heads(wide, kv_heads, fill):
    placed = []
    for g in range(kv_heads):
        base = wide[:, (g // 2) * PAIR : (g // 2) * PAIR + PAIR] if wide.shape[1] >= PAIR else wide
        lane = lax.broadcasted_iota(jnp.int32, base.shape, 1)
        moved = pltpu.roll(base, HEAD_DIM, 1)
        for p in range(2):
            source = base if g % 2 == p else moved
            inside = (lane // HEAD_DIM) == p
            placed.append(jnp.where(inside, source, jnp.full_like(source, fill)))
    return placed


def attention_forward_kernel(kv_heads, blocks, place, comm, *refs):
    jobs = len(comm.operands)
    inputs, operands, outs, comm_outs, own, scratch = split_refs(
        refs, 6, jobs, 4, jobs, 3, len(comm.scratch)
    )
    q_ref, kv_ref, cos_ref, sin_ref, member_ref, sees_ref = inputs
    out_ref, q_out_ref, kv_out_ref, lse_ref = outs
    keys, values, bias = own
    step = pl.program_id(0)
    comm.enter(operands, comm_outs, scratch, step == 0)
    comm.advance(step, blocks)
    tree = q_ref.shape[0]
    rows = tree // blocks
    kv_width = kv_heads * HEAD_DIM

    @pl.when(step == 0)
    def _():
        for b in range(blocks):
            here = pl.ds(b * rows, rows)
            raw = kv_ref[pl.ds(pl.multiple_of(place(b) * rows, rows), rows), :]
            cosine, sine = cos_ref[here, :], sin_ref[here, :]
            if kv_width >= PAIR:
                turned = jnp.concatenate(
                    [
                        turn(raw[:, c : c + PAIR], cosine, sine)
                        for c in range(0, kv_width, PAIR)
                    ],
                    axis=1,
                )
                plain = raw[:, kv_width:]
            else:
                lane = lax.broadcasted_iota(jnp.int32, raw.shape, 1)
                turned = turn(raw, cosine, sine)
                plain = pltpu.roll(raw, HEAD_DIM, 1)
                both = jnp.where(lane < HEAD_DIM, turned, raw)
            if kv_width >= PAIR:
                both = jnp.concatenate([turned, plain], axis=1)
            kv_out_ref[here, :] = both.astype(BF16)
            for index, placed in enumerate(place_heads(turned, kv_heads, 0.0)):
                keys[index, here, :] = placed.astype(BF16)
            for index, placed in enumerate(place_heads(plain, kv_heads, 1.0)):
                values[index, here, :] = placed.astype(BF16)

    here = pl.ds(pl.multiple_of(step * rows, rows), rows)
    there = pl.ds(pl.multiple_of(place(step) * rows, rows), rows)
    cosine, sine = cos_ref[here, :], sin_ref[here, :]
    for j in range(q_ref.shape[1] // PAIR):
        lanes = slice(j * PAIR, j * PAIR + PAIR)
        turned = turn(q_ref[there, lanes], cosine, sine).astype(BF16)
        q_out_ref[:, lanes] = turned * BF16(ATTN_SCALE)

    link = dot_nt(sees_ref[here, :], member_ref[...])
    row_index = lax.broadcasted_iota(jnp.int32, (rows, tree), 0) + step * rows
    col_index = lax.broadcasted_iota(jnp.int32, (rows, tree), 1)
    bias[...] = jnp.where((link > 0.5) & (col_index <= row_index), 0.0, NEGATIVE)

    lane = lax.broadcasted_iota(jnp.int32, (rows, PAIR), 1)
    for block in range(blocks):
        width = (block + 1) * rows

        @pl.when(step == block)
        def _(width=width):
            lse = jnp.zeros((rows, PAIR), F32)
            for j in range(q_ref.shape[1] // PAIR):
                lanes = slice(j * PAIR, j * PAIR + PAIR)
                group = 2 * j // GROUP
                mixed, tops = [], []
                for p in range(2):
                    scores = dot_nt(q_out_ref[:, lanes], keys[group * 2 + p, :width, :])
                    scores = scores + bias[:, :width]
                    top = jnp.max(scores, axis=1, keepdims=True)
                    expo = jnp.exp(scores - top).astype(BF16)
                    mixed.append(dot_nn(expo, values[group * 2 + p, :width, :]))
                    tops.append(top)
                upper = lane >= HEAD_DIM
                total = pltpu.roll(jnp.where(upper, mixed[0], mixed[1]), HEAD_DIM, 1)
                out_ref[there, lanes] = (jnp.where(upper, mixed[1], mixed[0]) / total).astype(BF16)
                logs = jnp.log(total)
                lse = jnp.where(lane == 2 * j, tops[0] + logs[:, :1], lse)
                lse = jnp.where(lane == 2 * j + 1, tops[1] + logs[:, HEAD_DIM : HEAD_DIM + 1], lse)
            lse_ref[...] = lse

    comm.finish(step == blocks - 1)


def attention_forward(place, qkv, cosine, sine, member, sees, q_width, blocks, comm):
    tree = qkv.shape[0]
    rows = tree // blocks
    kv_width = (qkv.shape[1] - q_width) // 2
    kv_heads = kv_width // HEAD_DIM
    whole = lambda width: pl.BlockSpec((tree, width), lambda i: (0, 0))
    natural = lambda width: pl.BlockSpec((rows, width), lambda i: (i, 0))
    out = pl.pallas_call(
        functools.partial(attention_forward_kernel, kv_heads, blocks, place, comm),
        grid_spec=pl.GridSpec(
            grid=(blocks,),
            in_specs=[
                whole(q_width),
                pl.BlockSpec((tree, 2 * kv_width), lambda i: (0, q_width // (2 * kv_width))),
                whole(PAIR),
                whole(PAIR),
                whole(PAIR),
                whole(PAIR),
                *comm.in_specs,
            ],
            out_specs=[
                whole(q_width),
                natural(q_width),
                whole(2 * kv_width),
                natural(PAIR),
                *comm.out_specs,
            ],
            scratch_shapes=[
                pltpu.VMEM((2 * kv_heads, tree, PAIR), BF16),
                pltpu.VMEM((2 * kv_heads, tree, PAIR), BF16),
                pltpu.VMEM((rows, tree), F32),
                *comm.scratch,
            ],
        ),
        out_shape=[
            jax.ShapeDtypeStruct((tree, q_width), BF16),
            jax.ShapeDtypeStruct((tree, q_width), BF16),
            jax.ShapeDtypeStruct((tree, 2 * kv_width), BF16),
            jax.ShapeDtypeStruct((tree, PAIR), F32),
            *comm.out_shapes,
        ],
        compiler_params=comm_params(comm, 58),
        cost_estimate=pl.CostEstimate(
            flops=10_000_000_000, bytes_accessed=12_000_000, transcendentals=5_000_000
        ),
        name="attention_forward",
    )(qkv, qkv, cosine, sine, member, sees, *comm.operands)
    return out[:4], out[4:]


def attention_backward_kernel(kv_heads, blocks, trees, place, comm, *refs):
    jobs = len(comm.operands)
    inputs, operands, outs, comm_outs, own, scratch = split_refs(
        refs, 8 * trees, jobs, 1, jobs, 6, len(comm.scratch)
    )
    pairs = inputs[1].shape[1] // PAIR
    each = blocks * pairs
    step = pl.program_id(0)
    comm.enter(operands, comm_outs, scratch, step == 0)
    comm.advance(step, each * trees)
    for t in range(trees):

        @pl.when((step >= t * each) & (step < (t + 1) * each))
        def _(t=t):
            local = step - t * each
            attention_backward_step(
                kv_heads,
                blocks,
                pairs,
                place,
                local // pairs,
                local % pairs,
                t,
                inputs[8 * t : 8 * t + 8],
                outs[0],
                own,
            )

    comm.finish(step == each * trees - 1)


def attention_backward_step(kv_heads, blocks, pairs, place, step, j, t, inputs, out_ref, own):
    grad_ref, q_ref, kv_ref, lse_ref, cos_ref, sin_ref, member_ref, sees_ref = inputs
    keys, values, bias, lse_rows, key_sum, value_sum = own
    tree, rows = grad_ref.shape[0], q_ref.shape[0]
    kv_width = kv_heads * HEAD_DIM
    q_width = q_ref.shape[1]
    base = t * tree

    @pl.when((step == 0) & (j == 0))
    def _():
        for b in range(blocks):
            here = pl.ds(b * rows, rows)
            both = kv_ref[here, :].astype(F32)
            if kv_width >= PAIR:
                turned, plain = both[:, :kv_width], both[:, kv_width:]
            else:
                turned, plain = both, pltpu.roll(both, HEAD_DIM, 1)
            for index, placed in enumerate(place_heads(turned, kv_heads, 0.0)):
                keys[index, here, :] = placed.astype(BF16)
            for index, placed in enumerate(place_heads(plain, kv_heads, 0.0)):
                values[index, here, :] = placed.astype(BF16)
        key_sum[...] = jnp.zeros_like(key_sum)
        value_sum[...] = jnp.zeros_like(value_sum)

    here = pl.ds(pl.multiple_of(step * rows, rows), rows)

    @pl.when(j == 0)
    def _():
        link = dot_nt(member_ref[...], sees_ref[here, :])
        key_index = lax.broadcasted_iota(jnp.int32, (tree, rows), 0)
        query_index = lax.broadcasted_iota(jnp.int32, (tree, rows), 1) + step * rows
        bias[...] = jnp.where((link > 0.5) & (key_index <= query_index), 0.0, NEGATIVE)
        lse_rows[...] = jnp.transpose(lse_ref[...])

    there = pl.ds(pl.multiple_of(place(step) * rows, rows), rows)
    out_rows = pl.ds(pl.multiple_of(base + place(step) * rows, rows), rows)
    lanes = pl.ds(pl.multiple_of(j * PAIR, PAIR), PAIR)
    group = 2 * j // GROUP
    for block in range(blocks):
        width = (block + 1) * rows

        @pl.when(step == block)
        def _(width=width):
            cosine, sine = cos_ref[here, :], sin_ref[here, :]
            query, grad = q_ref[:, lanes], grad_ref[there, lanes]
            dq = jnp.zeros((rows, PAIR), F32)
            for p in range(2):
                index = group * 2 + p
                scores = dot_nt(keys[index, :width, :], query) + bias[:width, :]
                probs = jnp.exp(scores - lse_rows[pl.ds(2 * j + p, 1), :])
                probs_grad = dot_nt(values[index, :width, :], grad)
                value_sum[index, :width, :] += dot_nn(probs.astype(BF16), grad)
                weighted = probs * probs_grad
                delta = jnp.sum(weighted, axis=0, keepdims=True)
                score_grad = (weighted - probs * delta).astype(BF16)
                key_sum[index, :width, :] += dot_nn(score_grad, query)
                dq = dq + dot_tn(score_grad, keys[index, :width, :])
            out_ref[out_rows, lanes] = turn(dq * ATTN_SCALE, cosine, -sine).astype(BF16)

    @pl.when((step == blocks - 1) & (j == pairs - 1))
    def _():
        for b in range(blocks):
            here = pl.ds(b * rows, rows)
            there = pl.ds(pl.multiple_of(base + place(b) * rows, rows), rows)
            cosine, sine = cos_ref[here, :], sin_ref[here, :]
            lane = lax.broadcasted_iota(jnp.int32, (rows, PAIR), 1)
            lower = lane < HEAD_DIM
            for c in range(0, kv_heads, 2):
                halves = []
                for acc in (key_sum, value_sum):
                    own, other = [], []
                    for g in range(c, min(c + 2, kv_heads)):
                        own.append(acc[g * 2, here, :])
                        other.append(acc[g * 2 + 1, here, :])
                    first = own[0] + pltpu.roll(other[0], HEAD_DIM, 1)
                    if len(own) == 2:
                        second = other[1] + pltpu.roll(own[1], HEAD_DIM, 1)
                    else:
                        second = first
                    halves.append(jnp.where(lower, first, second))
                turned = turn(halves[0], cosine, -sine)
                if kv_width >= PAIR:
                    begin = q_width + c * HEAD_DIM
                    out_ref[there, begin : begin + PAIR] = turned.astype(BF16)
                    begin += kv_width
                    out_ref[there, begin : begin + PAIR] = halves[1].astype(BF16)
                else:
                    moved = pltpu.roll(halves[1], HEAD_DIM, 1)
                    both = jnp.where(lower, turned, moved)
                    out_ref[there, q_width : q_width + PAIR] = both.astype(BF16)


def attention_backward(place, arrays, blocks, comm):
    trees = len(arrays)
    tree, q_width = arrays[0][1].shape
    rows = tree // blocks
    kv_width = arrays[0][2].shape[1] // 2
    kv_heads = kv_width // HEAD_DIM
    each = blocks * (q_width // PAIR)
    whole = lambda width: pl.BlockSpec((tree, width), lambda i: (0, 0))

    def natural(width, t):
        return pl.BlockSpec(
            (rows, width),
            lambda i: (jnp.clip((i - t * each) // (q_width // PAIR), 0, blocks - 1), 0),
        )

    in_specs = []
    for t in range(trees):
        in_specs += [whole(q_width), natural(q_width, t), whole(2 * kv_width), natural(PAIR, t)]
        in_specs += [whole(PAIR)] * 4
    total = q_width + 2 * kv_width
    out = pl.pallas_call(
        functools.partial(attention_backward_kernel, kv_heads, blocks, trees, place, comm),
        grid=(each * trees,),
        in_specs=in_specs + list(comm.in_specs),
        out_specs=[pl.BlockSpec((trees * tree, total), lambda i: (0, 0))] + list(comm.out_specs),
        out_shape=[jax.ShapeDtypeStruct((trees * tree, total), BF16)] + list(comm.out_shapes),
        scratch_shapes=[
            pltpu.VMEM((2 * kv_heads, tree, PAIR), BF16),
            pltpu.VMEM((2 * kv_heads, tree, PAIR), BF16),
            pltpu.VMEM((tree, rows), F32),
            pltpu.VMEM((PAIR, rows), F32),
            pltpu.VMEM((2 * kv_heads, tree, PAIR), F32),
            pltpu.VMEM((2 * kv_heads, tree, PAIR), F32),
            *comm.scratch,
        ],
        compiler_params=comm_params(comm, 60),
        cost_estimate=pl.CostEstimate(
            flops=40_000_000_000, bytes_accessed=24_000_000, transcendentals=10_000_000
        ),
        name="attention_backward",
    )(*[array for per_tree in arrays for array in per_tree], *comm.operands)
    return out[:1], out[1:]


def sync(*values):
    return lax.optimization_barrier(values)


class Square:
    def __init__(self, shard, replica):
        self.shard, self.replica = shard, replica
        self.x = [(i, i ^ 1) for i in range(shard)]
        self.y = [(i, i ^ 2) for i in range(shard)]
        self.d = [(i, i ^ 3) for i in range(shard)]

    def place(self, block):
        shard = lax.axis_index("shard")
        return (block + shard) % 2 + 2 * ((block // 2 + shard // 2) % 2)

    def reorder(self, blocks, axis):
        me = lax.axis_index("shard")
        return jnp.concatenate(
            [lax.dynamic_slice_in_dim(blocks, n ^ me, 1, axis) for n in range(self.shard)], axis=axis
        )

    def first(self, small, own):
        padded = jnp.pad(small, (0, -small.shape[0] % 2048)).reshape(16, -1)
        self.kernels += 1
        smalls, rows = transfer(Comm([SmallJob(padded), GatherJob(own, 1)], self.kernels))
        return smalls.reshape(self.shard, -1)[:, : small.shape[0]], rows

    def sum_small(self, values, beside):
        share = values.shape[1] // self.shard
        blocks = values.reshape(values.shape[0], self.shard, share)
        blocks = self.reorder(blocks, 1)
        hops = [[("shard", perm) for perm in (self.x, self.y, self.d)]]
        hops += [[("replica", [(i, i ^ k) for i in range(self.replica)])] for k in (1, 2, 4)]
        total, done = blocks[:, 0], []
        for number, hop in enumerate(hops):
            got = [
                lax.ppermute(blocks[:, k + 1] if number == 0 else total, axis, perm)
                for k, (axis, perm) in enumerate(hop)
            ]
            if number < len(beside):
                done.append(beside[number](total))
                got, done[-1] = sync(got, done[-1])
            total = total + sum(got)
        return total, done

    def carry(self, compute, gathers=(), sums=(), totals=()):
        jobs = [GatherJob(*own) for own in gathers] + [SumJob(*part) for part in sums]
        jobs += [LineJob(grad) for grad in totals]
        self.kernels += 1
        comm = Comm(jobs, self.kernels)
        if compute is None:
            results, moved = None, transfer(comm)
        else:
            results, moved = compute(comm)
        return (results, *map(list, split_refs(moved, len(gathers), len(sums), len(totals))))

    def start(self):
        self.kernels = 0


class General:
    def __init__(self, shard, replica):
        self.shard, self.replica = shard, replica

    def place(self, block):
        return block

    def first(self, small, own):
        rows = lax.all_gather(own, "shard", axis=0, tiled=True)
        return lax.all_gather(small, "shard", axis=0, tiled=False), rows

    def carry(self, compute, gathers=(), sums=(), totals=()):
        results = None if compute is None else compute(NoComm())[0]
        rows = lambda array, trees: array.reshape(trees, -1, array.shape[1])
        gathered = [
            lax.all_gather(rows(own, trees), "shard", axis=1, tiled=True).reshape(-1, own.shape[1])
            for own, trees in gathers
        ]
        summed = [
            lax.psum_scatter(
                rows(part, trees)[tree], "shard", scatter_dimension=0, tiled=True
            ).astype(F32)
            for part, trees, tree in sums
        ]
        return results, gathered, summed, [lax.psum(grad, "replica") for grad in totals]

    def sum_small(self, values, beside):
        share = lax.psum_scatter(values, "shard", scatter_dimension=1, tiled=True)
        return lax.psum(share, "replica"), [f(share) for f in beside]

    def start(self):
        pass


def rms_scale(values):
    return lax.rsqrt(jnp.mean(values * values, axis=-1, keepdims=True) + EPSILON)


def normalized(piece, gain):
    values = piece.astype(F32)
    return (values * rms_scale(values) * gain).astype(BF16)


def norm_back(values, scale, gain, grad_in):
    scaled = values * scale
    weighted = grad_in * gain
    back = scale * (weighted - scaled * jnp.mean(weighted * scaled, axis=-1, keepdims=True))
    return back, jnp.sum(grad_in * scaled, axis=0)


def body(
    links,
    tokens,
    gain_attn,
    w_query,
    w_key,
    w_value,
    w_out,
    gain_ff,
    w_gate,
    w_up,
    w_down,
    cotangent,
    segment_ids,
    parents,
):
    trees, _, own_rows, width = tokens.shape
    shard = links.shard
    q_width, kv_width = w_query.shape[0], w_key.shape[0]
    tree_rows = own_rows * shard
    links.start()
    share = gain_attn.shape[0]
    w_qkv = jnp.concatenate([w_query, w_key, w_value], axis=0)
    token_rows = [tokens[t, 0] for t in range(trees)]
    cot_rows = [cotangent[t, 0] for t in range(trees)]

    small = jnp.concatenate(
        [gain_attn, gain_ff] + [segment_ids[t, 0].astype(BF16) for t in range(trees)]
    )
    smalls, rows_0 = links.first(small, token_rows[0])
    gain_first = smalls[:, :share].reshape(width).astype(F32)
    gain_second = smalls[:, share : 2 * share].reshape(width).astype(F32)
    masks, tables = [], []
    for t in range(trees):
        begin = 2 * share + t * own_rows
        segments = smalls[:, begin : begin + own_rows].reshape(tree_rows).astype(jnp.int32)
        position, member, sees = tree_layout(segments, parents[t, 0])
        masks.append((member, sees))
        tables.append(rope_tables(position))

    def attention(t, qkv):
        return lambda comm: attention_forward(
            links.place, qkv, *tables[t], *masks[t], q_width, shard, comm
        )

    def after_attention(t, branch):
        value = token_rows[t].astype(F32) + RESIDUAL * branch
        scale = rms_scale(value)
        return value, scale, (value * scale * gain_second).astype(BF16)

    normed_0 = normalized(rows_0, gain_first)
    saved_0, (rows_1,), _, _ = links.carry(
        attention(0, dot_nt(normed_0, w_qkv)), gathers=[(token_rows[1], 1)]
    )
    part_0 = dot_nn(saved_0[0], w_out).astype(BF16)
    normed_1 = normalized(rows_1, gain_first)
    saved_1, _, (branch_0,), _ = links.carry(attention(1, dot_nt(normed_1, w_qkv)), sums=[(part_0, 1, 0)])
    part_1 = dot_nn(saved_1[0], w_out).astype(BF16)
    middle_0, scale_0, own_0 = after_attention(0, branch_0)
    _, _, (branch_1,), _ = links.carry(None, sums=[(part_1, 1, 0)])
    middle_1, scale_1, own_1 = after_attention(1, branch_1)
    own_all = jnp.concatenate([own_0, own_1], axis=0)
    _, (rows_all,), _, _ = links.carry(None, gathers=[(own_all, trees)])

    cot_own = jnp.concatenate([(RESIDUAL * cot.astype(F32)).astype(BF16) for cot in cot_rows], axis=0)
    (gate, upper, hidden), (cot_all,), _, _ = links.carry(
        lambda comm: feed_forward(rows_all, w_gate, w_up, 256, comm), gathers=[(cot_own, trees)]
    )
    grad_down = dot_tn(hidden, cot_all).astype(BF16)
    hidden_grad = dot_nt(cot_all, w_down)
    wide = gate.astype(F32)
    sigma = jax.nn.sigmoid(wide)
    gate_grad = (
        hidden_grad * upper.astype(F32) * sigma * (1.0 + wide * (1.0 - sigma))
    ).astype(BF16)
    up_grad = (hidden_grad * wide * sigma).astype(BF16)
    ff_part = (dot_nn(gate_grad, w_gate) + dot_nn(up_grad, w_up)).astype(BF16)
    parts = lambda whole: [(whole, trees, t) for t in range(trees)]
    (grad_gate, grad_up), _, ff_grad, (total_down,) = links.carry(
        lambda comm: products([(gate_grad, rows_all, True), (up_grad, rows_all, True)], 256, comm),
        sums=parts(ff_part),
        totals=[grad_down],
    )
    out_own, middle_grads = [], []
    gain_ff_sum = jnp.zeros((width,), F32)
    for t, (middle, scale) in enumerate(((middle_0, scale_0), (middle_1, scale_1))):
        middle_back, term = norm_back(middle, scale, gain_second, ff_grad[t])
        gain_ff_sum = gain_ff_sum + term
        middle_grads.append(cot_rows[t].astype(F32) + middle_back)
        out_own.append((RESIDUAL * middle_grads[t]).astype(BF16))
    (down_part,), (out_all,), _, (total_gate,) = links.carry(
        lambda comm: products([(hidden, w_down, False)], 256, comm),
        gathers=[(jnp.concatenate(out_own, axis=0), trees)],
        totals=[grad_gate],
    )
    arrays = []
    for t, (_, query, kv, lse) in enumerate((saved_0, saved_1)):
        attended_grad = dot_nt(out_all[t * tree_rows : (t + 1) * tree_rows], w_out).astype(BF16)
        arrays.append((attended_grad, query, kv, lse, *tables[t], *masks[t]))
    (qkv_grad,), _, downs, (total_up,) = links.carry(
        lambda comm: attention_backward(links.place, arrays, shard, comm),
        sums=parts(down_part),
        totals=[grad_up],
    )
    results = [
        (middle + RESIDUAL * down).astype(BF16) for middle, down in zip((middle_0, middle_1), downs)
    ]
    normed_part = dot_nn(qkv_grad, w_qkv).astype(BF16)
    (grad_attn,), _ = products(
        [
            ((saved_0[0], saved_1[0]), out_all, True),
            (qkv_grad, (normed_0, normed_1), True),
        ],
        128 if shard > 4 else 256,
        NoComm(),
        joined=True,
    )
    _, _, normed_grads, (total_attn,) = links.carry(
        None, sums=parts(normed_part), totals=[grad_attn]
    )
    input_grads = []
    gain_attn_sum = jnp.zeros((width,), F32)
    for t in range(trees):
        inputs = token_rows[t].astype(F32)
        input_back, term = norm_back(inputs, rms_scale(inputs), gain_first, normed_grads[t])
        gain_attn_sum = gain_attn_sum + term
        input_grads.append(middle_grads[t] + input_back)
    totals = (total_down, total_gate, total_up)

    def convert(index):
        return lambda after: sync(totals[index], after)[0].astype(F32)

    gains, converted = links.sum_small(
        jnp.stack([gain_attn_sum, gain_ff_sum]), [convert(0), convert(1), convert(2)]
    )
    rows = lambda begin, count: total_attn[begin : begin + count].astype(F32)
    return (
        jnp.stack(results)[:, None],
        jnp.stack(input_grads)[:, None],
        gains[0],
        rows(q_width, q_width),
        rows(2 * q_width, kv_width),
        rows(2 * q_width + kv_width, kv_width),
        rows(0, q_width),
        gains[1],
        converted[1],
        converted[2],
        converted[0],
    )


def solution(mesh):
    shard, replica = mesh.shape["shard"], mesh.shape["replica"]
    links = (Square if (shard, replica) == (4, 8) else General)(shard, replica)
    in_specs = (
        P(None, "replica", "shard", None),
        P("shard"),
        P("shard", None),
        P("shard", None),
        P("shard", None),
        P("shard", None),
        P("shard"),
        P("shard", None),
        P("shard", None),
        P("shard", None),
        P(None, "replica", "shard", None),
        P(None, "replica", "shard"),
        P(None, "replica", None),
    )
    out_specs = (
        P(None, "replica", "shard", None),
        P(None, "replica", "shard", None),
        P("shard"),
        P("shard", None),
        P("shard", None),
        P("shard", None),
        P("shard", None),
        P("shard"),
        P("shard", None),
        P("shard", None),
        P("shard", None),
    )
    return jax.shard_map(
        functools.partial(body, links),
        mesh=mesh,
        in_specs=in_specs,
        out_specs=out_specs,
        check_vma=False,
    )
```
